32 devices in a mesh: box: 8 (over z, y), dir: 4 (over x, core).
Axes of the slice: x: 2, y: 2, z: 4, core: 2. Of those that a mesh axis runs over, the one named last changes fastest.
Arguments:
- coarse_field: float32 [512, 2, 4, 2048], P('box', None, None, 'dir'), may hold values from -6 to 6
- trans_table: float32 [316, 2, 2048], P(None, None, 'dir'), may hold values from -1.5 to 1.5
- partner_ids: int32 [512, 30], P('box'), may hold values from 0 to 511, as said below
- partner_types: int32 [512, 30], P('box'), may hold values from 0 to 315
- partner_count: int32 [512], P('box'), may hold values from 15 to 30
- child_count: int32 [512], P('box'), may hold values from 1 to 7, as said below
- child_octant: int32 [2048], P('box'), may hold values from 0 to 7
- dir_angles: float32 [2, 2048], replicated, may hold values from -3.140625 to 3.140625
- stencil_ids: int32 [2048, 4], replicated, may hold values from 0 to 511, as said below
- stencil_weights: float32 [2048, 4], replicated, may hold values from -1.8 to 1.8
Outputs:
- fine_field: float32 [2048, 2, 4, 512], P(('box', 'dir'))
The draws below stay inside these ranges and needn't reach their ends.
Inputs may be any that keep to these rules, and one draw needn't show every extreme that they name: `partner_ids`: coarse box b sits on a grid whose z coordinate takes the two highest bits of b (the higher one as its bit 1) and whose x and y coordinates take the lower bits in turn (x from bit 0, y from bit 1, x from bit 2, and so on); the slots of b name distinct boxes that are children of neighbours of b's parent and not adjacent to b. `child_count`: each aligned block of 64 coarse boxes has exactly 256 children in all. stencil_ids[c, s] lies within 2 of c // 4, counted circularly over 512 directions.
All inputs are finite; a program needn't handle non-finite values.
Results may differ from the reference program's by a relative error of at most 0.0003.
Values sent between devices are 32-bit elements; how exact they have to be, the bound alone decides.
No kernel may reach another device: no remote copies, remote signals or barrier semaphores. Data moves between devices by JAX's collectives and lax.ppermute only.
A program may use at most 64 MiB of HBM per device.

```python
import jax
import jax.numpy as jnp
from jax import lax

BC = 64
NS = 4
J = 30
NT = 316
KC = 2048
S = 4
KF = 512
NBC = 512
NBF = 2048
N_BOX = 8


def bit_plan(total_bits):
    plan = []
    for position in range(total_bits):
        if position >= total_bits - 2:
            plan.append((2, position - (total_bits - 2)))
        else:
            plan.append((position % 2, position // 2))
    return plan


def morton_split(box_ids, total_bits):
    coordinates = [jnp.zeros_like(box_ids) for which in range(3)]
    for position, entry in enumerate(bit_plan(total_bits)):
        coordinates[entry[0]] = coordinates[entry[0]] + box_ids // 2 ** position % 2 * 2 ** entry[1]
    return coordinates


def morton_join(coordinates, total_bits):
    joined = jnp.zeros_like(coordinates[0])
    for position, entry in enumerate(bit_plan(total_bits)):
        joined = joined + coordinates[entry[0]] // 2 ** entry[1] % 2 * 2 ** position
    return joined


def draw_partner_ids(key, part):
    total_bits = NBC.bit_length() - 1
    plan = bit_plan(total_bits)
    extents = [2 ** len([entry for entry in plan if entry[0] == which]) for which in range(3)]
    box_ids = jnp.arange(NBC, dtype=jnp.int32)
    coordinates = morton_split(box_ids, total_bits)
    steps_six = jnp.arange(6, dtype=jnp.int32)
    offset_grid = [jnp.broadcast_to(steps_six[:, None, None], (6, 6, 6)).reshape(216), jnp.broadcast_to(steps_six[None, :, None], (6, 6, 6)).reshape(216), jnp.broadcast_to(steps_six[None, None, :], (6, 6, 6)).reshape(216)]
    candidates = []
    valid = jnp.ones((NBC, 216), dtype=bool)
    farthest = jnp.zeros((NBC, 216), jnp.int32)
    for which in range(3):
        offsets = offset_grid[which][None, :] - 2 - (coordinates[which] % 2)[:, None]
        placed = coordinates[which][:, None] + offsets
        valid = valid & (placed >= 0) & (placed < extents[which])
        farthest = jnp.maximum(farthest, jnp.abs(offsets))
        candidates.append(jnp.clip(placed, 0, extents[which] - 1))
    valid = valid & (farthest >= 2)
    cand_ids = morton_join(candidates, total_bits)
    scores = jax.random.randint(key, (NBC, 216), 0, 2 ** 20) * 256 + jnp.arange(216, dtype=jnp.int32)[None, :]
    scores = jnp.where(valid, scores, -1)
    unused, chosen = lax.top_k(scores, J)
    return jnp.take_along_axis(cand_ids, chosen, axis=1).astype(jnp.int32)


def draw_partner_count(key, part):
    counts = jax.random.randint(key, (NBC,), J // 2, J + 1)
    counts = counts.at[0].set(J).at[1].set(J // 2)
    return counts.astype(jnp.int32)


def draw_child_count(key, part):
    moved = jax.random.randint(key, (NBC // 2,), -3, 4)
    moved = moved.at[0].set(3)
    counts = jnp.stack([4 + moved, 4 - moved], axis=1).reshape(NBC)
    return counts.astype(jnp.int32)


def draw_stencil_ids(key, part):
    jitter = jax.random.randint(key, (KC, 2), 0, 2)
    centre = jnp.arange(KC, dtype=jnp.int32) // 4
    offsets = jnp.stack([jnp.full((KC,), -2, jnp.int32), jitter[:, 0] - 1, jitter[:, 1], jnp.full((KC,), 2, jnp.int32)], axis=1)
    return ((centre[:, None] + offsets) % KF).astype(jnp.int32)


def plant(array, rng, smallest, largest):
    longest = array.shape.index(max(array.shape))
    spots = []
    for shift in (0, 1):
        where = [jax.random.randint(jax.random.fold_in(rng, axis), (), 0, length) for axis, length in enumerate(array.shape)]
        where[longest] = (where[longest] + shift) % array.shape[longest]
        spots.append(tuple(where))
    return array.at[spots[0]].set(smallest).at[spots[1]].set(largest)


def level_of(stream_key, shape, cuts, low, high):
    level, own = 1.0, jax.random.fold_in(stream_key, 6)
    for dim, shards_of in cuts:
        draws = jnp.exp(jax.random.uniform(jax.random.fold_in(own, dim), (shards_of,), jnp.float32, low / len(cuts), high / len(cuts)))
        level = level * jnp.repeat(draws, shape[dim] // shards_of).reshape([-1 if axis == dim else 1 for axis in range(len(shape))])
    return level


def bell_draw(rng, dims, deviation, limit, shards=(), kind=jnp.bfloat16):
    loudness = level_of(rng, dims, shards, -0.22, 0.18) if shards else 1.0
    result = jax.random.normal(rng, dims, jnp.float32) * deviation * loudness
    return jnp.minimum(jnp.maximum(result, -limit), limit).astype(kind)


def setup_inputs(seed: int = 0) -> dict:
    streams_of = jax.random.split(jax.random.key(seed), 11)
    coarse_field = bell_draw(streams_of[0], (NBC, 2, NS, KC), 1.0, 6.0, ((0, 8), (3, 4)), jnp.float32)
    trans_table = bell_draw(streams_of[1], (NT, 2, KC), 0.25, 1.5, ((2, 4),), jnp.float32)
    partner_ids = draw_partner_ids(jax.random.fold_in(streams_of[10], 71), 0)
    partner_types = plant(jax.random.randint(streams_of[3], (NBC, J), 0, NT), jax.random.fold_in(streams_of[3], 1), 0, NT - 1).astype(jnp.int32)
    partner_count = draw_partner_count(jax.random.fold_in(streams_of[10], 71), 0)
    child_count = draw_child_count(jax.random.fold_in(streams_of[10], 71), 0)
    child_octant = plant(jax.random.randint(streams_of[6], (NBF,), 0, 8), jax.random.fold_in(streams_of[6], 1), 0, 7).astype(jnp.int32)
    dir_angles = jnp.clip(jax.random.uniform(streams_of[7], (2, KC), jnp.float32, -3.140625, 3.140625), -3.140625, 3.140625)
    stencil_ids = draw_stencil_ids(jax.random.fold_in(streams_of[10], 71), 0)
    stencil_weights = bell_draw(streams_of[9], (KC, S), 0.3, 1.8, (), jnp.float32)
    return dict(coarse_field=coarse_field, trans_table=trans_table, partner_ids=partner_ids, partner_types=partner_types, partner_count=partner_count, child_count=child_count, child_octant=child_octant, dir_angles=dir_angles, stencil_ids=stencil_ids, stencil_weights=stencil_weights)


wave_scale = 3.0


def reference(coarse_field, trans_table, partner_ids, partner_types, partner_count, child_count, child_octant, dir_angles, stencil_ids, stencil_weights):
    live_mask = (jnp.arange(J, dtype=jnp.int32)[None, :] < partner_count[:, None]).astype(jnp.float32)

    def translate(running, column):
        part_ids, type_ids, weight = column
        source = jnp.take(coarse_field, part_ids, axis=0)
        tab_row = jnp.take(trans_table, type_ids, axis=0)
        table_real = tab_row[:, 0, None, :] * weight[:, None, None]
        table_imag = tab_row[:, 1, None, :] * weight[:, None, None]
        real_part = table_real * source[:, 0] + table_imag * source[:, 1]
        imag_part = table_real * source[:, 1] - table_imag * source[:, 0]
        return running + jnp.stack([real_part, imag_part], axis=1), None

    zeros_init = jnp.zeros((NBC, 2, NS, KC), jnp.float32)
    translated, _ = lax.scan(translate, zeros_init, (partner_ids.T, partner_types.T, live_mask.T))

    bounds = jnp.cumsum(child_count).astype(jnp.int32)
    parent = jnp.searchsorted(bounds, jnp.arange(NBF, dtype=jnp.int32), side="right").astype(jnp.int32)

    theta_cols = dir_angles[0]
    phi_cols = dir_angles[1]
    unit_x = jnp.sin(theta_cols) * jnp.cos(phi_cols)
    unit_y = jnp.sin(theta_cols) * jnp.sin(phi_cols)
    unit_z = jnp.cos(theta_cols)

    matrix = jnp.zeros((KC, KF), jnp.float32)
    targets = jnp.arange(KF, dtype=jnp.int32)
    for point in range(S):
        matrix = matrix + jnp.where(stencil_ids[:, point, None] == targets[None, :], stencil_weights[:, point, None], 0.0)

    def level_block(pieces):
        parent_blk, octant_blk = pieces
        sign_x = 1.0 - 2.0 * (octant_blk % 2).astype(jnp.float32)
        sign_y = 1.0 - 2.0 * ((octant_blk // 2) % 2).astype(jnp.float32)
        sign_z = 1.0 - 2.0 * (octant_blk // 4).astype(jnp.float32)
        phase_angle = wave_scale * (sign_x[:, None] * unit_x[None, :] + sign_y[:, None] * unit_y[None, :] + sign_z[:, None] * unit_z[None, :])
        cosine = jnp.cos(phase_angle)[:, None, :]
        sine = jnp.sin(phase_angle)[:, None, :]
        gathered = jnp.take(translated, parent_blk, axis=0)
        real_part = gathered[:, 0] * cosine + gathered[:, 1] * sine
        imag_part = gathered[:, 1] * cosine - gathered[:, 0] * sine
        shifted = jnp.stack([real_part, imag_part], axis=1)
        return jnp.einsum("rtnc,cf->rtnf", shifted, matrix, precision=lax.Precision.HIGHEST)

    blocks = lax.map(level_block, (parent.reshape(N_BOX, 4 * BC), child_octant.reshape(N_BOX, 4 * BC)))
    return blocks.reshape(NBF, 2, NS, KF)
```

```python
import functools

import jax
import jax.numpy as jnp
from jax import lax
from jax.experimental import pallas as pl
from jax.experimental.pallas import tpu as pltpu
from jax.sharding import Mesh
from jax.sharding import PartitionSpec as P

wave_scale = 3.0
planes = 4
lanes = 128
half = 4
rim = 2


def up(size, step):
    return -(-size // step) * step


def edge_bits(rows):
    bits = rows.bit_length() - 1
    return bits, [place for place in range(2, bits) if place % 2 == bits % 2]


def near_edge(block, ring):
    bits, fixed = edge_bits(block.shape[0])
    tail = block.shape[1:]
    picked = block.reshape((2,) * bits + tail)
    for place in fixed:
        picked = lax.dynamic_index_in_dim(picked, 1 - ring, axis=bits - 1 - place, keepdims=True)
    return picked.reshape((block.shape[0] >> len(fixed),) + tail)


def edge_rank(local, rows):
    bits, fixed = edge_bits(rows)
    rank = jnp.zeros_like(local)
    taken = 0
    for place in range(bits):
        if place not in fixed:
            rank = rank + (local // 2**place % 2) * 2**taken
            taken += 1
    return rank


def split(value):
    high = value.astype(jnp.bfloat16)
    low = (value - high.astype(jnp.float32)).astype(jnp.bfloat16)
    return high, low


def three_pass(left, right, dims):
    dot = functools.partial(
        lax.dot_general, dimension_numbers=(dims, ((), ())), preferred_element_type=jnp.float32
    )
    return dot(left[0], right[0]) + (dot(left[0], right[1]) + dot(left[1], right[0]))


def fine_kernel(
    rows, slots, fine_rows, piece_count, first, meta, *refs
):
    pieces = refs[:piece_count]
    tab_re, tab_im, cosine, sine, matrix, spill_re, spill_im, out = refs[piece_count : piece_count + 8]
    field, sems, moved, swapped, shifted = refs[piece_count + 8 :]
    copies = []
    start = 0
    for index, piece in enumerate(pieces):
        size = piece.shape[0]
        copies.append(pltpu.make_async_copy(piece, field.at[pl.ds(start, size)], sems.at[index]))
        copies[-1].start()
        start += size
    for copy in copies:
        copy.wait()

    sub = lax.broadcasted_iota(jnp.int32, (2 * half, lanes), 0)
    sign = jnp.where(sub < half, 1.0, -1.0).astype(jnp.float32)
    pairs = rows * slots
    stride = 2 * pairs + rows + 2 * fine_rows
    fixed_slots = slots // 2
    group = 5 if (slots - fixed_slots) % 5 == 0 else 1
    weights = split(matrix[...])
    spill_re_parts = split(spill_re[...])
    spill_im_parts = split(spill_im[...])
    dest_count = out.shape[1]
    dest_rows = fine_rows // dest_count

    def plane_step(plane, unused):
        base = plane * stride

        def box_step(box, unused):
            place = base + box * slots

            def add(slot, sums):
                row = meta[place + slot]
                kind = meta[place + pairs + slot]
                value = field[row]
                return sums[0] + tab_re[kind] * value, sums[1] + tab_im[kind] * value

            sums = (jnp.zeros((2 * half, lanes), jnp.float32),) * 2
            for slot in range(fixed_slots):
                sums = add(slot, sums)

            def more(turn, sums):
                for slot in range(group):
                    sums = add(fixed_slots + turn * group + slot, sums)
                return sums

            sums = lax.fori_loop(0, meta[base + 2 * pairs + box], more, sums)
            total = sums[0] + sign * pltpu.roll(sums[1], half, 0)
            moved[box] = total
            swapped[box] = pltpu.roll(total, half, 0)
            return unused

        lax.fori_loop(0, rows, box_step, 0)

        def fine_step(fine, unused):
            place = base + 2 * pairs + rows + fine
            parent = meta[place]
            octant = meta[place + fine_rows]
            shifted[pl.ds(pl.multiple_of(fine * 2 * half, 2 * half), 2 * half), :] = (
                moved[parent] * cosine[octant] + swapped[parent] * sine[octant]
            )
            return unused

        lax.fori_loop(0, fine_rows, fine_step, 0, unroll=8)
        spill = jnp.zeros((2 * half, fine_rows), jnp.float32)
        for part in range(2):
            left = jnp.concatenate(
                [
                    shifted[pl.ds(part * half + block, fine_rows, stride=2 * half), :]
                    for block in range(half)
                ],
                axis=1,
            )
            left = split(left)
            result = three_pass(left, weights, ((1,), (0,)))
            spill = spill + three_pass((spill_re_parts, spill_im_parts)[part], left, ((1,), (1,)))
            for dest in range(dest_count):
                out[plane, dest, part * dest_rows : (part + 1) * dest_rows, :] = result[
                    dest * dest_rows : (dest + 1) * dest_rows
                ]
        for dest in range(dest_count):
            out[plane, dest, 2 * dest_rows :, :] = jnp.concatenate(
                [
                    spill[:, dest * dest_rows : (dest + 1) * dest_rows],
                    jnp.zeros((2 * half, out.shape[3] - dest_rows), jnp.float32),
                ],
                axis=1,
            )
        return unused

    lax.fori_loop(0, planes, plane_step, 0)


def per_device(
    coarse_field,
    trans_table,
    partner_ids,
    partner_types,
    partner_count,
    child_count,
    child_octant,
    dir_angles,
    stencil_ids,
    stencil_weights,
):
    rows, _, source_count, kc_dev = coarse_field.shape
    slots = partner_ids.shape[1]
    type_count = trans_table.shape[0]
    fine_rows = child_octant.shape[0]
    ring_count = lax.axis_size("ring")
    dir_count = lax.axis_size("dir")
    zed = lax.axis_index("zed")
    ring = lax.axis_index("ring")
    dir_index = lax.axis_index("dir")
    fine_count = stencil_ids.shape[0] // 4
    kf_dev = fine_count // dir_count
    kc_pad = up(kc_dev, half * lanes)
    kf_pad = up(kf_dev, lanes)
    pad_dirs = kc_pad - kc_dev
    assert source_count == planes and kc_pad == half * lanes
    dest_rows = fine_rows // dir_count

    def to_blocks(piece):
        piece = jnp.pad(piece, ((0, 0), (0, 0), (0, pad_dirs)))
        return piece.reshape(rows, 2 * half, lanes)

    sent = [
        to_blocks(lax.dynamic_index_in_dim(coarse_field, zed ^ step, axis=2, keepdims=False))
        for step in range(planes)
    ]
    if ring_count == 2:
        sent_edges = [near_edge(piece, ring) for piece in sent]

    def hop(piece, step, ring_step):
        if step == 0 and ring_step == 0:
            return piece
        pairs = [
            (z * ring_count + r, (z ^ step) * ring_count + (r ^ ring_step))
            for z in range(planes)
            for r in range(ring_count)
        ]
        return lax.ppermute(piece, ("zed", "ring"), pairs)

    plane_of = partner_ids // (ring_count * rows)
    ring_of = partner_ids // rows % ring_count
    local = partner_ids % rows
    live = jnp.arange(slots, dtype=jnp.int32)[None, :] < partner_count[:, None]
    if ring_count == 2:
        edge_rows = rows >> len(edge_bits(rows)[1])
        place = jnp.where(
            ring_of == ring,
            plane_of * rows + local,
            planes * rows + plane_of * edge_rows + edge_rank(local, rows),
        )
    else:
        place = partner_ids
    place = jnp.where(live, place, 0)
    kinds = jnp.where(live, partner_types, type_count)
    fixed_slots = slots // 2
    group = 5 if (slots - fixed_slots) % 5 == 0 else 1
    turns = jnp.maximum((partner_count - fixed_slots + group - 1) // group, 0)
    order = jnp.arange(rows, dtype=jnp.int32)
    bounds = jnp.sum(jnp.where(order[None, :] <= order[:, None], child_count[None, :], 0), axis=1)
    parent = jnp.sum(
        (bounds[None, :] <= jnp.arange(fine_rows, dtype=jnp.int32)[:, None]).astype(jnp.int32), axis=1
    )
    meta = jnp.concatenate([place.reshape(-1), kinds.reshape(-1), turns, parent, child_octant])
    meta = lax.all_gather(meta, "zed", axis=0, tiled=True)

    arrived = [hop(piece, step, 0) for step, piece in enumerate(sent)]
    natural = [None] * planes
    stacked = jnp.stack(arrived)
    natural = [lax.dynamic_index_in_dim(stacked, zed ^ plane, axis=0, keepdims=False) for plane in range(planes)]
    if ring_count == 2:
        edges = jnp.stack([hop(piece, step, 1) for step, piece in enumerate(sent_edges)])
        natural += [
            lax.dynamic_index_in_dim(edges, zed ^ plane, axis=0, keepdims=False) for plane in range(planes)
        ]
    else:
        natural = [lax.all_gather(piece, "ring", axis=0, tiled=True) for piece in natural]

    def doubled(table, sign):
        table = jnp.pad(table, ((0, 0), (0, pad_dirs))).reshape(-1, half, lanes)
        return jnp.concatenate([table, sign * table], axis=1)

    padded_table = jnp.pad(trans_table, ((0, 1), (0, 0), (0, 0)))
    tab_re = doubled(padded_table[:, 0], 1.0)
    tab_im = doubled(padded_table[:, 1], 1.0)
    angles = lax.dynamic_slice_in_dim(dir_angles, dir_index * kc_dev, kc_dev, axis=1)
    octants = jnp.arange(8, dtype=jnp.int32)
    sign_x = 1.0 - 2.0 * (octants % 2).astype(jnp.float32)
    sign_y = 1.0 - 2.0 * (octants // 2 % 2).astype(jnp.float32)
    sign_z = 1.0 - 2.0 * (octants // 4).astype(jnp.float32)
    unit_x = jnp.sin(angles[0]) * jnp.cos(angles[1])
    unit_y = jnp.sin(angles[0]) * jnp.sin(angles[1])
    unit_z = jnp.cos(angles[0])
    phase = wave_scale * (
        sign_x[:, None] * unit_x[None, :] + sign_y[:, None] * unit_y[None, :] + sign_z[:, None] * unit_z[None, :]
    )
    cosine = doubled(jnp.cos(phase), 1.0)
    sine = doubled(jnp.sin(phase), -1.0)

    ids = lax.dynamic_slice_in_dim(stencil_ids, dir_index * kc_dev, kc_dev, axis=0).T
    weights = lax.dynamic_slice_in_dim(stencil_weights, dir_index * kc_dev, kc_dev, axis=0).T

    def interp(targets):
        matrix = jnp.zeros((targets.shape[0], kc_dev), jnp.float32)
        for point in range(ids.shape[0]):
            matrix = matrix + jnp.where(
                ids[point][None, :] == targets[:, None], weights[point][None, :], 0.0
            )
        return jnp.pad(matrix, ((0, 0), (0, pad_dirs)))

    first_fine = dir_index * kf_dev
    own = jnp.arange(kf_dev, dtype=jnp.int32)
    outside = jnp.concatenate(
        [jnp.arange(-rim, 0, dtype=jnp.int32), jnp.arange(kf_dev, kf_dev + rim, dtype=jnp.int32)]
    )
    matrix = jnp.pad(interp(first_fine + own).T, ((0, 0), (0, kf_pad - kf_dev)))
    spill = interp((first_fine + outside) % fine_count)
    blank = jnp.zeros_like(spill)
    spill_re = jnp.concatenate([spill, blank], axis=0)
    spill_im = jnp.concatenate([blank, spill], axis=0)

    field_rows = sum(piece.shape[0] for piece in natural)
    whole = pl.BlockSpec(memory_space=pltpu.VMEM)
    local_fine = pl.pallas_call(
        functools.partial(fine_kernel, rows, slots, fine_rows, len(natural), 0),
        out_shape=jax.ShapeDtypeStruct((planes, dir_count, 2 * dest_rows + 2 * half, kf_pad), jnp.float32),
        in_specs=[pl.BlockSpec(memory_space=pltpu.SMEM)]
        + [pl.BlockSpec(memory_space=pl.ANY)] * len(natural)
        + [whole] * 7,
        out_specs=whole,
        scratch_shapes=[
            pltpu.VMEM((field_rows, 2 * half, lanes), jnp.float32),
            pltpu.SemaphoreType.DMA((len(natural),)),
            pltpu.VMEM((rows, 2 * half, lanes), jnp.float32),
            pltpu.VMEM((rows, 2 * half, lanes), jnp.float32),
            pltpu.VMEM((fine_rows * 2 * half, lanes), jnp.float32),
        ],
        compiler_params=pltpu.CompilerParams(vmem_limit_bytes=48 * 2**20),
        name="translate_and_interpolate",
    )(meta, *natural, tab_re, tab_im, cosine, sine, matrix, spill_re, spill_im)

    local_fine = local_fine.reshape((planes * dir_count,) + local_fine.shape[2:])
    parts = lax.all_to_all(local_fine, ("zed", "dir"), split_axis=0, concat_axis=0, tiled=True)
    parts = parts.reshape((planes, dir_count) + parts.shape[1:])
    main = parts[:, :, : 2 * dest_rows, :kf_dev].reshape(planes, dir_count, 2, dest_rows, kf_dev)
    over = parts[:, :, 2 * dest_rows :, :dest_rows].reshape(planes, dir_count, 2, 2 * rim, dest_rows)
    low = jnp.roll(over[:, :, :, :rim], -1, axis=1)
    high = jnp.roll(over[:, :, :, rim:], 1, axis=1)
    middle = jnp.zeros((planes, dir_count, 2, kf_dev - 2 * rim, dest_rows), jnp.float32)
    fix = jnp.concatenate([high, middle, low], axis=3)
    total = main.transpose(3, 2, 0, 1, 4) + fix.transpose(4, 2, 0, 1, 3)
    return total.reshape(dest_rows, 2, source_count, fine_count)


def solution(mesh):
    boxes, dirs = mesh.shape["box"], mesh.shape["dir"]
    fine_mesh = Mesh(mesh.devices.reshape(planes, boxes // planes, dirs), ("zed", "ring", "dir"))
    box = ("zed", "ring")
    placed = (
        P(box, None, None, "dir"),
        P(None, None, "dir"),
        P(box, None),
        P(box, None),
        P(box),
        P(box),
        P(box),
        P(),
        P(),
        P(),
    )
    return jax.shard_map(
        per_device,
        mesh=fine_mesh,
        in_specs=placed,
        out_specs=P(("zed", "ring", "dir"), None, None, None),
        check_vma=False,
    )
```

```python
import functools

import jax
import jax.numpy as jnp
from jax import lax
from jax.experimental import pallas as pl
from jax.experimental.pallas import tpu as pltpu
from jax.sharding import Mesh
from jax.sharding import PartitionSpec as P

wave_scale = 3.0
planes = 4
lanes = 128
half = 4
rim = 2


def up(size, step):
    return -(-size // step) * step


def edge_bits(rows):
    bits = rows.bit_length() - 1
    return bits, [place for place in range(2, bits) if place % 2 == bits % 2]


def near_edge(block, ring):
    count, rows = block.shape[:2]
    bits, fixed = edge_bits(rows)
    tail = block.shape[2:]
    picked = block.reshape((count,) + (2,) * bits + tail)
    for place in fixed:
        picked = lax.dynamic_index_in_dim(picked, 1 - ring, axis=bits - place, keepdims=True)
    return picked.reshape((count, rows >> len(fixed)) + tail)


def edge_rank(local, rows):
    bits, fixed = edge_bits(rows)
    rank = jnp.zeros_like(local)
    taken = 0
    for place in range(bits):
        if place not in fixed:
            rank = rank + (local // 2**place % 2) * 2**taken
            taken += 1
    return rank


def split(value):
    high = value.astype(jnp.bfloat16)
    low = (value - high.astype(jnp.float32)).astype(jnp.bfloat16)
    return high, low


def three_pass(left, right, dims):
    dot = functools.partial(
        lax.dot_general, dimension_numbers=(dims, ((), ())), preferred_element_type=jnp.float32
    )
    return dot(left[0], right[0]) + (dot(left[0], right[1]) + dot(left[1], right[0]))


def pack_kernel(source_count, field, out, whole):
    rows, _, _, width = field.shape
    stride = 2 * source_count

    def row_step(row, unused):
        both = jnp.concatenate([field[row, 0], field[row, 1]], axis=0)
        for block in range(half):
            whole[block, pl.ds(pl.multiple_of(row * stride, stride), stride), :] = both[
                :, block * lanes : (block + 1) * lanes
            ]
        return unused

    lax.fori_loop(0, rows, row_step, 0, unroll=8)
    for source in range(source_count):
        for part in range(2):
            for block in range(half):
                out[source, pl.ds(part * half + block, rows, stride=2 * half), :] = whole[
                    block, pl.ds(part * source_count + source, rows, stride=stride), :
                ]


def fine_kernel(rows, slots, fine_rows, meta_stride, piece_count, meta, *refs):
    pieces = refs[:piece_count]
    table, cosine, sine, matrix, spill_re, spill_im, out = refs[piece_count : piece_count + 7]
    field, turned, sems, moved, swapped, shifted = refs[piece_count + 7 :]
    copies = []
    start = 0
    for index, piece in enumerate(pieces):
        size = piece.shape[0]
        copies.append(pltpu.make_async_copy(piece, field.at[pl.ds(start, size)], sems.at[index]))
        copies[-1].start()
        start += size
    for copy in copies:
        copy.wait()

    def turn_step(row, unused):
        turned[row] = pltpu.roll(field[row], half, 0)
        return unused

    lax.fori_loop(0, start, turn_step, 0, unroll=8)
    sub = lax.broadcasted_iota(jnp.int32, (2 * half, lanes), 0)
    pairs = rows * slots
    weights = split(matrix[...])
    spill_parts = (split(spill_re[...]), split(spill_im[...]))
    dest_count = out.shape[1]
    dest_rows = fine_rows // dest_count

    def plane_step(plane, unused):
        base = plane * meta_stride

        def box_step(box, unused):
            place = base + box * slots
            straight = jnp.zeros((2 * half, lanes), jnp.float32)
            crossed = straight
            for slot in range(slots):
                row = meta[place + slot]
                factor = table[meta[place + pairs + slot]]
                straight = straight + factor * field[row]
                crossed = crossed + factor * turned[row]
            total = jnp.where(
                sub < half,
                straight + pltpu.roll(straight, half, 0),
                pltpu.roll(crossed, half, 0) - crossed,
            )
            moved[box] = total
            swapped[box] = pltpu.roll(total, half, 0)
            return unused

        lax.fori_loop(0, rows, box_step, 0, unroll=2)

        def fine_step(fine, unused):
            place = base + 2 * pairs + fine
            parent = meta[place]
            octant = meta[place + fine_rows]
            shifted[pl.ds(pl.multiple_of(fine * 2 * half, 2 * half), 2 * half), :] = (
                moved[parent] * cosine[octant] + swapped[parent] * sine[octant]
            )
            return unused

        lax.fori_loop(0, fine_rows, fine_step, 0, unroll=8)
        spill = jnp.zeros((2 * half, fine_rows), jnp.float32)
        for part in range(2):
            left = jnp.concatenate(
                [
                    shifted[pl.ds(part * half + block, fine_rows, stride=2 * half), :]
                    for block in range(half)
                ],
                axis=1,
            )
            left = split(left)
            result = three_pass(left, weights, ((1,), (0,)))
            spill = spill + three_pass(spill_parts[part], left, ((1,), (1,)))
            for dest in range(dest_count):
                out[plane, dest, part * dest_rows : (part + 1) * dest_rows, :] = result[
                    dest * dest_rows : (dest + 1) * dest_rows
                ]
        for dest in range(dest_count):
            out[plane, dest, 2 * dest_rows :, :] = jnp.concatenate(
                [
                    spill[:, dest * dest_rows : (dest + 1) * dest_rows],
                    jnp.zeros((2 * half, out.shape[3] - dest_rows), jnp.float32),
                ],
                axis=1,
            )
        return unused

    lax.fori_loop(0, planes, plane_step, 0)


def join_kernel(source_count, parts, out, whole):
    dest_rows = out.shape[0]
    dirs = parts.shape[0] // source_count
    over = jnp.concatenate(
        [parts[index, 2 * dest_rows :, :lanes] for index in range(parts.shape[0])], axis=0
    ).T[:dest_rows]
    lane = lax.broadcasted_iota(jnp.int32, (dest_rows, lanes), 1)
    for source in range(source_count):
        for part in range(2):
            turned = []
            for index in range(dirs):
                first = (source * dirs + index) * 2 * half + part * half
                turned.append(pltpu.roll(over, (lanes - rim - first) % lanes, 1))
            for index in range(dirs):
                fix = jnp.where(lane < rim, turned[index - 1], 0.0) + jnp.where(
                    lane >= lanes - rim, turned[(index + 1) % dirs], 0.0
                )
                whole[
                    index, pl.ds(part * source_count + source, dest_rows, stride=2 * source_count), :
                ] = parts[source * dirs + index, part * dest_rows : (part + 1) * dest_rows, :] + fix

    def row_step(row, unused):
        start = pl.multiple_of(row * 2 * source_count, 2 * source_count)
        both = jnp.concatenate(
            [whole[index, pl.ds(start, 2 * source_count), :] for index in range(dirs)], axis=1
        )
        out[row, 0] = both[:source_count]
        out[row, 1] = both[source_count:]
        return unused

    lax.fori_loop(0, dest_rows, row_step, 0, unroll=8)


def per_device(
    coarse_field,
    trans_table,
    partner_ids,
    partner_types,
    partner_count,
    child_count,
    child_octant,
    dir_angles,
    stencil_ids,
    stencil_weights,
):
    rows, _, source_count, kc_dev = coarse_field.shape
    slots = partner_ids.shape[1]
    type_count = trans_table.shape[0]
    fine_rows = child_octant.shape[0]
    ring_count = lax.axis_size("ring")
    dir_count = lax.axis_size("dir")
    zed = lax.axis_index("zed")
    ring = lax.axis_index("ring")
    dir_index = lax.axis_index("dir")
    fine_count = stencil_ids.shape[0] // 4
    kf_dev = fine_count // dir_count
    kc_pad = up(kc_dev, half * lanes)
    kf_pad = up(kf_dev, lanes)
    pad_dirs = kc_pad - kc_dev
    assert source_count == planes and kc_pad == half * lanes
    dest_rows = fine_rows // dir_count

    whole = pl.BlockSpec(memory_space=pltpu.VMEM)
    packed = pl.pallas_call(
        functools.partial(pack_kernel, source_count),
        out_shape=jax.ShapeDtypeStruct((source_count, rows * 2 * half, lanes), jnp.float32),
        in_specs=[whole],
        out_specs=whole,
        scratch_shapes=[pltpu.VMEM((half, rows * 2 * source_count, lanes), jnp.float32)],
        name="pack_sources",
    )(jnp.pad(coarse_field, ((0, 0), (0, 0), (0, 0), (0, pad_dirs))))
    arrived = lax.all_to_all(packed, "zed", split_axis=0, concat_axis=0, tiled=True)
    arrived = arrived.reshape(planes, rows, 2 * half, lanes)
    if ring_count == 2:
        edges = near_edge(arrived, ring)
        edge_rows = edges.shape[1]
        edges = lax.ppermute(edges, "ring", [(0, 1), (1, 0)])
        pieces = [
            arrived.reshape(planes * rows, 2 * half, lanes),
            edges.reshape(planes * edge_rows, 2 * half, lanes),
        ]
    else:
        pieces = [lax.all_gather(arrived, "ring", axis=1, tiled=True).reshape(-1, 2 * half, lanes)]

    plane_of = partner_ids // (ring_count * rows)
    ring_of = partner_ids // rows % ring_count
    local = partner_ids % rows
    live = jnp.arange(slots, dtype=jnp.int32)[None, :] < partner_count[:, None]
    if ring_count == 2:
        place = jnp.where(
            ring_of == ring,
            plane_of * rows + local,
            planes * rows + plane_of * edge_rows + edge_rank(local, rows),
        )
    else:
        place = partner_ids
    place = jnp.where(live, place, 0)
    kinds = jnp.where(live, partner_types, type_count)
    order = jnp.arange(rows, dtype=jnp.int32)
    bounds = jnp.sum(jnp.where(order[None, :] <= order[:, None], child_count[None, :], 0), axis=1)
    parent = jnp.sum(
        (bounds[None, :] <= jnp.arange(fine_rows, dtype=jnp.int32)[:, None]).astype(jnp.int32), axis=1
    )
    meta = jnp.concatenate([place.reshape(-1), kinds.reshape(-1), parent, child_octant])
    meta_stride = up(meta.shape[0], 8 * lanes)
    meta = jnp.pad(meta, (0, meta_stride - meta.shape[0])).reshape(1, meta_stride // lanes, lanes)
    meta = jnp.broadcast_to(meta, (planes,) + meta.shape[1:])
    meta = lax.all_to_all(meta, "zed", split_axis=0, concat_axis=0, tiled=True).reshape(-1)

    def blocks(table):
        return jnp.pad(table, ((0, 0), (0, pad_dirs))).reshape(-1, half, lanes)

    def doubled(table, sign):
        return jnp.concatenate([blocks(table), sign * blocks(table)], axis=1)

    table = jnp.pad(trans_table, ((0, 1), (0, 0), (0, pad_dirs))).reshape(-1, 2 * half, lanes)
    angles = lax.dynamic_slice_in_dim(dir_angles, dir_index * kc_dev, kc_dev, axis=1)
    octants = jnp.arange(8, dtype=jnp.int32)
    sign_x = 1.0 - 2.0 * (octants % 2).astype(jnp.float32)
    sign_y = 1.0 - 2.0 * (octants // 2 % 2).astype(jnp.float32)
    sign_z = 1.0 - 2.0 * (octants // 4).astype(jnp.float32)
    unit_x = jnp.sin(angles[0]) * jnp.cos(angles[1])
    unit_y = jnp.sin(angles[0]) * jnp.sin(angles[1])
    unit_z = jnp.cos(angles[0])
    phase = wave_scale * (
        sign_x[:, None] * unit_x[None, :] + sign_y[:, None] * unit_y[None, :] + sign_z[:, None] * unit_z[None, :]
    )
    cosine = doubled(jnp.cos(phase), 1.0)
    sine = doubled(jnp.sin(phase), -1.0)

    ids = lax.dynamic_slice_in_dim(stencil_ids, dir_index * kc_dev, kc_dev, axis=0).T
    weights = lax.dynamic_slice_in_dim(stencil_weights, dir_index * kc_dev, kc_dev, axis=0).T

    def interp(targets):
        matrix = jnp.zeros((targets.shape[0], kc_dev), jnp.float32)
        for point in range(ids.shape[0]):
            matrix = matrix + jnp.where(
                ids[point][None, :] == targets[:, None], weights[point][None, :], 0.0
            )
        return jnp.pad(matrix, ((0, 0), (0, pad_dirs)))

    first_fine = dir_index * kf_dev
    own = jnp.arange(kf_dev, dtype=jnp.int32)
    outside = jnp.concatenate(
        [jnp.arange(-rim, 0, dtype=jnp.int32), jnp.arange(kf_dev, kf_dev + rim, dtype=jnp.int32)]
    )
    matrix = jnp.pad(interp(first_fine + own).T, ((0, 0), (0, kf_pad - kf_dev)))
    spill = interp((first_fine + outside) % fine_count)
    blank = jnp.zeros_like(spill)
    spill_re = jnp.concatenate([spill, blank], axis=0)
    spill_im = jnp.concatenate([blank, spill], axis=0)

    field_rows = sum(piece.shape[0] for piece in pieces)
    message = (2 * dest_rows + 2 * half, kf_pad)
    local_fine = pl.pallas_call(
        functools.partial(fine_kernel, rows, slots, fine_rows, meta_stride, len(pieces)),
        out_shape=jax.ShapeDtypeStruct((planes, dir_count) + message, jnp.float32),
        in_specs=[pl.BlockSpec(memory_space=pltpu.SMEM)]
        + [pl.BlockSpec(memory_space=pl.ANY)] * len(pieces)
        + [whole] * 6,
        out_specs=whole,
        scratch_shapes=[
            pltpu.VMEM((field_rows, 2 * half, lanes), jnp.float32),
            pltpu.VMEM((field_rows, 2 * half, lanes), jnp.float32),
            pltpu.SemaphoreType.DMA((len(pieces),)),
            pltpu.VMEM((rows, 2 * half, lanes), jnp.float32),
            pltpu.VMEM((rows, 2 * half, lanes), jnp.float32),
            pltpu.VMEM((fine_rows * 2 * half, lanes), jnp.float32),
        ],
        compiler_params=pltpu.CompilerParams(vmem_limit_bytes=48 * 2**20),
        name="translate_and_interpolate",
    )(meta, *pieces, table, cosine, sine, matrix, spill_re, spill_im)

    parts = lax.all_to_all(
        local_fine.reshape((planes * dir_count,) + message),
        ("zed", "dir"),
        split_axis=0,
        concat_axis=0,
        tiled=True,
    )
    result = (dest_rows, 2, source_count, fine_count)
    if kf_dev == lanes and planes * dir_count * 2 * half == lanes and dest_rows <= lanes:
        return pl.pallas_call(
            functools.partial(join_kernel, source_count),
            out_shape=jax.ShapeDtypeStruct(result, jnp.float32),
            in_specs=[whole],
            out_specs=whole,
            scratch_shapes=[pltpu.VMEM((dir_count, dest_rows * 2 * source_count, lanes), jnp.float32)],
            name="join_parts",
        )(parts)
    parts = parts.reshape((planes, dir_count) + message)
    main = parts[:, :, : 2 * dest_rows, :kf_dev].reshape(planes, dir_count, 2, dest_rows, kf_dev)
    over = parts[:, :, 2 * dest_rows :, :dest_rows].reshape(planes, dir_count, 2, 2 * rim, dest_rows)
    low = jnp.roll(over[:, :, :, :rim], -1, axis=1)
    high = jnp.roll(over[:, :, :, rim:], 1, axis=1)
    middle = jnp.zeros((planes, dir_count, 2, kf_dev - 2 * rim, dest_rows), jnp.float32)
    fix = jnp.concatenate([high, middle, low], axis=3)
    total = main.transpose(3, 2, 0, 1, 4) + fix.transpose(4, 2, 0, 1, 3)
    return total.reshape(result)


def solution(mesh):
    boxes, dirs = mesh.shape["box"], mesh.shape["dir"]
    fine_mesh = Mesh(mesh.devices.reshape(planes, boxes // planes, dirs), ("zed", "ring", "dir"))
    box = ("zed", "ring")
    placed = (
        P(box, None, None, "dir"),
        P(None, None, "dir"),
        P(box, None),
        P(box, None),
        P(box),
        P(box),
        P(box),
        P(),
        P(),
        P(),
    )
    return jax.shard_map(
        per_device,
        mesh=fine_mesh,
        in_specs=placed,
        out_specs=P(("zed", "ring", "dir"), None, None, None),
        check_vma=False,
    )
```

```python
import collections
import functools

import jax
import jax.numpy as jnp
from jax import lax
from jax.experimental import pallas as pl
from jax.experimental.pallas import tpu as pltpu
from jax.sharding import Mesh
from jax.sharding import PartitionSpec as P

wave_scale = 3.0
planes = 4
lanes = 128
half = 4
rim = 2


plan_fields = ["rows", "slots", "fine_rows", "stride", "kinds", "parent", "octant", "order", "turns"]
Plan = collections.namedtuple("Plan", plan_fields + ["together", "fixed", "group"])


def up(size, step):
    return -(-size // step) * step


def edge_bits(rows):
    bits = rows.bit_length() - 1
    return bits, [place for place in range(2, bits) if place % 2 == bits % 2]


def near_edge(block, ring):
    rows = block.shape[0]
    bits, fixed = edge_bits(rows)
    tail = block.shape[1:]
    picked = block.reshape((2,) * bits + tail)
    for place in fixed:
        picked = lax.dynamic_index_in_dim(picked, 1 - ring, axis=bits - 1 - place, keepdims=True)
    return picked.reshape((rows >> len(fixed),) + tail)


def edge_rank(local, rows):
    bits, fixed = edge_bits(rows)
    rank = jnp.zeros_like(local)
    taken = 0
    for place in range(bits):
        if place not in fixed:
            rank = rank + (local // 2**place % 2) * 2**taken
            taken += 1
    return rank


def split(value):
    high = value.astype(jnp.bfloat16)
    low = (value - high.astype(jnp.float32)).astype(jnp.bfloat16)
    return high, low


def three_pass(left, right, dims):
    dot = functools.partial(
        lax.dot_general, dimension_numbers=(dims, ((), ())), preferred_element_type=jnp.float32
    )
    return dot(left[0], right[0]) + (dot(left[0], right[1]) + dot(left[1], right[0]))


def pack_kernel(source_count, field, *refs):
    notes, (out, whole) = refs[:-2], refs[-2:]
    rows = field.shape[0]
    stride = 2 * source_count

    def row_step(row, unused):
        both = jnp.concatenate([field[row, 0], field[row, 1]], axis=0)
        for block in range(half):
            whole[block, pl.ds(pl.multiple_of(row * stride, stride), stride), :] = both[
                :, block * lanes : (block + 1) * lanes
            ]
        return unused

    lax.fori_loop(0, rows, row_step, 0, unroll=8)
    for source in range(source_count):
        for part in range(2):
            for block in range(half):
                out[source, pl.ds(part * half + block, rows, stride=2 * half), :] = whole[
                    block, pl.ds(part * source_count + source, rows, stride=stride), :
                ]
        for note in notes:
            out[source, rows * 2 * half :, :] = note[...]


def pack(field, notes):
    rows, _, source_count, width = field.shape
    length = rows * 2 * half + sum(note.shape[0] for note in notes)
    whole = pl.BlockSpec(memory_space=pltpu.VMEM)
    return pl.pallas_call(
        functools.partial(pack_kernel, source_count),
        out_shape=pltpu.HBM((source_count, length, lanes), jnp.float32),
        in_specs=[whole] * (1 + len(notes)),
        out_specs=whole,
        scratch_shapes=[pltpu.VMEM((half, rows * 2 * source_count, lanes), jnp.float32)],
        name="pack_sources",
    )(field, *notes)


def tile(start):
    return pl.ds(pl.multiple_of(start, 2 * half), 2 * half)


def fine_kernel(plan, size, edge_size, zed, meta, main, *refs):
    edges = refs[: planes if edge_size else 0]
    refs = refs[len(edges) :]
    table, phases, high, low, out, field, moved, shifted, ready, sems = refs
    rows, slots, fine_rows = plan.rows, plan.slots, plan.fine_rows
    own = zed[0]

    def fill(value, place):
        field[place, 0] = value
        field[place, 1] = pltpu.roll(value, half, 0)

    for plane in range(planes):

        def main_step(row, unused, plane=plane):
            fill(main[plane, tile(row * 2 * half), :], plane * size + row)
            return unused

        lax.fori_loop(0, size, main_step, 0, unroll=8)
    for step, edge in enumerate(edges):

        def edge_step(row, unused, step=step, edge=edge):
            fill(edge[tile(row * 2 * half), :], planes * size + (own ^ step) * edge_size + row)
            return unused

        lax.fori_loop(0, edge_size, edge_step, 0, unroll=8)
    blank = jnp.zeros((2 * half, lanes), jnp.float32)
    field[planes * (size + edge_size), 0] = blank
    field[planes * (size + edge_size), 1] = blank

    sub = lax.broadcasted_iota(jnp.int32, (2 * half, lanes), 0)
    dest_count = out.shape[1]
    dest_rows = fine_rows // dest_count

    def plane_step(plane, unused):
        base = (own ^ plane) * plan.stride

        def boxes_step(step, unused):
            boxes = [meta[base + plan.order + step * plan.together + each] for each in range(plan.together)]
            turns = meta[base + plan.turns + step]

            def work(slot_count):
                places = [base + box * slots for box in boxes]
                sums = [[blank, blank] for box in boxes]
                for slot in range(slot_count):
                    for each in range(plan.together):
                        value = field[meta[places[each] + slot]]
                        factor = table[meta[places[each] + plan.kinds + slot]]
                        sums[each][0] += factor * value[0]
                        sums[each][1] += factor * value[1]
                for each in range(plan.together):
                    straight, crossed = sums[each]
                    total = jnp.where(
                        sub < half,
                        straight + pltpu.roll(straight, half, 0),
                        pltpu.roll(crossed, half, 0) - crossed,
                    )
                    moved[boxes[each], 0] = total
                    moved[boxes[each], 1] = pltpu.roll(total, half, 0)

            for turn in range((slots - plan.fixed) // plan.group + 1):
                pl.when(turns == turn)(functools.partial(work, plan.fixed + turn * plan.group))
            return unused

        lax.fori_loop(0, rows // plan.together, boxes_step, 0)

        def fine_step(fine, unused):
            value = moved[meta[base + plan.parent + fine]]
            phase = phases[meta[base + plan.octant + fine]]
            shifted[tile(fine * 2 * half), :] = value[0] * phase[0] + value[1] * phase[1]
            return unused

        lax.fori_loop(0, fine_rows, fine_step, 0, unroll=16)
        width = ready.shape[3]
        left = jnp.concatenate(
            [
                jnp.concatenate(
                    [
                        shifted[pl.ds(part * half + block, fine_rows, stride=2 * half), :]
                        for block in range(half)
                    ],
                    axis=1,
                )
                for part in range(2)
            ],
            axis=0,
        )
        result = three_pass(split(left), (high[...], low[...]), ((1,), (0,)))
        for part in range(2):
            for dest in range(dest_count):
                start = part * fine_rows + dest * dest_rows
                ready[plane, dest, part * dest_rows : (part + 1) * dest_rows, :] = result[
                    start : start + dest_rows, :width
                ]
        spill = result[:fine_rows, width:] + pltpu.roll(result[fine_rows:, width:], half, 1)
        spill = spill.T[: 2 * half]
        for dest in range(dest_count):
            ready[plane, dest, 2 * dest_rows :, :] = jnp.concatenate(
                [
                    spill[:, dest * dest_rows : (dest + 1) * dest_rows],
                    jnp.zeros((2 * half, width - dest_rows), jnp.float32),
                ],
                axis=1,
            )
        pltpu.make_async_copy(ready.at[plane], out.at[plane], sems.at[plane]).start()
        return unused

    lax.fori_loop(0, planes, plane_step, 0)
    for plane in range(planes):
        pltpu.make_async_copy(ready.at[plane], out.at[plane], sems.at[plane]).wait()


def join_kernel(source_count, parts, out, whole):
    dest_rows = out.shape[0]
    dirs = parts.shape[0] // source_count
    over = jnp.concatenate(
        [parts[index, 2 * dest_rows :, :lanes] for index in range(parts.shape[0])], axis=0
    ).T[:dest_rows]
    lane = lax.broadcasted_iota(jnp.int32, (dest_rows, lanes), 1)
    for source in range(source_count):
        for part in range(2):
            turned = []
            for index in range(dirs):
                first = (source * dirs + index) * 2 * half + part * half
                turned.append(pltpu.roll(over, (lanes - rim - first) % lanes, 1))
            for index in range(dirs):
                fix = jnp.where(lane < rim, turned[index - 1], 0.0) + jnp.where(
                    lane >= lanes - rim, turned[(index + 1) % dirs], 0.0
                )
                whole[
                    index, pl.ds(part * source_count + source, dest_rows, stride=2 * source_count), :
                ] = parts[source * dirs + index, part * dest_rows : (part + 1) * dest_rows, :] + fix

    def row_step(row, unused):
        start = pl.multiple_of(row * 2 * source_count, 2 * source_count)
        both = jnp.concatenate(
            [whole[index, pl.ds(start, 2 * source_count), :] for index in range(dirs)], axis=1
        )
        out[row, 0] = both[:source_count]
        out[row, 1] = both[source_count:]
        return unused

    lax.fori_loop(0, dest_rows, row_step, 0, unroll=8)


def per_device(
    coarse_field,
    trans_table,
    partner_ids,
    partner_types,
    partner_count,
    child_count,
    child_octant,
    dir_angles,
    stencil_ids,
    stencil_weights,
):
    rows, _, source_count, kc_dev = coarse_field.shape
    slots = partner_ids.shape[1]
    type_count = trans_table.shape[0]
    fine_rows = child_octant.shape[0]
    ring_count = lax.axis_size("ring")
    dir_count = lax.axis_size("dir")
    zed = lax.axis_index("zed")
    ring = lax.axis_index("ring")
    dir_index = lax.axis_index("dir")
    fine_count = stencil_ids.shape[0] // 4
    kf_dev = fine_count // dir_count
    kc_pad = up(kc_dev, half * lanes)
    kf_pad = up(kf_dev, lanes)
    pad_dirs = kc_pad - kc_dev
    assert source_count == planes and kc_pad == half * lanes
    dest_rows = fine_rows // dir_count

    field = jnp.pad(coarse_field, ((0, 0), (0, 0), (0, 0), (0, pad_dirs)))
    edge_rows = 0
    if ring_count == 2:
        edges = lax.ppermute(near_edge(field, ring), "ring", [(0, 1), (1, 0)])
        edge_rows = edges.shape[0]
    arrived = lax.all_to_all(pack(field, []), "zed", split_axis=0, concat_axis=0, tiled=True)

    plane_of = partner_ids // (ring_count * rows)
    ring_of = partner_ids // rows % ring_count
    local = partner_ids % rows
    live = jnp.arange(slots, dtype=jnp.int32)[None, :] < partner_count[:, None]
    if ring_count == 2:
        size = rows
        place = jnp.where(
            ring_of == ring,
            plane_of * rows + local,
            planes * rows + plane_of * edge_rows + edge_rank(local, rows),
        )
    else:
        size = ring_count * rows
        place = partner_ids
    field_rows = planes * (size + edge_rows)
    place = jnp.where(live, place, field_rows)
    together = 4
    fixed = slots // 2
    group = 5 if (slots - fixed) % 5 == 0 else 1
    index = jnp.arange(rows, dtype=jnp.int32)
    before = (partner_count[None, :] > partner_count[:, None]) | (
        (partner_count[None, :] == partner_count[:, None]) & (index[None, :] < index[:, None])
    )
    rank = jnp.sum(before.astype(jnp.int32), axis=1)
    at_rank = rank[None, :] == index[:, None]
    order = jnp.sum(jnp.where(at_rank, index[None, :], 0), axis=1)
    first = rank[None, :] == index[: rows // together, None] * together
    longest = jnp.sum(jnp.where(first, partner_count[None, :], 0), axis=1)
    turns = jnp.maximum((longest - fixed + group - 1) // group, 0)
    bounds = jnp.sum(jnp.where(index[None, :] <= index[:, None], child_count[None, :], 0), axis=1)
    parent = jnp.sum(
        (bounds[None, :] <= jnp.arange(fine_rows, dtype=jnp.int32)[:, None]).astype(jnp.int32), axis=1
    )
    lists = [
        place.reshape(-1),
        partner_types.reshape(-1),
        parent,
        child_octant,
        order,
        turns,
    ]
    offsets = [sum(one.shape[0] for one in lists[:count]) for count in range(len(lists) + 1)]
    stride = up(offsets[-1], 8 * lanes)
    plan = Plan(rows, slots, fine_rows, stride, *offsets[1:-1], together, fixed, group)
    meta = jnp.pad(jnp.concatenate(lists), (0, stride - offsets[-1])).astype(jnp.float32)
    meta = meta.reshape(stride // lanes, lanes)

    if ring_count == 2:
        notes = pack(edges, [meta])
    else:
        notes = jnp.broadcast_to(meta[None], (planes,) + meta.shape)
    received = []
    for step in range(planes):
        note = lax.dynamic_index_in_dim(notes, zed ^ step, axis=0, keepdims=False)
        if step:
            note = lax.ppermute(note, "zed", [(plane, plane ^ step) for plane in range(planes)])
        received.append(note)
    edge_part = edge_rows * 2 * half
    meta = jnp.concatenate([note[edge_part:] for note in received]).astype(jnp.int32).reshape(-1)
    if ring_count == 2:
        pieces = [arrived] + received
    else:
        pieces = [lax.all_gather(arrived, "ring", axis=1, tiled=True)]

    def blocks(table):
        return jnp.pad(table, ((0, 0), (0, pad_dirs))).reshape(-1, half, lanes)

    def doubled(table, sign):
        return jnp.concatenate([blocks(table), sign * blocks(table)], axis=1)

    table = jnp.pad(trans_table, ((0, 0), (0, 0), (0, pad_dirs))).reshape(-1, 2 * half, lanes)
    angles = lax.dynamic_slice_in_dim(dir_angles, dir_index * kc_dev, kc_dev, axis=1)
    octants = jnp.arange(8, dtype=jnp.int32)
    sign_x = 1.0 - 2.0 * (octants % 2).astype(jnp.float32)
    sign_y = 1.0 - 2.0 * (octants // 2 % 2).astype(jnp.float32)
    sign_z = 1.0 - 2.0 * (octants // 4).astype(jnp.float32)
    unit_x = jnp.sin(angles[0]) * jnp.cos(angles[1])
    unit_y = jnp.sin(angles[0]) * jnp.sin(angles[1])
    unit_z = jnp.cos(angles[0])
    phase = wave_scale * (
        sign_x[:, None] * unit_x[None, :] + sign_y[:, None] * unit_y[None, :] + sign_z[:, None] * unit_z[None, :]
    )
    phases = jnp.concatenate(
        [doubled(jnp.cos(phase), 1.0), doubled(jnp.sin(phase), -1.0)], axis=1
    ).reshape(-1, 2, 2 * half, lanes)

    ids = lax.dynamic_slice_in_dim(stencil_ids, dir_index * kc_dev, kc_dev, axis=0).T
    weights = lax.dynamic_slice_in_dim(stencil_weights, dir_index * kc_dev, kc_dev, axis=0).T

    def interp(targets):
        matrix = jnp.zeros((targets.shape[0], kc_dev), jnp.float32)
        for point in range(ids.shape[0]):
            matrix = matrix + jnp.where(
                ids[point][None, :] == targets[:, None], weights[point][None, :], 0.0
            )
        return jnp.pad(matrix, ((0, 0), (0, pad_dirs)))

    first_fine = dir_index * kf_dev
    own = jnp.arange(kf_dev, dtype=jnp.int32)
    outside = jnp.concatenate(
        [jnp.arange(-rim, 0, dtype=jnp.int32), jnp.arange(kf_dev, kf_dev + rim, dtype=jnp.int32)]
    )
    matrix = jnp.pad(interp(first_fine + own), ((0, kf_pad - kf_dev), (0, 0)))
    spill = interp((first_fine + outside) % fine_count)
    matrices = jnp.concatenate([matrix, jnp.pad(spill, ((0, lanes - half), (0, 0)))], axis=0).T
    rounded = lax.reduce_precision(matrices, 8, 7)
    high = rounded.astype(jnp.bfloat16)
    low = (matrices - rounded).astype(jnp.bfloat16)

    whole = pl.BlockSpec(memory_space=pltpu.VMEM)
    message = (2 * dest_rows + 2 * half, kf_pad)
    local_fine = pl.pallas_call(
        functools.partial(fine_kernel, plan, size, edge_rows),
        out_shape=pltpu.HBM((planes, dir_count) + message, jnp.float32),
        in_specs=[pl.BlockSpec(memory_space=pltpu.SMEM)] * 2 + [whole] * (len(pieces) + 4),
        out_specs=pl.BlockSpec(memory_space=pltpu.HBM),
        scratch_shapes=[
            pltpu.VMEM((field_rows + 1, 2, 2 * half, lanes), jnp.float32),
            pltpu.VMEM((rows, 2, 2 * half, lanes), jnp.float32),
            pltpu.VMEM((fine_rows * 2 * half, lanes), jnp.float32),
            pltpu.VMEM((planes, dir_count) + message, jnp.float32),
            pltpu.SemaphoreType.DMA((planes,)),
        ],
        compiler_params=pltpu.CompilerParams(vmem_limit_bytes=48 * 2**20),
        name="translate_and_interpolate",
    )(zed.reshape(1), meta, *pieces, table, phases, high, low)

    parts = lax.all_to_all(
        local_fine.reshape((planes * dir_count,) + message),
        ("zed", "dir"),
        split_axis=0,
        concat_axis=0,
        tiled=True,
    )
    result = (dest_rows, 2, source_count, fine_count)
    if kf_dev == lanes and planes * dir_count * 2 * half == lanes and dest_rows <= lanes:
        return pl.pallas_call(
            functools.partial(join_kernel, source_count),
            out_shape=jax.ShapeDtypeStruct(result, jnp.float32),
            in_specs=[whole],
            out_specs=whole,
            scratch_shapes=[pltpu.VMEM((dir_count, dest_rows * 2 * source_count, lanes), jnp.float32)],
            name="join_parts",
        )(parts)
    parts = parts.reshape((planes, dir_count) + message)
    main = parts[:, :, : 2 * dest_rows, :kf_dev].reshape(planes, dir_count, 2, dest_rows, kf_dev)
    over = parts[:, :, 2 * dest_rows :, :dest_rows].reshape(planes, dir_count, 2, 2 * rim, dest_rows)
    low = jnp.roll(over[:, :, :, :rim], -1, axis=1)
    high = jnp.roll(over[:, :, :, rim:], 1, axis=1)
    middle = jnp.zeros((planes, dir_count, 2, kf_dev - 2 * rim, dest_rows), jnp.float32)
    fix = jnp.concatenate([high, middle, low], axis=3)
    total = main.transpose(3, 2, 0, 1, 4) + fix.transpose(4, 2, 0, 1, 3)
    return total.reshape(result)


def solution(mesh):
    boxes, dirs = mesh.shape["box"], mesh.shape["dir"]
    fine_mesh = Mesh(mesh.devices.reshape(planes, boxes // planes, dirs), ("zed", "ring", "dir"))
    box = ("zed", "ring")
    placed = (
        P(box, None, None, "dir"),
        P(None, None, "dir"),
        P(box, None),
        P(box, None),
        P(box),
        P(box),
        P(box),
        P(),
        P(),
        P(),
    )
    return jax.shard_map(
        per_device,
        mesh=fine_mesh,
        in_specs=placed,
        out_specs=P(("zed", "ring", "dir"), None, None, None),
        check_vma=False,
    )
```

```python
import collections
import functools

import jax
import jax.numpy as jnp
from jax import lax
from jax.experimental import pallas as pl
from jax.experimental.pallas import tpu as pltpu
from jax.sharding import Mesh
from jax.sharding import PartitionSpec as P

wave_scale = 3.0
planes = 4
lanes = 128
half = 4
rim = 2


plan_fields = ["rows", "slots", "fine_rows", "stride", "kinds", "parent", "octant", "order", "turns"]
Plan = collections.namedtuple("Plan", plan_fields + ["together", "fixed", "group"])


def up(size, step):
    return -(-size // step) * step


def edge_bits(rows):
    bits = rows.bit_length() - 1
    return bits, [place for place in range(2, bits) if place % 2 == bits % 2]


def near_edge(block, ring):
    rows = block.shape[0]
    bits, fixed = edge_bits(rows)
    tail = block.shape[1:]
    picked = block.reshape((2,) * bits + tail)
    for place in fixed:
        picked = lax.dynamic_index_in_dim(picked, 1 - ring, axis=bits - 1 - place, keepdims=True)
    return picked.reshape((rows >> len(fixed),) + tail)


def edge_rank(local, rows):
    bits, fixed = edge_bits(rows)
    rank = jnp.zeros_like(local)
    taken = 0
    for place in range(bits):
        if place not in fixed:
            rank = rank + (local // 2**place % 2) * 2**taken
            taken += 1
    return rank


def split(value):
    high = value.astype(jnp.bfloat16)
    low = (value - high.astype(jnp.float32)).astype(jnp.bfloat16)
    return high, low


def three_pass(left, right, dims):
    dot = functools.partial(
        lax.dot_general, dimension_numbers=(dims, ((), ())), preferred_element_type=jnp.float32
    )
    return dot(left[0], right[0]) + (dot(left[0], right[1]) + dot(left[1], right[0]))


def pack_kernel(source_count, field, *refs):
    notes, (out, whole) = refs[:-2], refs[-2:]
    rows = field.shape[0]
    stride = 2 * source_count

    def row_step(row, unused):
        both = jnp.concatenate([field[row, 0], field[row, 1]], axis=0)
        for block in range(half):
            whole[block, pl.ds(pl.multiple_of(row * stride, stride), stride), :] = both[
                :, block * lanes : (block + 1) * lanes
            ]
        return unused

    lax.fori_loop(0, rows, row_step, 0, unroll=8)
    for source in range(source_count):
        for part in range(2):
            for block in range(half):
                out[source, pl.ds(part * half + block, rows, stride=2 * half), :] = whole[
                    block, pl.ds(part * source_count + source, rows, stride=stride), :
                ]
        for note in notes:
            out[source, rows * 2 * half :, :] = note[...]


def pack(field, notes):
    rows, _, source_count, width = field.shape
    length = rows * 2 * half + sum(note.shape[0] for note in notes)
    whole = pl.BlockSpec(memory_space=pltpu.VMEM)
    return pl.pallas_call(
        functools.partial(pack_kernel, source_count),
        out_shape=pltpu.HBM((source_count, length, lanes), jnp.float32),
        in_specs=[whole] * (1 + len(notes)),
        out_specs=whole,
        scratch_shapes=[pltpu.VMEM((half, rows * 2 * source_count, lanes), jnp.float32)],
        name="pack_sources",
    )(field, *notes)


def tile(start):
    return pl.ds(pl.multiple_of(start, 2 * half), 2 * half)


def fine_kernel(plan, size, edge_size, zed, meta, main, *refs):
    edges = refs[: planes if edge_size else 0]
    refs = refs[len(edges) :]
    table, phases, high, low, out, field, moved, shifted, ready, sems = refs
    rows, fine_rows = plan.rows, plan.fine_rows
    own = zed[0]

    def both(start):
        return pl.ds(pl.multiple_of(start, 4 * half), 4 * half)

    def with_turned(value):
        return jnp.concatenate([value, pltpu.roll(value, half, 0)], axis=0)

    for plane in range(planes):

        def main_step(row, unused, plane=plane):
            value = main[plane, tile(row * 2 * half), :]
            field[both((plane * size + row) * 4 * half), :] = with_turned(value)
            return unused

        lax.fori_loop(0, size, main_step, 0, unroll=8)
    for step, edge in enumerate(edges):
        first = planes * size + (own ^ step) * edge_size

        def edge_step(row, unused, first=first, edge=edge):
            field[both((first + row) * 4 * half), :] = with_turned(edge[tile(row * 2 * half), :])
            return unused

        lax.fori_loop(0, edge_size, edge_step, 0, unroll=8)
    field[both(planes * (size + edge_size) * 4 * half), :] = jnp.zeros((4 * half, lanes), jnp.float32)

    blank = jnp.zeros((2 * half, lanes), jnp.float32)
    sub = lax.broadcasted_iota(jnp.int32, (2 * half, lanes), 0)
    dest_count = out.shape[1]
    dest_rows = fine_rows // dest_count

    def plane_step(plane, unused):
        base = (own ^ plane) * plan.stride

        def boxes_step(step, unused):
            ranks = [step * plan.together + each for each in range(plan.together)]
            boxes = [meta[base + plan.order, rank] for rank in ranks]
            turns = meta[base + plan.order, plan.turns + step]

            def work(slot_count):
                places = [base + box for box in boxes]
                sums = [[blank, blank] for box in boxes]
                for slot in range(slot_count):
                    for each in range(plan.together):
                        value = field[both(meta[places[each], slot]), :]
                        factor = table[tile(meta[places[each], plan.kinds + slot]), :]
                        sums[each][0] += factor * value[: 2 * half]
                        sums[each][1] += factor * value[2 * half :]
                for each in range(plan.together):
                    straight, crossed = sums[each]
                    total = jnp.where(
                        sub < half,
                        straight + pltpu.roll(straight, half, 0),
                        pltpu.roll(crossed, half, 0) - crossed,
                    )
                    moved[both(boxes[each] * 4 * half), :] = with_turned(total)

            for turn in range((plan.slots - plan.fixed) // plan.group + 1):
                pl.when(turns == turn)(functools.partial(work, plan.fixed + turn * plan.group))
            return unused

        lax.fori_loop(0, rows // plan.together, boxes_step, 0)

        def fine_step(block, unused):
            for each in range(lanes):
                value = moved[both(meta[base + plan.parent + block, each]), :]
                phase = phases[both(meta[base + plan.octant + block, each]), :]
                value = value * phase
                shifted[tile((block * lanes + each) * 2 * half), :] = value[: 2 * half] + value[2 * half :]
            return unused

        lax.fori_loop(0, fine_rows // lanes, fine_step, 0)
        width = ready.shape[3]
        left = jnp.concatenate(
            [
                jnp.concatenate(
                    [
                        shifted[pl.ds(part * half + block, fine_rows, stride=2 * half), :]
                        for block in range(half)
                    ],
                    axis=1,
                )
                for part in range(2)
            ],
            axis=0,
        )
        result = three_pass(split(left), (high[...], low[...]), ((1,), (0,)))
        for part in range(2):
            for dest in range(dest_count):
                start = part * fine_rows + dest * dest_rows
                ready[plane, dest, part * dest_rows : (part + 1) * dest_rows, :] = result[
                    start : start + dest_rows, :width
                ]
        spill = result[:fine_rows, width:] + pltpu.roll(result[fine_rows:, width:], half, 1)
        spill = spill.T[: 2 * half]
        for dest in range(dest_count):
            ready[plane, dest, 2 * dest_rows :, :] = jnp.concatenate(
                [
                    spill[:, dest * dest_rows : (dest + 1) * dest_rows],
                    jnp.zeros((2 * half, width - dest_rows), jnp.float32),
                ],
                axis=1,
            )
        pltpu.make_async_copy(ready.at[plane], out.at[plane], sems.at[plane]).start()
        return unused

    lax.fori_loop(0, planes, plane_step, 0)
    for plane in range(planes):
        pltpu.make_async_copy(ready.at[plane], out.at[plane], sems.at[plane]).wait()


def join_kernel(source_count, parts, out, whole):
    dest_rows = out.shape[0]
    dirs = parts.shape[0] // source_count
    over = jnp.concatenate(
        [parts[index, 2 * dest_rows :, :lanes] for index in range(parts.shape[0])], axis=0
    ).T[:dest_rows]
    lane = lax.broadcasted_iota(jnp.int32, (dest_rows, lanes), 1)
    for source in range(source_count):
        for part in range(2):
            turned = []
            for index in range(dirs):
                first = (source * dirs + index) * 2 * half + part * half
                turned.append(pltpu.roll(over, (lanes - rim - first) % lanes, 1))
            for index in range(dirs):
                fix = jnp.where(lane < rim, turned[index - 1], 0.0) + jnp.where(
                    lane >= lanes - rim, turned[(index + 1) % dirs], 0.0
                )
                whole[
                    index, pl.ds(part * source_count + source, dest_rows, stride=2 * source_count), :
                ] = parts[source * dirs + index, part * dest_rows : (part + 1) * dest_rows, :] + fix

    def row_step(row, unused):
        start = pl.multiple_of(row * 2 * source_count, 2 * source_count)
        both = jnp.concatenate(
            [whole[index, pl.ds(start, 2 * source_count), :] for index in range(dirs)], axis=1
        )
        out[row, 0] = both[:source_count]
        out[row, 1] = both[source_count:]
        return unused

    lax.fori_loop(0, dest_rows, row_step, 0, unroll=8)


def per_device(
    coarse_field,
    trans_table,
    partner_ids,
    partner_types,
    partner_count,
    child_count,
    child_octant,
    dir_angles,
    stencil_ids,
    stencil_weights,
):
    rows, _, source_count, kc_dev = coarse_field.shape
    slots = partner_ids.shape[1]
    type_count = trans_table.shape[0]
    fine_rows = child_octant.shape[0]
    ring_count = lax.axis_size("ring")
    dir_count = lax.axis_size("dir")
    zed = lax.axis_index("zed")
    ring = lax.axis_index("ring")
    dir_index = lax.axis_index("dir")
    fine_count = stencil_ids.shape[0] // 4
    kf_dev = fine_count // dir_count
    kc_pad = up(kc_dev, half * lanes)
    kf_pad = up(kf_dev, lanes)
    pad_dirs = kc_pad - kc_dev
    assert source_count == planes and kc_pad == half * lanes
    dest_rows = fine_rows // dir_count

    field = jnp.pad(coarse_field, ((0, 0), (0, 0), (0, 0), (0, pad_dirs)))
    packed = pack(field, [])
    edge_rows = 0
    if ring_count == 2:
        packed, field = lax.optimization_barrier((packed, field))
        edges = lax.ppermute(near_edge(field, ring), "ring", [(0, 1), (1, 0)])
        edge_rows = edges.shape[0]
    arrived = lax.all_to_all(packed, "zed", split_axis=0, concat_axis=0, tiled=True)

    plane_of = partner_ids // (ring_count * rows)
    ring_of = partner_ids // rows % ring_count
    local = partner_ids % rows
    live = jnp.arange(slots, dtype=jnp.int32)[None, :] < partner_count[:, None]
    if ring_count == 2:
        size = rows
        place = jnp.where(
            ring_of == ring,
            plane_of * rows + local,
            planes * rows + plane_of * edge_rows + edge_rank(local, rows),
        )
    else:
        size = ring_count * rows
        place = partner_ids
    field_rows = planes * (size + edge_rows)
    place = jnp.where(live, place, field_rows)
    together = 4
    fixed = slots // 2
    group = 5 if (slots - fixed) % 5 == 0 else 1
    index = jnp.arange(rows, dtype=jnp.int32)
    before = (partner_count[None, :] > partner_count[:, None]) | (
        (partner_count[None, :] == partner_count[:, None]) & (index[None, :] < index[:, None])
    )
    rank = jnp.sum(before.astype(jnp.int32), axis=1)
    at_rank = rank[None, :] == index[:, None]
    order = jnp.sum(jnp.where(at_rank, index[None, :], 0), axis=1)
    first = rank[None, :] == index[: rows // together, None] * together
    longest = jnp.sum(jnp.where(first, partner_count[None, :], 0), axis=1)
    turns = jnp.maximum((longest - fixed + group - 1) // group, 0)
    bounds = jnp.sum(jnp.where(index[None, :] <= index[:, None], child_count[None, :], 0), axis=1)
    parent = jnp.sum(
        (bounds[None, :] <= jnp.arange(fine_rows, dtype=jnp.int32)[:, None]).astype(jnp.int32), axis=1
    )
    def across(one, width=lanes):
        return jnp.pad(one, ((0, 0), (0, width - one.shape[1])))

    kinds_at = up(slots, lanes // 2)
    turns_at = lanes // 2
    assert 2 * kinds_at <= lanes and rows <= turns_at and fine_rows % lanes == 0
    lists = [
        jnp.concatenate(
            [across(place * 4 * half, kinds_at), across(partner_types * 2 * half, lanes - kinds_at)], axis=1
        ),
        (parent * 4 * half).reshape(-1, lanes),
        (child_octant * 4 * half).reshape(-1, lanes),
        across(jnp.concatenate([across(order[None], turns_at), turns[None]], axis=1)),
    ]
    offsets = [sum(one.shape[0] for one in lists[:count]) for count in range(len(lists) + 1)]
    stride = up(offsets[-1], 8)
    plan = Plan(rows, slots, fine_rows, stride, kinds_at, *offsets[1:-1], turns_at, together, fixed, group)
    meta = jnp.pad(jnp.concatenate(lists), ((0, stride - offsets[-1]), (0, 0))).astype(jnp.float32)

    if ring_count == 2:
        notes = pack(edges, [meta])
    else:
        notes = jnp.broadcast_to(meta[None], (planes,) + meta.shape)
    received = []
    for step in range(planes):
        note = lax.dynamic_index_in_dim(notes, zed ^ step, axis=0, keepdims=False)
        if step:
            note = lax.ppermute(note, "zed", [(plane, plane ^ step) for plane in range(planes)])
        received.append(note)
    edge_part = edge_rows * 2 * half
    meta = jnp.concatenate([note[edge_part:] for note in received]).astype(jnp.int32)
    if ring_count == 2:
        pieces = [arrived] + received
    else:
        pieces = [lax.all_gather(arrived, "ring", axis=1, tiled=True)]

    def blocks(table):
        return jnp.pad(table, ((0, 0), (0, pad_dirs))).reshape(-1, half, lanes)

    def doubled(table, sign):
        return jnp.concatenate([blocks(table), sign * blocks(table)], axis=1)

    table = jnp.pad(trans_table, ((0, 0), (0, 0), (0, pad_dirs))).reshape(-1, lanes)
    angles = lax.dynamic_slice_in_dim(dir_angles, dir_index * kc_dev, kc_dev, axis=1)
    octants = jnp.arange(8, dtype=jnp.int32)
    sign_x = 1.0 - 2.0 * (octants % 2).astype(jnp.float32)
    sign_y = 1.0 - 2.0 * (octants // 2 % 2).astype(jnp.float32)
    sign_z = 1.0 - 2.0 * (octants // 4).astype(jnp.float32)
    unit_x = jnp.sin(angles[0]) * jnp.cos(angles[1])
    unit_y = jnp.sin(angles[0]) * jnp.sin(angles[1])
    unit_z = jnp.cos(angles[0])
    phase = wave_scale * (
        sign_x[:, None] * unit_x[None, :] + sign_y[:, None] * unit_y[None, :] + sign_z[:, None] * unit_z[None, :]
    )
    phases = jnp.concatenate(
        [doubled(jnp.cos(phase), 1.0), doubled(jnp.sin(phase), -1.0)], axis=1
    ).reshape(-1, lanes)

    ids = lax.dynamic_slice_in_dim(stencil_ids, dir_index * kc_dev, kc_dev, axis=0).T
    weights = lax.dynamic_slice_in_dim(stencil_weights, dir_index * kc_dev, kc_dev, axis=0).T

    def interp(targets):
        matrix = jnp.zeros((targets.shape[0], kc_dev), jnp.float32)
        for point in range(ids.shape[0]):
            matrix = matrix + jnp.where(
                ids[point][None, :] == targets[:, None], weights[point][None, :], 0.0
            )
        return jnp.pad(matrix, ((0, 0), (0, pad_dirs)))

    first_fine = dir_index * kf_dev
    own = jnp.arange(kf_dev, dtype=jnp.int32)
    outside = jnp.concatenate(
        [jnp.arange(-rim, 0, dtype=jnp.int32), jnp.arange(kf_dev, kf_dev + rim, dtype=jnp.int32)]
    )
    matrix = jnp.pad(interp(first_fine + own), ((0, kf_pad - kf_dev), (0, 0)))
    spill = interp((first_fine + outside) % fine_count)
    matrices = jnp.concatenate([matrix, jnp.pad(spill, ((0, lanes - half), (0, 0)))], axis=0).T
    rounded = lax.reduce_precision(matrices, 8, 7)
    high = rounded.astype(jnp.bfloat16)
    low = (matrices - rounded).astype(jnp.bfloat16)

    whole = pl.BlockSpec(memory_space=pltpu.VMEM)
    message = (2 * dest_rows + 2 * half, kf_pad)
    local_fine = pl.pallas_call(
        functools.partial(fine_kernel, plan, size, edge_rows),
        out_shape=pltpu.HBM((planes, dir_count) + message, jnp.float32),
        in_specs=[pl.BlockSpec(memory_space=pltpu.SMEM)] * 2 + [whole] * (len(pieces) + 4),
        out_specs=pl.BlockSpec(memory_space=pltpu.HBM),
        scratch_shapes=[
            pltpu.VMEM(((field_rows + 1) * 4 * half, lanes), jnp.float32),
            pltpu.VMEM((rows * 4 * half, lanes), jnp.float32),
            pltpu.VMEM((fine_rows * 2 * half, lanes), jnp.float32),
            pltpu.VMEM((planes, dir_count) + message, jnp.float32),
            pltpu.SemaphoreType.DMA((planes,)),
        ],
        compiler_params=pltpu.CompilerParams(vmem_limit_bytes=48 * 2**20),
        name="translate_and_interpolate",
    )(zed.reshape(1), meta, *pieces, table, phases, high, low)

    parts = lax.all_to_all(
        local_fine.reshape((planes * dir_count,) + message),
        ("zed", "dir"),
        split_axis=0,
        concat_axis=0,
        tiled=True,
    )
    result = (dest_rows, 2, source_count, fine_count)
    if kf_dev == lanes and planes * dir_count * 2 * half == lanes and dest_rows <= lanes:
        return pl.pallas_call(
            functools.partial(join_kernel, source_count),
            out_shape=jax.ShapeDtypeStruct(result, jnp.float32),
            in_specs=[whole],
            out_specs=whole,
            scratch_shapes=[pltpu.VMEM((dir_count, dest_rows * 2 * source_count, lanes), jnp.float32)],
            compiler_params=pltpu.CompilerParams(vmem_limit_bytes=24 * 2**20),
            name="join_parts",
        )(parts)
    parts = parts.reshape((planes, dir_count) + message)
    main = parts[:, :, : 2 * dest_rows, :kf_dev].reshape(planes, dir_count, 2, dest_rows, kf_dev)
    over = parts[:, :, 2 * dest_rows :, :dest_rows].reshape(planes, dir_count, 2, 2 * rim, dest_rows)
    low = jnp.roll(over[:, :, :, :rim], -1, axis=1)
    high = jnp.roll(over[:, :, :, rim:], 1, axis=1)
    middle = jnp.zeros((planes, dir_count, 2, kf_dev - 2 * rim, dest_rows), jnp.float32)
    fix = jnp.concatenate([high, middle, low], axis=3)
    total = main.transpose(3, 2, 0, 1, 4) + fix.transpose(4, 2, 0, 1, 3)
    return total.reshape(result)


def solution(mesh):
    boxes, dirs = mesh.shape["box"], mesh.shape["dir"]
    fine_mesh = Mesh(mesh.devices.reshape(planes, boxes // planes, dirs), ("zed", "ring", "dir"))
    box = ("zed", "ring")
    placed = (
        P(box, None, None, "dir"),
        P(None, None, "dir"),
        P(box, None),
        P(box, None),
        P(box),
        P(box),
        P(box),
        P(),
        P(),
        P(),
    )
    return jax.shard_map(
        per_device,
        mesh=fine_mesh,
        in_specs=placed,
        out_specs=P(("zed", "ring", "dir"), None, None, None),
        check_vma=False,
    )
```

```python
import collections
import functools

import jax
import jax.numpy as jnp
from jax import lax
from jax.experimental import pallas as pl
from jax.experimental.pallas import tpu as pltpu
from jax.sharding import Mesh
from jax.sharding import PartitionSpec as P

wave_scale = 3.0
planes = 4
lanes = 128
half = 4
rim = 2


plan_fields = ["rows", "slots", "fine_rows", "stride", "kinds", "parent", "octant", "order", "turns"]
Plan = collections.namedtuple("Plan", plan_fields + ["together", "fixed", "group"])


def up(size, step):
    return -(-size // step) * step


def edge_bits(rows):
    bits = rows.bit_length() - 1
    return bits, [place for place in range(2, bits) if place % 2 == bits % 2]


def near_edge(block, ring):
    rows = block.shape[0]
    bits, fixed = edge_bits(rows)
    tail = block.shape[1:]
    picked = block.reshape((2,) * bits + tail)
    for place in fixed:
        picked = lax.dynamic_index_in_dim(picked, 1 - ring, axis=bits - 1 - place, keepdims=True)
    return picked.reshape((rows >> len(fixed),) + tail)


def edge_rank(local, rows):
    bits, fixed = edge_bits(rows)
    rank = jnp.zeros_like(local)
    taken = 0
    for place in range(bits):
        if place not in fixed:
            rank = rank + (local // 2**place % 2) * 2**taken
            taken += 1
    return rank


def split(value):
    high = value.astype(jnp.bfloat16)
    low = (value - high.astype(jnp.float32)).astype(jnp.bfloat16)
    return high, low


def three_pass(left, right, dims):
    dot = functools.partial(
        lax.dot_general, dimension_numbers=(dims, ((), ())), preferred_element_type=jnp.float32
    )
    return dot(left[0], right[0]) + (dot(left[0], right[1]) + dot(left[1], right[0]))


def pack_kernel(source_count, field, *refs):
    notes, (out, whole) = refs[:-2], refs[-2:]
    rows = field.shape[0]
    stride = 2 * source_count

    def row_step(row, unused):
        both = jnp.concatenate([field[row, 0], field[row, 1]], axis=0)
        for block in range(half):
            whole[block, pl.ds(pl.multiple_of(row * stride, stride), stride), :] = both[
                :, block * lanes : (block + 1) * lanes
            ]
        return unused

    lax.fori_loop(0, rows, row_step, 0, unroll=8)
    for source in range(source_count):
        for part in range(2):
            for block in range(half):
                out[source, pl.ds(part * half + block, rows, stride=2 * half), :] = whole[
                    block, pl.ds(part * source_count + source, rows, stride=stride), :
                ]
        for note in notes:
            out[source, rows * 2 * half :, :] = note[...]


def pack(field, notes):
    rows, _, source_count, width = field.shape
    length = rows * 2 * half + sum(note.shape[0] for note in notes)
    whole = pl.BlockSpec(memory_space=pltpu.VMEM)
    return pl.pallas_call(
        functools.partial(pack_kernel, source_count),
        out_shape=pltpu.HBM((source_count, length, lanes), jnp.float32),
        in_specs=[whole] * (1 + len(notes)),
        out_specs=whole,
        scratch_shapes=[pltpu.VMEM((half, rows * 2 * source_count, lanes), jnp.float32)],
        name="pack_sources",
    )(field, *notes)


def tile(start):
    return pl.ds(pl.multiple_of(start, 2 * half), 2 * half)


def fine_kernel(plan, size, edge_size, zed, lists, main, *refs):
    edges = refs[: planes if edge_size else 0]
    refs = refs[len(edges) :]
    table, phases, high, low, out, rims, meta, field, moved, shifted, ready, sems = refs
    rows, fine_rows = plan.rows, plan.fine_rows
    own = zed[0]

    def bring(step):
        return pltpu.make_async_copy(lists.at[step], meta.at[step % 2], sems.at[planes + step % 2])

    bring(0).start()
    lane = lax.broadcasted_iota(jnp.int32, rims.shape, 1)
    rims[...] = ((lane < rim) | (lane >= lanes - rim)).astype(jnp.float32)

    def both(start):
        return pl.ds(pl.multiple_of(start, 4 * half), 4 * half)

    def with_turned(value):
        return jnp.concatenate([value, pltpu.roll(value, half, 0)], axis=0)

    for plane in range(planes):

        def main_step(row, unused, plane=plane):
            value = main[plane, tile(row * 2 * half), :]
            field[both((plane * size + row) * 4 * half), :] = with_turned(value)
            return unused

        lax.fori_loop(0, size, main_step, 0, unroll=8)
    for step, edge in enumerate(edges):
        first = planes * size + (own ^ step) * edge_size

        def edge_step(row, unused, first=first, edge=edge):
            field[both((first + row) * 4 * half), :] = with_turned(edge[tile(row * 2 * half), :])
            return unused

        lax.fori_loop(0, edge_size, edge_step, 0, unroll=8)
    field[both(planes * (size + edge_size) * 4 * half), :] = jnp.zeros((4 * half, lanes), jnp.float32)

    blank = jnp.zeros((2 * half, lanes), jnp.float32)
    sub = lax.broadcasted_iota(jnp.int32, (2 * half, lanes), 0)
    dest_count = out.shape[1]
    dest_rows = fine_rows // dest_count

    def plane_step(turn, unused):
        plane = own ^ turn
        slot = turn % 2
        bring(turn).wait()

        @pl.when(turn + 1 < planes)
        def _():
            bring(turn + 1).start()


        def boxes_step(step, unused):
            ranks = [step * plan.together + each for each in range(plan.together)]
            boxes = [meta[slot, plan.order, rank] for rank in ranks]
            turns = meta[slot, plan.order, plan.turns + step]

            def work(slot_count):
                sums = [[blank, blank] for box in boxes]
                for pair in range(slot_count):
                    for each in range(plan.together):
                        value = field[both(meta[slot, boxes[each], pair]), :]
                        factor = table[tile(meta[slot, boxes[each], plan.kinds + pair]), :]
                        sums[each][0] += factor * value[: 2 * half]
                        sums[each][1] += factor * value[2 * half :]
                for each in range(plan.together):
                    straight, crossed = sums[each]
                    total = jnp.where(
                        sub < half,
                        straight + pltpu.roll(straight, half, 0),
                        pltpu.roll(crossed, half, 0) - crossed,
                    )
                    moved[both(boxes[each] * 4 * half), :] = with_turned(total)

            for more in range((plan.slots - plan.fixed) // plan.group + 1):
                pl.when(turns == more)(functools.partial(work, plan.fixed + more * plan.group))
            return unused

        lax.fori_loop(0, rows // plan.together, boxes_step, 0)

        def fine_step(block, unused):
            for each in range(lanes):
                value = moved[both(meta[slot, plan.parent + block, each]), :]
                phase = phases[both(meta[slot, plan.octant + block, each]), :]
                value = value * phase
                shifted[tile((block * lanes + each) * 2 * half), :] = value[: 2 * half] + value[2 * half :]
            return unused

        lax.fori_loop(0, fine_rows // lanes, fine_step, 0)
        width = ready.shape[3]
        left = jnp.concatenate(
            [
                jnp.concatenate(
                    [
                        shifted[pl.ds(part * half + block, fine_rows, stride=2 * half), :]
                        for block in range(half)
                    ],
                    axis=1,
                )
                for part in range(2)
            ],
            axis=0,
        )
        result = three_pass(split(left), (high[...], low[...]), ((1,), (0,)))
        for part in range(2):
            for dest in range(dest_count):
                start = part * fine_rows + dest * dest_rows
                ready[plane, dest, part * dest_rows : (part + 1) * dest_rows, :] = result[
                    start : start + dest_rows, :width
                ]
        spill = result[:fine_rows, width:] + pltpu.roll(result[fine_rows:, width:], half, 1)
        spill = spill.T[: 2 * half]
        for dest in range(dest_count):
            ready[plane, dest, 2 * dest_rows :, :] = jnp.concatenate(
                [
                    spill[:, dest * dest_rows : (dest + 1) * dest_rows],
                    jnp.zeros((2 * half, width - dest_rows), jnp.float32),
                ],
                axis=1,
            )
        pltpu.make_async_copy(ready.at[plane], out.at[plane], sems.at[plane]).start()
        return unused

    lax.fori_loop(0, planes, plane_step, 0)
    for plane in range(planes):
        pltpu.make_async_copy(ready.at[plane], out.at[plane], sems.at[plane]).wait()


def join_kernel(source_count, parts, rims, out, whole):
    dest_rows = out.shape[0]
    dirs = parts.shape[0] // source_count
    over = jnp.concatenate(
        [parts[index, 2 * dest_rows :, :lanes] for index in range(parts.shape[0])], axis=0
    ).T[:dest_rows]
    low = lax.broadcasted_iota(jnp.int32, (dest_rows, lanes), 1) < rim
    at_rim = jnp.broadcast_to(rims[...], (dest_rows, lanes)) < 0.5
    for source in range(source_count):
        for part in range(2):
            turned = []
            for index in range(dirs):
                first = (source * dirs + index) * 2 * half + part * half
                turned.append(pltpu.roll(over, (lanes - rim - first) % lanes, 1))
            for index in range(dirs):
                fix = jnp.where(at_rim, jnp.where(low, turned[index - 1], turned[(index + 1) % dirs]), 0.0)
                whole[
                    index, pl.ds(part * source_count + source, dest_rows, stride=2 * source_count), :
                ] = parts[source * dirs + index, part * dest_rows : (part + 1) * dest_rows, :] + fix

    def row_step(row, unused):
        start = pl.multiple_of(row * 2 * source_count, 2 * source_count)
        both = jnp.concatenate(
            [whole[index, pl.ds(start, 2 * source_count), :] for index in range(dirs)], axis=1
        )
        out[row, 0] = both[:source_count]
        out[row, 1] = both[source_count:]
        return unused

    lax.fori_loop(0, dest_rows, row_step, 0, unroll=8)


def per_device(
    coarse_field,
    trans_table,
    partner_ids,
    partner_types,
    partner_count,
    child_count,
    child_octant,
    dir_angles,
    stencil_ids,
    stencil_weights,
):
    rows, _, source_count, kc_dev = coarse_field.shape
    slots = partner_ids.shape[1]
    type_count = trans_table.shape[0]
    fine_rows = child_octant.shape[0]
    ring_count = lax.axis_size("ring")
    dir_count = lax.axis_size("dir")
    zed = lax.axis_index("zed")
    ring = lax.axis_index("ring")
    dir_index = lax.axis_index("dir")
    fine_count = stencil_ids.shape[0] // 4
    kf_dev = fine_count // dir_count
    kc_pad = up(kc_dev, half * lanes)
    kf_pad = up(kf_dev, lanes)
    pad_dirs = kc_pad - kc_dev
    assert source_count == planes and kc_pad == half * lanes
    dest_rows = fine_rows // dir_count

    field = jnp.pad(coarse_field, ((0, 0), (0, 0), (0, 0), (0, pad_dirs)))
    packed = pack(field, [])
    edge_rows = 0
    if ring_count == 2:
        packed, field = lax.optimization_barrier((packed, field))
        edges = lax.ppermute(near_edge(field, ring), "ring", [(0, 1), (1, 0)])
        edge_rows = edges.shape[0]
    arrived = lax.all_to_all(packed, "zed", split_axis=0, concat_axis=0, tiled=True)

    plane_of = partner_ids // (ring_count * rows)
    ring_of = partner_ids // rows % ring_count
    local = partner_ids % rows
    live = jnp.arange(slots, dtype=jnp.int32)[None, :] < partner_count[:, None]
    if ring_count == 2:
        size = rows
        place = jnp.where(
            ring_of == ring,
            plane_of * rows + local,
            planes * rows + plane_of * edge_rows + edge_rank(local, rows),
        )
    else:
        size = ring_count * rows
        place = partner_ids
    field_rows = planes * (size + edge_rows)
    place = jnp.where(live, place, field_rows)
    together = 4
    fixed = slots // 2
    group = 5 if (slots - fixed) % 5 == 0 else 1
    index = jnp.arange(rows, dtype=jnp.int32)
    before = (partner_count[None, :] > partner_count[:, None]) | (
        (partner_count[None, :] == partner_count[:, None]) & (index[None, :] < index[:, None])
    )
    rank = jnp.sum(before.astype(jnp.int32), axis=1)
    at_rank = rank[None, :] == index[:, None]
    order = jnp.sum(jnp.where(at_rank, index[None, :], 0), axis=1)
    first = rank[None, :] == index[: rows // together, None] * together
    longest = jnp.sum(jnp.where(first, partner_count[None, :], 0), axis=1)
    turns = jnp.maximum((longest - fixed + group - 1) // group, 0)
    bounds = jnp.sum(jnp.where(index[None, :] <= index[:, None], child_count[None, :], 0), axis=1)
    parent = jnp.sum(
        (bounds[None, :] <= jnp.arange(fine_rows, dtype=jnp.int32)[:, None]).astype(jnp.int32), axis=1
    )
    def across(one, width=lanes):
        return jnp.pad(one, ((0, 0), (0, width - one.shape[1])))

    kinds_at = slots
    width = up(2 * slots, lanes // 2)
    turns_at = lanes // 2
    packed_rows = rows * width // lanes
    assert width <= lanes and rows <= turns_at and fine_rows % lanes == 0
    pair_list = across(jnp.concatenate([place * 4 * half, partner_types * 2 * half], axis=1), width)
    lists = [
        pair_list.reshape(packed_rows, lanes),
        (parent * 4 * half).reshape(-1, lanes),
        (child_octant * 4 * half).reshape(-1, lanes),
        across(jnp.concatenate([across(order[None], turns_at), turns[None]], axis=1)),
    ]
    offsets = [sum(one.shape[0] for one in lists[:count]) for count in range(len(lists) + 1)]
    stride = up(offsets[-1], 8)
    shift = rows - packed_rows
    places = [offset + shift for offset in offsets[1:-1]]
    plan = Plan(rows, slots, fine_rows, stride + shift, kinds_at, *places, turns_at, together, fixed, group)
    meta = jnp.pad(jnp.concatenate(lists), ((0, stride - offsets[-1]), (0, 0))).astype(jnp.float32)

    if ring_count == 2:
        notes = pack(edges, [meta])
    else:
        notes = jnp.broadcast_to(meta[None], (planes,) + meta.shape)
    received = []
    for step in range(planes):
        note = lax.dynamic_index_in_dim(notes, zed ^ step, axis=0, keepdims=False)
        if step:
            note = lax.ppermute(note, "zed", [(plane, plane ^ step) for plane in range(planes)])
        received.append(note)
    edge_part = edge_rows * 2 * half
    meta = jnp.stack([note[edge_part:] for note in received]).astype(jnp.int32)
    pair_list = meta[:, :packed_rows].reshape(planes, rows, width)
    pair_list = jnp.pad(pair_list, ((0, 0), (0, 0), (0, lanes - width)))
    meta = jnp.concatenate([pair_list, meta[:, packed_rows:]], axis=1)
    if ring_count == 2:
        pieces = [arrived] + received
    else:
        pieces = [lax.all_gather(arrived, "ring", axis=1, tiled=True)]

    def blocks(table):
        return jnp.pad(table, ((0, 0), (0, pad_dirs))).reshape(-1, half, lanes)

    def doubled(table, sign):
        return jnp.concatenate([blocks(table), sign * blocks(table)], axis=1)

    table = jnp.pad(trans_table, ((0, 0), (0, 0), (0, pad_dirs))).reshape(-1, lanes)
    angles = lax.dynamic_slice_in_dim(dir_angles, dir_index * kc_dev, kc_dev, axis=1)
    octants = jnp.arange(8, dtype=jnp.int32)
    sign_x = 1.0 - 2.0 * (octants % 2).astype(jnp.float32)
    sign_y = 1.0 - 2.0 * (octants // 2 % 2).astype(jnp.float32)
    sign_z = 1.0 - 2.0 * (octants // 4).astype(jnp.float32)
    unit_x = jnp.sin(angles[0]) * jnp.cos(angles[1])
    unit_y = jnp.sin(angles[0]) * jnp.sin(angles[1])
    unit_z = jnp.cos(angles[0])
    phase = wave_scale * (
        sign_x[:, None] * unit_x[None, :] + sign_y[:, None] * unit_y[None, :] + sign_z[:, None] * unit_z[None, :]
    )
    phases = jnp.concatenate(
        [doubled(jnp.cos(phase), 1.0), doubled(jnp.sin(phase), -1.0)], axis=1
    ).reshape(-1, lanes)

    ids = lax.dynamic_slice_in_dim(stencil_ids, dir_index * kc_dev, kc_dev, axis=0).T
    weights = lax.dynamic_slice_in_dim(stencil_weights, dir_index * kc_dev, kc_dev, axis=0).T

    def interp(targets):
        matrix = jnp.zeros((targets.shape[0], kc_dev), jnp.float32)
        for point in range(ids.shape[0]):
            matrix = matrix + jnp.where(
                ids[point][None, :] == targets[:, None], weights[point][None, :], 0.0
            )
        return jnp.pad(matrix, ((0, 0), (0, pad_dirs)))

    first_fine = dir_index * kf_dev
    own = jnp.arange(kf_dev, dtype=jnp.int32)
    outside = jnp.concatenate(
        [jnp.arange(-rim, 0, dtype=jnp.int32), jnp.arange(kf_dev, kf_dev + rim, dtype=jnp.int32)]
    )
    matrix = jnp.pad(interp(first_fine + own), ((0, kf_pad - kf_dev), (0, 0)))
    spill = interp((first_fine + outside) % fine_count)
    matrices = jnp.concatenate([matrix, jnp.pad(spill, ((0, lanes - half), (0, 0)))], axis=0).T
    rounded = lax.reduce_precision(matrices, 8, 7)
    high = rounded.astype(jnp.bfloat16)
    low = (matrices - rounded).astype(jnp.bfloat16)

    whole = pl.BlockSpec(memory_space=pltpu.VMEM)
    message = (2 * dest_rows + 2 * half, kf_pad)
    local_fine, rims = pl.pallas_call(
        functools.partial(fine_kernel, plan, size, edge_rows),
        out_shape=[
            pltpu.HBM((planes, dir_count) + message, jnp.float32),
            jax.ShapeDtypeStruct((2 * half, lanes), jnp.float32),
        ],
        in_specs=[pl.BlockSpec(memory_space=pltpu.SMEM), pl.BlockSpec(memory_space=pl.ANY)]
        + [whole] * (len(pieces) + 4),
        out_specs=[pl.BlockSpec(memory_space=pltpu.HBM), whole],
        scratch_shapes=[
            pltpu.SMEM((2, plan.stride, lanes), jnp.int32),
            pltpu.VMEM(((field_rows + 1) * 4 * half, lanes), jnp.float32),
            pltpu.VMEM((rows * 4 * half, lanes), jnp.float32),
            pltpu.VMEM((fine_rows * 2 * half, lanes), jnp.float32),
            pltpu.VMEM((planes, dir_count) + message, jnp.float32),
            pltpu.SemaphoreType.DMA((planes + 2,)),
        ],
        compiler_params=pltpu.CompilerParams(vmem_limit_bytes=48 * 2**20),
        name="translate_and_interpolate",
    )(zed.reshape(1), meta, *pieces, table, phases, high, low)

    parts = lax.all_to_all(
        local_fine.reshape((planes * dir_count,) + message),
        ("zed", "dir"),
        split_axis=0,
        concat_axis=0,
        tiled=True,
    )
    result = (dest_rows, 2, source_count, fine_count)
    if kf_dev == lanes and planes * dir_count * 2 * half == lanes and dest_rows <= lanes:
        return pl.pallas_call(
            functools.partial(join_kernel, source_count),
            out_shape=jax.ShapeDtypeStruct(result, jnp.float32),
            in_specs=[whole] * 2,
            out_specs=whole,
            scratch_shapes=[pltpu.VMEM((dir_count, dest_rows * 2 * source_count, lanes), jnp.float32)],
            compiler_params=pltpu.CompilerParams(vmem_limit_bytes=24 * 2**20),
            name="join_parts",
        )(parts, 1.0 - rims[:1])
    parts = parts.reshape((planes, dir_count) + message)
    main = parts[:, :, : 2 * dest_rows, :kf_dev].reshape(planes, dir_count, 2, dest_rows, kf_dev)
    over = parts[:, :, 2 * dest_rows :, :dest_rows].reshape(planes, dir_count, 2, 2 * rim, dest_rows)
    low = jnp.roll(over[:, :, :, :rim], -1, axis=1)
    high = jnp.roll(over[:, :, :, rim:], 1, axis=1)
    middle = jnp.zeros((planes, dir_count, 2, kf_dev - 2 * rim, dest_rows), jnp.float32)
    fix = jnp.concatenate([high, middle, low], axis=3)
    total = main.transpose(3, 2, 0, 1, 4) + fix.transpose(4, 2, 0, 1, 3)
    return total.reshape(result)


def solution(mesh):
    boxes, dirs = mesh.shape["box"], mesh.shape["dir"]
    fine_mesh = Mesh(mesh.devices.reshape(planes, boxes // planes, dirs), ("zed", "ring", "dir"))
    box = ("zed", "ring")
    placed = (
        P(box, None, None, "dir"),
        P(None, None, "dir"),
        P(box, None),
        P(box, None),
        P(box),
        P(box),
        P(box),
        P(),
        P(),
        P(),
    )
    return jax.shard_map(
        per_device,
        mesh=fine_mesh,
        in_specs=placed,
        out_specs=P(("zed", "ring", "dir"), None, None, None),
        check_vma=False,
    )
```

```python
import collections
import functools

import jax
import jax.numpy as jnp
from jax import lax
from jax.experimental import pallas as pl
from jax.experimental.pallas import tpu as pltpu
from jax.sharding import Mesh
from jax.sharding import PartitionSpec as P

wave_scale = 3.0
planes = 4
lanes = 128
half = 4
rim = 2


plan_fields = ["rows", "slots", "fine_rows", "stride", "kinds", "parent", "octant", "order", "turns"]
Plan = collections.namedtuple("Plan", plan_fields + ["together", "fixed", "group"])


def up(size, step):
    return -(-size // step) * step


def edge_bits(rows):
    bits = rows.bit_length() - 1
    return bits, [place for place in range(2, bits) if place % 2 == bits % 2]


def near_edge(block, ring):
    rows = block.shape[0]
    bits, fixed = edge_bits(rows)
    tail = block.shape[1:]
    picked = block.reshape((2,) * bits + tail)
    for place in fixed:
        picked = lax.dynamic_index_in_dim(picked, 1 - ring, axis=bits - 1 - place, keepdims=True)
    return picked.reshape((rows >> len(fixed),) + tail)


def edge_rank(local, rows):
    bits, fixed = edge_bits(rows)
    rank = jnp.zeros_like(local)
    taken = 0
    for place in range(bits):
        if place not in fixed:
            rank = rank + (local // 2**place % 2) * 2**taken
            taken += 1
    return rank


def split(value):
    high = value.astype(jnp.bfloat16)
    low = (value - high.astype(jnp.float32)).astype(jnp.bfloat16)
    return high, low


def three_pass(left, right, dims):
    dot = functools.partial(
        lax.dot_general, dimension_numbers=(dims, ((), ())), preferred_element_type=jnp.float32
    )
    return dot(left[0], right[0]) + (dot(left[0], right[1]) + dot(left[1], right[0]))


def pack_kernel(source_count, field, *refs):
    notes, (out, whole) = refs[:-2], refs[-2:]
    rows = field.shape[0]
    stride = 2 * source_count

    def row_step(row, unused):
        both = jnp.concatenate([field[row, 0], field[row, 1]], axis=0)
        for block in range(half):
            whole[block, pl.ds(pl.multiple_of(row * stride, stride), stride), :] = both[
                :, block * lanes : (block + 1) * lanes
            ]
        return unused

    lax.fori_loop(0, rows, row_step, 0, unroll=8)
    for source in range(source_count):
        for part in range(2):
            for block in range(half):
                out[source, pl.ds(part * half + block, rows, stride=2 * half), :] = whole[
                    block, pl.ds(part * source_count + source, rows, stride=stride), :
                ]
        for note in notes:
            out[source, rows * 2 * half :, :] = note[...]


def pack(field, notes):
    rows, _, source_count, width = field.shape
    length = rows * 2 * half + sum(note.shape[0] for note in notes)
    whole = pl.BlockSpec(memory_space=pltpu.VMEM)
    return pl.pallas_call(
        functools.partial(pack_kernel, source_count),
        out_shape=pltpu.HBM((source_count, length, lanes), jnp.float32),
        in_specs=[whole] * (1 + len(notes)),
        out_specs=whole,
        scratch_shapes=[pltpu.VMEM((half, rows * 2 * source_count, lanes), jnp.float32)],
        name="pack_sources",
    )(field, *notes)


def tile(start):
    return pl.ds(pl.multiple_of(start, 2 * half), 2 * half)


def fine_kernel(plan, size, edge_size, steps, filled, here, lists, *refs):
    if filled:
        field, refs = refs[0], refs[1:]
        inputs = 0
    else:
        inputs = 1 + (planes if edge_size else 0)
        main, edges, refs = refs[0], refs[1:inputs], refs[inputs:]
    table, phases, high, low, refs = refs[0], refs[1], refs[2], refs[3], refs[4:]
    if not filled:
        field, refs = refs[0], refs[1:]
    outs, (meta, moved, shifted, ready, spilled, sems) = refs[:-6], refs[-6:]
    rows, fine_rows = plan.rows, plan.fine_rows
    own, own_dir = here[0], here[1]
    dest_count = len(outs) // len(steps)
    dest_rows = fine_rows // dest_count

    def bring(turn):
        return pltpu.make_async_copy(lists.at[steps[turn]], meta.at[turn], sems.at[turn])

    for turn in range(len(steps)):
        bring(turn).start()

    def both(start):
        return pl.ds(pl.multiple_of(start, 4 * half), 4 * half)

    def with_turned(value):
        return jnp.concatenate([value, pltpu.roll(value, half, 0)], axis=0)

    if not filled:
        for plane in range(planes):

            def main_step(row, unused, plane=plane):
                value = main[plane, tile(row * 2 * half), :]
                field[both((plane * size + row) * 4 * half), :] = with_turned(value)
                return unused

            lax.fori_loop(0, size, main_step, 0, unroll=8)
        for step, edge in enumerate(edges):
            first = planes * size + (own ^ step) * edge_size

            def edge_step(row, unused, first=first, edge=edge):
                field[both((first + row) * 4 * half), :] = with_turned(edge[tile(row * 2 * half), :])
                return unused

            lax.fori_loop(0, edge_size, edge_step, 0, unroll=8)
        field[both(planes * (size + edge_size) * 4 * half), :] = jnp.zeros((4 * half, lanes), jnp.float32)

    blank = jnp.zeros((2 * half, lanes), jnp.float32)
    sub = lax.broadcasted_iota(jnp.int32, (2 * half, lanes), 0)

    for slot in range(len(steps)):
        bring(slot).wait()

        def boxes_step(step, unused):
            ranks = [step * plan.together + each for each in range(plan.together)]
            boxes = [meta[slot, plan.order, rank] for rank in ranks]
            turns = meta[slot, plan.order, plan.turns + step]

            def work(slot_count):
                sums = [[blank, blank] for box in boxes]
                for pair in range(slot_count):
                    for each in range(plan.together):
                        value = field[both(meta[slot, boxes[each], pair]), :]
                        factor = table[tile(meta[slot, boxes[each], plan.kinds + pair]), :]
                        sums[each][0] += factor * value[: 2 * half]
                        sums[each][1] += factor * value[2 * half :]
                for each in range(plan.together):
                    straight, crossed = sums[each]
                    total = jnp.where(
                        sub < half,
                        straight + pltpu.roll(straight, half, 0),
                        pltpu.roll(crossed, half, 0) - crossed,
                    )
                    moved[both(boxes[each] * 4 * half), :] = with_turned(total)

            for more in range((plan.slots - plan.fixed) // plan.group + 1):
                pl.when(turns == more)(functools.partial(work, plan.fixed + more * plan.group))
            return unused

        lax.fori_loop(0, rows // plan.together, boxes_step, 0)

        def fine_step(block, unused):
            for each in range(lanes):
                value = moved[both(meta[slot, plan.parent + block, each]), :]
                phase = phases[both(meta[slot, plan.octant + block, each]), :]
                value = value * phase
                shifted[tile((block * lanes + each) * 2 * half), :] = value[: 2 * half] + value[2 * half :]
            return unused

        lax.fori_loop(0, fine_rows // lanes, fine_step, 0)
        left = jnp.concatenate(
            [
                jnp.concatenate(
                    [
                        shifted[pl.ds(part * half + block, fine_rows, stride=2 * half), :]
                        for block in range(half)
                    ],
                    axis=1,
                )
                for part in range(2)
            ],
            axis=0,
        )
        result = three_pass(split(left), (high[...], low[...]), ((1,), (0,)))
        width = ready.shape[1]
        ready[...] = result[:, :width]
        spilled[...] = result[:fine_rows, width:] + pltpu.roll(result[fine_rows:, width:], half, 1)
        for dest in range(dest_count):
            out = outs[slot * dest_count + dest]
            start = (own_dir ^ dest) * dest_rows
            for part in range(2):
                chosen = pl.ds(pl.multiple_of(part * fine_rows + start, dest_rows), dest_rows)
                out[part * dest_rows : (part + 1) * dest_rows, :] = ready[chosen, :]
            spill = spilled[pl.ds(pl.multiple_of(start, dest_rows), dest_rows), :].T[: 2 * half]
            blank_part = jnp.zeros((2 * half, width - dest_rows), jnp.float32)
            out[2 * dest_rows :, :] = jnp.concatenate([spill, blank_part], axis=1)


def join_kernel(source_count, here, *refs):
    parts, (out, whole, over) = refs[:-3], refs[-3:]
    dest_rows = out.shape[0]
    dirs = len(parts) // source_count
    low = lax.broadcasted_iota(jnp.int32, (dest_rows, lanes), 1) < rim
    high = lax.broadcasted_iota(jnp.int32, (dest_rows, lanes), 1) >= lanes - rim
    for index, part_ref in enumerate(parts):
        source = here[0] ^ (index // dirs)
        block = here[1] ^ (index % dirs)
        over[tile((source * dirs + block) * 2 * half), :] = part_ref[2 * dest_rows :, :]
        for part in range(2):
            whole[block, pl.ds(part * source_count + source, dest_rows, stride=2 * source_count), :] = part_ref[
                part * dest_rows : (part + 1) * dest_rows, :
            ]
    spill = over[...].T[:dest_rows]
    for source in range(source_count):
        for part in range(2):
            turned = []
            for index in range(dirs):
                first = (source * dirs + index) * 2 * half + part * half
                turned.append(pltpu.roll(spill, (lanes - rim - first) % lanes, 1))
            for index in range(dirs):
                place = pl.ds(part * source_count + source, dest_rows, stride=2 * source_count)
                fix = jnp.where(low, turned[index - 1], jnp.where(high, turned[(index + 1) % dirs], 0.0))
                whole[index, place, :] = whole[index, place, :] + fix

    def row_step(row, unused):
        start = pl.multiple_of(row * 2 * source_count, 2 * source_count)
        both = jnp.concatenate(
            [whole[index, pl.ds(start, 2 * source_count), :] for index in range(dirs)], axis=1
        )
        out[row, 0] = both[:source_count]
        out[row, 1] = both[source_count:]
        return unused

    lax.fori_loop(0, dest_rows, row_step, 0, unroll=8)


def per_device(
    coarse_field,
    trans_table,
    partner_ids,
    partner_types,
    partner_count,
    child_count,
    child_octant,
    dir_angles,
    stencil_ids,
    stencil_weights,
):
    rows, _, source_count, kc_dev = coarse_field.shape
    slots = partner_ids.shape[1]
    type_count = trans_table.shape[0]
    fine_rows = child_octant.shape[0]
    ring_count = lax.axis_size("ring")
    dir_count = lax.axis_size("dir")
    zed = lax.axis_index("zed")
    ring = lax.axis_index("ring")
    dir_index = lax.axis_index("dir")
    fine_count = stencil_ids.shape[0] // 4
    kf_dev = fine_count // dir_count
    kc_pad = up(kc_dev, half * lanes)
    kf_pad = up(kf_dev, lanes)
    pad_dirs = kc_pad - kc_dev
    assert source_count == planes and kc_pad == half * lanes
    dest_rows = fine_rows // dir_count

    field = jnp.pad(coarse_field, ((0, 0), (0, 0), (0, 0), (0, pad_dirs)))
    packed = pack(field, [])
    edge_rows = 0
    if ring_count == 2:
        packed, field = lax.optimization_barrier((packed, field))
        edges = lax.ppermute(near_edge(field, ring), "ring", [(0, 1), (1, 0)])
        edge_rows = edges.shape[0]
    arrived = lax.all_to_all(packed, "zed", split_axis=0, concat_axis=0, tiled=True)

    plane_of = partner_ids // (ring_count * rows)
    ring_of = partner_ids // rows % ring_count
    local = partner_ids % rows
    live = jnp.arange(slots, dtype=jnp.int32)[None, :] < partner_count[:, None]
    if ring_count == 2:
        size = rows
        place = jnp.where(
            ring_of == ring,
            plane_of * rows + local,
            planes * rows + plane_of * edge_rows + edge_rank(local, rows),
        )
    else:
        size = ring_count * rows
        place = partner_ids
    field_rows = planes * (size + edge_rows)
    place = jnp.where(live, place, field_rows)
    together = 4
    fixed = slots // 2
    group = 5 if (slots - fixed) % 5 == 0 else 1
    index = jnp.arange(rows, dtype=jnp.int32)
    before = (partner_count[None, :] > partner_count[:, None]) | (
        (partner_count[None, :] == partner_count[:, None]) & (index[None, :] < index[:, None])
    )
    rank = jnp.sum(before.astype(jnp.int32), axis=1)
    at_rank = rank[None, :] == index[:, None]
    order = jnp.sum(jnp.where(at_rank, index[None, :], 0), axis=1)
    first = rank[None, :] == index[: rows // together, None] * together
    longest = jnp.sum(jnp.where(first, partner_count[None, :], 0), axis=1)
    turns = jnp.maximum((longest - fixed + group - 1) // group, 0)
    bounds = jnp.sum(jnp.where(index[None, :] <= index[:, None], child_count[None, :], 0), axis=1)
    parent = jnp.sum(
        (bounds[None, :] <= jnp.arange(fine_rows, dtype=jnp.int32)[:, None]).astype(jnp.int32), axis=1
    )
    def across(one, width=lanes):
        return jnp.pad(one, ((0, 0), (0, width - one.shape[1])))

    kinds_at = slots
    width = up(2 * slots, lanes // 2)
    turns_at = lanes // 2
    packed_rows = rows * width // lanes
    assert width <= lanes and rows <= turns_at and fine_rows % lanes == 0
    pair_list = across(jnp.concatenate([place * 4 * half, partner_types * 2 * half], axis=1), width)
    lists = [
        pair_list.reshape(packed_rows, lanes),
        (parent * 4 * half).reshape(-1, lanes),
        (child_octant * 4 * half).reshape(-1, lanes),
        across(jnp.concatenate([across(order[None], turns_at), turns[None]], axis=1)),
    ]
    offsets = [sum(one.shape[0] for one in lists[:count]) for count in range(len(lists) + 1)]
    stride = up(offsets[-1], 8)
    shift = rows - packed_rows
    places = [offset + shift for offset in offsets[1:-1]]
    plan = Plan(rows, slots, fine_rows, stride + shift, kinds_at, *places, turns_at, together, fixed, group)
    meta = jnp.pad(jnp.concatenate(lists), ((0, stride - offsets[-1]), (0, 0))).astype(jnp.float32)

    def to_planes(note, step):
        if step == 0:
            return note
        return lax.ppermute(note, "zed", [(plane, plane ^ step) for plane in range(planes)])

    meta = jnp.stack([to_planes(meta, step) for step in range(planes)]).astype(jnp.int32)
    pair_list = meta[:, :packed_rows].reshape(planes, rows, width)
    pair_list = jnp.pad(pair_list, ((0, 0), (0, 0), (0, lanes - width)))
    meta = jnp.concatenate([pair_list, meta[:, packed_rows:]], axis=1)
    received = []
    if ring_count == 2:
        notes = pack(edges, [])
        received = [
            to_planes(lax.dynamic_index_in_dim(notes, zed ^ step, axis=0, keepdims=False), step)
            for step in range(planes)
        ]
    if ring_count == 2:
        pieces = [arrived] + received
    else:
        pieces = [lax.all_gather(arrived, "ring", axis=1, tiled=True)]

    def blocks(table):
        return jnp.pad(table, ((0, 0), (0, pad_dirs))).reshape(-1, half, lanes)

    def doubled(table, sign):
        return jnp.concatenate([blocks(table), sign * blocks(table)], axis=1)

    table = jnp.pad(trans_table, ((0, 0), (0, 0), (0, pad_dirs))).reshape(-1, lanes)
    angles = lax.dynamic_slice_in_dim(dir_angles, dir_index * kc_dev, kc_dev, axis=1)
    octants = jnp.arange(8, dtype=jnp.int32)
    sign_x = 1.0 - 2.0 * (octants % 2).astype(jnp.float32)
    sign_y = 1.0 - 2.0 * (octants // 2 % 2).astype(jnp.float32)
    sign_z = 1.0 - 2.0 * (octants // 4).astype(jnp.float32)
    unit_x = jnp.sin(angles[0]) * jnp.cos(angles[1])
    unit_y = jnp.sin(angles[0]) * jnp.sin(angles[1])
    unit_z = jnp.cos(angles[0])
    phase = wave_scale * (
        sign_x[:, None] * unit_x[None, :] + sign_y[:, None] * unit_y[None, :] + sign_z[:, None] * unit_z[None, :]
    )
    phases = jnp.concatenate(
        [doubled(jnp.cos(phase), 1.0), doubled(jnp.sin(phase), -1.0)], axis=1
    ).reshape(-1, lanes)

    ids = lax.dynamic_slice_in_dim(stencil_ids, dir_index * kc_dev, kc_dev, axis=0).T
    weights = lax.dynamic_slice_in_dim(stencil_weights, dir_index * kc_dev, kc_dev, axis=0).T

    def interp(targets):
        matrix = jnp.zeros((targets.shape[0], kc_dev), jnp.float32)
        for point in range(ids.shape[0]):
            matrix = matrix + jnp.where(
                ids[point][None, :] == targets[:, None], weights[point][None, :], 0.0
            )
        return jnp.pad(matrix, ((0, 0), (0, pad_dirs)))

    first_fine = dir_index * kf_dev
    own = jnp.arange(kf_dev, dtype=jnp.int32)
    outside = jnp.concatenate(
        [jnp.arange(-rim, 0, dtype=jnp.int32), jnp.arange(kf_dev, kf_dev + rim, dtype=jnp.int32)]
    )
    matrix = jnp.pad(interp(first_fine + own), ((0, kf_pad - kf_dev), (0, 0)))
    spill = interp((first_fine + outside) % fine_count)
    matrices = jnp.concatenate([matrix, jnp.pad(spill, ((0, lanes - half), (0, 0)))], axis=0).T
    rounded = lax.reduce_precision(matrices, 8, 7)
    high = rounded.astype(jnp.bfloat16)
    low = (matrices - rounded).astype(jnp.bfloat16)

    whole = pl.BlockSpec(memory_space=pltpu.VMEM)
    message = (2 * dest_rows + 2 * half, kf_pad)
    scalars = pl.BlockSpec(memory_space=pltpu.SMEM)
    here = jnp.stack([zed, dir_index])
    field_shape = ((field_rows + 1) * 4 * half, lanes)
    tables = [table, phases, high, low]

    def fine(steps, inputs, filled):
        count = len(steps) * dir_count
        shapes = [] if filled else [jax.ShapeDtypeStruct(field_shape, jnp.float32)]
        shapes += [jax.ShapeDtypeStruct(message, jnp.float32)] * count
        return pl.pallas_call(
            functools.partial(fine_kernel, plan, size, edge_rows, steps, filled),
            out_shape=shapes,
            in_specs=[scalars, pl.BlockSpec(memory_space=pl.ANY)] + [whole] * (len(inputs) + len(tables)),
            out_specs=[whole] * len(shapes),
            scratch_shapes=[
                pltpu.SMEM((len(steps), plan.stride, lanes), jnp.int32),
                pltpu.VMEM((rows * 4 * half, lanes), jnp.float32),
                pltpu.VMEM((fine_rows * 2 * half, lanes), jnp.float32),
                pltpu.VMEM((2 * fine_rows, kf_pad), jnp.float32),
                pltpu.VMEM((fine_rows, lanes), jnp.float32),
                pltpu.SemaphoreType.DMA((len(steps),)),
            ],
            compiler_params=pltpu.CompilerParams(vmem_limit_bytes=32 * 2**20),
            name="translate_and_interpolate",
        )(here, meta, *inputs, *tables)

    field, *far = fine((3, 2), pieces, False)
    near = fine((1, 0), [field], True)
    order = [(step, turn) for step in (3, 2, 1, 0) for turn in range(dir_count)]
    messages = dict(zip(order, [*far, *near]))
    result = (dest_rows, 2, source_count, fine_count)
    if kf_dev == lanes and planes * dir_count * 2 * half == lanes and dest_rows <= lanes:

        def direct(step, turn):
            if step == 0 and turn == 0:
                return messages[step, turn]
            pairs = [
                (z * dir_count + d, (z ^ step) * dir_count + (d ^ turn))
                for z in range(planes)
                for d in range(dir_count)
            ]
            return lax.ppermute(messages[step, turn], ("zed", "dir"), pairs)

        parts = {key: direct(*key) for key in order}
        return pl.pallas_call(
            functools.partial(join_kernel, source_count),
            out_shape=jax.ShapeDtypeStruct(result, jnp.float32),
            in_specs=[scalars] + [whole] * len(order),
            out_specs=whole,
            scratch_shapes=[
                pltpu.VMEM((dir_count, dest_rows * 2 * source_count, lanes), jnp.float32),
                pltpu.VMEM((planes * dir_count * 2 * half, lanes), jnp.float32),
            ],
            compiler_params=pltpu.CompilerParams(vmem_limit_bytes=24 * 2**20),
            name="join_parts",
        )(here, *[parts[key] for key in sorted(order)])
    parts = jnp.stack([messages[key] for key in sorted(order)]).reshape((planes, dir_count) + message)
    parts = jnp.take(parts, zed ^ jnp.arange(planes, dtype=jnp.int32), axis=0)
    parts = jnp.take(parts, dir_index ^ jnp.arange(dir_count, dtype=jnp.int32), axis=1)
    parts = lax.all_to_all(
        parts.reshape((planes * dir_count,) + message), ("zed", "dir"), split_axis=0, concat_axis=0, tiled=True
    )
    parts = parts.reshape((planes, dir_count) + message)
    main = parts[:, :, : 2 * dest_rows, :kf_dev].reshape(planes, dir_count, 2, dest_rows, kf_dev)
    over = parts[:, :, 2 * dest_rows :, :dest_rows].reshape(planes, dir_count, 2, 2 * rim, dest_rows)
    low = jnp.roll(over[:, :, :, :rim], -1, axis=1)
    high = jnp.roll(over[:, :, :, rim:], 1, axis=1)
    middle = jnp.zeros((planes, dir_count, 2, kf_dev - 2 * rim, dest_rows), jnp.float32)
    fix = jnp.concatenate([high, middle, low], axis=3)
    total = main.transpose(3, 2, 0, 1, 4) + fix.transpose(4, 2, 0, 1, 3)
    return total.reshape(result)


def solution(mesh):
    boxes, dirs = mesh.shape["box"], mesh.shape["dir"]
    fine_mesh = Mesh(mesh.devices.reshape(planes, boxes // planes, dirs), ("zed", "ring", "dir"))
    box = ("zed", "ring")
    placed = (
        P(box, None, None, "dir"),
        P(None, None, "dir"),
        P(box, None),
        P(box, None),
        P(box),
        P(box),
        P(box),
        P(),
        P(),
        P(),
    )
    return jax.shard_map(
        per_device,
        mesh=fine_mesh,
        in_specs=placed,
        out_specs=P(("zed", "ring", "dir"), None, None, None),
        check_vma=False,
    )
```

```python
import collections
import functools

import jax
import jax.numpy as jnp
from jax import lax
from jax.experimental import pallas as pl
from jax.experimental.pallas import tpu as pltpu
from jax.sharding import Mesh
from jax.sharding import PartitionSpec as P

wave_scale = 3.0
planes = 4
lanes = 128
half = 4
rim = 2


plan_fields = ["rows", "slots", "fine_rows", "stride", "kinds", "parent", "octant", "order", "turns"]
Plan = collections.namedtuple("Plan", plan_fields + ["together", "fixed", "group"])


def up(size, step):
    return -(-size // step) * step


def edge_bits(rows):
    bits = rows.bit_length() - 1
    return bits, [place for place in range(2, bits) if place % 2 == bits % 2]


def near_edge(block, ring):
    rows = block.shape[0]
    bits, fixed = edge_bits(rows)
    tail = block.shape[1:]
    picked = block.reshape((2,) * bits + tail)
    for place in fixed:
        picked = lax.dynamic_index_in_dim(picked, 1 - ring, axis=bits - 1 - place, keepdims=True)
    return picked.reshape((rows >> len(fixed),) + tail)


def edge_rank(local, rows):
    bits, fixed = edge_bits(rows)
    rank = jnp.zeros_like(local)
    taken = 0
    for place in range(bits):
        if place not in fixed:
            rank = rank + (local // 2**place % 2) * 2**taken
            taken += 1
    return rank


def split(value):
    high = value.astype(jnp.bfloat16)
    low = (value - high.astype(jnp.float32)).astype(jnp.bfloat16)
    return high, low


def three_pass(left, right, dims):
    dot = functools.partial(
        lax.dot_general, dimension_numbers=(dims, ((), ())), preferred_element_type=jnp.float32
    )
    return dot(left[0], right[0]) + (dot(left[0], right[1]) + dot(left[1], right[0]))


def pack_kernel(source_count, field, *refs):
    notes, (out, whole) = refs[:-2], refs[-2:]
    rows = field.shape[0]
    stride = 2 * source_count

    def row_step(row, unused):
        both = jnp.concatenate([field[row, 0], field[row, 1]], axis=0)
        for block in range(half):
            whole[block, pl.ds(pl.multiple_of(row * stride, stride), stride), :] = both[
                :, block * lanes : (block + 1) * lanes
            ]
        return unused

    lax.fori_loop(0, rows, row_step, 0, unroll=8)
    for source in range(source_count):
        for part in range(2):
            for block in range(half):
                out[source, pl.ds(part * half + block, rows, stride=2 * half), :] = whole[
                    block, pl.ds(part * source_count + source, rows, stride=stride), :
                ]
        for note in notes:
            out[source, rows * 2 * half :, :] = note[...]


def pack(field, notes):
    rows, _, source_count, width = field.shape
    length = rows * 2 * half + sum(note.shape[0] for note in notes)
    whole = pl.BlockSpec(memory_space=pltpu.VMEM)
    return pl.pallas_call(
        functools.partial(pack_kernel, source_count),
        out_shape=pltpu.HBM((source_count, length, lanes), jnp.float32),
        in_specs=[whole] * (1 + len(notes)),
        out_specs=whole,
        scratch_shapes=[pltpu.VMEM((half, rows * 2 * source_count, lanes), jnp.float32)],
        name="pack_sources",
    )(field, *notes)


def tile(start):
    return pl.ds(pl.multiple_of(start, 2 * half), 2 * half)


def fine_kernel(plan, size, edge_size, zed, lists, main, *refs):
    edges = refs[: planes if edge_size else 0]
    refs = refs[len(edges) :]
    table, phases, high, low, out, rims, meta, field, moved, shifted, ready, sems = refs
    rows, fine_rows = plan.rows, plan.fine_rows
    own = zed[0]

    def bring(step):
        return pltpu.make_async_copy(lists.at[step], meta.at[step % 2], sems.at[planes + step % 2])

    bring(0).start()
    lane = lax.broadcasted_iota(jnp.int32, rims.shape, 1)
    rims[...] = ((lane < rim) | (lane >= lanes - rim)).astype(jnp.float32)

    def both(start):
        return pl.ds(pl.multiple_of(start, 4 * half), 4 * half)

    def with_turned(value):
        return jnp.concatenate([value, pltpu.roll(value, half, 0)], axis=0)

    part = size * 2 * half
    edge_part = edge_size * 2 * half
    for plane in range(planes):
        field[plane * part : (plane + 1) * part, :] = main[plane, :part, :]
    for step, edge in enumerate(edges):
        first = planes * part + (own ^ step) * edge_part
        field[pl.ds(pl.multiple_of(first, edge_part), edge_part), :] = edge[:edge_part, :]
    field[tile(planes * (part + edge_part)), :] = jnp.zeros((2 * half, lanes), jnp.float32)

    blank = jnp.zeros((2 * half, lanes), jnp.float32)
    sub = lax.broadcasted_iota(jnp.int32, (2 * half, lanes), 0)
    dest_count = out.shape[1]
    dest_rows = fine_rows // dest_count

    def plane_step(turn, unused):
        plane = own ^ turn
        slot = turn % 2
        bring(turn).wait()

        @pl.when(turn + 1 < planes)
        def _():
            bring(turn + 1).start()


        def boxes_step(step, unused):
            ranks = [step * plan.together + each for each in range(plan.together)]
            boxes = [meta[slot, plan.order, rank] for rank in ranks]
            turns = meta[slot, plan.order, plan.turns + step]

            def work(slot_count):
                sums = [[blank, blank] for box in boxes]
                for pair in range(slot_count):
                    for each in range(plan.together):
                        value = field[tile(meta[slot, boxes[each], pair]), :]
                        factor = table[tile(meta[slot, boxes[each], plan.kinds + pair]), :]
                        sums[each][0] += factor * value
                        sums[each][1] += factor * pltpu.roll(value, half, 0)
                for each in range(plan.together):
                    straight, crossed = sums[each]
                    total = jnp.where(
                        sub < half,
                        straight + pltpu.roll(straight, half, 0),
                        pltpu.roll(crossed, half, 0) - crossed,
                    )
                    moved[both(boxes[each] * 4 * half), :] = with_turned(total)

            for more in range((plan.slots - plan.fixed) // plan.group + 1):
                pl.when(turns == more)(functools.partial(work, plan.fixed + more * plan.group))
            return unused

        lax.fori_loop(0, rows // plan.together, boxes_step, 0)

        def fine_step(block, unused):
            for each in range(lanes):
                value = moved[both(meta[slot, plan.parent + block, each]), :]
                phase = phases[both(meta[slot, plan.octant + block, each]), :]
                value = value * phase
                shifted[tile((block * lanes + each) * 2 * half), :] = value[: 2 * half] + value[2 * half :]
            return unused

        lax.fori_loop(0, fine_rows // lanes, fine_step, 0)
        width = ready.shape[3]
        left = jnp.concatenate(
            [
                jnp.concatenate(
                    [
                        shifted[pl.ds(part * half + block, fine_rows, stride=2 * half), :]
                        for block in range(half)
                    ],
                    axis=1,
                )
                for part in range(2)
            ],
            axis=0,
        )
        result = three_pass(split(left), (high[...], low[...]), ((1,), (0,)))
        for part in range(2):
            for dest in range(dest_count):
                start = part * fine_rows + dest * dest_rows
                ready[plane, dest, part * dest_rows : (part + 1) * dest_rows, :] = result[
                    start : start + dest_rows, :width
                ]
        spill = result[:fine_rows, width:] + pltpu.roll(result[fine_rows:, width:], half, 1)
        spill = spill.T[: 2 * half]
        for dest in range(dest_count):
            ready[plane, dest, 2 * dest_rows :, :] = jnp.concatenate(
                [
                    spill[:, dest * dest_rows : (dest + 1) * dest_rows],
                    jnp.zeros((2 * half, width - dest_rows), jnp.float32),
                ],
                axis=1,
            )
        pltpu.make_async_copy(ready.at[plane], out.at[plane], sems.at[plane]).start()
        return unused

    lax.fori_loop(0, planes, plane_step, 0)
    for plane in range(planes):
        pltpu.make_async_copy(ready.at[plane], out.at[plane], sems.at[plane]).wait()


def join_kernel(source_count, parts, rims, out, whole):
    dest_rows = out.shape[0]
    dirs = parts.shape[0] // source_count
    over = jnp.concatenate(
        [parts[index, 2 * dest_rows :, :lanes] for index in range(parts.shape[0])], axis=0
    ).T[:dest_rows]
    low = lax.broadcasted_iota(jnp.int32, (dest_rows, lanes), 1) < rim
    at_rim = jnp.broadcast_to(rims[...], (dest_rows, lanes)) < 0.5
    for source in range(source_count):
        for part in range(2):
            turned = []
            for index in range(dirs):
                first = (source * dirs + index) * 2 * half + part * half
                turned.append(pltpu.roll(over, (lanes - rim - first) % lanes, 1))
            for index in range(dirs):
                fix = jnp.where(at_rim, jnp.where(low, turned[index - 1], turned[(index + 1) % dirs]), 0.0)
                whole[
                    index, pl.ds(part * source_count + source, dest_rows, stride=2 * source_count), :
                ] = parts[source * dirs + index, part * dest_rows : (part + 1) * dest_rows, :] + fix

    def row_step(row, unused):
        start = pl.multiple_of(row * 2 * source_count, 2 * source_count)
        both = jnp.concatenate(
            [whole[index, pl.ds(start, 2 * source_count), :] for index in range(dirs)], axis=1
        )
        out[row, 0] = both[:source_count]
        out[row, 1] = both[source_count:]
        return unused

    lax.fori_loop(0, dest_rows, row_step, 0, unroll=8)


def per_device(
    coarse_field,
    trans_table,
    partner_ids,
    partner_types,
    partner_count,
    child_count,
    child_octant,
    dir_angles,
    stencil_ids,
    stencil_weights,
):
    rows, _, source_count, kc_dev = coarse_field.shape
    slots = partner_ids.shape[1]
    type_count = trans_table.shape[0]
    fine_rows = child_octant.shape[0]
    ring_count = lax.axis_size("ring")
    dir_count = lax.axis_size("dir")
    zed = lax.axis_index("zed")
    ring = lax.axis_index("ring")
    dir_index = lax.axis_index("dir")
    fine_count = stencil_ids.shape[0] // 4
    kf_dev = fine_count // dir_count
    kc_pad = up(kc_dev, half * lanes)
    kf_pad = up(kf_dev, lanes)
    pad_dirs = kc_pad - kc_dev
    assert source_count == planes and kc_pad == half * lanes
    dest_rows = fine_rows // dir_count

    field = jnp.pad(coarse_field, ((0, 0), (0, 0), (0, 0), (0, pad_dirs)))
    packed = pack(field, [])
    edge_rows = 0
    after_pack = lax.optimization_barrier(
        (packed, field, partner_ids, partner_types, partner_count, child_count, child_octant)
    )
    packed, field, partner_ids, partner_types, partner_count, child_count, child_octant = after_pack
    if ring_count == 2:
        edges = lax.ppermute(near_edge(field, ring), "ring", [(0, 1), (1, 0)])
        edge_rows = edges.shape[0]
    arrived = lax.all_to_all(packed, "zed", split_axis=0, concat_axis=0, tiled=True)

    plane_of = partner_ids // (ring_count * rows)
    ring_of = partner_ids // rows % ring_count
    local = partner_ids % rows
    live = jnp.arange(slots, dtype=jnp.int32)[None, :] < partner_count[:, None]
    if ring_count == 2:
        size = rows
        place = jnp.where(
            ring_of == ring,
            plane_of * rows + local,
            planes * rows + plane_of * edge_rows + edge_rank(local, rows),
        )
    else:
        size = ring_count * rows
        place = partner_ids
    field_rows = planes * (size + edge_rows)
    place = jnp.where(live, place, field_rows)
    together = 4
    fixed = slots // 2
    group = 3 if (slots - fixed) % 3 == 0 else 1
    index = jnp.arange(rows, dtype=jnp.int32)
    before = (partner_count[None, :] > partner_count[:, None]) | (
        (partner_count[None, :] == partner_count[:, None]) & (index[None, :] < index[:, None])
    )
    rank = jnp.sum(before.astype(jnp.int32), axis=1)
    at_rank = rank[None, :] == index[:, None]
    order = jnp.sum(jnp.where(at_rank, index[None, :], 0), axis=1)
    first = rank[None, :] == index[: rows // together, None] * together
    longest = jnp.sum(jnp.where(first, partner_count[None, :], 0), axis=1)
    turns = jnp.maximum((longest - fixed + group - 1) // group, 0)
    bounds = jnp.sum(jnp.where(index[None, :] <= index[:, None], child_count[None, :], 0), axis=1)
    parent = jnp.sum(
        (bounds[None, :] <= jnp.arange(fine_rows, dtype=jnp.int32)[:, None]).astype(jnp.int32), axis=1
    )
    def across(one, width=lanes):
        return jnp.pad(one, ((0, 0), (0, width - one.shape[1])))

    kinds_at = slots
    width = up(2 * slots, lanes // 2)
    turns_at = lanes // 2
    packed_rows = rows * width // lanes
    assert width <= lanes and rows <= turns_at and fine_rows % lanes == 0
    pair_list = across(jnp.concatenate([place * 2 * half, partner_types * 2 * half], axis=1), width)
    lists = [
        pair_list.reshape(packed_rows, lanes),
        (parent * 4 * half).reshape(-1, lanes),
        (child_octant * 4 * half).reshape(-1, lanes),
        across(jnp.concatenate([across(order[None], turns_at), turns[None]], axis=1)),
    ]
    offsets = [sum(one.shape[0] for one in lists[:count]) for count in range(len(lists) + 1)]
    stride = up(offsets[-1], 8)
    shift = rows - packed_rows
    places = [offset + shift for offset in offsets[1:-1]]
    plan = Plan(rows, slots, fine_rows, stride + shift, kinds_at, *places, turns_at, together, fixed, group)
    meta = jnp.pad(jnp.concatenate(lists), ((0, stride - offsets[-1]), (0, 0))).astype(jnp.float32)

    def to_planes(note, step):
        if step == 0:
            return note
        return lax.ppermute(note, "zed", [(plane, plane ^ step) for plane in range(planes)])

    meta = jnp.stack([to_planes(meta, step) for step in range(planes)]).astype(jnp.int32)
    pair_list = meta[:, :packed_rows].reshape(planes, rows, width)
    pair_list = jnp.pad(pair_list, ((0, 0), (0, 0), (0, lanes - width)))
    meta = jnp.concatenate([pair_list, meta[:, packed_rows:]], axis=1)
    received = []
    if ring_count == 2:
        notes = pack(edges, [])
        received = [
            to_planes(lax.dynamic_index_in_dim(notes, zed ^ step, axis=0, keepdims=False), step)
            for step in range(planes)
        ]
    if ring_count == 2:
        pieces = [arrived] + received
    else:
        pieces = [lax.all_gather(arrived, "ring", axis=1, tiled=True)]

    def blocks(table):
        return jnp.pad(table, ((0, 0), (0, pad_dirs))).reshape(-1, half, lanes)

    def doubled(table, sign):
        return jnp.concatenate([blocks(table), sign * blocks(table)], axis=1)

    table = jnp.pad(trans_table, ((0, 0), (0, 0), (0, pad_dirs))).reshape(-1, lanes)
    angles = lax.dynamic_slice_in_dim(dir_angles, dir_index * kc_dev, kc_dev, axis=1)
    octants = jnp.arange(8, dtype=jnp.int32)
    sign_x = 1.0 - 2.0 * (octants % 2).astype(jnp.float32)
    sign_y = 1.0 - 2.0 * (octants // 2 % 2).astype(jnp.float32)
    sign_z = 1.0 - 2.0 * (octants // 4).astype(jnp.float32)
    unit_x = jnp.sin(angles[0]) * jnp.cos(angles[1])
    unit_y = jnp.sin(angles[0]) * jnp.sin(angles[1])
    unit_z = jnp.cos(angles[0])
    phase = wave_scale * (
        sign_x[:, None] * unit_x[None, :] + sign_y[:, None] * unit_y[None, :] + sign_z[:, None] * unit_z[None, :]
    )
    phases = jnp.concatenate(
        [doubled(jnp.cos(phase), 1.0), doubled(jnp.sin(phase), -1.0)], axis=1
    ).reshape(-1, lanes)

    ids = lax.dynamic_slice_in_dim(stencil_ids, dir_index * kc_dev, kc_dev, axis=0).T
    weights = lax.dynamic_slice_in_dim(stencil_weights, dir_index * kc_dev, kc_dev, axis=0).T

    def interp(targets):
        matrix = jnp.zeros((targets.shape[0], kc_dev), jnp.float32)
        for point in range(ids.shape[0]):
            matrix = matrix + jnp.where(
                ids[point][None, :] == targets[:, None], weights[point][None, :], 0.0
            )
        return jnp.pad(matrix, ((0, 0), (0, pad_dirs)))

    first_fine = dir_index * kf_dev
    own = jnp.arange(kf_dev, dtype=jnp.int32)
    outside = jnp.concatenate(
        [jnp.arange(-rim, 0, dtype=jnp.int32), jnp.arange(kf_dev, kf_dev + rim, dtype=jnp.int32)]
    )
    matrix = jnp.pad(interp(first_fine + own), ((0, kf_pad - kf_dev), (0, 0)))
    spill = interp((first_fine + outside) % fine_count)
    matrices = jnp.concatenate([matrix, jnp.pad(spill, ((0, lanes - half), (0, 0)))], axis=0).T
    rounded = lax.reduce_precision(matrices, 8, 7)
    high = rounded.astype(jnp.bfloat16)
    low = (matrices - rounded).astype(jnp.bfloat16)

    whole = pl.BlockSpec(memory_space=pltpu.VMEM)
    message = (2 * dest_rows + 2 * half, kf_pad)
    local_fine, rims = pl.pallas_call(
        functools.partial(fine_kernel, plan, size, edge_rows),
        out_shape=[
            pltpu.HBM((planes, dir_count) + message, jnp.float32),
            jax.ShapeDtypeStruct((2 * half, lanes), jnp.float32),
        ],
        in_specs=[pl.BlockSpec(memory_space=pltpu.SMEM), pl.BlockSpec(memory_space=pl.ANY)]
        + [whole] * (len(pieces) + 4),
        out_specs=[pl.BlockSpec(memory_space=pltpu.HBM), whole],
        scratch_shapes=[
            pltpu.SMEM((2, plan.stride, lanes), jnp.int32),
            pltpu.VMEM(((field_rows + 1) * 2 * half, lanes), jnp.float32),
            pltpu.VMEM((rows * 4 * half, lanes), jnp.float32),
            pltpu.VMEM((fine_rows * 2 * half, lanes), jnp.float32),
            pltpu.VMEM((planes, dir_count) + message, jnp.float32),
            pltpu.SemaphoreType.DMA((planes + 2,)),
        ],
        compiler_params=pltpu.CompilerParams(vmem_limit_bytes=48 * 2**20),
        name="translate_and_interpolate",
    )(zed.reshape(1), meta, *pieces, table, phases, high, low)

    parts = lax.all_to_all(
        local_fine.reshape((planes * dir_count,) + message),
        ("zed", "dir"),
        split_axis=0,
        concat_axis=0,
        tiled=True,
    )
    result = (dest_rows, 2, source_count, fine_count)
    if kf_dev == lanes and planes * dir_count * 2 * half == lanes and dest_rows <= lanes:
        return pl.pallas_call(
            functools.partial(join_kernel, source_count),
            out_shape=jax.ShapeDtypeStruct(result, jnp.float32),
            in_specs=[whole] * 2,
            out_specs=whole,
            scratch_shapes=[pltpu.VMEM((dir_count, dest_rows * 2 * source_count, lanes), jnp.float32)],
            compiler_params=pltpu.CompilerParams(vmem_limit_bytes=24 * 2**20),
            name="join_parts",
        )(parts, 1.0 - rims[:1])
    parts = parts.reshape((planes, dir_count) + message)
    main = parts[:, :, : 2 * dest_rows, :kf_dev].reshape(planes, dir_count, 2, dest_rows, kf_dev)
    over = parts[:, :, 2 * dest_rows :, :dest_rows].reshape(planes, dir_count, 2, 2 * rim, dest_rows)
    low = jnp.roll(over[:, :, :, :rim], -1, axis=1)
    high = jnp.roll(over[:, :, :, rim:], 1, axis=1)
    middle = jnp.zeros((planes, dir_count, 2, kf_dev - 2 * rim, dest_rows), jnp.float32)
    fix = jnp.concatenate([high, middle, low], axis=3)
    total = main.transpose(3, 2, 0, 1, 4) + fix.transpose(4, 2, 0, 1, 3)
    return total.reshape(result)


def solution(mesh):
    boxes, dirs = mesh.shape["box"], mesh.shape["dir"]
    fine_mesh = Mesh(mesh.devices.reshape(planes, boxes // planes, dirs), ("zed", "ring", "dir"))
    box = ("zed", "ring")
    placed = (
        P(box, None, None, "dir"),
        P(None, None, "dir"),
        P(box, None),
        P(box, None),
        P(box),
        P(box),
        P(box),
        P(),
        P(),
        P(),
    )
    return jax.shard_map(
        per_device,
        mesh=fine_mesh,
        in_specs=placed,
        out_specs=P(("zed", "ring", "dir"), None, None, None),
        check_vma=False,
    )
```

```python
import collections
import functools

import jax
import jax.numpy as jnp
from jax import lax
from jax.experimental import pallas as pl
from jax.experimental.pallas import tpu as pltpu
from jax.sharding import Mesh
from jax.sharding import PartitionSpec as P

wave_scale = 3.0
planes = 4
lanes = 128
half = 4
rim = 2
word_bits = 13


plan_fields = ["rows", "slots", "fine_rows", "stride", "width", "parent", "order", "turns"]
Plan = collections.namedtuple("Plan", plan_fields + ["together", "fixed", "group"])


def up(size, step):
    return -(-size // step) * step


def edge_bits(rows):
    bits = rows.bit_length() - 1
    return bits, [place for place in range(2, bits) if place % 2 == bits % 2]


def near_edge(block, ring):
    rows = block.shape[0]
    bits, fixed = edge_bits(rows)
    tail = block.shape[1:]
    picked = block.reshape((2,) * bits + tail)
    for place in fixed:
        picked = lax.dynamic_index_in_dim(picked, 1 - ring, axis=bits - 1 - place, keepdims=True)
    return picked.reshape((rows >> len(fixed),) + tail)


def edge_rank(local, rows):
    bits, fixed = edge_bits(rows)
    rank = jnp.zeros_like(local)
    taken = 0
    for place in range(bits):
        if place not in fixed:
            rank = rank + (local // 2**place % 2) * 2**taken
            taken += 1
    return rank


def split(value):
    high = value.astype(jnp.bfloat16)
    low = (value - high.astype(jnp.float32)).astype(jnp.bfloat16)
    return high, low


def pack_kernel(source_count, field, *refs):
    notes, (out, whole) = refs[:-2], refs[-2:]
    rows = field.shape[0]
    stride = 2 * source_count

    def row_step(row, unused):
        both = jnp.concatenate([field[row, 0], field[row, 1]], axis=0)
        for block in range(half):
            whole[block, pl.ds(pl.multiple_of(row * stride, stride), stride), :] = both[
                :, block * lanes : (block + 1) * lanes
            ]
        return unused

    lax.fori_loop(0, rows, row_step, 0, unroll=8)
    for source in range(source_count):
        for part in range(2):
            for block in range(half):
                out[source, pl.ds(part * half + block, rows, stride=2 * half), :] = whole[
                    block, pl.ds(part * source_count + source, rows, stride=stride), :
                ]
        for note in notes:
            out[source, rows * 2 * half :, :] = note[...]


def pack(field, notes):
    rows, _, source_count, width = field.shape
    length = rows * 2 * half + sum(note.shape[0] for note in notes)
    whole = pl.BlockSpec(memory_space=pltpu.VMEM)
    return pl.pallas_call(
        functools.partial(pack_kernel, source_count),
        out_shape=pltpu.HBM((source_count, length, lanes), jnp.float32),
        in_specs=[whole] * (1 + len(notes)),
        out_specs=whole,
        scratch_shapes=[pltpu.VMEM((half, rows * 2 * source_count, lanes), jnp.float32)],
        name="pack_sources",
    )(field, *notes)


def parts_of(word):
    return lax.shift_right_logical(word, word_bits), word & (2**word_bits - 1)


def tile(start):
    return pl.ds(pl.multiple_of(start, 2 * half), 2 * half)


def fine_kernel(plan, size, edge_size, zed, lists, main, *refs):
    edges = refs[: planes if edge_size else 0]
    refs = refs[len(edges) :]
    table, phases, weights, out, rims, meta, field, moved, shifted, ready, sems = refs
    rows, fine_rows = plan.rows, plan.fine_rows
    own = zed[0]

    def bring(step):
        return pltpu.make_async_copy(lists.at[step], meta.at[step % 2], sems.at[planes + step % 2])

    bring(0).start()
    lane = lax.broadcasted_iota(jnp.int32, rims.shape, 1)
    rims[...] = ((lane < rim) | (lane >= lanes - rim)).astype(jnp.float32)

    def both(start):
        return pl.ds(pl.multiple_of(start, 4 * half), 4 * half)

    def with_turned(value):
        return jnp.concatenate([value, pltpu.roll(value, half, 0)], axis=0)

    for plane in range(planes):

        def main_step(row, unused, plane=plane):
            value = main[plane, tile(row * 2 * half), :]
            field[both((plane * size + row) * 4 * half), :] = with_turned(value)
            return unused

        lax.fori_loop(0, size, main_step, 0, unroll=8)
    for step, edge in enumerate(edges):
        first = planes * size + (own ^ step) * edge_size

        def edge_step(row, unused, first=first, edge=edge):
            field[both((first + row) * 4 * half), :] = with_turned(edge[tile(row * 2 * half), :])
            return unused

        lax.fori_loop(0, edge_size, edge_step, 0, unroll=8)
    field[both(planes * (size + edge_size) * 4 * half), :] = jnp.zeros((4 * half, lanes), jnp.float32)

    blank = jnp.zeros((2 * half, lanes), jnp.float32)
    sub = lax.broadcasted_iota(jnp.int32, (2 * half, lanes), 0)
    dest_count = out.shape[1]
    dest_rows = fine_rows // dest_count

    def plane_step(turn, unused):
        plane = own ^ turn
        slot = turn % 2
        bring(turn).wait()

        @pl.when(turn + 1 < planes)
        def _():
            bring(turn + 1).start()


        def boxes_step(step, unused):
            ranks = [step * plan.together + each for each in range(plan.together)]
            boxes = [meta[slot, plan.order, rank] for rank in ranks]
            turns = meta[slot, plan.order, plan.turns + step]

            def work(slot_count):
                sums = [[blank, blank] for box in boxes]
                for pair in range(slot_count):
                    for each in range(plan.together):
                        place, kind = parts_of(meta[slot, step, each * plan.width + pair])
                        value = field[both(place), :]
                        factor = table[tile(kind), :]
                        sums[each][0] += factor * value[: 2 * half]
                        sums[each][1] += factor * value[2 * half :]
                for each in range(plan.together):
                    straight, crossed = sums[each]
                    total = jnp.where(
                        sub < half,
                        straight + pltpu.roll(straight, half, 0),
                        pltpu.roll(crossed, half, 0) - crossed,
                    )
                    moved[both(boxes[each] * 4 * half), :] = with_turned(total)

            for more in range((plan.slots - plan.fixed) // plan.group + 1):
                pl.when(turns == more)(functools.partial(work, plan.fixed + more * plan.group))
            return unused

        lax.fori_loop(0, rows // plan.together, boxes_step, 0)

        def fine_step(block, unused):
            for each in range(lanes):
                parent, octant = parts_of(meta[slot, plan.parent + block, each])
                value = moved[both(parent), :] * phases[both(octant), :]
                shifted[tile((block * lanes + each) * 2 * half), :] = value[: 2 * half] + value[2 * half :]
            return unused

        lax.fori_loop(0, fine_rows // lanes, fine_step, 0)
        width = ready.shape[3]
        left = jnp.concatenate(
            [
                jnp.concatenate(
                    [
                        shifted[pl.ds(part * half + block, fine_rows, stride=2 * half), :]
                        for block in range(half)
                    ],
                    axis=1,
                )
                for part in range(2)
            ],
            axis=0,
        )
        first, second = split(left)
        result = jnp.dot(
            jnp.concatenate([first, first, second], axis=1), weights[...], preferred_element_type=jnp.float32
        )
        for part in range(2):
            for dest in range(dest_count):
                start = part * fine_rows + dest * dest_rows
                ready[plane, dest, part * dest_rows : (part + 1) * dest_rows, :] = result[
                    start : start + dest_rows, :width
                ]
        spill = result[:fine_rows, width:] + pltpu.roll(result[fine_rows:, width:], half, 1)
        spill = spill.T[: 2 * half]
        for dest in range(dest_count):
            ready[plane, dest, 2 * dest_rows :, :] = jnp.concatenate(
                [
                    spill[:, dest * dest_rows : (dest + 1) * dest_rows],
                    jnp.zeros((2 * half, width - dest_rows), jnp.float32),
                ],
                axis=1,
            )
        pltpu.make_async_copy(ready.at[plane], out.at[plane], sems.at[plane]).start()
        return unused

    lax.fori_loop(0, planes, plane_step, 0)
    for plane in range(planes):
        pltpu.make_async_copy(ready.at[plane], out.at[plane], sems.at[plane]).wait()


def join_kernel(source_count, parts, rims, out, whole):
    dest_rows = out.shape[0]
    dirs = parts.shape[0] // source_count
    over = jnp.concatenate(
        [parts[index, 2 * dest_rows :, :lanes] for index in range(parts.shape[0])], axis=0
    ).T[:dest_rows]
    low = lax.broadcasted_iota(jnp.int32, (dest_rows, lanes), 1) < rim
    at_rim = jnp.broadcast_to(rims[...], (dest_rows, lanes)) < 0.5
    for source in range(source_count):
        for part in range(2):
            turned = []
            for index in range(dirs):
                first = (source * dirs + index) * 2 * half + part * half
                turned.append(pltpu.roll(over, (lanes - rim - first) % lanes, 1))
            for index in range(dirs):
                fix = jnp.where(at_rim, jnp.where(low, turned[index - 1], turned[(index + 1) % dirs]), 0.0)
                whole[
                    index, pl.ds(part * source_count + source, dest_rows, stride=2 * source_count), :
                ] = parts[source * dirs + index, part * dest_rows : (part + 1) * dest_rows, :] + fix

    def row_step(row, unused):
        start = pl.multiple_of(row * 2 * source_count, 2 * source_count)
        both = jnp.concatenate(
            [whole[index, pl.ds(start, 2 * source_count), :] for index in range(dirs)], axis=1
        )
        out[row, 0] = both[:source_count]
        out[row, 1] = both[source_count:]
        return unused

    lax.fori_loop(0, dest_rows, row_step, 0, unroll=8)


def per_device(
    coarse_field,
    trans_table,
    partner_ids,
    partner_types,
    partner_count,
    child_count,
    child_octant,
    dir_angles,
    stencil_ids,
    stencil_weights,
):
    rows, _, source_count, kc_dev = coarse_field.shape
    slots = partner_ids.shape[1]
    type_count = trans_table.shape[0]
    fine_rows = child_octant.shape[0]
    ring_count = lax.axis_size("ring")
    dir_count = lax.axis_size("dir")
    zed = lax.axis_index("zed")
    ring = lax.axis_index("ring")
    dir_index = lax.axis_index("dir")
    fine_count = stencil_ids.shape[0] // 4
    kf_dev = fine_count // dir_count
    kc_pad = up(kc_dev, half * lanes)
    kf_pad = up(kf_dev, lanes)
    pad_dirs = kc_pad - kc_dev
    assert source_count == planes and kc_pad == half * lanes
    dest_rows = fine_rows // dir_count

    field = jnp.pad(coarse_field, ((0, 0), (0, 0), (0, 0), (0, pad_dirs)))
    packed = pack(field, [])
    edge_rows = 0
    if ring_count == 2:
        packed, field = lax.optimization_barrier((packed, field))
        edges = lax.ppermute(near_edge(field, ring), "ring", [(0, 1), (1, 0)])
        edge_rows = edges.shape[0]
    arrived = lax.all_to_all(packed, "zed", split_axis=0, concat_axis=0, tiled=True)

    plane_of = partner_ids // (ring_count * rows)
    ring_of = partner_ids // rows % ring_count
    local = partner_ids % rows
    live = jnp.arange(slots, dtype=jnp.int32)[None, :] < partner_count[:, None]
    if ring_count == 2:
        size = rows
        place = jnp.where(
            ring_of == ring,
            plane_of * rows + local,
            planes * rows + plane_of * edge_rows + edge_rank(local, rows),
        )
    else:
        size = ring_count * rows
        place = partner_ids
    field_rows = planes * (size + edge_rows)
    place = jnp.where(live, place, field_rows)
    together = 4
    fixed = slots // 2
    group = 3 if (slots - fixed) % 3 == 0 else 1
    index = jnp.arange(rows, dtype=jnp.int32)
    before = (partner_count[None, :] > partner_count[:, None]) | (
        (partner_count[None, :] == partner_count[:, None]) & (index[None, :] < index[:, None])
    )
    rank = jnp.sum(before.astype(jnp.int32), axis=1)
    at_rank = rank[None, :] == index[:, None]
    order = jnp.sum(jnp.where(at_rank, index[None, :], 0), axis=1)
    first = rank[None, :] == index[: rows // together, None] * together
    longest = jnp.sum(jnp.where(first, partner_count[None, :], 0), axis=1)
    turns = jnp.maximum((longest - fixed + group - 1) // group, 0)
    bounds = jnp.sum(jnp.where(index[None, :] <= index[:, None], child_count[None, :], 0), axis=1)
    parent = jnp.sum(
        (bounds[None, :] <= jnp.arange(fine_rows, dtype=jnp.int32)[:, None]).astype(jnp.int32), axis=1
    )
    def across(one, width=lanes):
        return jnp.pad(one, ((0, 0), (0, width - one.shape[1])))

    width = lanes // together
    turns_at = lanes // 2
    assert slots <= width and rows <= turns_at and fine_rows % lanes == 0
    assert (field_rows + 1) * 4 * half < 2 ** (31 - word_bits) and type_count * 2 * half < 2**word_bits

    def in_order(one):
        one = jnp.sum(jnp.where(at_rank[:, :, None], across(one, width)[None], 0), axis=1)
        return one.reshape(rows // together, lanes)

    list_rows = rows // together
    fine_lists = fine_rows // lanes
    last = across(jnp.concatenate([across(order[None], turns_at), turns[None]], axis=1))
    stride = up(list_rows + fine_lists + 1, 8)

    def stacked(*parts):
        meta = jnp.concatenate(parts)
        return jnp.pad(meta, ((0, stride - meta.shape[0]), (0, 0))).astype(jnp.float32)

    meta = jnp.concatenate(
        [
            stacked(in_order(place * 4 * half), (parent * 4 * half).reshape(-1, lanes)),
            stacked(in_order(partner_types * 2 * half), (child_octant * 4 * half).reshape(-1, lanes), last),
        ]
    )
    plan = Plan(
        rows, slots, fine_rows, stride, width, list_rows, list_rows + fine_lists, turns_at, together, fixed, group
    )

    if ring_count == 2:
        notes = pack(edges, [meta])
    else:
        notes = jnp.broadcast_to(meta[None], (planes,) + meta.shape)
    received = []
    for step in range(planes):
        note = lax.dynamic_index_in_dim(notes, zed ^ step, axis=0, keepdims=False)
        if step:
            note = lax.ppermute(note, "zed", [(plane, plane ^ step) for plane in range(planes)])
        received.append(note)
    edge_part = edge_rows * 2 * half
    numbers = jnp.stack([note[edge_part:] for note in received]).astype(jnp.int32)
    meta = numbers[:, :stride] * 2**word_bits + numbers[:, stride:]
    if ring_count == 2:
        pieces = [arrived] + received
    else:
        pieces = [lax.all_gather(arrived, "ring", axis=1, tiled=True)]

    def blocks(table):
        return jnp.pad(table, ((0, 0), (0, pad_dirs))).reshape(-1, half, lanes)

    def doubled(table, sign):
        return jnp.concatenate([blocks(table), sign * blocks(table)], axis=1)

    table = jnp.pad(trans_table, ((0, 0), (0, 0), (0, pad_dirs))).reshape(-1, lanes)
    angles = lax.dynamic_slice_in_dim(dir_angles, dir_index * kc_dev, kc_dev, axis=1)
    octants = jnp.arange(8, dtype=jnp.int32)
    sign_x = 1.0 - 2.0 * (octants % 2).astype(jnp.float32)
    sign_y = 1.0 - 2.0 * (octants // 2 % 2).astype(jnp.float32)
    sign_z = 1.0 - 2.0 * (octants // 4).astype(jnp.float32)
    unit_x = jnp.sin(angles[0]) * jnp.cos(angles[1])
    unit_y = jnp.sin(angles[0]) * jnp.sin(angles[1])
    unit_z = jnp.cos(angles[0])
    phase = wave_scale * (
        sign_x[:, None] * unit_x[None, :] + sign_y[:, None] * unit_y[None, :] + sign_z[:, None] * unit_z[None, :]
    )
    phases = jnp.concatenate(
        [doubled(jnp.cos(phase), 1.0), doubled(jnp.sin(phase), -1.0)], axis=1
    ).reshape(-1, lanes)

    ids = lax.dynamic_slice_in_dim(stencil_ids, dir_index * kc_dev, kc_dev, axis=0).T
    weights = lax.dynamic_slice_in_dim(stencil_weights, dir_index * kc_dev, kc_dev, axis=0).T

    def interp(targets):
        matrix = jnp.zeros((targets.shape[0], kc_dev), jnp.float32)
        for point in range(ids.shape[0]):
            matrix = matrix + jnp.where(
                ids[point][None, :] == targets[:, None], weights[point][None, :], 0.0
            )
        return jnp.pad(matrix, ((0, 0), (0, pad_dirs)))

    first_fine = dir_index * kf_dev
    own = jnp.arange(kf_dev, dtype=jnp.int32)
    outside = jnp.concatenate(
        [jnp.arange(-rim, 0, dtype=jnp.int32), jnp.arange(kf_dev, kf_dev + rim, dtype=jnp.int32)]
    )
    matrix = jnp.pad(interp(first_fine + own), ((0, kf_pad - kf_dev), (0, 0)))
    spill = interp((first_fine + outside) % fine_count)
    matrices = jnp.concatenate([matrix, jnp.pad(spill, ((0, lanes - half), (0, 0)))], axis=0).T
    rounded = lax.reduce_precision(matrices, 8, 7)
    high = rounded.astype(jnp.bfloat16)
    low = (matrices - rounded).astype(jnp.bfloat16)
    passes = jnp.concatenate([high, low, high], axis=0)

    whole = pl.BlockSpec(memory_space=pltpu.VMEM)
    message = (2 * dest_rows + 2 * half, kf_pad)
    local_fine, rims = pl.pallas_call(
        functools.partial(fine_kernel, plan, size, edge_rows),
        out_shape=[
            pltpu.HBM((planes, dir_count) + message, jnp.float32),
            jax.ShapeDtypeStruct((2 * half, lanes), jnp.float32),
        ],
        in_specs=[pl.BlockSpec(memory_space=pltpu.SMEM), pl.BlockSpec(memory_space=pl.ANY)]
        + [whole] * (len(pieces) + 3),
        out_specs=[pl.BlockSpec(memory_space=pltpu.HBM), whole],
        scratch_shapes=[
            pltpu.SMEM((2, plan.stride, lanes), jnp.int32),
            pltpu.VMEM(((field_rows + 1) * 4 * half, lanes), jnp.float32),
            pltpu.VMEM((rows * 4 * half, lanes), jnp.float32),
            pltpu.VMEM((fine_rows * 2 * half, lanes), jnp.float32),
            pltpu.VMEM((planes, dir_count) + message, jnp.float32),
            pltpu.SemaphoreType.DMA((planes + 2,)),
        ],
        compiler_params=pltpu.CompilerParams(vmem_limit_bytes=48 * 2**20),
        name="translate_and_interpolate",
    )(zed.reshape(1), meta, *pieces, table, phases, passes)

    parts = lax.all_to_all(
        local_fine.reshape((planes * dir_count,) + message),
        ("zed", "dir"),
        split_axis=0,
        concat_axis=0,
        tiled=True,
    )
    result = (dest_rows, 2, source_count, fine_count)
    if kf_dev == lanes and planes * dir_count * 2 * half == lanes and dest_rows <= lanes:
        return pl.pallas_call(
            functools.partial(join_kernel, source_count),
            out_shape=jax.ShapeDtypeStruct(result, jnp.float32),
            in_specs=[whole] * 2,
            out_specs=whole,
            scratch_shapes=[pltpu.VMEM((dir_count, dest_rows * 2 * source_count, lanes), jnp.float32)],
            compiler_params=pltpu.CompilerParams(vmem_limit_bytes=24 * 2**20),
            name="join_parts",
        )(parts, 1.0 - rims[:1])
    parts = parts.reshape((planes, dir_count) + message)
    main = parts[:, :, : 2 * dest_rows, :kf_dev].reshape(planes, dir_count, 2, dest_rows, kf_dev)
    over = parts[:, :, 2 * dest_rows :, :dest_rows].reshape(planes, dir_count, 2, 2 * rim, dest_rows)
    low = jnp.roll(over[:, :, :, :rim], -1, axis=1)
    high = jnp.roll(over[:, :, :, rim:], 1, axis=1)
    middle = jnp.zeros((planes, dir_count, 2, kf_dev - 2 * rim, dest_rows), jnp.float32)
    fix = jnp.concatenate([high, middle, low], axis=3)
    total = main.transpose(3, 2, 0, 1, 4) + fix.transpose(4, 2, 0, 1, 3)
    return total.reshape(result)


def solution(mesh):
    boxes, dirs = mesh.shape["box"], mesh.shape["dir"]
    fine_mesh = Mesh(mesh.devices.reshape(planes, boxes // planes, dirs), ("zed", "ring", "dir"))
    box = ("zed", "ring")
    placed = (
        P(box, None, None, "dir"),
        P(None, None, "dir"),
        P(box, None),
        P(box, None),
        P(box),
        P(box),
        P(box),
        P(),
        P(),
        P(),
    )
    return jax.shard_map(
        per_device,
        mesh=fine_mesh,
        in_specs=placed,
        out_specs=P(("zed", "ring", "dir"), None, None, None),
        check_vma=False,
    )
```

```python
import collections
import functools

import jax
import jax.numpy as jnp
from jax import lax
from jax.experimental import pallas as pl
from jax.experimental.pallas import tpu as pltpu
from jax.sharding import Mesh
from jax.sharding import PartitionSpec as P

wave_scale = 3.0
planes = 4
lanes = 128
half = 4
rim = 2
word_bits = 13


plan_fields = ["rows", "slots", "fine_rows", "stride", "width", "parent", "order", "turns"]
Plan = collections.namedtuple("Plan", plan_fields + ["together", "fixed", "group"])


def up(size, step):
    return -(-size // step) * step


def edge_bits(rows):
    bits = rows.bit_length() - 1
    return bits, [place for place in range(2, bits) if place % 2 == bits % 2]


def near_edge(block, ring):
    rows = block.shape[0]
    bits, fixed = edge_bits(rows)
    tail = block.shape[1:]
    picked = block.reshape((2,) * bits + tail)
    for place in fixed:
        picked = lax.dynamic_index_in_dim(picked, 1 - ring, axis=bits - 1 - place, keepdims=True)
    return picked.reshape((rows >> len(fixed),) + tail)


def edge_rank(local, rows):
    bits, fixed = edge_bits(rows)
    rank = jnp.zeros_like(local)
    taken = 0
    for place in range(bits):
        if place not in fixed:
            rank = rank + (local // 2**place % 2) * 2**taken
            taken += 1
    return rank


def split(value):
    high = value.astype(jnp.bfloat16)
    low = (value - high.astype(jnp.float32)).astype(jnp.bfloat16)
    return high, low


def pack_kernel(source_count, note_count, field, *refs):
    notes, outs, whole = refs[:note_count], refs[note_count:-1], refs[-1]
    rows = field.shape[0]
    stride = 2 * source_count

    def row_step(row, unused):
        both = jnp.concatenate([field[row, 0], field[row, 1]], axis=0)
        for block in range(half):
            whole[block, pl.ds(pl.multiple_of(row * stride, stride), stride), :] = both[
                :, block * lanes : (block + 1) * lanes
            ]
        return unused

    lax.fori_loop(0, rows, row_step, 0, unroll=8)
    for source in range(source_count):
        for side in range(2):
            out = outs[side % len(outs)]
            first = (side - side % len(outs)) * rows * half
            for part in range(2):
                for block in range(half // 2):
                    out[source, pl.ds(first + part * half // 2 + block, rows, stride=half), :] = whole[
                        side * half // 2 + block, pl.ds(part * source_count + source, rows, stride=stride), :
                    ]
        for note in notes:
            outs[0][source, 2 * rows * half :, :] = note[...]


def pack(field, notes):
    rows, _, source_count, width = field.shape
    whole = pl.BlockSpec(memory_space=pltpu.VMEM)
    if notes:
        lengths = [2 * rows * half + notes[0].shape[0]]
    else:
        lengths = [rows * half] * 2
    return pl.pallas_call(
        functools.partial(pack_kernel, source_count, len(notes)),
        out_shape=[pltpu.HBM((source_count, length, lanes), jnp.float32) for length in lengths],
        in_specs=[whole] * (1 + len(notes)),
        out_specs=[whole] * len(lengths),
        scratch_shapes=[pltpu.VMEM((half, rows * 2 * source_count, lanes), jnp.float32)],
        name="pack_sources",
    )(field, *notes)


def parts_of(word):
    return lax.shift_right_logical(word, word_bits), word & (2**word_bits - 1)


def tile(start):
    return pl.ds(pl.multiple_of(start, 2 * half), 2 * half)


def fine_kernel(plan, size, edge_size, side, zed, lists, main, *refs):
    edges = refs[: planes if edge_size else 0]
    refs = refs[len(edges) :]
    table, phases, weights, out, rims, meta, field, factors, moved, shifted, ready, sems = refs
    rows, fine_rows = plan.rows, plan.fine_rows
    own = zed[0]

    def bring(step):
        return pltpu.make_async_copy(lists.at[step], meta.at[step % 2], sems.at[planes + step % 2])

    bring(0).start()
    lane = lax.broadcasted_iota(jnp.int32, rims.shape, 1)
    rims[...] = ((lane < rim) | (lane >= lanes - rim)).astype(jnp.float32)
    sub = lax.broadcasted_iota(jnp.int32, (2 * half, lanes), 0)
    pair_of = sub // 2

    def turned(value, by):
        return pltpu.roll(value, by % (2 * half), 0) if by % (2 * half) else value

    def gathered(value, sources):
        result = turned(value, -2 * sources[0])
        for index in range(1, len(sources)):
            result = jnp.where(pair_of == index, turned(value, 2 * (index - sources[index])), result)
        return result

    def fill_from(ref, count, first):
        def fill_step(step, unused):
            value = ref[tile(step * 2 * half), :]
            field[tile((first + 2 * step) * 2 * half), :] = gathered(value, (0, 1, 1, 0))
            field[tile((first + 2 * step + 1) * 2 * half), :] = gathered(value, (2, 3, 3, 2))
            return unused

        lax.fori_loop(0, count // 2, fill_step, 0, unroll=8)

    for plane in range(planes):
        fill_from(main.at[plane], size, plane * size)
    for step, edge in enumerate(edges):
        part = edge.at[side * edge_size * half : (side + 1) * edge_size * half]
        fill_from(part, edge_size, planes * size + (own ^ step) * edge_size)
    blank = jnp.zeros((2 * half, lanes), jnp.float32)
    field[tile(planes * (size + edge_size) * 2 * half), :] = blank

    def factor_step(kind, unused):
        factors[tile(kind * 2 * half), :] = gathered(table[tile(kind * 2 * half), :], (side, 2 + side) * 2)
        return unused

    lax.fori_loop(0, table.shape[0] // (2 * half), factor_step, 0, unroll=4)
    sign = jnp.where(sub < half, 1.0, -1.0).astype(jnp.float32)
    dest_count = out.shape[1]
    dest_rows = fine_rows // dest_count

    def plane_step(turn, unused):
        plane = own ^ turn
        slot = turn % 2
        bring(turn).wait()

        @pl.when(turn + 1 < planes)
        def _():
            bring(turn + 1).start()

        def boxes_step(step, unused):
            ranks = [step * plan.together + each for each in range(plan.together)]
            boxes = [meta[slot, plan.order, rank] for rank in ranks]
            turns = meta[slot, plan.order, plan.turns + step]
            across = lanes // plan.width

            def work(slot_count):
                sums = [blank for box in boxes]
                for pair in range(slot_count):
                    for each in range(plan.together):
                        row = step * (plan.together // across) + each // across
                        place, kind = parts_of(meta[slot, row, each % across * plan.width + pair])
                        sums[each] += factors[tile(kind), :] * field[tile(place), :]
                for each in range(plan.together):
                    total = sums[each] + sign * turned(sums[each], -2)
                    total = jnp.where(pair_of % 2 == 0, total, turned(total, -2))
                    moved[tile(boxes[each] * 2 * half), :] = total

            for more in range((plan.slots - plan.fixed) // plan.group + 1):
                pl.when(turns == more)(functools.partial(work, plan.fixed + more * plan.group))
            return unused

        lax.fori_loop(0, rows // plan.together, boxes_step, 0)

        def fine_step(block, unused):
            for each in range(lanes):
                parent, octant = parts_of(meta[slot, plan.parent + block, each])
                value = moved[tile(parent), :] * phases[tile(octant), :]
                shifted[tile((block * lanes + each) * 2 * half), :] = value + turned(value, half)
            return unused

        lax.fori_loop(0, fine_rows // lanes, fine_step, 0)
        left = jnp.concatenate(
            [shifted[pl.ds(block, fine_rows, stride=2 * half), :] for block in range(half)], axis=1
        )
        first, second = split(left)
        result = jnp.dot(
            jnp.concatenate([first, first, second], axis=1), weights[...], preferred_element_type=jnp.float32
        )
        spill = result[:, lanes:].T[: 2 * half]
        for dest in range(dest_count):
            rows_of = slice(dest * dest_rows, (dest + 1) * dest_rows)
            ready[plane, dest, :dest_rows, :] = result[rows_of, :lanes]
            ready[plane, dest, dest_rows:, :] = jnp.concatenate(
                [spill[:, rows_of], jnp.zeros((2 * half, lanes - dest_rows), jnp.float32)], axis=1
            )
        pltpu.make_async_copy(ready.at[plane], out.at[plane], sems.at[plane]).start()
        return unused

    lax.fori_loop(0, planes, plane_step, 0)
    for plane in range(planes):
        pltpu.make_async_copy(ready.at[plane], out.at[plane], sems.at[plane]).wait()


def join_kernel(source_count, first, second, rims, out, whole):
    dest_rows = out.shape[0]
    dirs = first.shape[0] // source_count
    lane = lax.broadcasted_iota(jnp.int32, (dest_rows, lanes), 1)
    middle = lanes // 2
    at_rim = jnp.broadcast_to(rims[...], (dest_rows, lanes)) < 0.5
    at_middle = (lane >= middle - rim) & (lane < middle + rim)

    def spills(parts):
        return jnp.concatenate(
            [parts[index, dest_rows:, :] for index in range(parts.shape[0])], axis=0
        ).T[:dest_rows]

    over = spills(first), spills(second)
    is_low = lane % (2 * rim) < rim
    outer = jnp.where(is_low, over[0], over[1])
    inner = jnp.where(is_low, over[1], over[0])
    for source in range(source_count):
        ends = [first[source * dirs + index, :dest_rows, :] for index in range(dirs)]
        starts = [second[source * dirs + index, :dest_rows, :] for index in range(dirs)]
        for part in range(2):
            turned = []
            places = [(source * dirs + index) * 2 * half + part * half for index in range(dirs)]
            for place in places:
                turned.append(pltpu.roll(outer, (lanes - rim - place) % lanes, 1))
            for index in range(dirs):
                low, high = ends[index], starts[index]
                if part == 0:
                    high = pltpu.roll(high, middle, 1)
                else:
                    low = pltpu.roll(low, middle, 1)
                within = pltpu.roll(inner, (middle - rim - places[index]) % lanes, 1)
                fix = jnp.where(lane < middle, turned[index - 1], turned[(index + 1) % dirs])
                fix = jnp.where(at_rim, fix, jnp.where(at_middle, within, 0.0))
                whole[
                    index, pl.ds(part * source_count + source, dest_rows, stride=2 * source_count), :
                ] = jnp.where(lane < middle, low, high) + fix

    def row_step(row, unused):
        start = pl.multiple_of(row * 2 * source_count, 2 * source_count)
        both = jnp.concatenate(
            [whole[index, pl.ds(start, 2 * source_count), :] for index in range(dirs)], axis=1
        )
        out[row, 0] = both[:source_count]
        out[row, 1] = both[source_count:]
        return unused

    lax.fori_loop(0, dest_rows, row_step, 0, unroll=8)


def per_device(
    coarse_field,
    trans_table,
    partner_ids,
    partner_types,
    partner_count,
    child_count,
    child_octant,
    dir_angles,
    stencil_ids,
    stencil_weights,
):
    rows, _, source_count, kc_dev = coarse_field.shape
    slots = partner_ids.shape[1]
    type_count = trans_table.shape[0]
    fine_rows = child_octant.shape[0]
    ring_count = lax.axis_size("ring")
    dir_count = lax.axis_size("dir")
    zed = lax.axis_index("zed")
    ring = lax.axis_index("ring")
    dir_index = lax.axis_index("dir")
    fine_count = stencil_ids.shape[0] // 4
    kf_dev = fine_count // dir_count
    kc_half, kf_half = kc_dev // 2, kf_dev // 2
    kc_pad = half * lanes
    pad_half = kc_pad // 2 - kc_half
    assert source_count == planes and pad_half >= 0 and kf_half <= lanes // 2
    dest_rows = fine_rows // dir_count

    def widen(array):
        array = array.reshape(array.shape[:-1] + (2, kc_half))
        array = jnp.pad(array, ((0, 0),) * (array.ndim - 1) + ((0, pad_half),))
        return array.reshape(array.shape[:-2] + (kc_pad,))

    field = widen(coarse_field) if pad_half else coarse_field
    packed = pack(field, [])
    edge_rows = 0
    if ring_count == 2:
        packed, field = lax.optimization_barrier((packed, field))
        edges = lax.ppermute(near_edge(field, ring), "ring", [(0, 1), (1, 0)])
        edge_rows = edges.shape[0]
    arrived = [lax.all_to_all(one, "zed", split_axis=0, concat_axis=0, tiled=True) for one in packed]

    plane_of = partner_ids // (ring_count * rows)
    ring_of = partner_ids // rows % ring_count
    local = partner_ids % rows
    live = jnp.arange(slots, dtype=jnp.int32)[None, :] < partner_count[:, None]
    if ring_count == 2:
        size = rows
        place = jnp.where(
            ring_of == ring,
            plane_of * rows + local,
            planes * rows + plane_of * edge_rows + edge_rank(local, rows),
        )
    else:
        size = ring_count * rows
        place = partner_ids
    field_rows = planes * (size + edge_rows)
    place = jnp.where(live, place, field_rows)
    together = 8
    fixed = slots // 2
    group = 5 if (slots - fixed) % 5 == 0 else 1
    index = jnp.arange(rows, dtype=jnp.int32)
    before = (partner_count[None, :] > partner_count[:, None]) | (
        (partner_count[None, :] == partner_count[:, None]) & (index[None, :] < index[:, None])
    )
    rank = jnp.sum(before.astype(jnp.int32), axis=1)
    at_rank = rank[None, :] == index[:, None]
    order = jnp.sum(jnp.where(at_rank, index[None, :], 0), axis=1)
    first = rank[None, :] == index[: rows // together, None] * together
    longest = jnp.sum(jnp.where(first, partner_count[None, :], 0), axis=1)
    turns = jnp.maximum((longest - fixed + group - 1) // group, 0)
    bounds = jnp.sum(jnp.where(index[None, :] <= index[:, None], child_count[None, :], 0), axis=1)
    parent = jnp.sum(
        (bounds[None, :] <= jnp.arange(fine_rows, dtype=jnp.int32)[:, None]).astype(jnp.int32), axis=1
    )
    def across(one, width=lanes):
        return jnp.pad(one, ((0, 0), (0, width - one.shape[1])))

    width = lanes // half
    turns_at = lanes // 2
    assert slots <= width and rows <= turns_at and fine_rows % lanes == 0
    assert (field_rows + 1) * 2 * half < 2 ** (31 - word_bits) and type_count * 2 * half < 2**word_bits

    def in_order(one):
        one = jnp.sum(jnp.where(at_rank[:, :, None], across(one, width)[None], 0), axis=1)
        return one.reshape(rows * width // lanes, lanes)

    list_rows = rows * width // lanes
    fine_lists = fine_rows // lanes
    last = across(jnp.concatenate([across(order[None], turns_at), turns[None]], axis=1))
    stride = up(list_rows + fine_lists + 1, 8)

    def stacked(*parts):
        meta = jnp.concatenate(parts)
        return jnp.pad(meta, ((0, stride - meta.shape[0]), (0, 0))).astype(jnp.float32)

    meta = jnp.concatenate(
        [
            stacked(in_order(place * 2 * half), (parent * 2 * half).reshape(-1, lanes)),
            stacked(in_order(partner_types * 2 * half), (child_octant * 2 * half).reshape(-1, lanes), last),
        ]
    )
    plan = Plan(
        rows, slots, fine_rows, stride, width, list_rows, list_rows + fine_lists, turns_at, together, fixed, group
    )

    if ring_count == 2:
        (notes,) = pack(edges, [meta])
    else:
        notes = jnp.broadcast_to(meta[None], (planes,) + meta.shape)
    received = []
    for step in range(planes):
        note = lax.dynamic_index_in_dim(notes, zed ^ step, axis=0, keepdims=False)
        if step:
            note = lax.ppermute(note, "zed", [(plane, plane ^ step) for plane in range(planes)])
        received.append(note)
    edge_part = edge_rows * 2 * half
    numbers = jnp.stack([note[edge_part:] for note in received]).astype(jnp.int32)
    meta = numbers[:, :stride] * 2**word_bits + numbers[:, stride:]
    if ring_count != 2:
        arrived = [lax.all_gather(one, "ring", axis=1, tiled=True) for one in arrived]
        received = []

    table = (widen(trans_table) if pad_half else trans_table).reshape(-1, lanes)
    angles = lax.dynamic_slice_in_dim(dir_angles, dir_index * kc_dev, kc_dev, axis=1)
    octants = jnp.arange(8, dtype=jnp.int32)
    sign_x = 1.0 - 2.0 * (octants % 2).astype(jnp.float32)
    sign_y = 1.0 - 2.0 * (octants // 2 % 2).astype(jnp.float32)
    sign_z = 1.0 - 2.0 * (octants // 4).astype(jnp.float32)
    unit_x = jnp.sin(angles[0]) * jnp.cos(angles[1])
    unit_y = jnp.sin(angles[0]) * jnp.sin(angles[1])
    unit_z = jnp.cos(angles[0])
    phase = wave_scale * (
        sign_x[:, None] * unit_x[None, :] + sign_y[:, None] * unit_y[None, :] + sign_z[:, None] * unit_z[None, :]
    )
    cosine, sine = [widen(one).reshape(-1, half, lanes) for one in (jnp.cos(phase), jnp.sin(phase))]

    def phases(side):
        chosen = slice(side * half // 2, (side + 1) * half // 2)
        rows_of = [cosine[:, chosen], cosine[:, chosen], sine[:, chosen], -sine[:, chosen]]
        return jnp.concatenate(rows_of, axis=1).reshape(-1, lanes)

    ids = lax.dynamic_slice_in_dim(stencil_ids, dir_index * kc_dev, kc_dev, axis=0).T
    weights = lax.dynamic_slice_in_dim(stencil_weights, dir_index * kc_dev, kc_dev, axis=0).T

    def interp(targets):
        matrix = jnp.zeros((targets.shape[0], kc_dev), jnp.float32)
        for point in range(ids.shape[0]):
            matrix = matrix + jnp.where(
                ids[point][None, :] == targets[:, None], weights[point][None, :], 0.0
            )
        return matrix

    def passes(side):
        first_fine = dir_index * kf_dev + side * kf_half
        own = jnp.arange(kf_half, dtype=jnp.int32)
        outside = jnp.concatenate(
            [jnp.arange(-rim, 0, dtype=jnp.int32), jnp.arange(kf_half, kf_half + rim, dtype=jnp.int32)]
        )
        chosen = slice(side * kc_half, (side + 1) * kc_half)
        main = jnp.pad(interp(first_fine + own)[:, chosen], ((0, lanes // 2 - kf_half), (0, pad_half)))
        spill = jnp.pad(interp((first_fine + outside) % fine_count)[:, chosen], ((0, 0), (0, pad_half)))
        wide = kc_pad // 2
        matrix = jnp.concatenate(
            [
                jnp.pad(one, ((0, 0), (part * wide, wide - part * wide)))
                for one in (main, spill)
                for part in range(2)
            ]
        )
        matrix = jnp.pad(matrix, ((0, 2 * lanes - matrix.shape[0]), (0, 0))).T
        rounded = lax.reduce_precision(matrix, 8, 7)
        high = rounded.astype(jnp.bfloat16)
        low = (matrix - rounded).astype(jnp.bfloat16)
        return jnp.concatenate([high, low, high], axis=0)

    whole = pl.BlockSpec(memory_space=pltpu.VMEM)
    message = (dest_rows + 2 * half, lanes)
    cost = pl.CostEstimate(
        flops=planes * fine_rows * 3 * kc_pad * 4 * lanes,
        bytes_accessed=planes * rows * slots * 2 * 2 * half * lanes * 4,
        transcendentals=0,
    )

    def fine(side):
        return pl.pallas_call(
            functools.partial(fine_kernel, plan, size, edge_rows, side),
            out_shape=[
                pltpu.HBM((planes, dir_count) + message, jnp.float32),
                jax.ShapeDtypeStruct((2 * half, lanes), jnp.float32),
            ],
            in_specs=[pl.BlockSpec(memory_space=pltpu.SMEM), pl.BlockSpec(memory_space=pl.ANY)]
            + [whole] * (4 + len(received)),
            out_specs=[pl.BlockSpec(memory_space=pltpu.HBM), whole],
            scratch_shapes=[
                pltpu.SMEM((2, plan.stride, lanes), jnp.int32),
                pltpu.VMEM(((field_rows + 1) * 2 * half, lanes), jnp.float32),
                pltpu.VMEM((type_count * 2 * half, lanes), jnp.float32),
                pltpu.VMEM((rows * 2 * half, lanes), jnp.float32),
                pltpu.VMEM((fine_rows * 2 * half, lanes), jnp.float32),
                pltpu.VMEM((planes, dir_count) + message, jnp.float32),
                pltpu.SemaphoreType.DMA((planes + 2,)),
            ],
            compiler_params=pltpu.CompilerParams(vmem_limit_bytes=48 * 2**20),
            cost_estimate=cost,
            name="translate_and_interpolate",
        )(zed.reshape(1), meta, arrived[side], *received, table, phases(side), passes(side))

    parts = []
    for side in range(2):
        local_fine, rims = fine(side)
        local_fine = local_fine.reshape((planes * dir_count,) + message)
        parts.append(lax.all_to_all(local_fine, ("zed", "dir"), split_axis=0, concat_axis=0, tiled=True))
    result = (dest_rows, 2, source_count, fine_count)
    if kf_dev == lanes and planes * dir_count * 2 * half == lanes and dest_rows <= lanes:
        return pl.pallas_call(
            functools.partial(join_kernel, source_count),
            out_shape=jax.ShapeDtypeStruct(result, jnp.float32),
            in_specs=[whole] * 3,
            out_specs=whole,
            scratch_shapes=[pltpu.VMEM((dir_count, dest_rows * 2 * source_count, lanes), jnp.float32)],
            compiler_params=pltpu.CompilerParams(vmem_limit_bytes=24 * 2**20),
            name="join_parts",
        )(*parts, 1.0 - rims[:1])
    parts = jnp.stack([one.reshape((planes, dir_count) + message) for one in parts], axis=2)
    main = parts[:, :, :, :dest_rows].reshape(planes, 2 * dir_count, dest_rows, 2, lanes // 2)[..., :kf_half]
    over = parts[:, :, :, dest_rows:, :dest_rows].reshape(planes, 2 * dir_count, 2, 2 * rim, dest_rows)
    low = jnp.roll(over[:, :, :, :rim], -1, axis=1)
    high = jnp.roll(over[:, :, :, rim:], 1, axis=1)
    middle = jnp.zeros((planes, 2 * dir_count, 2, kf_half - 2 * rim, dest_rows), jnp.float32)
    fix = jnp.concatenate([high, middle, low], axis=3)
    total = main.transpose(2, 3, 0, 1, 4) + fix.transpose(4, 2, 0, 1, 3)
    return total.reshape(result)


def solution(mesh):
    boxes, dirs = mesh.shape["box"], mesh.shape["dir"]
    fine_mesh = Mesh(mesh.devices.reshape(planes, boxes // planes, dirs), ("zed", "ring", "dir"))
    box = ("zed", "ring")
    placed = (
        P(box, None, None, "dir"),
        P(None, None, "dir"),
        P(box, None),
        P(box, None),
        P(box),
        P(box),
        P(box),
        P(),
        P(),
        P(),
    )
    return jax.shard_map(
        per_device,
        mesh=fine_mesh,
        in_specs=placed,
        out_specs=P(("zed", "ring", "dir"), None, None, None),
        check_vma=False,
    )
```

```python
import collections
import functools

import jax
import jax.numpy as jnp
from jax import lax
from jax.experimental import pallas as pl
from jax.experimental.pallas import tpu as pltpu
from jax.sharding import Mesh
from jax.sharding import PartitionSpec as P

wave_scale = 3.0
planes = 4
lanes = 128
half = 4
rim = 2
word_bits = 13


plan_fields = ["rows", "slots", "fine_rows", "stride", "width", "parent", "order", "turns"]
Plan = collections.namedtuple("Plan", plan_fields + ["together", "fixed", "group"])


def up(size, step):
    return -(-size // step) * step


def edge_bits(rows):
    bits = rows.bit_length() - 1
    return bits, [place for place in range(2, bits) if place % 2 == bits % 2]


def near_edge(block, ring):
    rows = block.shape[0]
    bits, fixed = edge_bits(rows)
    tail = block.shape[1:]
    picked = block.reshape((2,) * bits + tail)
    for place in fixed:
        picked = lax.dynamic_index_in_dim(picked, 1 - ring, axis=bits - 1 - place, keepdims=True)
    return picked.reshape((rows >> len(fixed),) + tail)


def edge_rank(local, rows):
    bits, fixed = edge_bits(rows)
    rank = jnp.zeros_like(local)
    taken = 0
    for place in range(bits):
        if place not in fixed:
            rank = rank + (local // 2**place % 2) * 2**taken
            taken += 1
    return rank


def split(value):
    high = value.astype(jnp.bfloat16)
    low = (value - high.astype(jnp.float32)).astype(jnp.bfloat16)
    return high, low


def pack_kernel(source_count, field, *refs):
    notes, (out, whole) = refs[:-2], refs[-2:]
    rows = field.shape[0]
    stride = 2 * source_count

    def row_step(row, unused):
        both = jnp.concatenate([field[row, 0], field[row, 1]], axis=0)
        for block in range(half):
            whole[block, pl.ds(pl.multiple_of(row * stride, stride), stride), :] = both[
                :, block * lanes : (block + 1) * lanes
            ]
        return unused

    lax.fori_loop(0, rows, row_step, 0, unroll=8)
    for source in range(source_count):
        for part in range(2):
            for block in range(half):
                out[source, pl.ds(part * half + block, rows, stride=2 * half), :] = whole[
                    block, pl.ds(part * source_count + source, rows, stride=stride), :
                ]
        for note in notes:
            out[source, rows * 2 * half :, :] = note[...]


def pack(field, notes):
    rows, _, source_count, width = field.shape
    length = rows * 2 * half + sum(note.shape[0] for note in notes)
    whole = pl.BlockSpec(memory_space=pltpu.VMEM)
    return pl.pallas_call(
        functools.partial(pack_kernel, source_count),
        out_shape=pltpu.HBM((source_count, length, lanes), jnp.float32),
        in_specs=[whole] * (1 + len(notes)),
        out_specs=whole,
        scratch_shapes=[pltpu.VMEM((half, rows * 2 * source_count, lanes), jnp.float32)],
        name="pack_sources",
    )(field, *notes)


def parts_of(word):
    return lax.shift_right_logical(word, word_bits), word & (2**word_bits - 1)


def tile(start):
    return pl.ds(pl.multiple_of(start, 2 * half), 2 * half)


def fine_kernel(plan, size, edge_size, zed, lists, main, *refs):
    edges = refs[: planes if edge_size else 0]
    refs = refs[len(edges) :]
    table, phases, weights, out, rims, meta, field, moved, shifted, ready, landed, sems = refs
    rows, fine_rows = plan.rows, plan.fine_rows
    own = zed[0]

    def bring(step):
        return pltpu.make_async_copy(lists.at[step], meta.at[step % 2], sems.at[planes + step % 2])

    bring(0).start()
    incoming = []
    for step, edge in enumerate(edges):
        chosen = edge.at[pl.ds(0, edge_size * 2 * half)]
        incoming.append(pltpu.make_async_copy(chosen, landed.at[step], sems.at[planes + 2 + step]))
        incoming[-1].start()
    lane = lax.broadcasted_iota(jnp.int32, rims.shape, 1)
    rims[...] = ((lane < rim) | (lane >= lanes - rim)).astype(jnp.float32)

    def both(start):
        return pl.ds(pl.multiple_of(start, 4 * half), 4 * half)

    def with_turned(value):
        return jnp.concatenate([value, pltpu.roll(value, half, 0)], axis=0)

    for plane in range(planes):

        def main_step(row, unused, plane=plane):
            value = main[plane, tile(row * 2 * half), :]
            field[both((plane * size + row) * 4 * half), :] = with_turned(value)
            return unused

        lax.fori_loop(0, size, main_step, 0, unroll=8)
    for step, edge in enumerate(edges):
        first = planes * size + (own ^ step) * edge_size
        incoming[step].wait()

        def edge_step(row, unused, first=first, step=step):
            field[both((first + row) * 4 * half), :] = with_turned(landed[step, tile(row * 2 * half), :])
            return unused

        lax.fori_loop(0, edge_size, edge_step, 0, unroll=8)
    field[both(planes * (size + edge_size) * 4 * half), :] = jnp.zeros((4 * half, lanes), jnp.float32)

    blank = jnp.zeros((2 * half, lanes), jnp.float32)
    sub = lax.broadcasted_iota(jnp.int32, (2 * half, lanes), 0)
    dest_count = out.shape[1]
    dest_rows = fine_rows // dest_count

    def plane_step(turn, unused):
        plane = own ^ turn
        slot = turn % 2
        bring(turn).wait()

        @pl.when(turn + 1 < planes)
        def _():
            bring(turn + 1).start()

        def boxes_step(slot_count, step, unused):
            ranks = [step * plan.together + each for each in range(plan.together)]
            boxes = [meta[slot, plan.order, rank] for rank in ranks]
            sums = [[blank, blank] for box in boxes]
            for pair in range(slot_count):
                for each in range(plan.together):
                    place, kind = parts_of(meta[slot, step, each * plan.width + pair])
                    value = field[both(place), :]
                    factor = table[tile(kind), :]
                    sums[each][0] += factor * value[: 2 * half]
                    sums[each][1] += factor * value[2 * half :]
            for each in range(plan.together):
                straight, crossed = sums[each]
                total = jnp.where(
                    sub < half,
                    straight + pltpu.roll(straight, half, 0),
                    pltpu.roll(crossed, half, 0) - crossed,
                )
                moved[both(boxes[each] * 4 * half), :] = with_turned(total)
            return unused

        start = 0
        for more in reversed(range((plan.slots - plan.fixed) // plan.group + 1)):
            end = meta[slot, plan.order, plan.turns + more]
            lax.fori_loop(start, end, functools.partial(boxes_step, plan.fixed + more * plan.group), 0)
            start = end

        def fine_step(block, unused):
            for each in range(lanes):
                parent, octant = parts_of(meta[slot, plan.parent + block, each])
                value = moved[both(parent), :] * phases[both(octant), :]
                shifted[tile((block * lanes + each) * 2 * half), :] = value[: 2 * half] + value[2 * half :]
            return unused

        lax.fori_loop(0, fine_rows // lanes, fine_step, 0)
        width = ready.shape[3]
        left = jnp.concatenate(
            [
                jnp.concatenate(
                    [
                        shifted[pl.ds(part * half + block, fine_rows, stride=2 * half), :]
                        for block in range(half)
                    ],
                    axis=1,
                )
                for part in range(2)
            ],
            axis=0,
        )
        first, second = split(left)
        result = jnp.dot(
            jnp.concatenate([first, first, second], axis=1), weights[...], preferred_element_type=jnp.float32
        )
        for part in range(2):
            for dest in range(dest_count):
                start = part * fine_rows + dest * dest_rows
                ready[plane, dest, part * dest_rows : (part + 1) * dest_rows, :] = result[
                    start : start + dest_rows, :width
                ]
        spill = result[:fine_rows, width:] + pltpu.roll(result[fine_rows:, width:], half, 1)
        spill = spill.T[: 2 * half]
        for dest in range(dest_count):
            ready[plane, dest, 2 * dest_rows :, :] = jnp.concatenate(
                [
                    spill[:, dest * dest_rows : (dest + 1) * dest_rows],
                    jnp.zeros((2 * half, width - dest_rows), jnp.float32),
                ],
                axis=1,
            )
        pltpu.make_async_copy(ready.at[plane], out.at[plane], sems.at[plane]).start()
        return unused

    lax.fori_loop(0, planes, plane_step, 0)
    for plane in range(planes):
        pltpu.make_async_copy(ready.at[plane], out.at[plane], sems.at[plane]).wait()


def join_kernel(source_count, parts, rims, out, whole):
    dest_rows = out.shape[0]
    dirs = parts.shape[0] // source_count
    over = jnp.concatenate(
        [parts[index, 2 * dest_rows :, :lanes] for index in range(parts.shape[0])], axis=0
    ).T[:dest_rows]
    low = lax.broadcasted_iota(jnp.int32, (dest_rows, lanes), 1) < rim
    at_rim = jnp.broadcast_to(rims[...], (dest_rows, lanes)) < 0.5
    for source in range(source_count):
        for part in range(2):
            turned = []
            for index in range(dirs):
                first = (source * dirs + index) * 2 * half + part * half
                turned.append(pltpu.roll(over, (lanes - rim - first) % lanes, 1))
            for index in range(dirs):
                fix = jnp.where(at_rim, jnp.where(low, turned[index - 1], turned[(index + 1) % dirs]), 0.0)
                whole[
                    index, pl.ds(part * source_count + source, dest_rows, stride=2 * source_count), :
                ] = parts[source * dirs + index, part * dest_rows : (part + 1) * dest_rows, :] + fix

    def row_step(row, unused):
        start = pl.multiple_of(row * 2 * source_count, 2 * source_count)
        both = jnp.concatenate(
            [whole[index, pl.ds(start, 2 * source_count), :] for index in range(dirs)], axis=1
        )
        out[row, 0] = both[:source_count]
        out[row, 1] = both[source_count:]
        return unused

    lax.fori_loop(0, dest_rows, row_step, 0, unroll=8)


def per_device(
    coarse_field,
    trans_table,
    partner_ids,
    partner_types,
    partner_count,
    child_count,
    child_octant,
    dir_angles,
    stencil_ids,
    stencil_weights,
):
    rows, _, source_count, kc_dev = coarse_field.shape
    slots = partner_ids.shape[1]
    type_count = trans_table.shape[0]
    fine_rows = child_octant.shape[0]
    ring_count = lax.axis_size("ring")
    dir_count = lax.axis_size("dir")
    zed = lax.axis_index("zed")
    ring = lax.axis_index("ring")
    dir_index = lax.axis_index("dir")
    fine_count = stencil_ids.shape[0] // 4
    kf_dev = fine_count // dir_count
    kc_pad = up(kc_dev, half * lanes)
    kf_pad = up(kf_dev, lanes)
    pad_dirs = kc_pad - kc_dev
    assert source_count == planes and kc_pad == half * lanes
    dest_rows = fine_rows // dir_count

    field = jnp.pad(coarse_field, ((0, 0), (0, 0), (0, 0), (0, pad_dirs)))
    packed = pack(field, [])
    edge_rows = 0
    if ring_count == 2:
        packed, field = lax.optimization_barrier((packed, field))
        edges = lax.ppermute(near_edge(field, ring), "ring", [(0, 1), (1, 0)])
        edge_rows = edges.shape[0]
    arrived = lax.all_to_all(packed, "zed", split_axis=0, concat_axis=0, tiled=True)

    plane_of = partner_ids // (ring_count * rows)
    ring_of = partner_ids // rows % ring_count
    local = partner_ids % rows
    live = jnp.arange(slots, dtype=jnp.int32)[None, :] < partner_count[:, None]
    if ring_count == 2:
        size = rows
        place = jnp.where(
            ring_of == ring,
            plane_of * rows + local,
            planes * rows + plane_of * edge_rows + edge_rank(local, rows),
        )
    else:
        size = ring_count * rows
        place = partner_ids
    field_rows = planes * (size + edge_rows)
    place = jnp.where(live, place, field_rows)
    together = 4
    fixed = slots // 2
    group = 3 if (slots - fixed) % 3 == 0 else 1
    index = jnp.arange(rows, dtype=jnp.int32)
    before = (partner_count[None, :] > partner_count[:, None]) | (
        (partner_count[None, :] == partner_count[:, None]) & (index[None, :] < index[:, None])
    )
    rank = jnp.sum(before.astype(jnp.int32), axis=1)
    at_rank = rank[None, :] == index[:, None]
    order = jnp.sum(jnp.where(at_rank, index[None, :], 0), axis=1)
    first = rank[None, :] == index[: rows // together, None] * together
    longest = jnp.sum(jnp.where(first, partner_count[None, :], 0), axis=1)
    turns = jnp.maximum((longest - fixed + group - 1) // group, 0)
    more = jnp.arange((slots - fixed) // group + 1, dtype=jnp.int32)
    ends = jnp.sum((turns[None, :] >= more[:, None]).astype(jnp.int32), axis=1)
    bounds = jnp.sum(jnp.where(index[None, :] <= index[:, None], child_count[None, :], 0), axis=1)
    parent = jnp.sum(
        (bounds[None, :] <= jnp.arange(fine_rows, dtype=jnp.int32)[:, None]).astype(jnp.int32), axis=1
    )
    def across(one, width=lanes):
        return jnp.pad(one, ((0, 0), (0, width - one.shape[1])))

    width = lanes // together
    turns_at = lanes // 2
    assert slots <= width and rows <= turns_at and fine_rows % lanes == 0
    assert (field_rows + 1) * 4 * half < 2 ** (31 - word_bits) and type_count * 2 * half < 2**word_bits

    def in_order(one):
        one = jnp.sum(jnp.where(at_rank[:, :, None], across(one, width)[None], 0), axis=1)
        return one.reshape(rows // together, lanes)

    list_rows = rows // together
    fine_lists = fine_rows // lanes
    last = across(jnp.concatenate([across(order[None], turns_at), ends[None]], axis=1))
    stride = up(list_rows + fine_lists + 1, 8)

    def stacked(*parts):
        meta = jnp.concatenate(parts)
        return jnp.pad(meta, ((0, stride - meta.shape[0]), (0, 0))).astype(jnp.float32)

    meta = jnp.concatenate(
        [
            stacked(in_order(place * 4 * half), (parent * 4 * half).reshape(-1, lanes)),
            stacked(in_order(partner_types * 2 * half), (child_octant * 4 * half).reshape(-1, lanes), last),
        ]
    )
    plan = Plan(
        rows, slots, fine_rows, stride, width, list_rows, list_rows + fine_lists, turns_at, together, fixed, group
    )

    if ring_count == 2:
        notes = pack(edges, [meta])
        after_notes = lax.optimization_barrier((notes, trans_table, dir_angles, stencil_ids, stencil_weights))
        notes, trans_table, dir_angles, stencil_ids, stencil_weights = after_notes
    else:
        notes = jnp.broadcast_to(meta[None], (planes,) + meta.shape)
    received = []
    for step in range(planes):
        note = lax.dynamic_index_in_dim(notes, zed ^ step, axis=0, keepdims=False)
        if step:
            note = lax.ppermute(note, "zed", [(plane, plane ^ step) for plane in range(planes)])
        received.append(note)
    edge_part = edge_rows * 2 * half
    numbers = jnp.stack([note[edge_part:] for note in received]).astype(jnp.int32)
    meta = numbers[:, :stride] * 2**word_bits + numbers[:, stride:]
    if ring_count == 2:
        pieces = [arrived] + received
    else:
        pieces = [lax.all_gather(arrived, "ring", axis=1, tiled=True)]

    def blocks(table):
        return jnp.pad(table, ((0, 0), (0, pad_dirs))).reshape(-1, half, lanes)

    def doubled(table, sign):
        return jnp.concatenate([blocks(table), sign * blocks(table)], axis=1)

    table = jnp.pad(trans_table, ((0, 0), (0, 0), (0, pad_dirs))).reshape(-1, lanes)
    angles = lax.dynamic_slice_in_dim(dir_angles, dir_index * kc_dev, kc_dev, axis=1)
    octants = jnp.arange(8, dtype=jnp.int32)
    sign_x = 1.0 - 2.0 * (octants % 2).astype(jnp.float32)
    sign_y = 1.0 - 2.0 * (octants // 2 % 2).astype(jnp.float32)
    sign_z = 1.0 - 2.0 * (octants // 4).astype(jnp.float32)
    unit_x = jnp.sin(angles[0]) * jnp.cos(angles[1])
    unit_y = jnp.sin(angles[0]) * jnp.sin(angles[1])
    unit_z = jnp.cos(angles[0])
    phase = wave_scale * (
        sign_x[:, None] * unit_x[None, :] + sign_y[:, None] * unit_y[None, :] + sign_z[:, None] * unit_z[None, :]
    )
    phases = jnp.concatenate(
        [doubled(jnp.cos(phase), 1.0), doubled(jnp.sin(phase), -1.0)], axis=1
    ).reshape(-1, lanes)

    ids = lax.dynamic_slice_in_dim(stencil_ids, dir_index * kc_dev, kc_dev, axis=0).T
    weights = lax.dynamic_slice_in_dim(stencil_weights, dir_index * kc_dev, kc_dev, axis=0).T

    def interp(targets):
        matrix = jnp.zeros((targets.shape[0], kc_dev), jnp.float32)
        for point in range(ids.shape[0]):
            matrix = matrix + jnp.where(
                ids[point][None, :] == targets[:, None], weights[point][None, :], 0.0
            )
        return jnp.pad(matrix, ((0, 0), (0, pad_dirs)))

    first_fine = dir_index * kf_dev
    own = jnp.arange(kf_dev, dtype=jnp.int32)
    outside = jnp.concatenate(
        [jnp.arange(-rim, 0, dtype=jnp.int32), jnp.arange(kf_dev, kf_dev + rim, dtype=jnp.int32)]
    )
    matrix = jnp.pad(interp(first_fine + own), ((0, kf_pad - kf_dev), (0, 0)))
    spill = interp((first_fine + outside) % fine_count)
    matrices = jnp.concatenate([matrix, jnp.pad(spill, ((0, lanes - half), (0, 0)))], axis=0).T
    rounded = lax.reduce_precision(matrices, 8, 7)
    high = rounded.astype(jnp.bfloat16)
    low = (matrices - rounded).astype(jnp.bfloat16)
    passes = jnp.concatenate([high, low, high], axis=0)

    whole = pl.BlockSpec(memory_space=pltpu.VMEM)
    message = (2 * dest_rows + 2 * half, kf_pad)
    local_fine, rims = pl.pallas_call(
        functools.partial(fine_kernel, plan, size, edge_rows),
        out_shape=[
            pltpu.HBM((planes, dir_count) + message, jnp.float32),
            jax.ShapeDtypeStruct((2 * half, lanes), jnp.float32),
        ],
        in_specs=[pl.BlockSpec(memory_space=pltpu.SMEM), pl.BlockSpec(memory_space=pl.ANY)]
        + [whole]
        + [pl.BlockSpec(memory_space=pl.ANY)] * (len(pieces) - 1)
        + [whole] * 3,
        out_specs=[pl.BlockSpec(memory_space=pltpu.HBM), whole],
        scratch_shapes=[
            pltpu.SMEM((2, plan.stride, lanes), jnp.int32),
            pltpu.VMEM(((field_rows + 1) * 4 * half, lanes), jnp.float32),
            pltpu.VMEM((rows * 4 * half, lanes), jnp.float32),
            pltpu.VMEM((fine_rows * 2 * half, lanes), jnp.float32),
            pltpu.VMEM((planes, dir_count) + message, jnp.float32),
            pltpu.VMEM((planes, max(edge_rows, 1) * 2 * half, lanes), jnp.float32),
            pltpu.SemaphoreType.DMA((2 * planes + 2,)),
        ],
        compiler_params=pltpu.CompilerParams(vmem_limit_bytes=48 * 2**20),
        name="translate_and_interpolate",
    )(zed.reshape(1), meta, *pieces, table, phases, passes)

    parts = lax.all_to_all(
        local_fine.reshape((planes * dir_count,) + message),
        ("zed", "dir"),
        split_axis=0,
        concat_axis=0,
        tiled=True,
    )
    result = (dest_rows, 2, source_count, fine_count)
    if kf_dev == lanes and planes * dir_count * 2 * half == lanes and dest_rows <= lanes:
        return pl.pallas_call(
            functools.partial(join_kernel, source_count),
            out_shape=jax.ShapeDtypeStruct(result, jnp.float32),
            in_specs=[whole] * 2,
            out_specs=whole,
            scratch_shapes=[pltpu.VMEM((dir_count, dest_rows * 2 * source_count, lanes), jnp.float32)],
            compiler_params=pltpu.CompilerParams(vmem_limit_bytes=24 * 2**20),
            name="join_parts",
        )(parts, 1.0 - rims[:1])
    parts = parts.reshape((planes, dir_count) + message)
    main = parts[:, :, : 2 * dest_rows, :kf_dev].reshape(planes, dir_count, 2, dest_rows, kf_dev)
    over = parts[:, :, 2 * dest_rows :, :dest_rows].reshape(planes, dir_count, 2, 2 * rim, dest_rows)
    low = jnp.roll(over[:, :, :, :rim], -1, axis=1)
    high = jnp.roll(over[:, :, :, rim:], 1, axis=1)
    middle = jnp.zeros((planes, dir_count, 2, kf_dev - 2 * rim, dest_rows), jnp.float32)
    fix = jnp.concatenate([high, middle, low], axis=3)
    total = main.transpose(3, 2, 0, 1, 4) + fix.transpose(4, 2, 0, 1, 3)
    return total.reshape(result)


def solution(mesh):
    boxes, dirs = mesh.shape["box"], mesh.shape["dir"]
    fine_mesh = Mesh(mesh.devices.reshape(planes, boxes // planes, dirs), ("zed", "ring", "dir"))
    box = ("zed", "ring")
    placed = (
        P(box, None, None, "dir"),
        P(None, None, "dir"),
        P(box, None),
        P(box, None),
        P(box),
        P(box),
        P(box),
        P(),
        P(),
        P(),
    )
    return jax.shard_map(
        per_device,
        mesh=fine_mesh,
        in_specs=placed,
        out_specs=P(("zed", "ring", "dir"), None, None, None),
        check_vma=False,
    )
```

```python
import collections
import functools

import jax
import jax.numpy as jnp
from jax import lax
from jax.experimental import pallas as pl
from jax.experimental.pallas import tpu as pltpu
from jax.sharding import Mesh
from jax.sharding import PartitionSpec as P

wave_scale = 3.0
planes = 4
lanes = 128
half = 4
rim = 2
word_bits = 13


plan_fields = ["rows", "slots", "fine_rows", "stride", "width", "parent", "order", "turns"]
Plan = collections.namedtuple("Plan", plan_fields + ["together", "fixed", "group"])


def up(size, step):
    return -(-size // step) * step


def edge_bits(rows):
    bits = rows.bit_length() - 1
    return bits, [place for place in range(2, bits) if place % 2 == bits % 2]


def near_edge(block, ring):
    rows = block.shape[0]
    bits, fixed = edge_bits(rows)
    tail = block.shape[1:]
    picked = block.reshape((2,) * bits + tail)
    for place in fixed:
        picked = lax.dynamic_index_in_dim(picked, 1 - ring, axis=bits - 1 - place, keepdims=True)
    return picked.reshape((rows >> len(fixed),) + tail)


def edge_rank(local, rows):
    bits, fixed = edge_bits(rows)
    rank = jnp.zeros_like(local)
    taken = 0
    for place in range(bits):
        if place not in fixed:
            rank = rank + (local // 2**place % 2) * 2**taken
            taken += 1
    return rank


def split(value):
    high = value.astype(jnp.bfloat16)
    low = (value - high.astype(jnp.float32)).astype(jnp.bfloat16)
    return high, low


def pack_kernel(source_count, note_count, zed, field, *refs):
    notes, outs, whole = refs[:note_count], refs[note_count:-1], refs[-1]
    rows = field.shape[0]
    stride = 2 * source_count

    def row_step(row, unused):
        both = jnp.concatenate([field[row, 0], field[row, 1]], axis=0)
        for block in range(half):
            whole[block, pl.ds(pl.multiple_of(row * stride, stride), stride), :] = both[
                :, block * lanes : (block + 1) * lanes
            ]
        return unused

    lax.fori_loop(0, rows, row_step, 0, unroll=8)
    for step, out in enumerate(outs):
        source = zed[0] ^ step
        for part in range(2):
            for block in range(half):
                out[pl.ds(part * half + block, rows, stride=2 * half), :] = whole[
                    block, pl.ds(part * source_count + source, rows, stride=stride), :
                ]
        for note in notes:
            out[rows * 2 * half :, :] = note[...]


def pack(zed, field, notes):
    rows, _, source_count, width = field.shape
    length = rows * 2 * half + sum(note.shape[0] for note in notes)
    whole = pl.BlockSpec(memory_space=pltpu.VMEM)
    return pl.pallas_call(
        functools.partial(pack_kernel, source_count, len(notes)),
        out_shape=[jax.ShapeDtypeStruct((length, lanes), jnp.float32)] * planes,
        in_specs=[pl.BlockSpec(memory_space=pltpu.SMEM)] + [whole] * (1 + len(notes)),
        out_specs=[whole] * planes,
        scratch_shapes=[pltpu.VMEM((half, rows * 2 * source_count, lanes), jnp.float32)],
        name="pack_sources",
    )(zed, field, *notes)


def parts_of(word):
    return lax.shift_right_logical(word, word_bits), word & (2**word_bits - 1)


def tile(start):
    return pl.ds(pl.multiple_of(start, 2 * half), 2 * half)


def fine_kernel(plan, size, edge_size, zed, lists, *refs):
    mains, refs = refs[:planes], refs[planes:]
    edges = refs[: planes if edge_size else 0]
    refs = refs[len(edges) :]
    table, phases, weights, out, rims, meta, field, moved, shifted, ready, landed, sems = refs
    rows, fine_rows = plan.rows, plan.fine_rows
    own = zed[0]

    def bring(step):
        return pltpu.make_async_copy(lists.at[step], meta.at[step % 2], sems.at[planes + step % 2])

    bring(0).start()
    incoming = []
    for step, edge in enumerate(edges):
        chosen = edge.at[pl.ds(0, edge_size * 2 * half)]
        incoming.append(pltpu.make_async_copy(chosen, landed.at[step], sems.at[planes + 2 + step]))
        incoming[-1].start()
    lane = lax.broadcasted_iota(jnp.int32, rims.shape, 1)
    rims[...] = ((lane < rim) | (lane >= lanes - rim)).astype(jnp.float32)

    def both(start):
        return pl.ds(pl.multiple_of(start, 4 * half), 4 * half)

    def with_turned(value):
        return jnp.concatenate([value, pltpu.roll(value, half, 0)], axis=0)

    for step, main in enumerate(mains):
        first = (own ^ step) * size

        def main_step(row, unused, first=first, main=main):
            field[both((first + row) * 4 * half), :] = with_turned(main[tile(row * 2 * half), :])
            return unused

        lax.fori_loop(0, size, main_step, 0, unroll=8)
    for step, edge in enumerate(edges):
        first = planes * size + (own ^ step) * edge_size
        incoming[step].wait()

        def edge_step(row, unused, first=first, step=step):
            field[both((first + row) * 4 * half), :] = with_turned(landed[step, tile(row * 2 * half), :])
            return unused

        lax.fori_loop(0, edge_size, edge_step, 0, unroll=8)
    field[both(planes * (size + edge_size) * 4 * half), :] = jnp.zeros((4 * half, lanes), jnp.float32)

    blank = jnp.zeros((2 * half, lanes), jnp.float32)
    sub = lax.broadcasted_iota(jnp.int32, (2 * half, lanes), 0)
    dest_count = out.shape[1]
    dest_rows = fine_rows // dest_count

    def plane_step(turn, unused):
        plane = own ^ turn
        slot = turn % 2
        bring(turn).wait()

        @pl.when(turn + 1 < planes)
        def _():
            bring(turn + 1).start()

        across = lanes // plan.width

        def boxes_step(slot_count, step, unused):
            ranks = [step * plan.together + each for each in range(plan.together)]
            boxes = [meta[slot, plan.order, rank] for rank in ranks]
            sums = [[blank, blank] for box in boxes]
            for pair in range(slot_count):
                for each in range(plan.together):
                    row = step * (plan.together // across) + each // across
                    place, kind = parts_of(meta[slot, row, each % across * plan.width + pair])
                    value = field[both(place), :]
                    factor = table[tile(kind), :]
                    sums[each][0] += factor * value[: 2 * half]
                    sums[each][1] += factor * value[2 * half :]
            for each in range(plan.together):
                straight, crossed = sums[each]
                total = jnp.where(
                    sub < half,
                    straight + pltpu.roll(straight, half, 0),
                    pltpu.roll(crossed, half, 0) - crossed,
                )
                moved[both(boxes[each] * 4 * half), :] = with_turned(total)
            return unused

        start = 0
        for more in reversed(range((plan.slots - plan.fixed) // plan.group + 1)):
            end = meta[slot, plan.order, plan.turns + more]
            lax.fori_loop(start, end, functools.partial(boxes_step, plan.fixed + more * plan.group), 0)
            start = end

        def fine_step(block, unused):
            for each in range(lanes):
                parent, octant = parts_of(meta[slot, plan.parent + block, each])
                value = moved[both(parent), :] * phases[both(octant), :]
                shifted[tile((block * lanes + each) * 2 * half), :] = value[: 2 * half] + value[2 * half :]
            return unused

        lax.fori_loop(0, fine_rows // lanes, fine_step, 0)
        width = ready.shape[3]
        left = jnp.concatenate(
            [
                jnp.concatenate(
                    [
                        shifted[pl.ds(part * half + block, fine_rows, stride=2 * half), :]
                        for block in range(half)
                    ],
                    axis=1,
                )
                for part in range(2)
            ],
            axis=0,
        )
        first, second = split(left)
        result = jnp.dot(
            jnp.concatenate([first, first, second], axis=1), weights[...], preferred_element_type=jnp.float32
        )
        for part in range(2):
            for dest in range(dest_count):
                start = part * fine_rows + dest * dest_rows
                ready[plane, dest, part * dest_rows : (part + 1) * dest_rows, :] = result[
                    start : start + dest_rows, :width
                ]
        spill = result[:fine_rows, width:] + pltpu.roll(result[fine_rows:, width:], half, 1)
        spill = spill.T[: 2 * half]
        for dest in range(dest_count):
            ready[plane, dest, 2 * dest_rows :, :] = jnp.concatenate(
                [
                    spill[:, dest * dest_rows : (dest + 1) * dest_rows],
                    jnp.zeros((2 * half, width - dest_rows), jnp.float32),
                ],
                axis=1,
            )
        pltpu.make_async_copy(ready.at[plane], out.at[plane], sems.at[plane]).start()
        return unused

    lax.fori_loop(0, planes, plane_step, 0)
    for plane in range(planes):
        pltpu.make_async_copy(ready.at[plane], out.at[plane], sems.at[plane]).wait()


def join_kernel(source_count, parts, rims, out, whole):
    dest_rows = out.shape[0]
    dirs = parts.shape[0] // source_count
    over = jnp.concatenate(
        [parts[index, 2 * dest_rows :, :lanes] for index in range(parts.shape[0])], axis=0
    ).T[:dest_rows]
    low = lax.broadcasted_iota(jnp.int32, (dest_rows, lanes), 1) < rim
    at_rim = jnp.broadcast_to(rims[...], (dest_rows, lanes)) < 0.5
    for source in range(source_count):
        for part in range(2):
            turned = []
            for index in range(dirs):
                first = (source * dirs + index) * 2 * half + part * half
                turned.append(pltpu.roll(over, (lanes - rim - first) % lanes, 1))
            for index in range(dirs):
                fix = jnp.where(at_rim, jnp.where(low, turned[index - 1], turned[(index + 1) % dirs]), 0.0)
                whole[
                    index, pl.ds(part * source_count + source, dest_rows, stride=2 * source_count), :
                ] = parts[source * dirs + index, part * dest_rows : (part + 1) * dest_rows, :] + fix

    def row_step(row, unused):
        start = pl.multiple_of(row * 2 * source_count, 2 * source_count)
        both = jnp.concatenate(
            [whole[index, pl.ds(start, 2 * source_count), :] for index in range(dirs)], axis=1
        )
        out[row, 0] = both[:source_count]
        out[row, 1] = both[source_count:]
        return unused

    lax.fori_loop(0, dest_rows, row_step, 0, unroll=8)


def per_device(
    coarse_field,
    trans_table,
    partner_ids,
    partner_types,
    partner_count,
    child_count,
    child_octant,
    dir_angles,
    stencil_ids,
    stencil_weights,
):
    rows, _, source_count, kc_dev = coarse_field.shape
    slots = partner_ids.shape[1]
    type_count = trans_table.shape[0]
    fine_rows = child_octant.shape[0]
    ring_count = lax.axis_size("ring")
    dir_count = lax.axis_size("dir")
    zed = lax.axis_index("zed")
    ring = lax.axis_index("ring")
    dir_index = lax.axis_index("dir")
    fine_count = stencil_ids.shape[0] // 4
    kf_dev = fine_count // dir_count
    kc_pad = up(kc_dev, half * lanes)
    kf_pad = up(kf_dev, lanes)
    pad_dirs = kc_pad - kc_dev
    assert source_count == planes and kc_pad == half * lanes
    dest_rows = fine_rows // dir_count

    field = jnp.pad(coarse_field, ((0, 0), (0, 0), (0, 0), (0, pad_dirs)))
    here = zed.reshape(1)
    packed = pack(here, field, [])
    edge_rows = 0
    if ring_count == 2:
        packed, field = lax.optimization_barrier((packed, field))
        edges = lax.ppermute(near_edge(field, ring), "ring", [(0, 1), (1, 0)])
        edge_rows = edges.shape[0]

    def to_planes(note, step):
        if step == 0:
            return note
        return lax.ppermute(note, "zed", [(plane, plane ^ step) for plane in range(planes)])

    arrived = [to_planes(packed[step], step) for step in (3, 2, 1, 0)][::-1]

    plane_of = partner_ids // (ring_count * rows)
    ring_of = partner_ids // rows % ring_count
    local = partner_ids % rows
    live = jnp.arange(slots, dtype=jnp.int32)[None, :] < partner_count[:, None]
    if ring_count == 2:
        size = rows
        place = jnp.where(
            ring_of == ring,
            plane_of * rows + local,
            planes * rows + plane_of * edge_rows + edge_rank(local, rows),
        )
    else:
        size = ring_count * rows
        place = partner_ids
    field_rows = planes * (size + edge_rows)
    place = jnp.where(live, place, field_rows)
    together = 8
    fixed = slots // 2
    group = 3 if (slots - fixed) % 3 == 0 else 1
    index = jnp.arange(rows, dtype=jnp.int32)
    before = (partner_count[None, :] > partner_count[:, None]) | (
        (partner_count[None, :] == partner_count[:, None]) & (index[None, :] < index[:, None])
    )
    rank = jnp.sum(before.astype(jnp.int32), axis=1)
    at_rank = rank[None, :] == index[:, None]
    order = jnp.sum(jnp.where(at_rank, index[None, :], 0), axis=1)
    first = rank[None, :] == index[: rows // together, None] * together
    longest = jnp.sum(jnp.where(first, partner_count[None, :], 0), axis=1)
    turns = jnp.maximum((longest - fixed + group - 1) // group, 0)
    more = jnp.arange((slots - fixed) // group + 1, dtype=jnp.int32)
    ends = jnp.sum((turns[None, :] >= more[:, None]).astype(jnp.int32), axis=1)
    bounds = jnp.sum(jnp.where(index[None, :] <= index[:, None], child_count[None, :], 0), axis=1)
    parent = jnp.sum(
        (bounds[None, :] <= jnp.arange(fine_rows, dtype=jnp.int32)[:, None]).astype(jnp.int32), axis=1
    )
    def across(one, width=lanes):
        return jnp.pad(one, ((0, 0), (0, width - one.shape[1])))

    width = lanes // half
    turns_at = lanes // 2
    assert slots <= width and rows <= turns_at and fine_rows % lanes == 0
    assert (field_rows + 1) * 4 * half < 2 ** (31 - word_bits) and type_count * 2 * half < 2**word_bits

    def in_order(one):
        one = jnp.sum(jnp.where(at_rank[:, :, None], across(one, width)[None], 0), axis=1)
        return one.reshape(rows * width // lanes, lanes)

    list_rows = rows * width // lanes
    fine_lists = fine_rows // lanes
    last = across(jnp.concatenate([across(order[None], turns_at), ends[None]], axis=1))
    stride = up(list_rows + fine_lists + 1, 8)

    def stacked(*parts):
        meta = jnp.concatenate(parts)
        return jnp.pad(meta, ((0, stride - meta.shape[0]), (0, 0))).astype(jnp.float32)

    meta = jnp.concatenate(
        [
            stacked(in_order(place * 4 * half), (parent * 4 * half).reshape(-1, lanes)),
            stacked(in_order(partner_types * 2 * half), (child_octant * 4 * half).reshape(-1, lanes), last),
        ]
    )
    plan = Plan(
        rows, slots, fine_rows, stride, width, list_rows, list_rows + fine_lists, turns_at, together, fixed, group
    )

    notes = pack(here, edges, [meta]) if ring_count == 2 else [meta] * planes
    after_notes = lax.optimization_barrier((notes, trans_table, dir_angles, stencil_ids, stencil_weights))
    notes, trans_table, dir_angles, stencil_ids, stencil_weights = after_notes
    received = [to_planes(notes[step], step) for step in (3, 2, 1, 0)][::-1]
    edge_part = edge_rows * 2 * half
    numbers = jnp.stack([note[edge_part:] for note in received]).astype(jnp.int32)
    meta = numbers[:, :stride] * 2**word_bits + numbers[:, stride:]
    if ring_count != 2:
        arrived = [lax.all_gather(one, "ring", axis=0, tiled=True) for one in arrived]
        received = []

    def blocks(table):
        return jnp.pad(table, ((0, 0), (0, pad_dirs))).reshape(-1, half, lanes)

    def doubled(table, sign):
        return jnp.concatenate([blocks(table), sign * blocks(table)], axis=1)

    table = jnp.pad(trans_table, ((0, 0), (0, 0), (0, pad_dirs))).reshape(-1, lanes)
    angles = lax.dynamic_slice_in_dim(dir_angles, dir_index * kc_dev, kc_dev, axis=1)
    octants = jnp.arange(8, dtype=jnp.int32)
    sign_x = 1.0 - 2.0 * (octants % 2).astype(jnp.float32)
    sign_y = 1.0 - 2.0 * (octants // 2 % 2).astype(jnp.float32)
    sign_z = 1.0 - 2.0 * (octants // 4).astype(jnp.float32)
    unit_x = jnp.sin(angles[0]) * jnp.cos(angles[1])
    unit_y = jnp.sin(angles[0]) * jnp.sin(angles[1])
    unit_z = jnp.cos(angles[0])
    phase = wave_scale * (
        sign_x[:, None] * unit_x[None, :] + sign_y[:, None] * unit_y[None, :] + sign_z[:, None] * unit_z[None, :]
    )
    phases = jnp.concatenate(
        [doubled(jnp.cos(phase), 1.0), doubled(jnp.sin(phase), -1.0)], axis=1
    ).reshape(-1, lanes)

    ids = lax.dynamic_slice_in_dim(stencil_ids, dir_index * kc_dev, kc_dev, axis=0).T
    weights = lax.dynamic_slice_in_dim(stencil_weights, dir_index * kc_dev, kc_dev, axis=0).T

    def interp(targets):
        matrix = jnp.zeros((targets.shape[0], kc_dev), jnp.float32)
        for point in range(ids.shape[0]):
            matrix = matrix + jnp.where(
                ids[point][None, :] == targets[:, None], weights[point][None, :], 0.0
            )
        return jnp.pad(matrix, ((0, 0), (0, pad_dirs)))

    first_fine = dir_index * kf_dev
    own = jnp.arange(kf_dev, dtype=jnp.int32)
    outside = jnp.concatenate(
        [jnp.arange(-rim, 0, dtype=jnp.int32), jnp.arange(kf_dev, kf_dev + rim, dtype=jnp.int32)]
    )
    matrix = jnp.pad(interp(first_fine + own), ((0, kf_pad - kf_dev), (0, 0)))
    spill = interp((first_fine + outside) % fine_count)
    matrices = jnp.concatenate([matrix, jnp.pad(spill, ((0, lanes - half), (0, 0)))], axis=0).T
    rounded = lax.reduce_precision(matrices, 8, 7)
    high = rounded.astype(jnp.bfloat16)
    low = (matrices - rounded).astype(jnp.bfloat16)
    passes = jnp.concatenate([high, low, high], axis=0)

    whole = pl.BlockSpec(memory_space=pltpu.VMEM)
    message = (2 * dest_rows + 2 * half, kf_pad)
    local_fine, rims = pl.pallas_call(
        functools.partial(fine_kernel, plan, size, edge_rows),
        out_shape=[
            pltpu.HBM((planes, dir_count) + message, jnp.float32),
            jax.ShapeDtypeStruct((2 * half, lanes), jnp.float32),
        ],
        in_specs=[pl.BlockSpec(memory_space=pltpu.SMEM), pl.BlockSpec(memory_space=pl.ANY)]
        + [whole] * planes
        + [pl.BlockSpec(memory_space=pl.ANY)] * len(received)
        + [whole] * 3,
        out_specs=[pl.BlockSpec(memory_space=pltpu.HBM), whole],
        scratch_shapes=[
            pltpu.SMEM((2, plan.stride, lanes), jnp.int32),
            pltpu.VMEM(((field_rows + 1) * 4 * half, lanes), jnp.float32),
            pltpu.VMEM((rows * 4 * half, lanes), jnp.float32),
            pltpu.VMEM((fine_rows * 2 * half, lanes), jnp.float32),
            pltpu.VMEM((planes, dir_count) + message, jnp.float32),
            pltpu.VMEM((planes, max(edge_rows, 1) * 2 * half, lanes), jnp.float32),
            pltpu.SemaphoreType.DMA((2 * planes + 2,)),
        ],
        compiler_params=pltpu.CompilerParams(vmem_limit_bytes=48 * 2**20),
        name="translate_and_interpolate",
    )(here, meta, *arrived, *received, table, phases, passes)

    parts = lax.all_to_all(
        local_fine.reshape((planes * dir_count,) + message),
        ("zed", "dir"),
        split_axis=0,
        concat_axis=0,
        tiled=True,
    )
    result = (dest_rows, 2, source_count, fine_count)
    if kf_dev == lanes and planes * dir_count * 2 * half == lanes and dest_rows <= lanes:
        return pl.pallas_call(
            functools.partial(join_kernel, source_count),
            out_shape=jax.ShapeDtypeStruct(result, jnp.float32),
            in_specs=[whole] * 2,
            out_specs=whole,
            scratch_shapes=[pltpu.VMEM((dir_count, dest_rows * 2 * source_count, lanes), jnp.float32)],
            compiler_params=pltpu.CompilerParams(vmem_limit_bytes=24 * 2**20),
            name="join_parts",
        )(parts, 1.0 - rims[:1])
    parts = parts.reshape((planes, dir_count) + message)
    main = parts[:, :, : 2 * dest_rows, :kf_dev].reshape(planes, dir_count, 2, dest_rows, kf_dev)
    over = parts[:, :, 2 * dest_rows :, :dest_rows].reshape(planes, dir_count, 2, 2 * rim, dest_rows)
    low = jnp.roll(over[:, :, :, :rim], -1, axis=1)
    high = jnp.roll(over[:, :, :, rim:], 1, axis=1)
    middle = jnp.zeros((planes, dir_count, 2, kf_dev - 2 * rim, dest_rows), jnp.float32)
    fix = jnp.concatenate([high, middle, low], axis=3)
    total = main.transpose(3, 2, 0, 1, 4) + fix.transpose(4, 2, 0, 1, 3)
    return total.reshape(result)


def solution(mesh):
    boxes, dirs = mesh.shape["box"], mesh.shape["dir"]
    fine_mesh = Mesh(mesh.devices.reshape(planes, boxes // planes, dirs), ("zed", "ring", "dir"))
    box = ("zed", "ring")
    placed = (
        P(box, None, None, "dir"),
        P(None, None, "dir"),
        P(box, None),
        P(box, None),
        P(box),
        P(box),
        P(box),
        P(),
        P(),
        P(),
    )
    return jax.shard_map(
        per_device,
        mesh=fine_mesh,
        in_specs=placed,
        out_specs=P(("zed", "ring", "dir"), None, None, None),
        check_vma=False,
    )
```

```python
import collections
import functools

import jax
import jax.numpy as jnp
from jax import lax
from jax.experimental import pallas as pl
from jax.experimental.pallas import tpu as pltpu
from jax.sharding import Mesh
from jax.sharding import PartitionSpec as P

wave_scale = 3.0
planes = 4
lanes = 128
half = 4
rim = 2
word_bits = 13


plan_fields = ["rows", "slots", "fine_rows", "stride", "width", "parent", "order", "turns"]
Plan = collections.namedtuple("Plan", plan_fields + ["together", "fixed", "group"])


def up(size, step):
    return -(-size // step) * step


def edge_bits(rows):
    bits = rows.bit_length() - 1
    return bits, [place for place in range(2, bits) if place % 2 == bits % 2]


def near_edge(block, ring):
    rows = block.shape[0]
    bits, fixed = edge_bits(rows)
    tail = block.shape[1:]
    picked = block.reshape((2,) * bits + tail)
    for place in fixed:
        picked = lax.dynamic_index_in_dim(picked, 1 - ring, axis=bits - 1 - place, keepdims=True)
    return picked.reshape((rows >> len(fixed),) + tail)


def edge_rank(local, rows):
    bits, fixed = edge_bits(rows)
    rank = jnp.zeros_like(local)
    taken = 0
    for place in range(bits):
        if place not in fixed:
            rank = rank + (local // 2**place % 2) * 2**taken
            taken += 1
    return rank


def split(value):
    high = value.astype(jnp.bfloat16)
    low = (value - high.astype(jnp.float32)).astype(jnp.bfloat16)
    return high, low


def pack_kernel(source_count, note_count, zed, field, *refs):
    notes, outs, whole = refs[:note_count], refs[note_count:-1], refs[-1]
    rows = field.shape[0]
    stride = 2 * source_count

    def row_step(row, unused):
        both = jnp.concatenate([field[row, 0], field[row, 1]], axis=0)
        for block in range(half):
            whole[block, pl.ds(pl.multiple_of(row * stride, stride), stride), :] = both[
                :, block * lanes : (block + 1) * lanes
            ]
        return unused

    lax.fori_loop(0, rows, row_step, 0, unroll=8)
    sides = len(outs) // planes
    for side in range(2):
        for step in range(planes):
            source = zed[0] ^ step
            out = outs[side % sides * planes + step]
            first = (side - side % sides) * rows * half
            for part in range(2):
                for block in range(half // 2):
                    out[pl.ds(first + part * half // 2 + block, rows, stride=half), :] = whole[
                        side * half // 2 + block, pl.ds(part * source_count + source, rows, stride=stride), :
                    ]
            for note in notes:
                out[2 * rows * half :, :] = note[...]


def pack(zed, field, notes):
    rows, _, source_count, width = field.shape
    whole = pl.BlockSpec(memory_space=pltpu.VMEM)
    if notes:
        lengths = [2 * rows * half + notes[0].shape[0]] * planes
    else:
        lengths = [rows * half] * (2 * planes)
    return pl.pallas_call(
        functools.partial(pack_kernel, source_count, len(notes)),
        out_shape=[jax.ShapeDtypeStruct((length, lanes), jnp.float32) for length in lengths],
        in_specs=[pl.BlockSpec(memory_space=pltpu.SMEM)] + [whole] * (1 + len(notes)),
        out_specs=[whole] * len(lengths),
        scratch_shapes=[pltpu.VMEM((half, rows * 2 * source_count, lanes), jnp.float32)],
        name="pack_sources",
    )(zed, field, *notes)


def parts_of(word):
    return lax.shift_right_logical(word, word_bits), word & (2**word_bits - 1)


def tile(start):
    return pl.ds(pl.multiple_of(start, 2 * half), 2 * half)


def fine_kernel(plan, size, edge_size, side, zed, lists, *refs):
    mains, refs = refs[:planes], refs[planes:]
    edges = refs[: planes if edge_size else 0]
    refs = refs[len(edges) :]
    table, phases, weights, out, rims, meta, field, factors, moved, shifted, ready, landed, sems = refs
    rows, fine_rows = plan.rows, plan.fine_rows
    own = zed[0]

    def bring(step):
        return pltpu.make_async_copy(lists.at[step], meta.at[step % 2], sems.at[planes + step % 2])

    bring(0).start()
    incoming = []
    for step, edge in enumerate(edges):
        chosen = edge.at[pl.ds(side * edge_size * half, edge_size * half)]
        incoming.append(pltpu.make_async_copy(chosen, landed.at[step], sems.at[planes + 2 + step]))
        incoming[-1].start()
    lane = lax.broadcasted_iota(jnp.int32, rims.shape, 1)
    rims[...] = ((lane < rim) | (lane >= lanes - rim)).astype(jnp.float32)
    sub = lax.broadcasted_iota(jnp.int32, (2 * half, lanes), 0)
    pair_of = sub // 2

    def turned(value, by):
        return pltpu.roll(value, by % (2 * half), 0) if by % (2 * half) else value

    def gathered(value, sources):
        result = turned(value, -2 * sources[0])
        for index in range(1, len(sources)):
            result = jnp.where(pair_of == index, turned(value, 2 * (index - sources[index])), result)
        return result

    def fill_from(ref, count, first):
        def fill_step(step, unused):
            value = ref[tile(step * 2 * half), :]
            field[tile((first + 2 * step) * 2 * half), :] = gathered(value, (0, 1, 1, 0))
            field[tile((first + 2 * step + 1) * 2 * half), :] = gathered(value, (2, 3, 3, 2))
            return unused

        lax.fori_loop(0, count // 2, fill_step, 0, unroll=8)

    for step, main in enumerate(mains):
        fill_from(main, size, (own ^ step) * size)
    blank = jnp.zeros((2 * half, lanes), jnp.float32)
    field[tile(planes * (size + edge_size) * 2 * half), :] = blank

    def factor_step(kind, unused):
        factors[tile(kind * 2 * half), :] = gathered(table[tile(kind * 2 * half), :], (side, 2 + side) * 2)
        return unused

    lax.fori_loop(0, table.shape[0] // (2 * half), factor_step, 0, unroll=4)
    for step, copy in enumerate(incoming):
        copy.wait()
        fill_from(landed.at[step], edge_size, planes * size + (own ^ step) * edge_size)
    sign = jnp.where(sub < half, 1.0, -1.0).astype(jnp.float32)
    dest_count = out.shape[1]
    dest_rows = fine_rows // dest_count

    def plane_step(turn, unused):
        plane = own ^ turn
        slot = turn % 2
        bring(turn).wait()

        @pl.when(turn + 1 < planes)
        def _():
            bring(turn + 1).start()

        across = lanes // plan.width

        def boxes_step(slot_count, step, unused):
            boxes = [meta[slot, plan.order, step * plan.together + each] for each in range(plan.together)]
            sums = [blank for box in boxes]
            for pair in range(slot_count):
                for each in range(plan.together):
                    row = step * (plan.together // across) + each // across
                    place, kind = parts_of(meta[slot, row, each % across * plan.width + pair])
                    sums[each] += factors[tile(kind), :] * field[tile(place), :]
            for each in range(plan.together):
                total = sums[each] + sign * turned(sums[each], -2)
                total = jnp.where(pair_of % 2 == 0, total, turned(total, -2))
                moved[tile(boxes[each] * 2 * half), :] = total
            return unused

        start = 0
        for more in reversed(range((plan.slots - plan.fixed) // plan.group + 1)):
            end = meta[slot, plan.order, plan.turns + more]
            lax.fori_loop(start, end, functools.partial(boxes_step, plan.fixed + more * plan.group), 0)
            start = end

        def fine_step(block, unused):
            for each in range(lanes):
                parent, octant = parts_of(meta[slot, plan.parent + block, each])
                value = moved[tile(parent), :] * phases[tile(octant), :]
                shifted[tile((block * lanes + each) * 2 * half), :] = value + turned(value, half)
            return unused

        lax.fori_loop(0, fine_rows // lanes, fine_step, 0)
        left = jnp.concatenate(
            [shifted[pl.ds(block, fine_rows, stride=2 * half), :] for block in range(half)], axis=1
        )
        first, second = split(left)
        result = jnp.dot(
            jnp.concatenate([first, first, second], axis=1), weights[...], preferred_element_type=jnp.float32
        )
        spill = result[:, lanes:].T[: 2 * half]
        for dest in range(dest_count):
            rows_of = slice(dest * dest_rows, (dest + 1) * dest_rows)
            ready[plane, dest, :dest_rows, :] = result[rows_of, :lanes]
            ready[plane, dest, dest_rows:, :] = jnp.concatenate(
                [spill[:, rows_of], jnp.zeros((2 * half, lanes - dest_rows), jnp.float32)], axis=1
            )
        pltpu.make_async_copy(ready.at[plane], out.at[plane], sems.at[plane]).start()
        return unused

    lax.fori_loop(0, planes, plane_step, 0)
    for plane in range(planes):
        pltpu.make_async_copy(ready.at[plane], out.at[plane], sems.at[plane]).wait()


def join_kernel(source_count, first, second, rims, out, whole):
    dest_rows = out.shape[0]
    dirs = first.shape[0] // source_count
    lane = lax.broadcasted_iota(jnp.int32, (dest_rows, lanes), 1)
    middle = lanes // 2
    at_rim = jnp.broadcast_to(rims[...], (dest_rows, lanes)) < 0.5
    at_middle = (lane >= middle - rim) & (lane < middle + rim)

    def spills(parts):
        return jnp.concatenate(
            [parts[index, dest_rows:, :] for index in range(parts.shape[0])], axis=0
        ).T[:dest_rows]

    over = spills(first), spills(second)
    is_low = lane % (2 * rim) < rim
    outer = jnp.where(is_low, over[0], over[1])
    inner = jnp.where(is_low, over[1], over[0])
    for source in range(source_count):
        ends = [first[source * dirs + index, :dest_rows, :] for index in range(dirs)]
        starts = [second[source * dirs + index, :dest_rows, :] for index in range(dirs)]
        for part in range(2):
            turned = []
            places = [(source * dirs + index) * 2 * half + part * half for index in range(dirs)]
            for place in places:
                turned.append(pltpu.roll(outer, (lanes - rim - place) % lanes, 1))
            for index in range(dirs):
                low, high = ends[index], starts[index]
                if part == 0:
                    high = pltpu.roll(high, middle, 1)
                else:
                    low = pltpu.roll(low, middle, 1)
                within = pltpu.roll(inner, (middle - rim - places[index]) % lanes, 1)
                fix = jnp.where(lane < middle, turned[index - 1], turned[(index + 1) % dirs])
                fix = jnp.where(at_rim, fix, jnp.where(at_middle, within, 0.0))
                whole[
                    index, pl.ds(part * source_count + source, dest_rows, stride=2 * source_count), :
                ] = jnp.where(lane < middle, low, high) + fix

    def row_step(row, unused):
        start = pl.multiple_of(row * 2 * source_count, 2 * source_count)
        both = jnp.concatenate(
            [whole[index, pl.ds(start, 2 * source_count), :] for index in range(dirs)], axis=1
        )
        out[row, 0] = both[:source_count]
        out[row, 1] = both[source_count:]
        return unused

    lax.fori_loop(0, dest_rows, row_step, 0, unroll=8)


def per_device(
    coarse_field,
    trans_table,
    partner_ids,
    partner_types,
    partner_count,
    child_count,
    child_octant,
    dir_angles,
    stencil_ids,
    stencil_weights,
):
    rows, _, source_count, kc_dev = coarse_field.shape
    slots = partner_ids.shape[1]
    type_count = trans_table.shape[0]
    fine_rows = child_octant.shape[0]
    ring_count = lax.axis_size("ring")
    dir_count = lax.axis_size("dir")
    zed = lax.axis_index("zed")
    ring = lax.axis_index("ring")
    dir_index = lax.axis_index("dir")
    fine_count = stencil_ids.shape[0] // 4
    kf_dev = fine_count // dir_count
    kc_half, kf_half = kc_dev // 2, kf_dev // 2
    kc_pad = half * lanes
    pad_half = kc_pad // 2 - kc_half
    assert source_count == planes and pad_half >= 0 and kf_half <= lanes // 2
    dest_rows = fine_rows // dir_count

    def widen(array):
        array = array.reshape(array.shape[:-1] + (2, kc_half))
        array = jnp.pad(array, ((0, 0),) * (array.ndim - 1) + ((0, pad_half),))
        return array.reshape(array.shape[:-2] + (kc_pad,))

    field = widen(coarse_field) if pad_half else coarse_field
    here = zed.reshape(1)
    packed = list(pack(here, field, []))
    edge_rows = 0
    if ring_count == 2:
        packed, field = lax.optimization_barrier((packed, field))
        edges = lax.ppermute(near_edge(field, ring), "ring", [(0, 1), (1, 0)])
        edge_rows = edges.shape[0]

    def to_planes(notes):
        moves = [[(plane, plane ^ step) for plane in range(planes)] for step in range(planes)]
        return [lax.ppermute(notes[step], "zed", moves[step]) for step in (3, 2, 1)][::-1]

    arrived = [packed[:1] + to_planes(packed[:planes])]

    plane_of = partner_ids // (ring_count * rows)
    ring_of = partner_ids // rows % ring_count
    local = partner_ids % rows
    live = jnp.arange(slots, dtype=jnp.int32)[None, :] < partner_count[:, None]
    if ring_count == 2:
        size = rows
        place = jnp.where(
            ring_of == ring,
            plane_of * rows + local,
            planes * rows + plane_of * edge_rows + edge_rank(local, rows),
        )
    else:
        size = ring_count * rows
        place = partner_ids
    field_rows = planes * (size + edge_rows)
    place = jnp.where(live, place, field_rows)
    together = 8
    fixed = slots // 2
    group = 3 if (slots - fixed) % 3 == 0 else 1
    index = jnp.arange(rows, dtype=jnp.int32)
    before = (partner_count[None, :] > partner_count[:, None]) | (
        (partner_count[None, :] == partner_count[:, None]) & (index[None, :] < index[:, None])
    )
    rank = jnp.sum(before.astype(jnp.int32), axis=1)
    at_rank = rank[None, :] == index[:, None]
    order = jnp.sum(jnp.where(at_rank, index[None, :], 0), axis=1)
    first = rank[None, :] == index[: rows // together, None] * together
    longest = jnp.sum(jnp.where(first, partner_count[None, :], 0), axis=1)
    turns = jnp.maximum((longest - fixed + group - 1) // group, 0)
    more = jnp.arange((slots - fixed) // group + 1, dtype=jnp.int32)
    ends = jnp.sum((turns[None, :] >= more[:, None]).astype(jnp.int32), axis=1)
    bounds = jnp.sum(jnp.where(index[None, :] <= index[:, None], child_count[None, :], 0), axis=1)
    parent = jnp.sum(
        (bounds[None, :] <= jnp.arange(fine_rows, dtype=jnp.int32)[:, None]).astype(jnp.int32), axis=1
    )
    def across(one, width=lanes):
        return jnp.pad(one, ((0, 0), (0, width - one.shape[1])))

    width = lanes // half
    turns_at = lanes // 2
    assert slots <= width and rows <= turns_at and fine_rows % lanes == 0
    assert (field_rows + 1) * 2 * half < 2 ** (31 - word_bits) and type_count * 2 * half < 2**word_bits

    def in_order(one):
        one = jnp.sum(jnp.where(at_rank[:, :, None], across(one, width)[None], 0), axis=1)
        return one.reshape(rows * width // lanes, lanes)

    list_rows = rows * width // lanes
    fine_lists = fine_rows // lanes
    last = across(jnp.concatenate([across(order[None], turns_at), ends[None]], axis=1))
    stride = up(list_rows + fine_lists + 1, 8)

    def stacked(*parts):
        meta = jnp.concatenate(parts)
        return jnp.pad(meta, ((0, stride - meta.shape[0]), (0, 0))).astype(jnp.float32)

    meta = jnp.concatenate(
        [
            stacked(in_order(place * 2 * half), (parent * 2 * half).reshape(-1, lanes)),
            stacked(in_order(partner_types * 2 * half), (child_octant * 2 * half).reshape(-1, lanes), last),
        ]
    )
    plan = Plan(
        rows, slots, fine_rows, stride, width, list_rows, list_rows + fine_lists, turns_at, together, fixed, group
    )

    notes = list(pack(here, edges, [meta])) if ring_count == 2 else [meta] * planes
    after_notes = lax.optimization_barrier(
        (notes, packed[planes:], trans_table, dir_angles, stencil_ids, stencil_weights)
    )
    notes, later, trans_table, dir_angles, stencil_ids, stencil_weights = after_notes
    notes, later = list(notes), list(later)
    received = notes[:1] + to_planes(notes)
    arrived.append(later[:1] + to_planes(later))
    edge_part = edge_rows * 2 * half
    numbers = jnp.stack([note[edge_part:] for note in received]).astype(jnp.int32)
    meta = numbers[:, :stride] * 2**word_bits + numbers[:, stride:]
    if ring_count != 2:
        arrived = [[lax.all_gather(one, "ring", axis=0, tiled=True) for one in side] for side in arrived]
        received = []

    table = (widen(trans_table) if pad_half else trans_table).reshape(-1, lanes)
    angles = lax.dynamic_slice_in_dim(dir_angles, dir_index * kc_dev, kc_dev, axis=1)
    angles = widen(angles).reshape(2, half, lanes)
    octants = jnp.arange(8, dtype=jnp.int32)[:, None, None]
    sign_x = 1.0 - 2.0 * (octants % 2).astype(jnp.float32)
    sign_y = 1.0 - 2.0 * (octants // 2 % 2).astype(jnp.float32)
    sign_z = 1.0 - 2.0 * (octants // 4).astype(jnp.float32)
    kind = jnp.arange(2 * half, dtype=jnp.int32)[None, :, None] // 2

    def phases(side):
        chosen = jnp.concatenate([angles[:, side * half // 2 : (side + 1) * half // 2]] * 4, axis=1)
        unit_x = jnp.sin(chosen[0]) * jnp.cos(chosen[1])
        unit_y = jnp.sin(chosen[0]) * jnp.sin(chosen[1])
        unit_z = jnp.cos(chosen[0])
        phase = wave_scale * (sign_x * unit_x + sign_y * unit_y + sign_z * unit_z)
        sine = jnp.sin(phase)
        return jnp.where(kind < 2, jnp.cos(phase), jnp.where(kind == 2, sine, -sine)).reshape(-1, lanes)

    ids = lax.dynamic_slice_in_dim(stencil_ids, dir_index * kc_dev, kc_dev, axis=0).T
    weights = lax.dynamic_slice_in_dim(stencil_weights, dir_index * kc_dev, kc_dev, axis=0).T

    def interp(targets):
        matrix = jnp.zeros((targets.shape[0], kc_dev), jnp.float32)
        for point in range(ids.shape[0]):
            matrix = matrix + jnp.where(
                ids[point][None, :] == targets[:, None], weights[point][None, :], 0.0
            )
        return matrix

    def passes(side):
        first_fine = dir_index * kf_dev + side * kf_half
        own = jnp.arange(kf_half, dtype=jnp.int32)
        outside = jnp.concatenate(
            [jnp.arange(-rim, 0, dtype=jnp.int32), jnp.arange(kf_half, kf_half + rim, dtype=jnp.int32)]
        )
        chosen = slice(side * kc_half, (side + 1) * kc_half)
        main = jnp.pad(interp(first_fine + own)[:, chosen], ((0, lanes // 2 - kf_half), (0, pad_half)))
        spill = jnp.pad(interp((first_fine + outside) % fine_count)[:, chosen], ((0, 0), (0, pad_half)))
        wide = kc_pad // 2
        matrix = jnp.concatenate(
            [
                jnp.pad(one, ((0, 0), (part * wide, wide - part * wide)))
                for one in (main, spill)
                for part in range(2)
            ]
        )
        matrix = jnp.pad(matrix, ((0, 2 * lanes - matrix.shape[0]), (0, 0))).T
        rounded = lax.reduce_precision(matrix, 8, 7)
        high = rounded.astype(jnp.bfloat16)
        low = (matrix - rounded).astype(jnp.bfloat16)
        return jnp.concatenate([high, low, high], axis=0)

    whole = pl.BlockSpec(memory_space=pltpu.VMEM)
    message = (dest_rows + 2 * half, lanes)
    cost = pl.CostEstimate(
        flops=planes * fine_rows * 3 * kc_pad * 4 * lanes,
        bytes_accessed=planes * rows * slots * 2 * 2 * half * lanes * 4,
        transcendentals=0,
    )

    def fine(side):
        return pl.pallas_call(
            functools.partial(fine_kernel, plan, size, edge_rows, side),
            out_shape=[
                pltpu.HBM((planes, dir_count) + message, jnp.float32),
                jax.ShapeDtypeStruct((2 * half, lanes), jnp.float32),
            ],
            in_specs=[pl.BlockSpec(memory_space=pltpu.SMEM), pl.BlockSpec(memory_space=pl.ANY)]
            + [whole] * planes
            + [pl.BlockSpec(memory_space=pl.ANY)] * len(received)
            + [whole] * 3,
            out_specs=[pl.BlockSpec(memory_space=pltpu.HBM), whole],
            scratch_shapes=[
                pltpu.SMEM((2, plan.stride, lanes), jnp.int32),
                pltpu.VMEM(((field_rows + 1) * 2 * half, lanes), jnp.float32),
                pltpu.VMEM((type_count * 2 * half, lanes), jnp.float32),
                pltpu.VMEM((rows * 2 * half, lanes), jnp.float32),
                pltpu.VMEM((fine_rows * 2 * half, lanes), jnp.float32),
                pltpu.VMEM((planes, dir_count) + message, jnp.float32),
                pltpu.VMEM((planes, max(edge_rows, 2) * half, lanes), jnp.float32),
                pltpu.SemaphoreType.DMA((2 * planes + 2,)),
            ],
            compiler_params=pltpu.CompilerParams(vmem_limit_bytes=48 * 2**20),
            cost_estimate=cost,
            name="translate_and_interpolate",
        )(here, meta, *arrived[side], *received, table, phases(side), passes(side))

    parts = []
    for side in range(2):
        local_fine, rims = fine(side)
        local_fine = local_fine.reshape((planes * dir_count,) + message)
        parts.append(lax.all_to_all(local_fine, ("zed", "dir"), split_axis=0, concat_axis=0, tiled=True))
    result = (dest_rows, 2, source_count, fine_count)
    if kf_dev == lanes and planes * dir_count * 2 * half == lanes and dest_rows <= lanes:
        return pl.pallas_call(
            functools.partial(join_kernel, source_count),
            out_shape=jax.ShapeDtypeStruct(result, jnp.float32),
            in_specs=[whole] * 3,
            out_specs=whole,
            scratch_shapes=[pltpu.VMEM((dir_count, dest_rows * 2 * source_count, lanes), jnp.float32)],
            compiler_params=pltpu.CompilerParams(vmem_limit_bytes=24 * 2**20),
            name="join_parts",
        )(*parts, 1.0 - rims[:1])
    parts = jnp.stack([one.reshape((planes, dir_count) + message) for one in parts], axis=2)
    main = parts[:, :, :, :dest_rows].reshape(planes, 2 * dir_count, dest_rows, 2, lanes // 2)[..., :kf_half]
    over = parts[:, :, :, dest_rows:, :dest_rows].reshape(planes, 2 * dir_count, 2, 2 * rim, dest_rows)
    low = jnp.roll(over[:, :, :, :rim], -1, axis=1)
    high = jnp.roll(over[:, :, :, rim:], 1, axis=1)
    middle = jnp.zeros((planes, 2 * dir_count, 2, kf_half - 2 * rim, dest_rows), jnp.float32)
    fix = jnp.concatenate([high, middle, low], axis=3)
    total = main.transpose(2, 3, 0, 1, 4) + fix.transpose(4, 2, 0, 1, 3)
    return total.reshape(result)


def solution(mesh):
    boxes, dirs = mesh.shape["box"], mesh.shape["dir"]
    fine_mesh = Mesh(mesh.devices.reshape(planes, boxes // planes, dirs), ("zed", "ring", "dir"))
    box = ("zed", "ring")
    placed = (
        P(box, None, None, "dir"),
        P(None, None, "dir"),
        P(box, None),
        P(box, None),
        P(box),
        P(box),
        P(box),
        P(),
        P(),
        P(),
    )
    return jax.shard_map(
        per_device,
        mesh=fine_mesh,
        in_specs=placed,
        out_specs=P(("zed", "ring", "dir"), None, None, None),
        check_vma=False,
    )
```

```python
import collections
import functools

import jax
import jax.numpy as jnp
from jax import lax
from jax.experimental import pallas as pl
from jax.experimental.pallas import tpu as pltpu
from jax.sharding import Mesh
from jax.sharding import PartitionSpec as P

wave_scale = 3.0
planes = 4
lanes = 128
half = 4
rim = 2
word_bits = 13
grain = 32


plan_fields = ["rows", "slots", "fine_rows", "stride", "width", "parent", "order", "turns"]
Plan = collections.namedtuple("Plan", plan_fields + ["together", "fixed", "group"])


def up(size, step):
    return -(-size // step) * step


def edge_bits(rows):
    bits = rows.bit_length() - 1
    return bits, [place for place in range(2, bits) if place % 2 == bits % 2]


def edge_rank(local, rows):
    bits, fixed = edge_bits(rows)
    rank = jnp.zeros_like(local)
    taken = 0
    for place in range(bits):
        if place not in fixed:
            rank = rank + (local // 2**place % 2) * 2**taken
            taken += 1
    return rank


def split(value):
    high = value.astype(jnp.bfloat16)
    low = (value - high.astype(jnp.float32)).astype(jnp.bfloat16)
    return high, low


def pack_kernel(source_count, note_count, here, field, *refs):
    notes, outs, whole = refs[:note_count], refs[note_count:-1], refs[-1]
    rows = field.shape[0]
    stride = 2 * source_count
    if len(outs) > planes:
        bits, fixed = edge_bits(rows)
        free = [place for place in range(bits) if place not in fixed]
        side = (1 - here[1]) * sum(2**place for place in fixed)
        for index in range(outs[planes].shape[0]):
            base = sum((index // 2**order % 2) * 2**place for order, place in enumerate(free))
            outs[planes][index] = field[base + side]

    def row_step(row, unused):
        both = jnp.concatenate([field[row, 0], field[row, 1]], axis=0)
        for block in range(half):
            whole[block, pl.ds(pl.multiple_of(row * stride, stride), stride), :] = both[
                :, block * lanes : (block + 1) * lanes
            ]
        return unused

    lax.fori_loop(0, rows, row_step, 0, unroll=8)
    for step, out in enumerate(outs[:planes]):
        source = here[0] ^ step
        for part in range(2):
            for block in range(half):
                out[pl.ds(part * half + block, rows, stride=2 * half), :] = whole[
                    block, pl.ds(part * source_count + source, rows, stride=stride), :
                ]
        for note in notes:
            out[rows * 2 * half :, :] = note[...]


def pack(here, field, notes, edge_rows):
    rows, _, source_count, width = field.shape
    length = rows * 2 * half + sum(note.shape[0] for note in notes)
    whole = pl.BlockSpec(memory_space=pltpu.VMEM)
    edges = [jax.ShapeDtypeStruct((edge_rows,) + field.shape[1:], jnp.float32)] if edge_rows else []
    return pl.pallas_call(
        functools.partial(pack_kernel, source_count, len(notes)),
        out_shape=[jax.ShapeDtypeStruct((length, lanes), jnp.float32)] * planes + edges,
        in_specs=[pl.BlockSpec(memory_space=pltpu.SMEM)] + [whole] * (1 + len(notes)),
        out_specs=[whole] * (planes + len(edges)),
        scratch_shapes=[pltpu.VMEM((half, rows * 2 * source_count, lanes), jnp.float32)],
        name="pack_sources",
    )(here, field, *notes)


def parts_of(word):
    return lax.shift_right_logical(word, word_bits), word & (2**word_bits - 1)


def tile(start):
    return pl.ds(pl.multiple_of(start, 2 * half), 2 * half)


def fine_kernel(plan, size, edge_size, zed, lists, *refs):
    mains, refs = refs[:planes], refs[planes:]
    edges = refs[: planes if edge_size else 0]
    refs = refs[len(edges) :]
    table, phases, weights, out, rims, meta, field, moved, shifted, left, ready, landed, sems = refs
    rows, fine_rows = plan.rows, plan.fine_rows
    own = zed[0]

    def bring(step):
        return pltpu.make_async_copy(lists.at[step], meta.at[step % 2], sems.at[planes + step % 2])

    bring(0).start()
    incoming = []
    for step, edge in enumerate(edges):
        chosen = edge.at[pl.ds(0, edge_size * 2 * half)]
        incoming.append(pltpu.make_async_copy(chosen, landed.at[step], sems.at[planes + 2 + step]))
        incoming[-1].start()
    lane = lax.broadcasted_iota(jnp.int32, rims.shape, 1)
    rims[...] = ((lane < rim) | (lane >= lanes - rim)).astype(jnp.float32)

    def both(start):
        return pl.ds(pl.multiple_of(start, 4 * half), 4 * half)

    def with_turned(value):
        return jnp.concatenate([value, pltpu.roll(value, half, 0)], axis=0)

    for step, main in enumerate(mains):
        first = (own ^ step) * size

        def main_step(row, unused, first=first, main=main):
            field[both((first + row) * 4 * half), :] = with_turned(main[tile(row * 2 * half), :])
            return unused

        lax.fori_loop(0, size, main_step, 0, unroll=8)
    for step, edge in enumerate(edges):
        first = planes * size + (own ^ step) * edge_size
        incoming[step].wait()

        def edge_step(row, unused, first=first, step=step):
            field[both((first + row) * 4 * half), :] = with_turned(landed[step, tile(row * 2 * half), :])
            return unused

        lax.fori_loop(0, edge_size, edge_step, 0, unroll=8)
    field[both(planes * (size + edge_size) * 4 * half), :] = jnp.zeros((4 * half, lanes), jnp.float32)

    blank = jnp.zeros((2 * half, lanes), jnp.float32)
    sub = lax.broadcasted_iota(jnp.int32, (2 * half, lanes), 0)
    dest_count = out.shape[1]
    dest_rows = fine_rows // dest_count

    def plane_step(turn, unused):
        plane = own ^ turn
        slot = turn % 2
        bring(turn).wait()

        @pl.when(turn + 1 < planes)
        def _():
            bring(turn + 1).start()

        across = lanes // plan.width

        def boxes_step(slot_count, step, unused):
            ranks = [step * plan.together + each for each in range(plan.together)]
            boxes = [meta[slot, plan.order, rank] for rank in ranks]
            sums = [[blank, blank] for box in boxes]
            for pair in range(slot_count):
                for each in range(plan.together):
                    row = step * (plan.together // across) + each // across
                    place, kind = parts_of(meta[slot, row, each % across * plan.width + pair])
                    value = field[both(place), :]
                    factor = table[tile(kind), :]
                    sums[each][0] += factor * value[: 2 * half]
                    sums[each][1] += factor * value[2 * half :]
            for each in range(plan.together):
                straight, crossed = sums[each]
                total = jnp.where(
                    sub < half,
                    straight + pltpu.roll(straight, half, 0),
                    pltpu.roll(crossed, half, 0) - crossed,
                )
                moved[both(boxes[each] * 4 * half), :] = with_turned(total)
            return unused

        start = 0
        for more in reversed(range((plan.slots - plan.fixed) // plan.group + 1)):
            end = meta[slot, plan.order, plan.turns + more]
            lax.fori_loop(start, end, functools.partial(boxes_step, plan.fixed + more * plan.group), 0)
            start = end

        def fine_step(block, unused):
            for each in range(lanes):
                parent, octant = parts_of(meta[slot, plan.parent + block, each])
                value = moved[both(parent), :] * phases[both(octant), :]
                shifted[tile((block * lanes + each) * 2 * half), :] = value[: 2 * half] + value[2 * half :]
            return unused

        lax.fori_loop(0, fine_rows // lanes, fine_step, 0)
        width = ready.shape[3]
        depth = half * lanes

        def split_step(chunk, unused):
            for part in range(2):
                rows_of = pl.ds(pl.multiple_of(part * fine_rows + chunk * grain, grain), grain)
                for block in range(half):
                    begin = chunk * grain * 2 * half + part * half + block
                    value = shifted[pl.ds(begin, grain, stride=2 * half), :]
                    high, low = split(value)
                    left[rows_of, block * lanes : (block + 1) * lanes] = high
                    left[rows_of, depth + block * lanes : depth + (block + 1) * lanes] = low
            return unused

        lax.fori_loop(0, fine_rows // grain, split_step, 0, unroll=2)
        result = jnp.dot(
            jnp.concatenate([left[:, :depth], left[...]], axis=1), weights[...], preferred_element_type=jnp.float32
        )
        for part in range(2):
            for dest in range(dest_count):
                start = part * fine_rows + dest * dest_rows
                ready[plane, dest, part * dest_rows : (part + 1) * dest_rows, :] = result[
                    start : start + dest_rows, :width
                ]
        spill = result[:fine_rows, width:] + pltpu.roll(result[fine_rows:, width:], half, 1)
        spill = spill.T[: 2 * half]
        for dest in range(dest_count):
            ready[plane, dest, 2 * dest_rows :, :] = jnp.concatenate(
                [
                    spill[:, dest * dest_rows : (dest + 1) * dest_rows],
                    jnp.zeros((2 * half, width - dest_rows), jnp.float32),
                ],
                axis=1,
            )
        pltpu.make_async_copy(ready.at[plane], out.at[plane], sems.at[plane]).start()
        return unused

    lax.fori_loop(0, planes, plane_step, 0)
    for plane in range(planes):
        pltpu.make_async_copy(ready.at[plane], out.at[plane], sems.at[plane]).wait()


def join_kernel(source_count, parts, rims, out, whole):
    dest_rows = out.shape[0]
    dirs = parts.shape[0] // source_count
    over = jnp.concatenate(
        [parts[index, 2 * dest_rows :, :lanes] for index in range(parts.shape[0])], axis=0
    ).T[:dest_rows]
    low = lax.broadcasted_iota(jnp.int32, (dest_rows, lanes), 1) < rim
    at_rim = jnp.broadcast_to(rims[...], (dest_rows, lanes)) < 0.5
    for source in range(source_count):
        for part in range(2):
            turned = []
            for index in range(dirs):
                first = (source * dirs + index) * 2 * half + part * half
                turned.append(pltpu.roll(over, (lanes - rim - first) % lanes, 1))
            for index in range(dirs):
                fix = jnp.where(at_rim, jnp.where(low, turned[index - 1], turned[(index + 1) % dirs]), 0.0)
                whole[
                    index, pl.ds(part * source_count + source, dest_rows, stride=2 * source_count), :
                ] = parts[source * dirs + index, part * dest_rows : (part + 1) * dest_rows, :] + fix

    def row_step(row, unused):
        start = pl.multiple_of(row * 2 * source_count, 2 * source_count)
        both = jnp.concatenate(
            [whole[index, pl.ds(start, 2 * source_count), :] for index in range(dirs)], axis=1
        )
        out[row, 0] = both[:source_count]
        out[row, 1] = both[source_count:]
        return unused

    lax.fori_loop(0, dest_rows, row_step, 0, unroll=8)


def per_device(
    coarse_field,
    trans_table,
    partner_ids,
    partner_types,
    partner_count,
    child_count,
    child_octant,
    dir_angles,
    stencil_ids,
    stencil_weights,
):
    rows, _, source_count, kc_dev = coarse_field.shape
    slots = partner_ids.shape[1]
    type_count = trans_table.shape[0]
    fine_rows = child_octant.shape[0]
    ring_count = lax.axis_size("ring")
    dir_count = lax.axis_size("dir")
    zed = lax.axis_index("zed")
    ring = lax.axis_index("ring")
    dir_index = lax.axis_index("dir")
    fine_count = stencil_ids.shape[0] // 4
    kf_dev = fine_count // dir_count
    kc_pad = up(kc_dev, half * lanes)
    kf_pad = up(kf_dev, lanes)
    pad_dirs = kc_pad - kc_dev
    assert source_count == planes and kc_pad == half * lanes
    dest_rows = fine_rows // dir_count

    field = jnp.pad(coarse_field, ((0, 0), (0, 0), (0, 0), (0, pad_dirs)))
    here = jnp.stack([zed, ring])
    edge_rows = rows >> len(edge_bits(rows)[1]) if ring_count == 2 else 0
    packed = pack(here, field, [], edge_rows)
    after_pack = lax.optimization_barrier(
        (packed, partner_ids, partner_types, partner_count, child_count, child_octant)
    )
    packed, partner_ids, partner_types, partner_count, child_count, child_octant = after_pack
    if edge_rows:
        edges = lax.ppermute(packed[planes], "ring", [(0, 1), (1, 0)])

    def to_planes(note, step):
        if step == 0:
            return note
        return lax.ppermute(note, "zed", [(plane, plane ^ step) for plane in range(planes)])

    arrived = [to_planes(packed[step], step) for step in (3, 2, 1, 0)][::-1]

    plane_of = partner_ids // (ring_count * rows)
    ring_of = partner_ids // rows % ring_count
    local = partner_ids % rows
    live = jnp.arange(slots, dtype=jnp.int32)[None, :] < partner_count[:, None]
    if ring_count == 2:
        size = rows
        place = jnp.where(
            ring_of == ring,
            plane_of * rows + local,
            planes * rows + plane_of * edge_rows + edge_rank(local, rows),
        )
    else:
        size = ring_count * rows
        place = partner_ids
    field_rows = planes * (size + edge_rows)
    place = jnp.where(live, place, field_rows)
    together = 4
    fixed = slots // 2
    group = 3 if (slots - fixed) % 3 == 0 else 1
    index = jnp.arange(rows, dtype=jnp.int32)
    before = (partner_count[None, :] > partner_count[:, None]) | (
        (partner_count[None, :] == partner_count[:, None]) & (index[None, :] < index[:, None])
    )
    rank = jnp.sum(before.astype(jnp.int32), axis=1)
    at_rank = rank[None, :] == index[:, None]
    order = jnp.sum(jnp.where(at_rank, index[None, :], 0), axis=1)
    first = rank[None, :] == index[: rows // together, None] * together
    longest = jnp.sum(jnp.where(first, partner_count[None, :], 0), axis=1)
    turns = jnp.maximum((longest - fixed + group - 1) // group, 0)
    more = jnp.arange((slots - fixed) // group + 1, dtype=jnp.int32)
    ends = jnp.sum((turns[None, :] >= more[:, None]).astype(jnp.int32), axis=1)
    bounds = jnp.sum(jnp.where(index[None, :] <= index[:, None], child_count[None, :], 0), axis=1)
    parent = jnp.sum(
        (bounds[None, :] <= jnp.arange(fine_rows, dtype=jnp.int32)[:, None]).astype(jnp.int32), axis=1
    )
    def across(one, width=lanes):
        return jnp.pad(one, ((0, 0), (0, width - one.shape[1])))

    width = lanes // half
    turns_at = lanes // 2
    assert slots <= width and rows <= turns_at and fine_rows % lanes == 0
    assert (field_rows + 1) * 4 * half < 2 ** (31 - word_bits) and type_count * 2 * half < 2**word_bits

    def in_order(one):
        one = jnp.sum(jnp.where(at_rank[:, :, None], across(one, width)[None], 0), axis=1)
        return one.reshape(rows * width // lanes, lanes)

    list_rows = rows * width // lanes
    fine_lists = fine_rows // lanes
    last = across(jnp.concatenate([across(order[None], turns_at), ends[None]], axis=1))
    stride = up(list_rows + fine_lists + 1, 8)

    def stacked(*parts):
        meta = jnp.concatenate(parts)
        return jnp.pad(meta, ((0, stride - meta.shape[0]), (0, 0))).astype(jnp.float32)

    meta = jnp.concatenate(
        [
            stacked(in_order(place * 4 * half), (parent * 4 * half).reshape(-1, lanes)),
            stacked(in_order(partner_types * 2 * half), (child_octant * 4 * half).reshape(-1, lanes), last),
        ]
    )
    plan = Plan(
        rows, slots, fine_rows, stride, width, list_rows, list_rows + fine_lists, turns_at, together, fixed, group
    )

    notes = pack(here, edges, [meta], 0) if edge_rows else [meta] * planes
    after_notes = lax.optimization_barrier((notes, trans_table, dir_angles, stencil_ids, stencil_weights))
    notes, trans_table, dir_angles, stencil_ids, stencil_weights = after_notes
    received = [to_planes(notes[step], step) for step in (3, 2, 1, 0)][::-1]
    edge_part = edge_rows * 2 * half
    numbers = jnp.stack([note[edge_part:] for note in received]).astype(jnp.int32)
    meta = numbers[:, :stride] * 2**word_bits + numbers[:, stride:]
    if ring_count != 2:
        arrived = [lax.all_gather(one, "ring", axis=0, tiled=True) for one in arrived]
        received = []

    def blocks(table):
        return jnp.pad(table, ((0, 0), (0, pad_dirs))).reshape(-1, half, lanes)

    def doubled(table, sign):
        return jnp.concatenate([blocks(table), sign * blocks(table)], axis=1)

    table = jnp.pad(trans_table, ((0, 0), (0, 0), (0, pad_dirs))).reshape(-1, lanes)
    angles = lax.dynamic_slice_in_dim(dir_angles, dir_index * kc_dev, kc_dev, axis=1)
    octants = jnp.arange(8, dtype=jnp.int32)
    sign_x = 1.0 - 2.0 * (octants % 2).astype(jnp.float32)
    sign_y = 1.0 - 2.0 * (octants // 2 % 2).astype(jnp.float32)
    sign_z = 1.0 - 2.0 * (octants // 4).astype(jnp.float32)
    unit_x = jnp.sin(angles[0]) * jnp.cos(angles[1])
    unit_y = jnp.sin(angles[0]) * jnp.sin(angles[1])
    unit_z = jnp.cos(angles[0])
    phase = wave_scale * (
        sign_x[:, None] * unit_x[None, :] + sign_y[:, None] * unit_y[None, :] + sign_z[:, None] * unit_z[None, :]
    )
    phases = jnp.concatenate(
        [doubled(jnp.cos(phase), 1.0), doubled(jnp.sin(phase), -1.0)], axis=1
    ).reshape(-1, lanes)

    ids = lax.dynamic_slice_in_dim(stencil_ids, dir_index * kc_dev, kc_dev, axis=0).T
    weights = lax.dynamic_slice_in_dim(stencil_weights, dir_index * kc_dev, kc_dev, axis=0).T

    def interp(targets):
        matrix = jnp.zeros((targets.shape[0], kc_dev), jnp.float32)
        for point in range(ids.shape[0]):
            matrix = matrix + jnp.where(
                ids[point][None, :] == targets[:, None], weights[point][None, :], 0.0
            )
        return jnp.pad(matrix, ((0, 0), (0, pad_dirs)))

    first_fine = dir_index * kf_dev
    own = jnp.arange(kf_dev, dtype=jnp.int32)
    outside = jnp.concatenate(
        [jnp.arange(-rim, 0, dtype=jnp.int32), jnp.arange(kf_dev, kf_dev + rim, dtype=jnp.int32)]
    )
    matrix = jnp.pad(interp(first_fine + own), ((0, kf_pad - kf_dev), (0, 0)))
    spill = interp((first_fine + outside) % fine_count)
    matrices = jnp.concatenate([matrix, jnp.pad(spill, ((0, lanes - half), (0, 0)))], axis=0).T
    rounded = lax.reduce_precision(matrices, 8, 7)
    high = rounded.astype(jnp.bfloat16)
    low = (matrices - rounded).astype(jnp.bfloat16)
    passes = jnp.concatenate([low, high, high], axis=0)

    whole = pl.BlockSpec(memory_space=pltpu.VMEM)
    message = (2 * dest_rows + 2 * half, kf_pad)
    local_fine, rims = pl.pallas_call(
        functools.partial(fine_kernel, plan, size, edge_rows),
        out_shape=[
            pltpu.HBM((planes, dir_count) + message, jnp.float32),
            jax.ShapeDtypeStruct((2 * half, lanes), jnp.float32),
        ],
        in_specs=[pl.BlockSpec(memory_space=pltpu.SMEM), pl.BlockSpec(memory_space=pl.ANY)]
        + [whole] * planes
        + [pl.BlockSpec(memory_space=pl.ANY)] * len(received)
        + [whole] * 3,
        out_specs=[pl.BlockSpec(memory_space=pltpu.HBM), whole],
        scratch_shapes=[
            pltpu.SMEM((2, plan.stride, lanes), jnp.int32),
            pltpu.VMEM(((field_rows + 1) * 4 * half, lanes), jnp.float32),
            pltpu.VMEM((rows * 4 * half, lanes), jnp.float32),
            pltpu.VMEM((fine_rows * 2 * half, lanes), jnp.float32),
            pltpu.VMEM((2 * fine_rows, 2 * kc_pad), jnp.bfloat16),
            pltpu.VMEM((planes, dir_count) + message, jnp.float32),
            pltpu.VMEM((planes, max(edge_rows, 1) * 2 * half, lanes), jnp.float32),
            pltpu.SemaphoreType.DMA((2 * planes + 2,)),
        ],
        compiler_params=pltpu.CompilerParams(vmem_limit_bytes=48 * 2**20),
        name="translate_and_interpolate",
    )(here, meta, *arrived, *received, table, phases, passes)

    parts = lax.all_to_all(
        local_fine.reshape((planes * dir_count,) + message),
        ("zed", "dir"),
        split_axis=0,
        concat_axis=0,
        tiled=True,
    )
    result = (dest_rows, 2, source_count, fine_count)
    if kf_dev == lanes and planes * dir_count * 2 * half == lanes and dest_rows <= lanes:
        return pl.pallas_call(
            functools.partial(join_kernel, source_count),
            out_shape=jax.ShapeDtypeStruct(result, jnp.float32),
            in_specs=[whole] * 2,
            out_specs=whole,
            scratch_shapes=[pltpu.VMEM((dir_count, dest_rows * 2 * source_count, lanes), jnp.float32)],
            compiler_params=pltpu.CompilerParams(vmem_limit_bytes=24 * 2**20),
            name="join_parts",
        )(parts, 1.0 - rims[:1])
    parts = parts.reshape((planes, dir_count) + message)
    main = parts[:, :, : 2 * dest_rows, :kf_dev].reshape(planes, dir_count, 2, dest_rows, kf_dev)
    over = parts[:, :, 2 * dest_rows :, :dest_rows].reshape(planes, dir_count, 2, 2 * rim, dest_rows)
    low = jnp.roll(over[:, :, :, :rim], -1, axis=1)
    high = jnp.roll(over[:, :, :, rim:], 1, axis=1)
    middle = jnp.zeros((planes, dir_count, 2, kf_dev - 2 * rim, dest_rows), jnp.float32)
    fix = jnp.concatenate([high, middle, low], axis=3)
    total = main.transpose(3, 2, 0, 1, 4) + fix.transpose(4, 2, 0, 1, 3)
    return total.reshape(result)


def solution(mesh):
    boxes, dirs = mesh.shape["box"], mesh.shape["dir"]
    fine_mesh = Mesh(mesh.devices.reshape(planes, boxes // planes, dirs), ("zed", "ring", "dir"))
    box = ("zed", "ring")
    placed = (
        P(box, None, None, "dir"),
        P(None, None, "dir"),
        P(box, None),
        P(box, None),
        P(box),
        P(box),
        P(box),
        P(),
        P(),
        P(),
    )
    return jax.shard_map(
        per_device,
        mesh=fine_mesh,
        in_specs=placed,
        out_specs=P(("zed", "ring", "dir"), None, None, None),
        check_vma=False,
    )
```

```python
import collections
import functools

import jax
import jax.numpy as jnp
from jax import lax
from jax.experimental import pallas as pl
from jax.experimental.pallas import tpu as pltpu
from jax.sharding import Mesh
from jax.sharding import PartitionSpec as P

wave_scale = 3.0
planes = 4
lanes = 128
half = 4
rim = 2
word_bits = 13
grain = 32


plan_fields = ["rows", "slots", "fine_rows", "stride", "width", "parent", "order", "turns"]
Plan = collections.namedtuple("Plan", plan_fields + ["together", "fixed", "group"])


def up(size, step):
    return -(-size // step) * step


def edge_bits(rows):
    bits = rows.bit_length() - 1
    return bits, [place for place in range(2, bits) if place % 2 == bits % 2]


def edge_rank(local, rows):
    bits, fixed = edge_bits(rows)
    rank = jnp.zeros_like(local)
    taken = 0
    for place in range(bits):
        if place not in fixed:
            rank = rank + (local // 2**place % 2) * 2**taken
            taken += 1
    return rank


def split(value):
    high = value.astype(jnp.bfloat16)
    low = (value - high.astype(jnp.float32)).astype(jnp.bfloat16)
    return high, low


def pack_kernel(source_count, note_count, zed, ring, field, *refs):
    notes, outs, whole = refs[:note_count], refs[note_count:-1], refs[-1]
    rows = field.shape[0]
    stride = 2 * source_count
    if len(outs) > planes:
        bits, fixed = edge_bits(rows)
        free = [place for place in range(bits) if place not in fixed]
        side = (1 - ring[0]) * sum(2**place for place in fixed)
        for index in range(outs[planes].shape[0]):
            base = sum((index // 2**order % 2) * 2**place for order, place in enumerate(free))
            outs[planes][index] = field[base + side]

    def row_step(row, unused):
        both = jnp.concatenate([field[row, 0], field[row, 1]], axis=0)
        for block in range(half):
            whole[block, pl.ds(pl.multiple_of(row * stride, stride), stride), :] = both[
                :, block * lanes : (block + 1) * lanes
            ]
        return unused

    lax.fori_loop(0, rows, row_step, 0, unroll=8)
    for step, out in enumerate(outs[:planes]):
        source = zed[0] ^ step
        for part in range(2):
            for block in range(half):
                out[pl.ds(part * half + block, rows, stride=2 * half), :] = whole[
                    block, pl.ds(part * source_count + source, rows, stride=stride), :
                ]
        for note in notes:
            out[rows * 2 * half :, :] = note[...]


def pack(here, field, notes, edge_rows):
    rows, _, source_count, width = field.shape
    length = rows * 2 * half + sum(note.shape[0] for note in notes)
    whole = pl.BlockSpec(memory_space=pltpu.VMEM)
    edges = [jax.ShapeDtypeStruct((edge_rows,) + field.shape[1:], jnp.float32)] if edge_rows else []
    return pl.pallas_call(
        functools.partial(pack_kernel, source_count, len(notes)),
        out_shape=[jax.ShapeDtypeStruct((length, lanes), jnp.float32)] * planes + edges,
        in_specs=[pl.BlockSpec(memory_space=pltpu.SMEM)] * 2 + [whole] * (1 + len(notes)),
        out_specs=[whole] * (planes + len(edges)),
        scratch_shapes=[pltpu.VMEM((half, rows * 2 * source_count, lanes), jnp.float32)],
        name="pack_sources",
    )(*here, field, *notes)


def parts_of(word):
    return lax.shift_right_logical(word, word_bits), word & (2**word_bits - 1)


def tile(start):
    return pl.ds(pl.multiple_of(start, 2 * half), 2 * half)


def fine_kernel(plan, size, edge_size, zed, lists, *refs):
    mains, refs = refs[:planes], refs[planes:]
    edges = refs[: planes if edge_size else 0]
    refs = refs[len(edges) :]
    table, phases, weights, out, rims, meta, field, moved, shifted, left, ready, landed, sems = refs
    rows, fine_rows = plan.rows, plan.fine_rows
    own = zed[0]

    def bring(step):
        return pltpu.make_async_copy(lists.at[step], meta.at[step % 2], sems.at[planes + step % 2])

    bring(0).start()
    incoming = []
    for step, edge in enumerate(edges):
        chosen = edge.at[pl.ds(0, edge_size * 2 * half)]
        incoming.append(pltpu.make_async_copy(chosen, landed.at[step], sems.at[planes + 2 + step]))
        incoming[-1].start()
    lane = lax.broadcasted_iota(jnp.int32, rims.shape, 1)
    rims[...] = ((lane < rim) | (lane >= lanes - rim)).astype(jnp.float32)

    def both(start):
        return pl.ds(pl.multiple_of(start, 4 * half), 4 * half)

    def with_turned(value):
        return jnp.concatenate([value, pltpu.roll(value, half, 0)], axis=0)

    for step, main in enumerate(mains):
        first = (own ^ step) * size

        def main_step(row, unused, first=first, main=main):
            field[both((first + row) * 4 * half), :] = with_turned(main[tile(row * 2 * half), :])
            return unused

        lax.fori_loop(0, size, main_step, 0, unroll=8)
    for step, edge in enumerate(edges):
        first = planes * size + (own ^ step) * edge_size
        incoming[step].wait()

        def edge_step(row, unused, first=first, step=step):
            field[both((first + row) * 4 * half), :] = with_turned(landed[step, tile(row * 2 * half), :])
            return unused

        lax.fori_loop(0, edge_size, edge_step, 0, unroll=8)
    field[both(planes * (size + edge_size) * 4 * half), :] = jnp.zeros((4 * half, lanes), jnp.float32)

    blank = jnp.zeros((2 * half, lanes), jnp.float32)
    sub = lax.broadcasted_iota(jnp.int32, (2 * half, lanes), 0)
    dest_count = out.shape[1]
    dest_rows = fine_rows // dest_count

    def plane_step(turn, unused):
        plane = own ^ turn
        slot = turn % 2
        bring(turn).wait()

        @pl.when(turn + 1 < planes)
        def _():
            bring(turn + 1).start()

        across = lanes // plan.width

        def boxes_step(slot_count, step, unused):
            ranks = [step * plan.together + each for each in range(plan.together)]
            boxes = [meta[slot, plan.order, rank] for rank in ranks]
            sums = [[blank, blank] for box in boxes]
            for pair in range(slot_count):
                for each in range(plan.together):
                    row = step * (plan.together // across) + each // across
                    place, kind = parts_of(meta[slot, row, each % across * plan.width + pair])
                    value = field[both(place), :]
                    factor = table[tile(kind), :]
                    sums[each][0] += factor * value[: 2 * half]
                    sums[each][1] += factor * value[2 * half :]
            for each in range(plan.together):
                straight, crossed = sums[each]
                total = jnp.where(
                    sub < half,
                    straight + pltpu.roll(straight, half, 0),
                    pltpu.roll(crossed, half, 0) - crossed,
                )
                moved[both(boxes[each] * 4 * half), :] = with_turned(total)
            return unused

        start = 0
        for more in reversed(range((plan.slots - plan.fixed) // plan.group + 1)):
            end = meta[slot, plan.order, plan.turns + more]
            lax.fori_loop(start, end, functools.partial(boxes_step, plan.fixed + more * plan.group), 0)
            start = end

        def fine_step(block, unused):
            for each in range(lanes):
                parent, octant = parts_of(meta[slot, plan.parent + block, each])
                value = moved[both(parent), :] * phases[both(octant), :]
                shifted[tile((block * lanes + each) * 2 * half), :] = value[: 2 * half] + value[2 * half :]
            return unused

        lax.fori_loop(0, fine_rows // lanes, fine_step, 0)
        width = ready.shape[3]
        depth = half * lanes

        def split_step(chunk, unused):
            for part in range(2):
                rows_of = pl.ds(pl.multiple_of(part * fine_rows + chunk * grain, grain), grain)
                for block in range(half):
                    begin = chunk * grain * 2 * half + part * half + block
                    value = shifted[pl.ds(begin, grain, stride=2 * half), :]
                    high, low = split(value)
                    left[rows_of, block * lanes : (block + 1) * lanes] = high
                    left[rows_of, depth + block * lanes : depth + (block + 1) * lanes] = low
            return unused

        lax.fori_loop(0, fine_rows // grain, split_step, 0, unroll=2)
        result = jnp.dot(
            jnp.concatenate([left[:, :depth], left[...]], axis=1), weights[...], preferred_element_type=jnp.float32
        )
        for part in range(2):
            for dest in range(dest_count):
                start = part * fine_rows + dest * dest_rows
                ready[plane, dest, part * dest_rows : (part + 1) * dest_rows, :] = result[
                    start : start + dest_rows, :width
                ]
        spill = result[:fine_rows, width:] + pltpu.roll(result[fine_rows:, width:], half, 1)
        spill = spill.T[: 2 * half]
        for dest in range(dest_count):
            ready[plane, dest, 2 * dest_rows :, :] = jnp.concatenate(
                [
                    spill[:, dest * dest_rows : (dest + 1) * dest_rows],
                    jnp.zeros((2 * half, width - dest_rows), jnp.float32),
                ],
                axis=1,
            )
        pltpu.make_async_copy(ready.at[plane], out.at[plane], sems.at[plane]).start()
        return unused

    lax.fori_loop(0, planes, plane_step, 0)
    for plane in range(planes):
        pltpu.make_async_copy(ready.at[plane], out.at[plane], sems.at[plane]).wait()


def join_kernel(source_count, parts, rims, out, whole):
    dest_rows = out.shape[0]
    dirs = parts.shape[0] // source_count
    over = jnp.concatenate(
        [parts[index, 2 * dest_rows :, :lanes] for index in range(parts.shape[0])], axis=0
    ).T[:dest_rows]
    low = lax.broadcasted_iota(jnp.int32, (dest_rows, lanes), 1) < rim
    at_rim = jnp.broadcast_to(rims[...], (dest_rows, lanes)) < 0.5
    for source in range(source_count):
        for part in range(2):
            turned = []
            for index in range(dirs):
                first = (source * dirs + index) * 2 * half + part * half
                turned.append(pltpu.roll(over, (lanes - rim - first) % lanes, 1))
            for index in range(dirs):
                fix = jnp.where(at_rim, jnp.where(low, turned[index - 1], turned[(index + 1) % dirs]), 0.0)
                whole[
                    index, pl.ds(part * source_count + source, dest_rows, stride=2 * source_count), :
                ] = parts[source * dirs + index, part * dest_rows : (part + 1) * dest_rows, :] + fix

    def row_step(row, unused):
        start = pl.multiple_of(row * 2 * source_count, 2 * source_count)
        both = jnp.concatenate(
            [whole[index, pl.ds(start, 2 * source_count), :] for index in range(dirs)], axis=1
        )
        out[row, 0] = both[:source_count]
        out[row, 1] = both[source_count:]
        return unused

    lax.fori_loop(0, dest_rows, row_step, 0, unroll=8)


def per_device(
    coarse_field,
    trans_table,
    partner_ids,
    partner_types,
    partner_count,
    child_count,
    child_octant,
    dir_angles,
    stencil_ids,
    stencil_weights,
):
    rows, _, source_count, kc_dev = coarse_field.shape
    slots = partner_ids.shape[1]
    type_count = trans_table.shape[0]
    fine_rows = child_octant.shape[0]
    ring_count = lax.axis_size("ring")
    dir_count = lax.axis_size("dir")
    zed = lax.axis_index("zed")
    ring = lax.axis_index("ring")
    dir_index = lax.axis_index("dir")
    fine_count = stencil_ids.shape[0] // 4
    kf_dev = fine_count // dir_count
    kc_pad = up(kc_dev, half * lanes)
    kf_pad = up(kf_dev, lanes)
    pad_dirs = kc_pad - kc_dev
    assert source_count == planes and kc_pad == half * lanes
    dest_rows = fine_rows // dir_count

    field = jnp.pad(coarse_field, ((0, 0), (0, 0), (0, 0), (0, pad_dirs)))
    here = zed.reshape(1), ring.reshape(1)
    edge_rows = rows >> len(edge_bits(rows)[1]) if ring_count == 2 else 0
    packed = pack(here, field, [], edge_rows)
    if edge_rows:
        edges = lax.ppermute(packed[planes], "ring", [(0, 1), (1, 0)])

    def to_planes(note, step):
        if step == 0:
            return note
        return lax.ppermute(note, "zed", [(plane, plane ^ step) for plane in range(planes)])

    arrived = [to_planes(packed[step], step) for step in (3, 2, 1, 0)][::-1]

    plane_of = partner_ids // (ring_count * rows)
    ring_of = partner_ids // rows % ring_count
    local = partner_ids % rows
    live = jnp.arange(slots, dtype=jnp.int32)[None, :] < partner_count[:, None]
    if ring_count == 2:
        size = rows
        place = jnp.where(
            ring_of == ring,
            plane_of * rows + local,
            planes * rows + plane_of * edge_rows + edge_rank(local, rows),
        )
    else:
        size = ring_count * rows
        place = partner_ids
    field_rows = planes * (size + edge_rows)
    place = jnp.where(live, place, field_rows)
    together = 4
    fixed = slots // 2
    group = 5 if (slots - fixed) % 5 == 0 else 1
    index = jnp.arange(rows, dtype=jnp.int32)
    before = (partner_count[None, :] > partner_count[:, None]) | (
        (partner_count[None, :] == partner_count[:, None]) & (index[None, :] < index[:, None])
    )
    rank = jnp.sum(before.astype(jnp.int32), axis=1)
    at_rank = rank[None, :] == index[:, None]
    order = jnp.sum(jnp.where(at_rank, index[None, :], 0), axis=1)
    first = rank[None, :] == index[: rows // together, None] * together
    longest = jnp.sum(jnp.where(first, partner_count[None, :], 0), axis=1)
    turns = jnp.maximum((longest - fixed + group - 1) // group, 0)
    more = jnp.arange((slots - fixed) // group + 1, dtype=jnp.int32)
    ends = jnp.sum((turns[None, :] >= more[:, None]).astype(jnp.int32), axis=1)
    bounds = jnp.sum(jnp.where(index[None, :] <= index[:, None], child_count[None, :], 0), axis=1)
    parent = jnp.sum(
        (bounds[None, :] <= jnp.arange(fine_rows, dtype=jnp.int32)[:, None]).astype(jnp.int32), axis=1
    )
    def across(one, width=lanes):
        return jnp.pad(one, ((0, 0), (0, width - one.shape[1])))

    width = lanes // half
    turns_at = lanes // 2
    assert slots <= width and rows <= turns_at and fine_rows % lanes == 0
    assert (field_rows + 1) * 4 * half < 2 ** (31 - word_bits) and type_count * 2 * half < 2**word_bits

    def in_order(one):
        one = jnp.sum(jnp.where(at_rank[:, :, None], across(one, width)[None], 0), axis=1)
        return one.reshape(rows * width // lanes, lanes)

    list_rows = rows * width // lanes
    fine_lists = fine_rows // lanes
    last = across(jnp.concatenate([across(order[None], turns_at), ends[None]], axis=1))
    stride = up(list_rows + fine_lists + 1, 8)

    def stacked(*parts):
        meta = jnp.concatenate(parts)
        return jnp.pad(meta, ((0, stride - meta.shape[0]), (0, 0))).astype(jnp.float32)

    meta = jnp.concatenate(
        [
            stacked(in_order(place * 4 * half), (parent * 4 * half).reshape(-1, lanes)),
            stacked(in_order(partner_types * 2 * half), (child_octant * 4 * half).reshape(-1, lanes), last),
        ]
    )
    plan = Plan(
        rows, slots, fine_rows, stride, width, list_rows, list_rows + fine_lists, turns_at, together, fixed, group
    )

    notes = pack(here, edges, [meta], 0) if edge_rows else [meta] * planes
    after_notes = lax.optimization_barrier((notes, trans_table, dir_angles, stencil_ids, stencil_weights))
    notes, trans_table, dir_angles, stencil_ids, stencil_weights = after_notes
    received = [to_planes(notes[step], step) for step in (3, 2, 1, 0)][::-1]
    edge_part = edge_rows * 2 * half
    numbers = jnp.stack([note[edge_part:] for note in received]).astype(jnp.int32)
    meta = numbers[:, :stride] * 2**word_bits + numbers[:, stride:]
    if ring_count != 2:
        arrived = [lax.all_gather(one, "ring", axis=0, tiled=True) for one in arrived]
        received = []

    def blocks(table):
        return jnp.pad(table, ((0, 0), (0, pad_dirs))).reshape(-1, half, lanes)

    def doubled(table, sign):
        return jnp.concatenate([blocks(table), sign * blocks(table)], axis=1)

    table = jnp.pad(trans_table, ((0, 0), (0, 0), (0, pad_dirs))).reshape(-1, lanes)
    angles = lax.dynamic_slice_in_dim(dir_angles, dir_index * kc_dev, kc_dev, axis=1)
    octants = jnp.arange(8, dtype=jnp.int32)
    sign_x = 1.0 - 2.0 * (octants % 2).astype(jnp.float32)
    sign_y = 1.0 - 2.0 * (octants // 2 % 2).astype(jnp.float32)
    sign_z = 1.0 - 2.0 * (octants // 4).astype(jnp.float32)
    unit_x = jnp.sin(angles[0]) * jnp.cos(angles[1])
    unit_y = jnp.sin(angles[0]) * jnp.sin(angles[1])
    unit_z = jnp.cos(angles[0])
    phase = wave_scale * (
        sign_x[:, None] * unit_x[None, :] + sign_y[:, None] * unit_y[None, :] + sign_z[:, None] * unit_z[None, :]
    )
    phases = jnp.concatenate(
        [doubled(jnp.cos(phase), 1.0), doubled(jnp.sin(phase), -1.0)], axis=1
    ).reshape(-1, lanes)

    ids = lax.dynamic_slice_in_dim(stencil_ids, dir_index * kc_dev, kc_dev, axis=0).T
    weights = lax.dynamic_slice_in_dim(stencil_weights, dir_index * kc_dev, kc_dev, axis=0).T

    def interp(targets):
        matrix = jnp.zeros((targets.shape[0], kc_dev), jnp.float32)
        for point in range(ids.shape[0]):
            matrix = matrix + jnp.where(
                ids[point][None, :] == targets[:, None], weights[point][None, :], 0.0
            )
        return jnp.pad(matrix, ((0, 0), (0, pad_dirs)))

    first_fine = dir_index * kf_dev
    own = jnp.arange(kf_dev, dtype=jnp.int32)
    outside = jnp.concatenate(
        [jnp.arange(-rim, 0, dtype=jnp.int32), jnp.arange(kf_dev, kf_dev + rim, dtype=jnp.int32)]
    )
    matrix = jnp.pad(interp(first_fine + own), ((0, kf_pad - kf_dev), (0, 0)))
    spill = interp((first_fine + outside) % fine_count)
    matrices = jnp.concatenate([matrix, jnp.pad(spill, ((0, lanes - half), (0, 0)))], axis=0).T
    rounded = lax.reduce_precision(matrices, 8, 7)
    high = rounded.astype(jnp.bfloat16)
    low = (matrices - rounded).astype(jnp.bfloat16)
    passes = jnp.concatenate([low, high, high], axis=0)

    whole = pl.BlockSpec(memory_space=pltpu.VMEM)
    message = (2 * dest_rows + 2 * half, kf_pad)
    local_fine, rims = pl.pallas_call(
        functools.partial(fine_kernel, plan, size, edge_rows),
        out_shape=[
            pltpu.HBM((planes, dir_count) + message, jnp.float32),
            jax.ShapeDtypeStruct((2 * half, lanes), jnp.float32),
        ],
        in_specs=[pl.BlockSpec(memory_space=pltpu.SMEM), pl.BlockSpec(memory_space=pl.ANY)]
        + [whole] * planes
        + [pl.BlockSpec(memory_space=pl.ANY)] * len(received)
        + [whole] * 3,
        out_specs=[pl.BlockSpec(memory_space=pltpu.HBM), whole],
        scratch_shapes=[
            pltpu.SMEM((2, plan.stride, lanes), jnp.int32),
            pltpu.VMEM(((field_rows + 1) * 4 * half, lanes), jnp.float32),
            pltpu.VMEM((rows * 4 * half, lanes), jnp.float32),
            pltpu.VMEM((fine_rows * 2 * half, lanes), jnp.float32),
            pltpu.VMEM((2 * fine_rows, 2 * kc_pad), jnp.bfloat16),
            pltpu.VMEM((planes, dir_count) + message, jnp.float32),
            pltpu.VMEM((planes, max(edge_rows, 1) * 2 * half, lanes), jnp.float32),
            pltpu.SemaphoreType.DMA((2 * planes + 2,)),
        ],
        compiler_params=pltpu.CompilerParams(vmem_limit_bytes=48 * 2**20),
        name="translate_and_interpolate",
    )(here[0], meta, *arrived, *received, table, phases, passes)

    parts = lax.all_to_all(
        local_fine.reshape((planes * dir_count,) + message),
        ("zed", "dir"),
        split_axis=0,
        concat_axis=0,
        tiled=True,
    )
    result = (dest_rows, 2, source_count, fine_count)
    if kf_dev == lanes and planes * dir_count * 2 * half == lanes and dest_rows <= lanes:
        return pl.pallas_call(
            functools.partial(join_kernel, source_count),
            out_shape=jax.ShapeDtypeStruct(result, jnp.float32),
            in_specs=[whole] * 2,
            out_specs=whole,
            scratch_shapes=[pltpu.VMEM((dir_count, dest_rows * 2 * source_count, lanes), jnp.float32)],
            compiler_params=pltpu.CompilerParams(vmem_limit_bytes=24 * 2**20),
            name="join_parts",
        )(parts, 1.0 - rims[:1])
    parts = parts.reshape((planes, dir_count) + message)
    main = parts[:, :, : 2 * dest_rows, :kf_dev].reshape(planes, dir_count, 2, dest_rows, kf_dev)
    over = parts[:, :, 2 * dest_rows :, :dest_rows].reshape(planes, dir_count, 2, 2 * rim, dest_rows)
    low = jnp.roll(over[:, :, :, :rim], -1, axis=1)
    high = jnp.roll(over[:, :, :, rim:], 1, axis=1)
    middle = jnp.zeros((planes, dir_count, 2, kf_dev - 2 * rim, dest_rows), jnp.float32)
    fix = jnp.concatenate([high, middle, low], axis=3)
    total = main.transpose(3, 2, 0, 1, 4) + fix.transpose(4, 2, 0, 1, 3)
    return total.reshape(result)


def solution(mesh):
    boxes, dirs = mesh.shape["box"], mesh.shape["dir"]
    fine_mesh = Mesh(mesh.devices.reshape(planes, boxes // planes, dirs), ("zed", "ring", "dir"))
    box = ("zed", "ring")
    placed = (
        P(box, None, None, "dir"),
        P(None, None, "dir"),
        P(box, None),
        P(box, None),
        P(box),
        P(box),
        P(box),
        P(),
        P(),
        P(),
    )
    return jax.shard_map(
        per_device,
        mesh=fine_mesh,
        in_specs=placed,
        out_specs=P(("zed", "ring", "dir"), None, None, None),
        check_vma=False,
    )
```

```python
import collections
import functools

import jax
import jax.numpy as jnp
from jax import lax
from jax.experimental import pallas as pl
from jax.experimental.pallas import tpu as pltpu
from jax.sharding import Mesh
from jax.sharding import PartitionSpec as P

wave_scale = 3.0
planes = 4
lanes = 128
half = 4
rim = 2
word_bits = 13
grain = 32


plan_fields = ["rows", "slots", "fine_rows", "stride", "width", "parent", "order", "turns"]
Plan = collections.namedtuple("Plan", plan_fields + ["together", "fixed", "group"])


def up(size, step):
    return -(-size // step) * step


def edge_bits(rows):
    bits = rows.bit_length() - 1
    return bits, [place for place in range(2, bits) if place % 2 == bits % 2]


def edge_rank(local, rows):
    bits, fixed = edge_bits(rows)
    rank = jnp.zeros_like(local)
    taken = 0
    for place in range(bits):
        if place not in fixed:
            rank = rank + (local // 2**place % 2) * 2**taken
            taken += 1
    return rank


def split(value):
    high = value.astype(jnp.bfloat16)
    low = (value - high.astype(jnp.float32)).astype(jnp.bfloat16)
    return high, low


def pack_kernel(source_count, note_count, zed, ring, field, *refs):
    notes, outs, whole = refs[:note_count], refs[note_count:-1], refs[-1]
    if note_count:
        near, notes = notes[-1], notes[:-1]
    rows = field.shape[0]
    stride = 2 * source_count
    if len(outs) > planes:
        bits, fixed = edge_bits(rows)
        free = [place for place in range(bits) if place not in fixed]
        side = (1 - ring[0]) * sum(2**place for place in fixed)
        for index in range(outs[planes].shape[0]):
            base = sum((index // 2**order % 2) * 2**place for order, place in enumerate(free))
            outs[planes][index] = field[base + side]

    def row_step(row, unused):
        both = jnp.concatenate([field[row, 0], field[row, 1]], axis=0)
        for block in range(half):
            whole[block, pl.ds(pl.multiple_of(row * stride, stride), stride), :] = both[
                :, block * lanes : (block + 1) * lanes
            ]
        return unused

    lax.fori_loop(0, rows, row_step, 0, unroll=8)
    for step, out in enumerate(outs[:planes]):
        source = zed[0] ^ step
        for part in range(2):
            for block in range(half):
                out[pl.ds(part * half + block, rows, stride=2 * half), :] = whole[
                    block, pl.ds(part * source_count + source, rows, stride=stride), :
                ]
        end = rows * 2 * half
        for note in notes:
            out[end : end + note.shape[0], :] = note[...]
            end += note.shape[0]
        if note_count and step == 1:
            out[end:, :] = near[...]


def pack(here, field, notes, edge_rows):
    rows, _, source_count, width = field.shape
    lengths = [rows * 2 * half + sum(note.shape[0] for note in notes[:-1])] * planes
    lengths[1] += sum(note.shape[0] for note in notes[-1:])
    whole = pl.BlockSpec(memory_space=pltpu.VMEM)
    edges = [jax.ShapeDtypeStruct((edge_rows,) + field.shape[1:], jnp.float32)] if edge_rows else []
    return pl.pallas_call(
        functools.partial(pack_kernel, source_count, len(notes)),
        out_shape=[jax.ShapeDtypeStruct((length, lanes), jnp.float32) for length in lengths] + edges,
        in_specs=[pl.BlockSpec(memory_space=pltpu.SMEM)] * 2 + [whole] * (1 + len(notes)),
        out_specs=[whole] * (planes + len(edges)),
        scratch_shapes=[pltpu.VMEM((half, rows * 2 * source_count, lanes), jnp.float32)],
        name="pack_sources",
    )(*here, field, *notes)


def parts_of(word):
    return lax.shift_right_logical(word, word_bits), word & (2**word_bits - 1)


def tile(start):
    return pl.ds(pl.multiple_of(start, 2 * half), 2 * half)


def fine_kernel(plan, size, edge_size, near_at, zed, lists, *refs):
    mains, refs = refs[:planes], refs[planes:]
    edges = refs[: planes - 1 if edge_size else 0]
    refs = refs[len(edges) :]
    if edge_size:
        edges = [edges[0], edges[1], mains[2], edges[2]]
    table, phases, weights, out, rims, meta, field, moved, shifted, left, ready, landed, sems = refs
    rows, fine_rows = plan.rows, plan.fine_rows
    own = zed[0]

    def bring(step):
        return pltpu.make_async_copy(lists.at[step], meta.at[step % 2], sems.at[planes + step % 2])

    bring(0).start()
    incoming = []
    for index, edge in enumerate(edges):
        step = planes - 1 - index
        chosen = edge.at[pl.ds(0, edge_size * 2 * half)]
        incoming.append(pltpu.make_async_copy(chosen, landed.at[step], sems.at[planes + 2 + step]))
        incoming[-1].start()
    lane = lax.broadcasted_iota(jnp.int32, rims.shape, 1)
    rims[...] = ((lane < rim) | (lane >= lanes - rim)).astype(jnp.float32)

    def both(start):
        return pl.ds(pl.multiple_of(start, 4 * half), 4 * half)

    def with_turned(value):
        return jnp.concatenate([value, pltpu.roll(value, half, 0)], axis=0)

    for index, main in enumerate(mains):
        step = planes - 1 - index
        first = (own ^ step) * size
        begin = near_at if step == 1 else 0

        def main_step(row, unused, first=first, main=main, begin=begin):
            field[both((first + row) * 4 * half), :] = with_turned(main[tile(begin + row * 2 * half), :])
            return unused

        lax.fori_loop(0, size, main_step, 0, unroll=8)
    for index in range(len(edges)):
        step = planes - 1 - index
        first = planes * size + (own ^ step) * edge_size
        incoming[index].wait()

        def edge_step(row, unused, first=first, step=step):
            field[both((first + row) * 4 * half), :] = with_turned(landed[step, tile(row * 2 * half), :])
            return unused

        lax.fori_loop(0, edge_size, edge_step, 0, unroll=8)
    field[both(planes * (size + edge_size) * 4 * half), :] = jnp.zeros((4 * half, lanes), jnp.float32)

    blank = jnp.zeros((2 * half, lanes), jnp.float32)
    sub = lax.broadcasted_iota(jnp.int32, (2 * half, lanes), 0)
    dest_count = out.shape[1]
    dest_rows = fine_rows // dest_count

    def plane_step(turn, unused):
        plane = own ^ (planes - 1 - turn)
        slot = turn % 2
        bring(turn).wait()

        @pl.when(turn + 1 < planes)
        def _():
            bring(turn + 1).start()

        across = lanes // plan.width

        def boxes_step(slot_count, step, unused):
            ranks = [step * plan.together + each for each in range(plan.together)]
            boxes = [meta[slot, plan.order, rank] for rank in ranks]
            sums = [[blank, blank] for box in boxes]
            for pair in range(slot_count):
                for each in range(plan.together):
                    row = step * (plan.together // across) + each // across
                    place, kind = parts_of(meta[slot, row, each % across * plan.width + pair])
                    value = field[both(place), :]
                    factor = table[tile(kind), :]
                    sums[each][0] += factor * value[: 2 * half]
                    sums[each][1] += factor * value[2 * half :]
            for each in range(plan.together):
                straight, crossed = sums[each]
                total = jnp.where(
                    sub < half,
                    straight + pltpu.roll(straight, half, 0),
                    pltpu.roll(crossed, half, 0) - crossed,
                )
                moved[both(boxes[each] * 4 * half), :] = with_turned(total)
            return unused

        start = 0
        for more in reversed(range((plan.slots - plan.fixed) // plan.group + 1)):
            end = meta[slot, plan.order, plan.turns + more]
            lax.fori_loop(start, end, functools.partial(boxes_step, plan.fixed + more * plan.group), 0)
            start = end

        def fine_step(block, unused):
            for each in range(lanes):
                parent, octant = parts_of(meta[slot, plan.parent + block, each])
                value = moved[both(parent), :] * phases[both(octant), :]
                shifted[tile((block * lanes + each) * 2 * half), :] = value[: 2 * half] + value[2 * half :]
            return unused

        lax.fori_loop(0, fine_rows // lanes, fine_step, 0)
        width = ready.shape[3]
        depth = half * lanes

        def split_step(chunk, unused):
            for part in range(2):
                rows_of = pl.ds(pl.multiple_of(part * fine_rows + chunk * grain, grain), grain)
                for block in range(half):
                    begin = chunk * grain * 2 * half + part * half + block
                    value = shifted[pl.ds(begin, grain, stride=2 * half), :]
                    high, low = split(value)
                    left[rows_of, block * lanes : (block + 1) * lanes] = high
                    left[rows_of, depth + block * lanes : depth + (block + 1) * lanes] = low
            return unused

        lax.fori_loop(0, fine_rows // grain, split_step, 0, unroll=2)
        result = jnp.dot(
            jnp.concatenate([left[:, :depth], left[...]], axis=1), weights[...], preferred_element_type=jnp.float32
        )
        for part in range(2):
            for dest in range(dest_count):
                start = part * fine_rows + dest * dest_rows
                ready[plane, dest, part * dest_rows : (part + 1) * dest_rows, :] = result[
                    start : start + dest_rows, :width
                ]
        spill = result[:fine_rows, width:] + pltpu.roll(result[fine_rows:, width:], half, 1)
        spill = spill.T[: 2 * half]
        for dest in range(dest_count):
            ready[plane, dest, 2 * dest_rows :, :] = jnp.concatenate(
                [
                    spill[:, dest * dest_rows : (dest + 1) * dest_rows],
                    jnp.zeros((2 * half, width - dest_rows), jnp.float32),
                ],
                axis=1,
            )
        pltpu.make_async_copy(ready.at[plane], out.at[plane], sems.at[plane]).start()
        return unused

    lax.fori_loop(0, planes, plane_step, 0)
    for plane in range(planes):
        pltpu.make_async_copy(ready.at[plane], out.at[plane], sems.at[plane]).wait()


def join_kernel(source_count, parts, rims, out, whole):
    dest_rows = out.shape[0]
    dirs = parts.shape[0] // source_count
    over = jnp.concatenate(
        [parts[index, 2 * dest_rows :, :lanes] for index in range(parts.shape[0])], axis=0
    ).T[:dest_rows]
    low = lax.broadcasted_iota(jnp.int32, (dest_rows, lanes), 1) < rim
    at_rim = jnp.broadcast_to(rims[...], (dest_rows, lanes)) < 0.5
    for source in range(source_count):
        for part in range(2):
            turned = []
            for index in range(dirs):
                first = (source * dirs + index) * 2 * half + part * half
                turned.append(pltpu.roll(over, (lanes - rim - first) % lanes, 1))
            for index in range(dirs):
                fix = jnp.where(at_rim, jnp.where(low, turned[index - 1], turned[(index + 1) % dirs]), 0.0)
                whole[
                    index, pl.ds(part * source_count + source, dest_rows, stride=2 * source_count), :
                ] = parts[source * dirs + index, part * dest_rows : (part + 1) * dest_rows, :] + fix

    def row_step(row, unused):
        start = pl.multiple_of(row * 2 * source_count, 2 * source_count)
        both = jnp.concatenate(
            [whole[index, pl.ds(start, 2 * source_count), :] for index in range(dirs)], axis=1
        )
        out[row, 0] = both[:source_count]
        out[row, 1] = both[source_count:]
        return unused

    lax.fori_loop(0, dest_rows, row_step, 0, unroll=8)


def per_device(
    coarse_field,
    trans_table,
    partner_ids,
    partner_types,
    partner_count,
    child_count,
    child_octant,
    dir_angles,
    stencil_ids,
    stencil_weights,
):
    rows, _, source_count, kc_dev = coarse_field.shape
    slots = partner_ids.shape[1]
    type_count = trans_table.shape[0]
    fine_rows = child_octant.shape[0]
    ring_count = lax.axis_size("ring")
    dir_count = lax.axis_size("dir")
    zed = lax.axis_index("zed")
    ring = lax.axis_index("ring")
    dir_index = lax.axis_index("dir")
    fine_count = stencil_ids.shape[0] // 4
    kf_dev = fine_count // dir_count
    kc_pad = up(kc_dev, half * lanes)
    kf_pad = up(kf_dev, lanes)
    pad_dirs = kc_pad - kc_dev
    assert source_count == planes and kc_pad == half * lanes
    dest_rows = fine_rows // dir_count

    field = jnp.pad(coarse_field, ((0, 0), (0, 0), (0, 0), (0, pad_dirs)))
    here = zed.reshape(1), ring.reshape(1)
    edge_rows = rows >> len(edge_bits(rows)[1]) if ring_count == 2 else 0
    packed = pack(here, field, [], edge_rows)
    if edge_rows:
        edges = lax.ppermute(packed[planes], "ring", [(0, 1), (1, 0)])

    def to_planes(note, step):
        if step == 0:
            return note
        return lax.ppermute(note, "zed", [(plane, plane ^ step) for plane in range(planes)])

    arrived = [to_planes(packed[step], step) for step in ((3, 2) if edge_rows else (3, 2, 1))]

    plane_of = partner_ids // (ring_count * rows)
    ring_of = partner_ids // rows % ring_count
    local = partner_ids % rows
    live = jnp.arange(slots, dtype=jnp.int32)[None, :] < partner_count[:, None]
    if ring_count == 2:
        size = rows
        place = jnp.where(
            ring_of == ring,
            plane_of * rows + local,
            planes * rows + plane_of * edge_rows + edge_rank(local, rows),
        )
    else:
        size = ring_count * rows
        place = partner_ids
    field_rows = planes * (size + edge_rows)
    place = jnp.where(live, place, field_rows)
    together = 4
    fixed = slots // 2
    group = 5 if (slots - fixed) % 5 == 0 else 1
    index = jnp.arange(rows, dtype=jnp.int32)
    before = (partner_count[None, :] > partner_count[:, None]) | (
        (partner_count[None, :] == partner_count[:, None]) & (index[None, :] < index[:, None])
    )
    rank = jnp.sum(before.astype(jnp.int32), axis=1)
    at_rank = rank[None, :] == index[:, None]
    order = jnp.sum(jnp.where(at_rank, index[None, :], 0), axis=1)
    first = rank[None, :] == index[: rows // together, None] * together
    longest = jnp.sum(jnp.where(first, partner_count[None, :], 0), axis=1)
    turns = jnp.maximum((longest - fixed + group - 1) // group, 0)
    more = jnp.arange((slots - fixed) // group + 1, dtype=jnp.int32)
    ends = jnp.sum((turns[None, :] >= more[:, None]).astype(jnp.int32), axis=1)
    bounds = jnp.sum(jnp.where(index[None, :] <= index[:, None], child_count[None, :], 0), axis=1)
    parent = jnp.sum(
        (bounds[None, :] <= jnp.arange(fine_rows, dtype=jnp.int32)[:, None]).astype(jnp.int32), axis=1
    )
    def across(one, width=lanes):
        return jnp.pad(one, ((0, 0), (0, width - one.shape[1])))

    width = lanes // half
    turns_at = lanes // 2
    assert slots <= width and rows <= turns_at and fine_rows % lanes == 0
    assert (field_rows + 1) * 4 * half < 2 ** (31 - word_bits) and type_count * 2 * half < 2**word_bits

    def in_order(one):
        one = jnp.sum(jnp.where(at_rank[:, :, None], across(one, width)[None], 0), axis=1)
        return one.reshape(rows * width // lanes, lanes)

    list_rows = rows * width // lanes
    fine_lists = fine_rows // lanes
    last = across(jnp.concatenate([across(order[None], turns_at), ends[None]], axis=1))
    stride = up(list_rows + fine_lists + 1, 8)

    def stacked(*parts):
        meta = jnp.concatenate(parts)
        return jnp.pad(meta, ((0, stride - meta.shape[0]), (0, 0))).astype(jnp.float32)

    meta = jnp.concatenate(
        [
            stacked(in_order(place * 4 * half), (parent * 4 * half).reshape(-1, lanes)),
            stacked(in_order(partner_types * 2 * half), (child_octant * 4 * half).reshape(-1, lanes), last),
        ]
    )
    plan = Plan(
        rows, slots, fine_rows, stride, width, list_rows, list_rows + fine_lists, turns_at, together, fixed, group
    )

    notes = pack(here, edges, [meta, packed[1]], 0) if edge_rows else [meta] * planes
    after_notes = lax.optimization_barrier((notes, trans_table, dir_angles, stencil_ids, stencil_weights))
    notes, trans_table, dir_angles, stencil_ids, stencil_weights = after_notes
    received = [to_planes(notes[step], step) for step in (3, 2, 1, 0)]
    edge_part = edge_rows * 2 * half
    numbers = jnp.stack([note[edge_part : edge_part + 2 * stride] for note in received]).astype(jnp.int32)
    meta = numbers[:, :stride] * 2**word_bits + numbers[:, stride:]
    near_at = 0
    if edge_rows:
        near_at = edge_part + 2 * stride
        arrived = arrived + [received.pop(2), packed[0]]
    else:
        arrived = [lax.all_gather(one, "ring", axis=0, tiled=True) for one in arrived + [packed[0]]]
        received = []

    def blocks(table):
        return jnp.pad(table, ((0, 0), (0, pad_dirs))).reshape(-1, half, lanes)

    def doubled(table, sign):
        return jnp.concatenate([blocks(table), sign * blocks(table)], axis=1)

    table = jnp.pad(trans_table, ((0, 0), (0, 0), (0, pad_dirs))).reshape(-1, lanes)
    angles = lax.dynamic_slice_in_dim(dir_angles, dir_index * kc_dev, kc_dev, axis=1)
    octants = jnp.arange(8, dtype=jnp.int32)
    sign_x = 1.0 - 2.0 * (octants % 2).astype(jnp.float32)
    sign_y = 1.0 - 2.0 * (octants // 2 % 2).astype(jnp.float32)
    sign_z = 1.0 - 2.0 * (octants // 4).astype(jnp.float32)
    unit_x = jnp.sin(angles[0]) * jnp.cos(angles[1])
    unit_y = jnp.sin(angles[0]) * jnp.sin(angles[1])
    unit_z = jnp.cos(angles[0])
    phase = wave_scale * (
        sign_x[:, None] * unit_x[None, :] + sign_y[:, None] * unit_y[None, :] + sign_z[:, None] * unit_z[None, :]
    )
    phases = jnp.concatenate(
        [doubled(jnp.cos(phase), 1.0), doubled(jnp.sin(phase), -1.0)], axis=1
    ).reshape(-1, lanes)

    ids = lax.dynamic_slice_in_dim(stencil_ids, dir_index * kc_dev, kc_dev, axis=0).T
    weights = lax.dynamic_slice_in_dim(stencil_weights, dir_index * kc_dev, kc_dev, axis=0).T

    def interp(targets):
        matrix = jnp.zeros((targets.shape[0], kc_dev), jnp.float32)
        for point in range(ids.shape[0]):
            matrix = matrix + jnp.where(
                ids[point][None, :] == targets[:, None], weights[point][None, :], 0.0
            )
        return jnp.pad(matrix, ((0, 0), (0, pad_dirs)))

    first_fine = dir_index * kf_dev
    own = jnp.arange(kf_dev, dtype=jnp.int32)
    outside = jnp.concatenate(
        [jnp.arange(-rim, 0, dtype=jnp.int32), jnp.arange(kf_dev, kf_dev + rim, dtype=jnp.int32)]
    )
    matrix = jnp.pad(interp(first_fine + own), ((0, kf_pad - kf_dev), (0, 0)))
    spill = interp((first_fine + outside) % fine_count)
    matrices = jnp.concatenate([matrix, jnp.pad(spill, ((0, lanes - half), (0, 0)))], axis=0).T
    rounded = lax.reduce_precision(matrices, 8, 7)
    high = rounded.astype(jnp.bfloat16)
    low = (matrices - rounded).astype(jnp.bfloat16)
    passes = jnp.concatenate([low, high, high], axis=0)

    whole = pl.BlockSpec(memory_space=pltpu.VMEM)
    message = (2 * dest_rows + 2 * half, kf_pad)
    local_fine, rims = pl.pallas_call(
        functools.partial(fine_kernel, plan, size, edge_rows, near_at),
        out_shape=[
            pltpu.HBM((planes, dir_count) + message, jnp.float32),
            jax.ShapeDtypeStruct((2 * half, lanes), jnp.float32),
        ],
        in_specs=[pl.BlockSpec(memory_space=pltpu.SMEM), pl.BlockSpec(memory_space=pl.ANY)]
        + [whole] * planes
        + [pl.BlockSpec(memory_space=pl.ANY)] * len(received)
        + [whole] * 3,
        out_specs=[pl.BlockSpec(memory_space=pltpu.HBM), whole],
        scratch_shapes=[
            pltpu.SMEM((2, plan.stride, lanes), jnp.int32),
            pltpu.VMEM(((field_rows + 1) * 4 * half, lanes), jnp.float32),
            pltpu.VMEM((rows * 4 * half, lanes), jnp.float32),
            pltpu.VMEM((fine_rows * 2 * half, lanes), jnp.float32),
            pltpu.VMEM((2 * fine_rows, 2 * kc_pad), jnp.bfloat16),
            pltpu.VMEM((planes, dir_count) + message, jnp.float32),
            pltpu.VMEM((planes, max(edge_rows, 1) * 2 * half, lanes), jnp.float32),
            pltpu.SemaphoreType.DMA((2 * planes + 2,)),
        ],
        compiler_params=pltpu.CompilerParams(vmem_limit_bytes=48 * 2**20),
        name="translate_and_interpolate",
    )(here[0], meta, *arrived, *received, table, phases, passes)

    parts = lax.all_to_all(
        local_fine.reshape((planes * dir_count,) + message),
        ("zed", "dir"),
        split_axis=0,
        concat_axis=0,
        tiled=True,
    )
    result = (dest_rows, 2, source_count, fine_count)
    if kf_dev == lanes and planes * dir_count * 2 * half == lanes and dest_rows <= lanes:
        return pl.pallas_call(
            functools.partial(join_kernel, source_count),
            out_shape=jax.ShapeDtypeStruct(result, jnp.float32),
            in_specs=[whole] * 2,
            out_specs=whole,
            scratch_shapes=[pltpu.VMEM((dir_count, dest_rows * 2 * source_count, lanes), jnp.float32)],
            compiler_params=pltpu.CompilerParams(vmem_limit_bytes=24 * 2**20),
            name="join_parts",
        )(parts, 1.0 - rims[:1])
    parts = parts.reshape((planes, dir_count) + message)
    main = parts[:, :, : 2 * dest_rows, :kf_dev].reshape(planes, dir_count, 2, dest_rows, kf_dev)
    over = parts[:, :, 2 * dest_rows :, :dest_rows].reshape(planes, dir_count, 2, 2 * rim, dest_rows)
    low = jnp.roll(over[:, :, :, :rim], -1, axis=1)
    high = jnp.roll(over[:, :, :, rim:], 1, axis=1)
    middle = jnp.zeros((planes, dir_count, 2, kf_dev - 2 * rim, dest_rows), jnp.float32)
    fix = jnp.concatenate([high, middle, low], axis=3)
    total = main.transpose(3, 2, 0, 1, 4) + fix.transpose(4, 2, 0, 1, 3)
    return total.reshape(result)


def solution(mesh):
    boxes, dirs = mesh.shape["box"], mesh.shape["dir"]
    fine_mesh = Mesh(mesh.devices.reshape(planes, boxes // planes, dirs), ("zed", "ring", "dir"))
    box = ("zed", "ring")
    placed = (
        P(box, None, None, "dir"),
        P(None, None, "dir"),
        P(box, None),
        P(box, None),
        P(box),
        P(box),
        P(box),
        P(),
        P(),
        P(),
    )
    return jax.shard_map(
        per_device,
        mesh=fine_mesh,
        in_specs=placed,
        out_specs=P(("zed", "ring", "dir"), None, None, None),
        check_vma=False,
    )
```

```python
import collections
import functools

import jax
import jax.numpy as jnp
from jax import lax
from jax.experimental import pallas as pl
from jax.experimental.pallas import tpu as pltpu
from jax.sharding import Mesh
from jax.sharding import PartitionSpec as P

wave_scale = 3.0
planes = 4
lanes = 128
half = 4
rim = 2
word_bits = 13
grain = 32


plan_fields = ["rows", "slots", "fine_rows", "stride", "width", "parent", "order", "turns"]
Plan = collections.namedtuple("Plan", plan_fields + ["together", "fixed", "group"])


def up(size, step):
    return -(-size // step) * step


def edge_bits(rows):
    bits = rows.bit_length() - 1
    return bits, [place for place in range(2, bits) if place % 2 == bits % 2]


def edge_rank(local, rows):
    bits, fixed = edge_bits(rows)
    rank = jnp.zeros_like(local)
    taken = 0
    for place in range(bits):
        if place not in fixed:
            rank = rank + (local // 2**place % 2) * 2**taken
            taken += 1
    return rank


def split(value):
    high = value.astype(jnp.bfloat16)
    low = (value - high.astype(jnp.float32)).astype(jnp.bfloat16)
    return high, low


def pack_kernel(source_count, note_count, zed, ring, field, *refs):
    notes, outs, whole = refs[:note_count], refs[note_count:-1], refs[-1]
    rows = field.shape[0]
    stride = 2 * source_count
    if len(outs) > planes:
        bits, fixed = edge_bits(rows)
        free = [place for place in range(bits) if place not in fixed]
        side = (1 - ring[0]) * sum(2**place for place in fixed)
        for index in range(outs[planes].shape[0]):
            base = sum((index // 2**order % 2) * 2**place for order, place in enumerate(free))
            outs[planes][index] = field[base + side]

    def row_step(row, unused):
        both = jnp.concatenate([field[row, 0], field[row, 1]], axis=0)
        for block in range(half):
            whole[block, pl.ds(pl.multiple_of(row * stride, stride), stride), :] = both[
                :, block * lanes : (block + 1) * lanes
            ]
        return unused

    lax.fori_loop(0, rows, row_step, 0, unroll=8)
    for step, out in enumerate(outs[:planes]):
        source = zed[0] ^ step
        for part in range(2):
            for block in range(half):
                out[pl.ds(part * half + block, rows, stride=2 * half), :] = whole[
                    block, pl.ds(part * source_count + source, rows, stride=stride), :
                ]
        for note in notes:
            out[rows * 2 * half :, :] = note[...]


def pack(here, field, notes, edge_rows):
    rows, _, source_count, width = field.shape
    length = rows * 2 * half + sum(note.shape[0] for note in notes)
    whole = pl.BlockSpec(memory_space=pltpu.VMEM)
    edges = [jax.ShapeDtypeStruct((edge_rows,) + field.shape[1:], jnp.float32)] if edge_rows else []
    return pl.pallas_call(
        functools.partial(pack_kernel, source_count, len(notes)),
        out_shape=[jax.ShapeDtypeStruct((length, lanes), jnp.float32)] * planes + edges,
        in_specs=[pl.BlockSpec(memory_space=pltpu.SMEM)] * 2 + [whole] * (1 + len(notes)),
        out_specs=[whole] * (planes + len(edges)),
        scratch_shapes=[pltpu.VMEM((half, rows * 2 * source_count, lanes), jnp.float32)],
        name="pack_sources",
    )(*here, field, *notes)


def parts_of(word):
    return lax.shift_right_logical(word, word_bits), word & (2**word_bits - 1)


def tile(start):
    return pl.ds(pl.multiple_of(start, 2 * half), 2 * half)


def fine_kernel(plan, size, edge_size, zed, *refs):
    mains, refs = refs[:planes], refs[planes:]
    edges = refs[: planes if edge_size else 0]
    lists, refs = refs[len(edges)], refs[len(edges) + 1 :]
    table, phases, weights, out, rims, meta, field, moved, shifted, left, ready, landed, sems = refs
    rows, fine_rows = plan.rows, plan.fine_rows
    own = zed[0]

    def bring(step):
        return pltpu.make_async_copy(lists.at[step], meta.at[step % 2], sems.at[planes + step % 2])

    bring(0).start()
    incoming = []
    for index, edge in enumerate(edges):
        chosen = edge.at[pl.ds(0, edge_size * 2 * half)]
        incoming.append(pltpu.make_async_copy(chosen, landed.at[index], sems.at[planes + 2 + index]))
        incoming[-1].start()
    lane = lax.broadcasted_iota(jnp.int32, rims.shape, 1)
    rims[...] = ((lane < rim) | (lane >= lanes - rim)).astype(jnp.float32)

    def both(start):
        return pl.ds(pl.multiple_of(start, 4 * half), 4 * half)

    def with_turned(value):
        return jnp.concatenate([value, pltpu.roll(value, half, 0)], axis=0)

    for step, main in enumerate(mains):
        first = (own ^ step) * size

        def main_step(row, unused, first=first, main=main):
            field[both((first + row) * 4 * half), :] = with_turned(main[tile(row * 2 * half), :])
            return unused

        lax.fori_loop(0, size, main_step, 0, unroll=8)
    for index in range(len(edges)):
        first = planes * size + (own ^ (planes - 1 - index)) * edge_size
        incoming[index].wait()

        def edge_step(row, unused, first=first, index=index):
            field[both((first + row) * 4 * half), :] = with_turned(landed[index, tile(row * 2 * half), :])
            return unused

        lax.fori_loop(0, edge_size, edge_step, 0, unroll=8)
    field[both(planes * (size + edge_size) * 4 * half), :] = jnp.zeros((4 * half, lanes), jnp.float32)

    blank = jnp.zeros((2 * half, lanes), jnp.float32)
    sub = lax.broadcasted_iota(jnp.int32, (2 * half, lanes), 0)
    dest_count = out.shape[1]
    dest_rows = fine_rows // dest_count

    def plane_step(turn, unused):
        plane = own ^ (planes - 1 - turn)
        slot = turn % 2
        bring(turn).wait()

        @pl.when(turn + 1 < planes)
        def _():
            bring(turn + 1).start()

        across = lanes // plan.width

        def boxes_step(slot_count, step, unused):
            ranks = [step * plan.together + each for each in range(plan.together)]
            boxes = [meta[slot, plan.order, rank] for rank in ranks]
            sums = [[blank, blank] for box in boxes]
            for pair in range(slot_count):
                for each in range(plan.together):
                    row = step * (plan.together // across) + each // across
                    place, kind = parts_of(meta[slot, row, each % across * plan.width + pair])
                    value = field[both(place), :]
                    factor = table[tile(kind), :]
                    sums[each][0] += factor * value[: 2 * half]
                    sums[each][1] += factor * value[2 * half :]
            for each in range(plan.together):
                straight, crossed = sums[each]
                total = jnp.where(
                    sub < half,
                    straight + pltpu.roll(straight, half, 0),
                    pltpu.roll(crossed, half, 0) - crossed,
                )
                moved[both(boxes[each] * 4 * half), :] = with_turned(total)
            return unused

        start = 0
        for more in reversed(range((plan.slots - plan.fixed) // plan.group + 1)):
            end = meta[slot, plan.order, plan.turns + more]
            lax.fori_loop(start, end, functools.partial(boxes_step, plan.fixed + more * plan.group), 0)
            start = end

        def fine_step(block, unused):
            for each in range(lanes):
                parent, octant = parts_of(meta[slot, plan.parent + block, each])
                value = moved[both(parent), :] * phases[both(octant), :]
                shifted[tile((block * lanes + each) * 2 * half), :] = value[: 2 * half] + value[2 * half :]
            return unused

        lax.fori_loop(0, fine_rows // lanes, fine_step, 0)
        width = ready.shape[3]
        depth = half * lanes

        def split_step(chunk, unused):
            for part in range(2):
                rows_of = pl.ds(pl.multiple_of(part * fine_rows + chunk * grain, grain), grain)
                for block in range(half):
                    begin = chunk * grain * 2 * half + part * half + block
                    value = shifted[pl.ds(begin, grain, stride=2 * half), :]
                    high, low = split(value)
                    left[rows_of, block * lanes : (block + 1) * lanes] = high
                    left[rows_of, depth + block * lanes : depth + (block + 1) * lanes] = low
            return unused

        lax.fori_loop(0, fine_rows // grain, split_step, 0, unroll=2)
        result = jnp.dot(
            jnp.concatenate([left[:, :depth], left[...]], axis=1), weights[...], preferred_element_type=jnp.float32
        )
        for part in range(2):
            for dest in range(dest_count):
                start = part * fine_rows + dest * dest_rows
                ready[plane, dest, part * dest_rows : (part + 1) * dest_rows, :] = result[
                    start : start + dest_rows, :width
                ]
        spill = result[:fine_rows, width:] + pltpu.roll(result[fine_rows:, width:], half, 1)
        spill = spill.T[: 2 * half]
        for dest in range(dest_count):
            ready[plane, dest, 2 * dest_rows :, :] = jnp.concatenate(
                [
                    spill[:, dest * dest_rows : (dest + 1) * dest_rows],
                    jnp.zeros((2 * half, width - dest_rows), jnp.float32),
                ],
                axis=1,
            )
        pltpu.make_async_copy(ready.at[plane], out.at[plane], sems.at[plane]).start()
        return unused

    lax.fori_loop(0, planes, plane_step, 0)
    for plane in range(planes):
        pltpu.make_async_copy(ready.at[plane], out.at[plane], sems.at[plane]).wait()


def join_kernel(source_count, parts, rims, out, whole):
    dest_rows = out.shape[0]
    dirs = parts.shape[0] // source_count
    over = jnp.concatenate(
        [parts[index, 2 * dest_rows :, :lanes] for index in range(parts.shape[0])], axis=0
    ).T[:dest_rows]
    low = lax.broadcasted_iota(jnp.int32, (dest_rows, lanes), 1) < rim
    at_rim = jnp.broadcast_to(rims[...], (dest_rows, lanes)) < 0.5
    for source in range(source_count):
        for part in range(2):
            turned = []
            for index in range(dirs):
                first = (source * dirs + index) * 2 * half + part * half
                turned.append(pltpu.roll(over, (lanes - rim - first) % lanes, 1))
            for index in range(dirs):
                fix = jnp.where(at_rim, jnp.where(low, turned[index - 1], turned[(index + 1) % dirs]), 0.0)
                whole[
                    index, pl.ds(part * source_count + source, dest_rows, stride=2 * source_count), :
                ] = parts[source * dirs + index, part * dest_rows : (part + 1) * dest_rows, :] + fix

    def row_step(row, unused):
        start = pl.multiple_of(row * 2 * source_count, 2 * source_count)
        both = jnp.concatenate(
            [whole[index, pl.ds(start, 2 * source_count), :] for index in range(dirs)], axis=1
        )
        out[row, 0] = both[:source_count]
        out[row, 1] = both[source_count:]
        return unused

    lax.fori_loop(0, dest_rows, row_step, 0, unroll=8)


def per_device(
    coarse_field,
    trans_table,
    partner_ids,
    partner_types,
    partner_count,
    child_count,
    child_octant,
    dir_angles,
    stencil_ids,
    stencil_weights,
):
    rows, _, source_count, kc_dev = coarse_field.shape
    slots = partner_ids.shape[1]
    type_count = trans_table.shape[0]
    fine_rows = child_octant.shape[0]
    ring_count = lax.axis_size("ring")
    dir_count = lax.axis_size("dir")
    zed = lax.axis_index("zed")
    ring = lax.axis_index("ring")
    dir_index = lax.axis_index("dir")
    fine_count = stencil_ids.shape[0] // 4
    kf_dev = fine_count // dir_count
    kc_pad = up(kc_dev, half * lanes)
    kf_pad = up(kf_dev, lanes)
    pad_dirs = kc_pad - kc_dev
    assert source_count == planes and kc_pad == half * lanes
    dest_rows = fine_rows // dir_count

    field = jnp.pad(coarse_field, ((0, 0), (0, 0), (0, 0), (0, pad_dirs)))
    here = zed.reshape(1), ring.reshape(1)
    edge_rows = rows >> len(edge_bits(rows)[1]) if ring_count == 2 else 0
    packed = pack(here, field, [], edge_rows)
    if edge_rows:
        edges = lax.ppermute(packed[planes], "ring", [(0, 1), (1, 0)])

    def to_planes(note, step):
        if step == 0:
            return note
        return lax.ppermute(note, "zed", [(plane, plane ^ step) for plane in range(planes)])

    arrived = [to_planes(packed[step], step) for step in (3, 2, 1, 0)][::-1]

    plane_of = partner_ids // (ring_count * rows)
    ring_of = partner_ids // rows % ring_count
    local = partner_ids % rows
    live = jnp.arange(slots, dtype=jnp.int32)[None, :] < partner_count[:, None]
    if ring_count == 2:
        size = rows
        place = jnp.where(
            ring_of == ring,
            plane_of * rows + local,
            planes * rows + plane_of * edge_rows + edge_rank(local, rows),
        )
    else:
        size = ring_count * rows
        place = partner_ids
    field_rows = planes * (size + edge_rows)
    place = jnp.where(live, place, field_rows)
    together = 4
    fixed = slots // 2
    group = 5 if (slots - fixed) % 5 == 0 else 1
    index = jnp.arange(rows, dtype=jnp.int32)
    before = (partner_count[None, :] > partner_count[:, None]) | (
        (partner_count[None, :] == partner_count[:, None]) & (index[None, :] < index[:, None])
    )
    rank = jnp.sum(before.astype(jnp.int32), axis=1)
    at_rank = rank[None, :] == index[:, None]
    order = jnp.sum(jnp.where(at_rank, index[None, :], 0), axis=1)
    first = rank[None, :] == index[: rows // together, None] * together
    longest = jnp.sum(jnp.where(first, partner_count[None, :], 0), axis=1)
    turns = jnp.maximum((longest - fixed + group - 1) // group, 0)
    more = jnp.arange((slots - fixed) // group + 1, dtype=jnp.int32)
    ends = jnp.sum((turns[None, :] >= more[:, None]).astype(jnp.int32), axis=1)
    bounds = jnp.sum(jnp.where(index[None, :] <= index[:, None], child_count[None, :], 0), axis=1)
    parent = jnp.sum(
        (bounds[None, :] <= jnp.arange(fine_rows, dtype=jnp.int32)[:, None]).astype(jnp.int32), axis=1
    )
    def across(one, width=lanes):
        return jnp.pad(one, ((0, 0), (0, width - one.shape[1])))

    width = lanes // half
    turns_at = lanes // 2
    assert slots <= width and rows <= turns_at and fine_rows % lanes == 0
    assert (field_rows + 1) * 4 * half < 2 ** (31 - word_bits) and type_count * 2 * half < 2**word_bits

    def in_order(one):
        one = jnp.sum(jnp.where(at_rank[:, :, None], across(one, width)[None], 0), axis=1)
        return one.reshape(rows * width // lanes, lanes)

    list_rows = rows * width // lanes
    fine_lists = fine_rows // lanes
    last = across(jnp.concatenate([across(order[None], turns_at), ends[None]], axis=1))
    stride = up(list_rows + fine_lists + 1, 8)

    def stacked(*parts):
        meta = jnp.concatenate(parts)
        return jnp.pad(meta, ((0, stride - meta.shape[0]), (0, 0))).astype(jnp.float32)

    meta = jnp.concatenate(
        [
            stacked(in_order(place * 4 * half), (parent * 4 * half).reshape(-1, lanes)),
            stacked(in_order(partner_types * 2 * half), (child_octant * 4 * half).reshape(-1, lanes), last),
        ]
    )
    plan = Plan(
        rows, slots, fine_rows, stride, width, list_rows, list_rows + fine_lists, turns_at, together, fixed, group
    )

    notes = pack(here, edges, [meta], 0) if edge_rows else [meta] * planes
    after_notes = lax.optimization_barrier((notes, trans_table, dir_angles, stencil_ids, stencil_weights))
    notes, trans_table, dir_angles, stencil_ids, stencil_weights = after_notes
    received = [to_planes(notes[step], step) for step in (3, 2, 1, 0)]
    edge_part = edge_rows * 2 * half
    numbers = jnp.stack([note[edge_part:] for note in received]).astype(jnp.int32)
    meta = numbers[:, :stride] * 2**word_bits + numbers[:, stride:]
    if ring_count != 2:
        arrived = [lax.all_gather(one, "ring", axis=0, tiled=True) for one in arrived]
        received = []

    def blocks(table):
        return jnp.pad(table, ((0, 0), (0, pad_dirs))).reshape(-1, half, lanes)

    def doubled(table, sign):
        return jnp.concatenate([blocks(table), sign * blocks(table)], axis=1)

    table = jnp.pad(trans_table, ((0, 0), (0, 0), (0, pad_dirs))).reshape(-1, lanes)
    angles = lax.dynamic_slice_in_dim(dir_angles, dir_index * kc_dev, kc_dev, axis=1)
    octants = jnp.arange(8, dtype=jnp.int32)
    sign_x = 1.0 - 2.0 * (octants % 2).astype(jnp.float32)
    sign_y = 1.0 - 2.0 * (octants // 2 % 2).astype(jnp.float32)
    sign_z = 1.0 - 2.0 * (octants // 4).astype(jnp.float32)
    unit_x = jnp.sin(angles[0]) * jnp.cos(angles[1])
    unit_y = jnp.sin(angles[0]) * jnp.sin(angles[1])
    unit_z = jnp.cos(angles[0])
    phase = wave_scale * (
        sign_x[:, None] * unit_x[None, :] + sign_y[:, None] * unit_y[None, :] + sign_z[:, None] * unit_z[None, :]
    )
    phases = jnp.concatenate(
        [doubled(jnp.cos(phase), 1.0), doubled(jnp.sin(phase), -1.0)], axis=1
    ).reshape(-1, lanes)

    ids = lax.dynamic_slice_in_dim(stencil_ids, dir_index * kc_dev, kc_dev, axis=0).T
    weights = lax.dynamic_slice_in_dim(stencil_weights, dir_index * kc_dev, kc_dev, axis=0).T

    def interp(targets):
        matrix = jnp.zeros((targets.shape[0], kc_dev), jnp.float32)
        for point in range(ids.shape[0]):
            matrix = matrix + jnp.where(
                ids[point][None, :] == targets[:, None], weights[point][None, :], 0.0
            )
        return jnp.pad(matrix, ((0, 0), (0, pad_dirs)))

    first_fine = dir_index * kf_dev
    own = jnp.arange(kf_dev, dtype=jnp.int32)
    outside = jnp.concatenate(
        [jnp.arange(-rim, 0, dtype=jnp.int32), jnp.arange(kf_dev, kf_dev + rim, dtype=jnp.int32)]
    )
    matrix = jnp.pad(interp(first_fine + own), ((0, kf_pad - kf_dev), (0, 0)))
    spill = interp((first_fine + outside) % fine_count)
    matrices = jnp.concatenate([matrix, jnp.pad(spill, ((0, lanes - half), (0, 0)))], axis=0).T
    rounded = lax.reduce_precision(matrices, 8, 7)
    high = rounded.astype(jnp.bfloat16)
    low = (matrices - rounded).astype(jnp.bfloat16)
    passes = jnp.concatenate([low, high, high], axis=0)

    whole = pl.BlockSpec(memory_space=pltpu.VMEM)
    message = (2 * dest_rows + 2 * half, kf_pad)
    local_fine, rims = pl.pallas_call(
        functools.partial(fine_kernel, plan, size, edge_rows),
        out_shape=[
            pltpu.HBM((planes, dir_count) + message, jnp.float32),
            jax.ShapeDtypeStruct((2 * half, lanes), jnp.float32),
        ],
        in_specs=[pl.BlockSpec(memory_space=pltpu.SMEM)]
        + [whole] * planes
        + [pl.BlockSpec(memory_space=pl.ANY)] * (len(received) + 1)
        + [whole] * 3,
        out_specs=[pl.BlockSpec(memory_space=pltpu.HBM), whole],
        scratch_shapes=[
            pltpu.SMEM((2, plan.stride, lanes), jnp.int32),
            pltpu.VMEM(((field_rows + 1) * 4 * half, lanes), jnp.float32),
            pltpu.VMEM((rows * 4 * half, lanes), jnp.float32),
            pltpu.VMEM((fine_rows * 2 * half, lanes), jnp.float32),
            pltpu.VMEM((2 * fine_rows, 2 * kc_pad), jnp.bfloat16),
            pltpu.VMEM((planes, dir_count) + message, jnp.float32),
            pltpu.VMEM((planes, max(edge_rows, 1) * 2 * half, lanes), jnp.float32),
            pltpu.SemaphoreType.DMA((2 * planes + 2,)),
        ],
        compiler_params=pltpu.CompilerParams(vmem_limit_bytes=48 * 2**20),
        name="translate_and_interpolate",
    )(here[0], *arrived, *received, meta, table, phases, passes)

    parts = lax.all_to_all(
        local_fine.reshape((planes * dir_count,) + message),
        ("zed", "dir"),
        split_axis=0,
        concat_axis=0,
        tiled=True,
    )
    result = (dest_rows, 2, source_count, fine_count)
    if kf_dev == lanes and planes * dir_count * 2 * half == lanes and dest_rows <= lanes:
        return pl.pallas_call(
            functools.partial(join_kernel, source_count),
            out_shape=jax.ShapeDtypeStruct(result, jnp.float32),
            in_specs=[whole] * 2,
            out_specs=whole,
            scratch_shapes=[pltpu.VMEM((dir_count, dest_rows * 2 * source_count, lanes), jnp.float32)],
            compiler_params=pltpu.CompilerParams(vmem_limit_bytes=24 * 2**20),
            name="join_parts",
        )(parts, 1.0 - rims[:1])
    parts = parts.reshape((planes, dir_count) + message)
    main = parts[:, :, : 2 * dest_rows, :kf_dev].reshape(planes, dir_count, 2, dest_rows, kf_dev)
    over = parts[:, :, 2 * dest_rows :, :dest_rows].reshape(planes, dir_count, 2, 2 * rim, dest_rows)
    low = jnp.roll(over[:, :, :, :rim], -1, axis=1)
    high = jnp.roll(over[:, :, :, rim:], 1, axis=1)
    middle = jnp.zeros((planes, dir_count, 2, kf_dev - 2 * rim, dest_rows), jnp.float32)
    fix = jnp.concatenate([high, middle, low], axis=3)
    total = main.transpose(3, 2, 0, 1, 4) + fix.transpose(4, 2, 0, 1, 3)
    return total.reshape(result)


def solution(mesh):
    boxes, dirs = mesh.shape["box"], mesh.shape["dir"]
    fine_mesh = Mesh(mesh.devices.reshape(planes, boxes // planes, dirs), ("zed", "ring", "dir"))
    box = ("zed", "ring")
    placed = (
        P(box, None, None, "dir"),
        P(None, None, "dir"),
        P(box, None),
        P(box, None),
        P(box),
        P(box),
        P(box),
        P(),
        P(),
        P(),
    )
    return jax.shard_map(
        per_device,
        mesh=fine_mesh,
        in_specs=placed,
        out_specs=P(("zed", "ring", "dir"), None, None, None),
        check_vma=False,
    )
```

```python
import collections
import functools

import jax
import jax.numpy as jnp
from jax import lax
from jax.experimental import pallas as pl
from jax.experimental.pallas import tpu as pltpu
from jax.sharding import Mesh
from jax.sharding import PartitionSpec as P

wave_scale = 3.0
planes = 4
lanes = 128
half = 4
rim = 2
word_bits = 13
grain = 32


plan_fields = ["rows", "slots", "fine_rows", "stride", "width", "parent", "order", "turns"]
Plan = collections.namedtuple("Plan", plan_fields + ["together", "fixed", "group"])


def up(size, step):
    return -(-size // step) * step


def edge_bits(rows):
    bits = rows.bit_length() - 1
    return bits, [place for place in range(2, bits) if place % 2 == bits % 2]


def edge_rank(local, rows):
    bits, fixed = edge_bits(rows)
    rank = jnp.zeros_like(local)
    taken = 0
    for place in range(bits):
        if place not in fixed:
            rank = rank + (local // 2**place % 2) * 2**taken
            taken += 1
    return rank


def split(value):
    high = value.astype(jnp.bfloat16)
    low = (value - high.astype(jnp.float32)).astype(jnp.bfloat16)
    return high, low


def pack_kernel(source_count, note_count, zed, ring, field, *refs):
    notes, outs, whole = refs[:note_count], refs[note_count:-1], refs[-1]
    rows = field.shape[0]
    stride = 2 * source_count
    if len(outs) > planes:
        bits, fixed = edge_bits(rows)
        free = [place for place in range(bits) if place not in fixed]
        side = (1 - ring[0]) * sum(2**place for place in fixed)
        for index in range(outs[planes].shape[0]):
            base = sum((index // 2**order % 2) * 2**place for order, place in enumerate(free))
            outs[planes][index] = field[base + side]

    def row_step(row, unused):
        both = jnp.concatenate([field[row, 0], field[row, 1]], axis=0)
        for block in range(half):
            whole[block, pl.ds(pl.multiple_of(row * stride, stride), stride), :] = both[
                :, block * lanes : (block + 1) * lanes
            ]
        return unused

    lax.fori_loop(0, rows, row_step, 0, unroll=8)
    for step, out in enumerate(outs[:planes]):
        source = zed[0] ^ step
        for part in range(2):
            for block in range(half):
                out[pl.ds(part * half + block, rows, stride=2 * half), :] = whole[
                    block, pl.ds(part * source_count + source, rows, stride=stride), :
                ]
        for note in notes:
            out[rows * 2 * half :, :] = note[...]


def pack(here, field, notes, edge_rows):
    rows, _, source_count, width = field.shape
    length = rows * 2 * half + sum(note.shape[0] for note in notes)
    whole = pl.BlockSpec(memory_space=pltpu.VMEM)
    edges = [jax.ShapeDtypeStruct((edge_rows,) + field.shape[1:], jnp.float32)] if edge_rows else []
    return pl.pallas_call(
        functools.partial(pack_kernel, source_count, len(notes)),
        out_shape=[jax.ShapeDtypeStruct((length, lanes), jnp.float32)] * planes + edges,
        in_specs=[pl.BlockSpec(memory_space=pltpu.SMEM)] * 2 + [whole] * (1 + len(notes)),
        out_specs=[whole] * (planes + len(edges)),
        scratch_shapes=[pltpu.VMEM((half, rows * 2 * source_count, lanes), jnp.float32)],
        compiler_params=pltpu.CompilerParams(vmem_limit_bytes=24 * 2**20),
        name="pack_sources",
    )(*here, field, *notes)


def parts_of(word):
    return lax.shift_right_logical(word, word_bits), word & (2**word_bits - 1)


def tile(start):
    return pl.ds(pl.multiple_of(start, 2 * half), 2 * half)


def fine_kernel(plan, size, edge_size, zed, *refs):
    mains, refs = refs[:planes], refs[planes:]
    edges = refs[: planes if edge_size else 0]
    lists, refs = refs[len(edges)], refs[len(edges) + 1 :]
    table, phases, weights, out, rims, meta, field, moved, shifted, left, ready, landed, sems = refs
    rows, fine_rows = plan.rows, plan.fine_rows
    own = zed[0]

    def bring(step):
        return pltpu.make_async_copy(lists.at[step], meta.at[step % 2], sems.at[planes + step % 2])

    bring(0).start()
    incoming = []
    for index, edge in enumerate(edges):
        chosen = edge.at[pl.ds(0, edge_size * 2 * half)]
        incoming.append(pltpu.make_async_copy(chosen, landed.at[index], sems.at[planes + 2 + index]))
        incoming[-1].start()
    lane = lax.broadcasted_iota(jnp.int32, rims.shape, 1)
    rims[...] = ((lane < rim) | (lane >= lanes - rim)).astype(jnp.float32)

    def both(start):
        return pl.ds(pl.multiple_of(start, 4 * half), 4 * half)

    def with_turned(value):
        return jnp.concatenate([value, pltpu.roll(value, half, 0)], axis=0)

    for step, main in enumerate(mains):
        first = (own ^ step) * size

        def main_step(row, unused, first=first, main=main):
            field[both((first + row) * 4 * half), :] = with_turned(main[tile(row * 2 * half), :])
            return unused

        lax.fori_loop(0, size, main_step, 0, unroll=8)
    for index in range(len(edges)):
        first = planes * size + (own ^ index) * edge_size
        incoming[index].wait()

        def edge_step(row, unused, first=first, index=index):
            field[both((first + row) * 4 * half), :] = with_turned(landed[index, tile(row * 2 * half), :])
            return unused

        lax.fori_loop(0, edge_size, edge_step, 0, unroll=8)
    field[both(planes * (size + edge_size) * 4 * half), :] = jnp.zeros((4 * half, lanes), jnp.float32)

    blank = jnp.zeros((2 * half, lanes), jnp.float32)
    sub = lax.broadcasted_iota(jnp.int32, (2 * half, lanes), 0)
    dest_count = out.shape[1]
    dest_rows = fine_rows // dest_count

    def plane_step(turn, unused):
        plane = own ^ turn
        slot = turn % 2
        bring(turn).wait()

        @pl.when(turn + 1 < planes)
        def _():
            bring(turn + 1).start()

        across = lanes // plan.width

        def boxes_step(slot_count, step, unused):
            ranks = [step * plan.together + each for each in range(plan.together)]
            boxes = [meta[slot, plan.order, rank] for rank in ranks]
            sums = [[blank, blank] for box in boxes]
            for pair in range(slot_count):
                for each in range(plan.together):
                    row = step * (plan.together // across) + each // across
                    place, kind = parts_of(meta[slot, row, each % across * plan.width + pair])
                    value = field[both(place), :]
                    factor = table[tile(kind), :]
                    sums[each][0] += factor * value[: 2 * half]
                    sums[each][1] += factor * value[2 * half :]
            for each in range(plan.together):
                straight, crossed = sums[each]
                total = jnp.where(
                    sub < half,
                    straight + pltpu.roll(straight, half, 0),
                    pltpu.roll(crossed, half, 0) - crossed,
                )
                moved[both(boxes[each] * 4 * half), :] = with_turned(total)
            return unused

        start = 0
        for more in reversed(range((plan.slots - plan.fixed) // plan.group + 1)):
            end = meta[slot, plan.order, plan.turns + more]
            lax.fori_loop(start, end, functools.partial(boxes_step, plan.fixed + more * plan.group), 0)
            start = end

        def fine_step(block, unused):
            for each in range(lanes):
                parent, octant = parts_of(meta[slot, plan.parent + block, each])
                value = moved[both(parent), :] * phases[both(octant), :]
                shifted[tile((block * lanes + each) * 2 * half), :] = value[: 2 * half] + value[2 * half :]
            return unused

        lax.fori_loop(0, fine_rows // lanes, fine_step, 0)
        width = ready.shape[3]
        depth = half * lanes

        def split_step(chunk, unused):
            for part in range(2):
                rows_of = pl.ds(pl.multiple_of(part * fine_rows + chunk * grain, grain), grain)
                for block in range(half):
                    begin = chunk * grain * 2 * half + part * half + block
                    value = shifted[pl.ds(begin, grain, stride=2 * half), :]
                    high, low = split(value)
                    left[rows_of, block * lanes : (block + 1) * lanes] = high
                    left[rows_of, depth + block * lanes : depth + (block + 1) * lanes] = low
            return unused

        lax.fori_loop(0, fine_rows // grain, split_step, 0, unroll=2)
        result = jnp.dot(
            jnp.concatenate([left[:, :depth], left[...]], axis=1), weights[...], preferred_element_type=jnp.float32
        )
        for part in range(2):
            for dest in range(dest_count):
                start = part * fine_rows + dest * dest_rows
                ready[plane, dest, part * dest_rows : (part + 1) * dest_rows, :] = result[
                    start : start + dest_rows, :width
                ]
        spill = result[:fine_rows, width:] + pltpu.roll(result[fine_rows:, width:], half, 1)
        spill = spill.T[: 2 * half]
        for dest in range(dest_count):
            ready[plane, dest, 2 * dest_rows :, :] = jnp.concatenate(
                [
                    spill[:, dest * dest_rows : (dest + 1) * dest_rows],
                    jnp.zeros((2 * half, width - dest_rows), jnp.float32),
                ],
                axis=1,
            )
        pltpu.make_async_copy(ready.at[plane], out.at[plane], sems.at[plane]).start()
        return unused

    lax.fori_loop(0, planes, plane_step, 0)
    for plane in range(planes):
        pltpu.make_async_copy(ready.at[plane], out.at[plane], sems.at[plane]).wait()


def join_kernel(source_count, parts, rims, out, whole):
    dest_rows = out.shape[0]
    dirs = parts.shape[0] // source_count
    over = jnp.concatenate(
        [parts[index, 2 * dest_rows :, :lanes] for index in range(parts.shape[0])], axis=0
    ).T[:dest_rows]
    low = lax.broadcasted_iota(jnp.int32, (dest_rows, lanes), 1) < rim
    at_rim = jnp.broadcast_to(rims[...], (dest_rows, lanes)) < 0.5
    for source in range(source_count):
        for part in range(2):
            turned = []
            for index in range(dirs):
                first = (source * dirs + index) * 2 * half + part * half
                turned.append(pltpu.roll(over, (lanes - rim - first) % lanes, 1))
            for index in range(dirs):
                fix = jnp.where(at_rim, jnp.where(low, turned[index - 1], turned[(index + 1) % dirs]), 0.0)
                whole[
                    index, pl.ds(part * source_count + source, dest_rows, stride=2 * source_count), :
                ] = parts[source * dirs + index, part * dest_rows : (part + 1) * dest_rows, :] + fix

    def row_step(row, unused):
        start = pl.multiple_of(row * 2 * source_count, 2 * source_count)
        both = jnp.concatenate(
            [whole[index, pl.ds(start, 2 * source_count), :] for index in range(dirs)], axis=1
        )
        out[row, 0] = both[:source_count]
        out[row, 1] = both[source_count:]
        return unused

    lax.fori_loop(0, dest_rows, row_step, 0, unroll=8)


def per_device(
    coarse_field,
    trans_table,
    partner_ids,
    partner_types,
    partner_count,
    child_count,
    child_octant,
    dir_angles,
    stencil_ids,
    stencil_weights,
):
    rows, _, source_count, kc_dev = coarse_field.shape
    slots = partner_ids.shape[1]
    type_count = trans_table.shape[0]
    fine_rows = child_octant.shape[0]
    ring_count = lax.axis_size("ring")
    dir_count = lax.axis_size("dir")
    zed = lax.axis_index("zed")
    ring = lax.axis_index("ring")
    dir_index = lax.axis_index("dir")
    fine_count = stencil_ids.shape[0] // 4
    kf_dev = fine_count // dir_count
    kc_pad = up(kc_dev, half * lanes)
    kf_pad = up(kf_dev, lanes)
    pad_dirs = kc_pad - kc_dev
    assert source_count == planes and kc_pad == half * lanes
    dest_rows = fine_rows // dir_count

    field = jnp.pad(coarse_field, ((0, 0), (0, 0), (0, 0), (0, pad_dirs)))
    here = zed.reshape(1), ring.reshape(1)
    edge_rows = rows >> len(edge_bits(rows)[1]) if ring_count == 2 else 0
    packed = pack(here, field, [], edge_rows)
    if edge_rows:
        edges = lax.ppermute(packed[planes], "ring", [(0, 1), (1, 0)])

    def to_planes(note, step):
        if step == 0:
            return note
        return lax.ppermute(note, "zed", [(plane, plane ^ step) for plane in range(planes)])

    arrived = [to_planes(packed[step], step) for step in (3, 2, 1, 0)][::-1]

    plane_of = partner_ids // (ring_count * rows)
    ring_of = partner_ids // rows % ring_count
    local = partner_ids % rows
    live = jnp.arange(slots, dtype=jnp.int32)[None, :] < partner_count[:, None]
    if ring_count == 2:
        size = rows
        place = jnp.where(
            ring_of == ring,
            plane_of * rows + local,
            planes * rows + plane_of * edge_rows + edge_rank(local, rows),
        )
    else:
        size = ring_count * rows
        place = partner_ids
    field_rows = planes * (size + edge_rows)
    place = jnp.where(live, place, field_rows)
    together = 4
    fixed = slots // 2
    group = 5 if (slots - fixed) % 5 == 0 else 1
    index = jnp.arange(rows, dtype=jnp.int32)
    before = (partner_count[None, :] > partner_count[:, None]) | (
        (partner_count[None, :] == partner_count[:, None]) & (index[None, :] < index[:, None])
    )
    rank = jnp.sum(before.astype(jnp.int32), axis=1)
    at_rank = rank[None, :] == index[:, None]
    order = jnp.sum(jnp.where(at_rank, index[None, :], 0), axis=1)
    first = rank[None, :] == index[: rows // together, None] * together
    longest = jnp.sum(jnp.where(first, partner_count[None, :], 0), axis=1)
    turns = jnp.maximum((longest - fixed + group - 1) // group, 0)
    more = jnp.arange((slots - fixed) // group + 1, dtype=jnp.int32)
    ends = jnp.sum((turns[None, :] >= more[:, None]).astype(jnp.int32), axis=1)
    bounds = jnp.sum(jnp.where(index[None, :] <= index[:, None], child_count[None, :], 0), axis=1)
    parent = jnp.sum(
        (bounds[None, :] <= jnp.arange(fine_rows, dtype=jnp.int32)[:, None]).astype(jnp.int32), axis=1
    )
    def across(one, width=lanes):
        return jnp.pad(one, ((0, 0), (0, width - one.shape[1])))

    width = lanes // half
    turns_at = lanes // 2
    assert slots <= width and rows <= turns_at and fine_rows % lanes == 0
    assert (field_rows + 1) * 4 * half < 2 ** (31 - word_bits) and type_count * 2 * half < 2**word_bits

    in_order = jnp.dot(
        at_rank.astype(jnp.float32),
        jnp.concatenate([across(place * 4 * half, width), across(partner_types * 2 * half, width)], axis=1).astype(
            jnp.float32
        ),
        precision=lax.Precision.HIGHEST,
        preferred_element_type=jnp.float32,
    )

    def listed(side):
        return in_order[:, side * width : (side + 1) * width].reshape(rows * width // lanes, lanes)

    list_rows = rows * width // lanes
    fine_lists = fine_rows // lanes
    last = across(jnp.concatenate([across(order[None], turns_at), ends[None]], axis=1))
    stride = up(list_rows + fine_lists + 1, 8)

    def stacked(*parts):
        meta = jnp.concatenate([part.astype(jnp.float32) for part in parts])
        return jnp.pad(meta, ((0, stride - meta.shape[0]), (0, 0)))

    meta = jnp.concatenate(
        [
            stacked(listed(0), (parent * 4 * half).reshape(-1, lanes)),
            stacked(listed(1), (child_octant * 4 * half).reshape(-1, lanes), last),
        ]
    )
    plan = Plan(
        rows, slots, fine_rows, stride, width, list_rows, list_rows + fine_lists, turns_at, together, fixed, group
    )

    notes = pack(here, edges, [meta], 0) if edge_rows else [meta] * planes
    after_notes = lax.optimization_barrier((notes, trans_table, dir_angles, stencil_ids, stencil_weights))
    notes, trans_table, dir_angles, stencil_ids, stencil_weights = after_notes
    received = [to_planes(notes[step], step) for step in range(planes)]
    edge_part = edge_rows * 2 * half
    numbers = jnp.stack([note[edge_part:] for note in received]).astype(jnp.int32)
    meta = numbers[:, :stride] * 2**word_bits + numbers[:, stride:]
    if ring_count != 2:
        arrived = [lax.all_gather(one, "ring", axis=0, tiled=True) for one in arrived]
        received = []

    def blocks(table):
        return jnp.pad(table, ((0, 0), (0, pad_dirs))).reshape(-1, half, lanes)

    def doubled(table, sign):
        return jnp.concatenate([blocks(table), sign * blocks(table)], axis=1)

    table = jnp.pad(trans_table, ((0, 0), (0, 0), (0, pad_dirs))).reshape(-1, lanes)
    angles = lax.dynamic_slice_in_dim(dir_angles, dir_index * kc_dev, kc_dev, axis=1)
    octants = jnp.arange(8, dtype=jnp.int32)
    sign_x = 1.0 - 2.0 * (octants % 2).astype(jnp.float32)
    sign_y = 1.0 - 2.0 * (octants // 2 % 2).astype(jnp.float32)
    sign_z = 1.0 - 2.0 * (octants // 4).astype(jnp.float32)
    unit_x = jnp.sin(angles[0]) * jnp.cos(angles[1])
    unit_y = jnp.sin(angles[0]) * jnp.sin(angles[1])
    unit_z = jnp.cos(angles[0])
    phase = wave_scale * (
        sign_x[:, None] * unit_x[None, :] + sign_y[:, None] * unit_y[None, :] + sign_z[:, None] * unit_z[None, :]
    )
    phases = jnp.concatenate(
        [doubled(jnp.cos(phase), 1.0), doubled(jnp.sin(phase), -1.0)], axis=1
    ).reshape(-1, lanes)

    ids = lax.dynamic_slice_in_dim(stencil_ids, dir_index * kc_dev, kc_dev, axis=0).T
    weights = lax.dynamic_slice_in_dim(stencil_weights, dir_index * kc_dev, kc_dev, axis=0).T

    def interp(targets):
        matrix = jnp.zeros((targets.shape[0], kc_dev), jnp.float32)
        for point in range(ids.shape[0]):
            matrix = matrix + jnp.where(
                ids[point][None, :] == targets[:, None], weights[point][None, :], 0.0
            )
        return jnp.pad(matrix, ((0, 0), (0, pad_dirs)))

    first_fine = dir_index * kf_dev
    own = jnp.arange(kf_dev, dtype=jnp.int32)
    outside = jnp.concatenate(
        [jnp.arange(-rim, 0, dtype=jnp.int32), jnp.arange(kf_dev, kf_dev + rim, dtype=jnp.int32)]
    )
    matrix = jnp.pad(interp(first_fine + own), ((0, kf_pad - kf_dev), (0, 0)))
    spill = interp((first_fine + outside) % fine_count)
    matrices = jnp.concatenate([matrix, jnp.pad(spill, ((0, lanes - half), (0, 0)))], axis=0).T
    rounded = lax.reduce_precision(matrices, 8, 7)
    high = rounded.astype(jnp.bfloat16)
    low = (matrices - rounded).astype(jnp.bfloat16)
    passes = jnp.concatenate([low, high, high], axis=0)

    whole = pl.BlockSpec(memory_space=pltpu.VMEM)
    message = (2 * dest_rows + 2 * half, kf_pad)
    local_fine, rims = pl.pallas_call(
        functools.partial(fine_kernel, plan, size, edge_rows),
        out_shape=[
            pltpu.HBM((planes, dir_count) + message, jnp.float32),
            jax.ShapeDtypeStruct((2 * half, lanes), jnp.float32),
        ],
        in_specs=[pl.BlockSpec(memory_space=pltpu.SMEM)]
        + [whole] * planes
        + [pl.BlockSpec(memory_space=pl.ANY)] * (len(received) + 1)
        + [whole] * 3,
        out_specs=[pl.BlockSpec(memory_space=pltpu.HBM), whole],
        scratch_shapes=[
            pltpu.SMEM((2, plan.stride, lanes), jnp.int32),
            pltpu.VMEM(((field_rows + 1) * 4 * half, lanes), jnp.float32),
            pltpu.VMEM((rows * 4 * half, lanes), jnp.float32),
            pltpu.VMEM((fine_rows * 2 * half, lanes), jnp.float32),
            pltpu.VMEM((2 * fine_rows, 2 * kc_pad), jnp.bfloat16),
            pltpu.VMEM((planes, dir_count) + message, jnp.float32),
            pltpu.VMEM((planes, max(edge_rows, 1) * 2 * half, lanes), jnp.float32),
            pltpu.SemaphoreType.DMA((2 * planes + 2,)),
        ],
        compiler_params=pltpu.CompilerParams(vmem_limit_bytes=48 * 2**20),
        name="translate_and_interpolate",
    )(here[0], *arrived, *received, meta, table, phases, passes)

    parts = lax.all_to_all(
        local_fine.reshape((planes * dir_count,) + message),
        ("zed", "dir"),
        split_axis=0,
        concat_axis=0,
        tiled=True,
    )
    result = (dest_rows, 2, source_count, fine_count)
    if kf_dev == lanes and planes * dir_count * 2 * half == lanes and dest_rows <= lanes:
        return pl.pallas_call(
            functools.partial(join_kernel, source_count),
            out_shape=jax.ShapeDtypeStruct(result, jnp.float32),
            in_specs=[whole] * 2,
            out_specs=whole,
            scratch_shapes=[pltpu.VMEM((dir_count, dest_rows * 2 * source_count, lanes), jnp.float32)],
            compiler_params=pltpu.CompilerParams(vmem_limit_bytes=24 * 2**20),
            name="join_parts",
        )(parts, 1.0 - rims[:1])
    parts = parts.reshape((planes, dir_count) + message)
    main = parts[:, :, : 2 * dest_rows, :kf_dev].reshape(planes, dir_count, 2, dest_rows, kf_dev)
    over = parts[:, :, 2 * dest_rows :, :dest_rows].reshape(planes, dir_count, 2, 2 * rim, dest_rows)
    low = jnp.roll(over[:, :, :, :rim], -1, axis=1)
    high = jnp.roll(over[:, :, :, rim:], 1, axis=1)
    middle = jnp.zeros((planes, dir_count, 2, kf_dev - 2 * rim, dest_rows), jnp.float32)
    fix = jnp.concatenate([high, middle, low], axis=3)
    total = main.transpose(3, 2, 0, 1, 4) + fix.transpose(4, 2, 0, 1, 3)
    return total.reshape(result)


def solution(mesh):
    boxes, dirs = mesh.shape["box"], mesh.shape["dir"]
    fine_mesh = Mesh(mesh.devices.reshape(planes, boxes // planes, dirs), ("zed", "ring", "dir"))
    box = ("zed", "ring")
    placed = (
        P(box, None, None, "dir"),
        P(None, None, "dir"),
        P(box, None),
        P(box, None),
        P(box),
        P(box),
        P(box),
        P(),
        P(),
        P(),
    )
    return jax.shard_map(
        per_device,
        mesh=fine_mesh,
        in_specs=placed,
        out_specs=P(("zed", "ring", "dir"), None, None, None),
        check_vma=False,
    )
```

```python
import collections
import functools

import jax
import jax.numpy as jnp
from jax import lax
from jax.experimental import pallas as pl
from jax.experimental.pallas import tpu as pltpu
from jax.sharding import Mesh
from jax.sharding import PartitionSpec as P

wave_scale = 3.0
planes = 4
lanes = 128
half = 4
rim = 2
word_bits = 13


plan_fields = ["rows", "slots", "fine_rows", "stride", "width", "parent", "order", "turns"]
Plan = collections.namedtuple("Plan", plan_fields + ["together", "fixed", "group"])


def up(size, step):
    return -(-size // step) * step


def edge_bits(rows):
    bits = rows.bit_length() - 1
    return bits, [place for place in range(2, bits) if place % 2 == bits % 2]


def edge_rank(local, rows):
    bits, fixed = edge_bits(rows)
    rank = jnp.zeros_like(local)
    taken = 0
    for place in range(bits):
        if place not in fixed:
            rank = rank + (local // 2**place % 2) * 2**taken
            taken += 1
    return rank


def split(value):
    high = value.astype(jnp.bfloat16)
    low = (value - high.astype(jnp.float32)).astype(jnp.bfloat16)
    return high, low


def pack_kernel(source_count, note_count, zed, ring, field, *refs):
    notes, outs, whole = refs[:note_count], refs[note_count:-1], refs[-1]
    rows = field.shape[0]
    stride = 2 * source_count
    if len(outs) > planes:
        bits, fixed = edge_bits(rows)
        free = [place for place in range(bits) if place not in fixed]
        side = (1 - ring[0]) * sum(2**place for place in fixed)
        for index in range(outs[planes].shape[0]):
            base = sum((index // 2**order % 2) * 2**place for order, place in enumerate(free))
            outs[planes][index] = field[base + side]

    def row_step(row, unused):
        both = jnp.concatenate([field[row, 0], field[row, 1]], axis=0)
        for block in range(half):
            whole[block, pl.ds(pl.multiple_of(row * stride, stride), stride), :] = both[
                :, block * lanes : (block + 1) * lanes
            ]
        return unused

    lax.fori_loop(0, rows, row_step, 0, unroll=8)
    for step, out in enumerate(outs[:planes]):
        source = zed[0] ^ step
        for part in range(2):
            for block in range(half):
                out[pl.ds(part * half + block, rows, stride=2 * half), :] = whole[
                    block, pl.ds(part * source_count + source, rows, stride=stride), :
                ]
        for note in notes:
            out[rows * 2 * half :, :] = note[...]


def pack(here, field, notes, edge_rows):
    rows, _, source_count, width = field.shape
    length = rows * 2 * half + sum(note.shape[0] for note in notes)
    whole = pl.BlockSpec(memory_space=pltpu.VMEM)
    edges = [jax.ShapeDtypeStruct((edge_rows,) + field.shape[1:], jnp.float32)] if edge_rows else []
    return pl.pallas_call(
        functools.partial(pack_kernel, source_count, len(notes)),
        out_shape=[jax.ShapeDtypeStruct((length, lanes), jnp.float32)] * planes + edges,
        in_specs=[pl.BlockSpec(memory_space=pltpu.SMEM)] * 2 + [whole] * (1 + len(notes)),
        out_specs=[whole] * (planes + len(edges)),
        scratch_shapes=[pltpu.VMEM((half, rows * 2 * source_count, lanes), jnp.float32)],
        compiler_params=pltpu.CompilerParams(vmem_limit_bytes=24 * 2**20),
        name="pack_sources",
    )(*here, field, *notes)


def parts_of(word):
    return lax.shift_right_logical(word, word_bits), word & (2**word_bits - 1)


def tile(start):
    return pl.ds(pl.multiple_of(start, 2 * half), 2 * half)


def fine_kernel(plan, size, edge_size, zed, *refs):
    mains, refs = refs[:planes], refs[planes:]
    edges = refs[: planes if edge_size else 0]
    lists, refs = refs[len(edges)], refs[len(edges) + 1 :]
    table, phases, weights, out, rims, meta, field, moved, shifted, ready, landed, sems = refs
    rows, fine_rows = plan.rows, plan.fine_rows
    own = zed[0]

    def bring(step):
        return pltpu.make_async_copy(lists.at[step], meta.at[step % 2], sems.at[planes + step % 2])

    bring(0).start()
    incoming = []
    for index, edge in enumerate(edges):
        chosen = edge.at[pl.ds(0, edge_size * 2 * half)]
        incoming.append(pltpu.make_async_copy(chosen, landed.at[index], sems.at[planes + 2 + index]))
        incoming[-1].start()
    lane = lax.broadcasted_iota(jnp.int32, rims.shape, 1)
    rims[...] = ((lane < rim) | (lane >= lanes - rim)).astype(jnp.float32)

    def both(start):
        return pl.ds(pl.multiple_of(start, 4 * half), 4 * half)

    def with_turned(value):
        return jnp.concatenate([value, pltpu.roll(value, half, 0)], axis=0)

    for index, main in enumerate(mains):
        first = (own ^ (planes - 1 - index)) * size

        def main_step(row, unused, first=first, main=main):
            field[both((first + row) * 4 * half), :] = with_turned(main[tile(row * 2 * half), :])
            return unused

        lax.fori_loop(0, size, main_step, 0, unroll=8)
    for index in range(len(edges)):
        first = planes * size + (own ^ index) * edge_size
        incoming[index].wait()

        def edge_step(row, unused, first=first, index=index):
            field[both((first + row) * 4 * half), :] = with_turned(landed[index, tile(row * 2 * half), :])
            return unused

        lax.fori_loop(0, edge_size, edge_step, 0, unroll=8)
    field[both(planes * (size + edge_size) * 4 * half), :] = jnp.zeros((4 * half, lanes), jnp.float32)

    blank = jnp.zeros((2 * half, lanes), jnp.float32)
    sub = lax.broadcasted_iota(jnp.int32, (2 * half, lanes), 0)
    dest_count = out.shape[1]
    dest_rows = fine_rows // dest_count

    def plane_step(turn, unused):
        plane = own ^ turn
        slot = turn % 2
        bring(turn).wait()

        @pl.when(turn + 1 < planes)
        def _():
            bring(turn + 1).start()

        across = lanes // plan.width

        def boxes_step(slot_count, step, unused):
            ranks = [step * plan.together + each for each in range(plan.together)]
            boxes = [meta[slot, plan.order, rank] for rank in ranks]
            sums = [[blank, blank] for box in boxes]
            for pair in range(slot_count):
                for each in range(plan.together):
                    row = step * (plan.together // across) + each // across
                    place, kind = parts_of(meta[slot, row, each % across * plan.width + pair])
                    value = field[both(place), :]
                    factor = table[tile(kind), :]
                    sums[each][0] += factor * value[: 2 * half]
                    sums[each][1] += factor * value[2 * half :]
            for each in range(plan.together):
                straight, crossed = sums[each]
                total = jnp.where(
                    sub < half,
                    straight + pltpu.roll(straight, half, 0),
                    pltpu.roll(crossed, half, 0) - crossed,
                )
                moved[both(boxes[each] * 4 * half), :] = with_turned(total)
            return unused

        start = 0
        for more in reversed(range((plan.slots - plan.fixed) // plan.group + 1)):
            end = meta[slot, plan.order, plan.turns + more]
            lax.fori_loop(start, end, functools.partial(boxes_step, plan.fixed + more * plan.group), 0)
            start = end

        def fine_step(block, unused):
            for each in range(lanes):
                parent, octant = parts_of(meta[slot, plan.parent + block, each])
                value = moved[both(parent), :] * phases[both(octant), :]
                shifted[tile((block * lanes + each) * 2 * half), :] = value[: 2 * half] + value[2 * half :]
            return unused

        lax.fori_loop(0, fine_rows // lanes, fine_step, 0)
        width = ready.shape[3]
        left = jnp.concatenate(
            [
                jnp.concatenate(
                    [
                        shifted[pl.ds(part * half + block, fine_rows, stride=2 * half), :]
                        for block in range(half)
                    ],
                    axis=1,
                )
                for part in range(2)
            ],
            axis=0,
        )
        first, second = split(left)
        result = jnp.dot(
            jnp.concatenate([first, first, second], axis=1), weights[...], preferred_element_type=jnp.float32
        )
        for part in range(2):
            for dest in range(dest_count):
                start = part * fine_rows + dest * dest_rows
                ready[plane, dest, part * dest_rows : (part + 1) * dest_rows, :] = result[
                    start : start + dest_rows, :width
                ]
        spill = result[:fine_rows, width:] + pltpu.roll(result[fine_rows:, width:], half, 1)
        spill = spill.T[: 2 * half]
        for dest in range(dest_count):
            ready[plane, dest, 2 * dest_rows :, :] = jnp.concatenate(
                [
                    spill[:, dest * dest_rows : (dest + 1) * dest_rows],
                    jnp.zeros((2 * half, width - dest_rows), jnp.float32),
                ],
                axis=1,
            )
        pltpu.make_async_copy(ready.at[plane], out.at[plane], sems.at[plane]).start()
        return unused

    lax.fori_loop(0, planes, plane_step, 0)
    for plane in range(planes):
        pltpu.make_async_copy(ready.at[plane], out.at[plane], sems.at[plane]).wait()


def join_kernel(source_count, parts, rims, out, whole):
    dest_rows = out.shape[0]
    dirs = parts.shape[0] // source_count
    over = jnp.concatenate(
        [parts[index, 2 * dest_rows :, :lanes] for index in range(parts.shape[0])], axis=0
    ).T[:dest_rows]
    low = lax.broadcasted_iota(jnp.int32, (dest_rows, lanes), 1) < rim
    at_rim = jnp.broadcast_to(rims[...], (dest_rows, lanes)) < 0.5
    for source in range(source_count):
        for part in range(2):
            turned = []
            for index in range(dirs):
                first = (source * dirs + index) * 2 * half + part * half
                turned.append(pltpu.roll(over, (lanes - rim - first) % lanes, 1))
            for index in range(dirs):
                fix = jnp.where(at_rim, jnp.where(low, turned[index - 1], turned[(index + 1) % dirs]), 0.0)
                whole[
                    index, pl.ds(part * source_count + source, dest_rows, stride=2 * source_count), :
                ] = parts[source * dirs + index, part * dest_rows : (part + 1) * dest_rows, :] + fix

    def row_step(row, unused):
        start = pl.multiple_of(row * 2 * source_count, 2 * source_count)
        both = jnp.concatenate(
            [whole[index, pl.ds(start, 2 * source_count), :] for index in range(dirs)], axis=1
        )
        out[row, 0] = both[:source_count]
        out[row, 1] = both[source_count:]
        return unused

    lax.fori_loop(0, dest_rows, row_step, 0, unroll=8)


def per_device(
    coarse_field,
    trans_table,
    partner_ids,
    partner_types,
    partner_count,
    child_count,
    child_octant,
    dir_angles,
    stencil_ids,
    stencil_weights,
):
    rows, _, source_count, kc_dev = coarse_field.shape
    slots = partner_ids.shape[1]
    type_count = trans_table.shape[0]
    fine_rows = child_octant.shape[0]
    ring_count = lax.axis_size("ring")
    dir_count = lax.axis_size("dir")
    zed = lax.axis_index("zed")
    ring = lax.axis_index("ring")
    dir_index = lax.axis_index("dir")
    fine_count = stencil_ids.shape[0] // 4
    kf_dev = fine_count // dir_count
    kc_pad = up(kc_dev, half * lanes)
    kf_pad = up(kf_dev, lanes)
    pad_dirs = kc_pad - kc_dev
    assert source_count == planes and kc_pad == half * lanes
    dest_rows = fine_rows // dir_count

    field = jnp.pad(coarse_field, ((0, 0), (0, 0), (0, 0), (0, pad_dirs)))
    here = zed.reshape(1), ring.reshape(1)
    edge_rows = rows >> len(edge_bits(rows)[1]) if ring_count == 2 else 0
    packed = pack(here, field, [], edge_rows)
    if edge_rows:
        edges = lax.ppermute(packed[planes], "ring", [(0, 1), (1, 0)])

    def to_planes(note, step):
        if step == 0:
            return note
        return lax.ppermute(note, "zed", [(plane, plane ^ step) for plane in range(planes)])

    arrived = [to_planes(packed[step], step) for step in (3, 2, 1, 0)]

    plane_of = partner_ids // (ring_count * rows)
    ring_of = partner_ids // rows % ring_count
    local = partner_ids % rows
    live = jnp.arange(slots, dtype=jnp.int32)[None, :] < partner_count[:, None]
    if ring_count == 2:
        size = rows
        place = jnp.where(
            ring_of == ring,
            plane_of * rows + local,
            planes * rows + plane_of * edge_rows + edge_rank(local, rows),
        )
    else:
        size = ring_count * rows
        place = partner_ids
    field_rows = planes * (size + edge_rows)
    place = jnp.where(live, place, field_rows)
    together = 4
    fixed = slots // 2
    group = 3 if (slots - fixed) % 3 == 0 else 1
    index = jnp.arange(rows, dtype=jnp.int32)
    before = (partner_count[None, :] > partner_count[:, None]) | (
        (partner_count[None, :] == partner_count[:, None]) & (index[None, :] < index[:, None])
    )
    rank = jnp.sum(before.astype(jnp.int32), axis=1)
    at_rank = rank[None, :] == index[:, None]
    order = jnp.sum(jnp.where(at_rank, index[None, :], 0), axis=1)
    first = rank[None, :] == index[: rows // together, None] * together
    longest = jnp.sum(jnp.where(first, partner_count[None, :], 0), axis=1)
    turns = jnp.maximum((longest - fixed + group - 1) // group, 0)
    more = jnp.arange((slots - fixed) // group + 1, dtype=jnp.int32)
    ends = jnp.sum((turns[None, :] >= more[:, None]).astype(jnp.int32), axis=1)
    bounds = jnp.sum(jnp.where(index[None, :] <= index[:, None], child_count[None, :], 0), axis=1)
    parent = jnp.sum(
        (bounds[None, :] <= jnp.arange(fine_rows, dtype=jnp.int32)[:, None]).astype(jnp.int32), axis=1
    )
    def across(one, width=lanes):
        return jnp.pad(one, ((0, 0), (0, width - one.shape[1])))

    width = lanes // half
    turns_at = lanes // 2
    assert slots <= width and rows <= turns_at and fine_rows % lanes == 0
    assert (field_rows + 1) * 4 * half < 2 ** (31 - word_bits) and type_count * 2 * half < 2**word_bits

    in_order = jnp.dot(
        at_rank.astype(jnp.float32),
        jnp.concatenate([across(place * 4 * half, width), across(partner_types * 2 * half, width)], axis=1).astype(
            jnp.float32
        ),
        precision=lax.Precision.HIGHEST,
        preferred_element_type=jnp.float32,
    )

    def listed(side):
        return in_order[:, side * width : (side + 1) * width].reshape(rows * width // lanes, lanes)

    list_rows = rows * width // lanes
    fine_lists = fine_rows // lanes
    last = across(jnp.concatenate([across(order[None], turns_at), ends[None]], axis=1))
    stride = up(list_rows + fine_lists + 1, 8)

    def stacked(*parts):
        meta = jnp.concatenate([part.astype(jnp.float32) for part in parts])
        return jnp.pad(meta, ((0, stride - meta.shape[0]), (0, 0)))

    meta = jnp.concatenate(
        [
            stacked(listed(0), (parent * 4 * half).reshape(-1, lanes)),
            stacked(listed(1), (child_octant * 4 * half).reshape(-1, lanes), last),
        ]
    )
    plan = Plan(
        rows, slots, fine_rows, stride, width, list_rows, list_rows + fine_lists, turns_at, together, fixed, group
    )

    notes = pack(here, edges, [meta], 0) if edge_rows else [meta] * planes
    after_notes = lax.optimization_barrier((notes, trans_table, dir_angles, stencil_ids, stencil_weights))
    notes, trans_table, dir_angles, stencil_ids, stencil_weights = after_notes
    received = [to_planes(notes[step], step) for step in range(planes)]
    edge_part = edge_rows * 2 * half
    numbers = jnp.stack([note[edge_part:] for note in received]).astype(jnp.int32)
    meta = numbers[:, :stride] * 2**word_bits + numbers[:, stride:]
    if ring_count != 2:
        arrived = [lax.all_gather(one, "ring", axis=0, tiled=True) for one in arrived]
        received = []

    def blocks(table):
        return jnp.pad(table, ((0, 0), (0, pad_dirs))).reshape(-1, half, lanes)

    def doubled(table, sign):
        return jnp.concatenate([blocks(table), sign * blocks(table)], axis=1)

    table = jnp.pad(trans_table, ((0, 0), (0, 0), (0, pad_dirs))).reshape(-1, lanes)
    angles = lax.dynamic_slice_in_dim(dir_angles, dir_index * kc_dev, kc_dev, axis=1)
    octants = jnp.arange(8, dtype=jnp.int32)
    sign_x = 1.0 - 2.0 * (octants % 2).astype(jnp.float32)
    sign_y = 1.0 - 2.0 * (octants // 2 % 2).astype(jnp.float32)
    sign_z = 1.0 - 2.0 * (octants // 4).astype(jnp.float32)
    unit_x = jnp.sin(angles[0]) * jnp.cos(angles[1])
    unit_y = jnp.sin(angles[0]) * jnp.sin(angles[1])
    unit_z = jnp.cos(angles[0])
    phase = wave_scale * (
        sign_x[:, None] * unit_x[None, :] + sign_y[:, None] * unit_y[None, :] + sign_z[:, None] * unit_z[None, :]
    )
    phases = jnp.concatenate(
        [doubled(jnp.cos(phase), 1.0), doubled(jnp.sin(phase), -1.0)], axis=1
    ).reshape(-1, lanes)

    ids = lax.dynamic_slice_in_dim(stencil_ids, dir_index * kc_dev, kc_dev, axis=0).T
    weights = lax.dynamic_slice_in_dim(stencil_weights, dir_index * kc_dev, kc_dev, axis=0).T

    def interp(targets):
        matrix = jnp.zeros((targets.shape[0], kc_dev), jnp.float32)
        for point in range(ids.shape[0]):
            matrix = matrix + jnp.where(
                ids[point][None, :] == targets[:, None], weights[point][None, :], 0.0
            )
        return jnp.pad(matrix, ((0, 0), (0, pad_dirs)))

    first_fine = dir_index * kf_dev
    own = jnp.arange(kf_dev, dtype=jnp.int32)
    outside = jnp.concatenate(
        [jnp.arange(-rim, 0, dtype=jnp.int32), jnp.arange(kf_dev, kf_dev + rim, dtype=jnp.int32)]
    )
    matrix = jnp.pad(interp(first_fine + own), ((0, kf_pad - kf_dev), (0, 0)))
    spill = interp((first_fine + outside) % fine_count)
    matrices = jnp.concatenate([matrix, jnp.pad(spill, ((0, lanes - half), (0, 0)))], axis=0).T
    rounded = lax.reduce_precision(matrices, 8, 7)
    high = rounded.astype(jnp.bfloat16)
    low = (matrices - rounded).astype(jnp.bfloat16)
    passes = jnp.concatenate([high, low, high], axis=0)

    whole = pl.BlockSpec(memory_space=pltpu.VMEM)
    message = (2 * dest_rows + 2 * half, kf_pad)
    local_fine, rims = pl.pallas_call(
        functools.partial(fine_kernel, plan, size, edge_rows),
        out_shape=[
            pltpu.HBM((planes, dir_count) + message, jnp.float32),
            jax.ShapeDtypeStruct((2 * half, lanes), jnp.float32),
        ],
        in_specs=[pl.BlockSpec(memory_space=pltpu.SMEM)]
        + [whole] * planes
        + [pl.BlockSpec(memory_space=pl.ANY)] * (len(received) + 1)
        + [whole] * 3,
        out_specs=[pl.BlockSpec(memory_space=pltpu.HBM), whole],
        scratch_shapes=[
            pltpu.SMEM((2, plan.stride, lanes), jnp.int32),
            pltpu.VMEM(((field_rows + 1) * 4 * half, lanes), jnp.float32),
            pltpu.VMEM((rows * 4 * half, lanes), jnp.float32),
            pltpu.VMEM((fine_rows * 2 * half, lanes), jnp.float32),
            pltpu.VMEM((planes, dir_count) + message, jnp.float32),
            pltpu.VMEM((planes, max(edge_rows, 1) * 2 * half, lanes), jnp.float32),
            pltpu.SemaphoreType.DMA((2 * planes + 2,)),
        ],
        compiler_params=pltpu.CompilerParams(vmem_limit_bytes=24 * 2**20),
        name="translate_and_interpolate",
    )(here[0], *arrived, *received, meta, table, phases, passes)

    parts = lax.all_to_all(
        local_fine.reshape((planes * dir_count,) + message),
        ("zed", "dir"),
        split_axis=0,
        concat_axis=0,
        tiled=True,
    )
    result = (dest_rows, 2, source_count, fine_count)
    if kf_dev == lanes and planes * dir_count * 2 * half == lanes and dest_rows <= lanes:
        return pl.pallas_call(
            functools.partial(join_kernel, source_count),
            out_shape=jax.ShapeDtypeStruct(result, jnp.float32),
            in_specs=[whole] * 2,
            out_specs=whole,
            scratch_shapes=[pltpu.VMEM((dir_count, dest_rows * 2 * source_count, lanes), jnp.float32)],
            compiler_params=pltpu.CompilerParams(vmem_limit_bytes=24 * 2**20),
            name="join_parts",
        )(parts, 1.0 - rims[:1])
    parts = parts.reshape((planes, dir_count) + message)
    main = parts[:, :, : 2 * dest_rows, :kf_dev].reshape(planes, dir_count, 2, dest_rows, kf_dev)
    over = parts[:, :, 2 * dest_rows :, :dest_rows].reshape(planes, dir_count, 2, 2 * rim, dest_rows)
    low = jnp.roll(over[:, :, :, :rim], -1, axis=1)
    high = jnp.roll(over[:, :, :, rim:], 1, axis=1)
    middle = jnp.zeros((planes, dir_count, 2, kf_dev - 2 * rim, dest_rows), jnp.float32)
    fix = jnp.concatenate([high, middle, low], axis=3)
    total = main.transpose(3, 2, 0, 1, 4) + fix.transpose(4, 2, 0, 1, 3)
    return total.reshape(result)


def solution(mesh):
    boxes, dirs = mesh.shape["box"], mesh.shape["dir"]
    fine_mesh = Mesh(mesh.devices.reshape(planes, boxes // planes, dirs), ("zed", "ring", "dir"))
    box = ("zed", "ring")
    placed = (
        P(box, None, None, "dir"),
        P(None, None, "dir"),
        P(box, None),
        P(box, None),
        P(box),
        P(box),
        P(box),
        P(),
        P(),
        P(),
    )
    return jax.shard_map(
        per_device,
        mesh=fine_mesh,
        in_specs=placed,
        out_specs=P(("zed", "ring", "dir"), None, None, None),
        check_vma=False,
    )
```

```python
import collections
import functools

import jax
import jax.numpy as jnp
from jax import lax
from jax.experimental import pallas as pl
from jax.experimental.pallas import tpu as pltpu
from jax.sharding import Mesh
from jax.sharding import PartitionSpec as P

wave_scale = 3.0
planes = 4
lanes = 128
half = 4
rim = 2
word_bits = 13


plan_fields = ["rows", "slots", "fine_rows", "stride", "width", "parent", "order", "turns"]
Plan = collections.namedtuple("Plan", plan_fields + ["together", "fixed", "group"])


def up(size, step):
    return -(-size // step) * step


def edge_bits(rows):
    bits = rows.bit_length() - 1
    return bits, [place for place in range(2, bits) if place % 2 == bits % 2]


def edge_rank(local, rows):
    bits, fixed = edge_bits(rows)
    rank = jnp.zeros_like(local)
    taken = 0
    for place in range(bits):
        if place not in fixed:
            rank = rank + (local // 2**place % 2) * 2**taken
            taken += 1
    return rank


def split(value):
    high = value.astype(jnp.bfloat16)
    low = (value - high.astype(jnp.float32)).astype(jnp.bfloat16)
    return high, low


def pack_kernel(source_count, note_count, zed, ring, field, *refs):
    notes, outs, whole = refs[:note_count], refs[note_count:-1], refs[-1]
    rows = field.shape[0]
    stride = 2 * source_count
    if len(outs) > planes:
        bits, fixed = edge_bits(rows)
        free = [place for place in range(bits) if place not in fixed]
        side = (1 - ring[0]) * sum(2**place for place in fixed)
        for index in range(outs[planes].shape[0]):
            base = sum((index // 2**order % 2) * 2**place for order, place in enumerate(free))
            outs[planes][index] = field[base + side]

    def row_step(row, unused):
        both = jnp.concatenate([field[row, 0], field[row, 1]], axis=0)
        for block in range(half):
            whole[block, pl.ds(pl.multiple_of(row * stride, stride), stride), :] = both[
                :, block * lanes : (block + 1) * lanes
            ]
        return unused

    lax.fori_loop(0, rows, row_step, 0, unroll=8)
    for step, out in enumerate(outs[:planes]):
        source = zed[0] ^ step
        for part in range(2):
            for block in range(half):
                out[pl.ds(part * half + block, rows, stride=2 * half), :] = whole[
                    block, pl.ds(part * source_count + source, rows, stride=stride), :
                ]
        for note in notes:
            out[rows * 2 * half :, :] = note[...]


def pack(here, field, notes, edge_rows):
    rows, _, source_count, width = field.shape
    length = rows * 2 * half + sum(note.shape[0] for note in notes)
    whole = pl.BlockSpec(memory_space=pltpu.VMEM)
    edges = [jax.ShapeDtypeStruct((edge_rows,) + field.shape[1:], jnp.float32)] if edge_rows else []
    return pl.pallas_call(
        functools.partial(pack_kernel, source_count, len(notes)),
        out_shape=[jax.ShapeDtypeStruct((length, lanes), jnp.float32)] * planes + edges,
        in_specs=[pl.BlockSpec(memory_space=pltpu.SMEM)] * 2 + [whole] * (1 + len(notes)),
        out_specs=[whole] * (planes + len(edges)),
        scratch_shapes=[pltpu.VMEM((half, rows * 2 * source_count, lanes), jnp.float32)],
        compiler_params=pltpu.CompilerParams(vmem_limit_bytes=24 * 2**20),
        name="pack_sources",
    )(*here, field, *notes)


def parts_of(word):
    return lax.shift_right_logical(word, word_bits), word & (2**word_bits - 1)


def tile(start):
    return pl.ds(pl.multiple_of(start, 2 * half), 2 * half)


def fine_kernel(plan, size, edge_size, zed, *refs):
    mains, refs = refs[:planes], refs[planes:]
    edges = refs[: planes if edge_size else 0]
    lists, refs = refs[len(edges)], refs[len(edges) + 1 :]
    table, phases, weights, out, rims, meta, field, moved, shifted, ready, landed, sems = refs
    rows, fine_rows = plan.rows, plan.fine_rows
    own = zed[0]

    def bring(step):
        return pltpu.make_async_copy(lists.at[step], meta.at[step % 2], sems.at[planes + step % 2])

    bring(0).start()
    incoming = []
    for index, edge in enumerate(edges):
        chosen = edge.at[pl.ds(0, edge_size * 2 * half)]
        incoming.append(pltpu.make_async_copy(chosen, landed.at[index], sems.at[planes + 2 + index]))
        incoming[-1].start()
    lane = lax.broadcasted_iota(jnp.int32, rims.shape, 1)
    rims[...] = ((lane < rim) | (lane >= lanes - rim)).astype(jnp.float32)

    def both(start):
        return pl.ds(pl.multiple_of(start, 4 * half), 4 * half)

    def with_turned(value):
        return jnp.concatenate([value, pltpu.roll(value, half, 0)], axis=0)

    for index, main in enumerate(mains):
        first = (own ^ (planes - 1 - index)) * size

        def main_step(row, unused, first=first, main=main):
            field[both((first + row) * 4 * half), :] = with_turned(main[tile(row * 2 * half), :])
            return unused

        lax.fori_loop(0, size, main_step, 0, unroll=8)
    for index in range(len(edges)):
        first = planes * size + (own ^ index) * edge_size
        incoming[index].wait()

        def edge_step(row, unused, first=first, index=index):
            field[both((first + row) * 4 * half), :] = with_turned(landed[index, tile(row * 2 * half), :])
            return unused

        lax.fori_loop(0, edge_size, edge_step, 0, unroll=8)
    field[both(planes * (size + edge_size) * 4 * half), :] = jnp.zeros((4 * half, lanes), jnp.float32)

    blank = jnp.zeros((2 * half, lanes), jnp.float32)
    sub = lax.broadcasted_iota(jnp.int32, (2 * half, lanes), 0)
    dest_count = out.shape[1]
    dest_rows = fine_rows // dest_count

    def plane_step(turn, unused):
        plane = own ^ turn
        slot = turn % 2
        bring(turn).wait()

        @pl.when(turn + 1 < planes)
        def _():
            bring(turn + 1).start()

        across = lanes // plan.width

        def boxes_step(slot_count, step, unused):
            ranks = [step * plan.together + each for each in range(plan.together)]
            boxes = [meta[slot, plan.order, rank] for rank in ranks]
            sums = [[blank, blank] for box in boxes]
            for pair in range(slot_count):
                for each in range(plan.together):
                    row = step * (plan.together // across) + each // across
                    place, kind = parts_of(meta[slot, row, each % across * plan.width + pair])
                    value = field[both(place), :]
                    factor = table[tile(kind), :]
                    sums[each][0] += factor * value[: 2 * half]
                    sums[each][1] += factor * value[2 * half :]
            for each in range(plan.together):
                straight, crossed = sums[each]
                total = jnp.where(
                    sub < half,
                    straight + pltpu.roll(straight, half, 0),
                    pltpu.roll(crossed, half, 0) - crossed,
                )
                moved[both(boxes[each] * 4 * half), :] = with_turned(total)
            return unused

        start = 0
        for more in reversed(range((plan.slots - plan.fixed) // plan.group + 1)):
            end = meta[slot, plan.order, plan.turns + more]
            lax.fori_loop(start, end, functools.partial(boxes_step, plan.fixed + more * plan.group), 0)
            start = end

        def fine_step(block, unused):
            for each in range(lanes):
                parent, octant = parts_of(meta[slot, plan.parent + block, each])
                value = moved[both(parent), :] * phases[both(octant), :]
                shifted[tile((block * lanes + each) * 2 * half), :] = value[: 2 * half] + value[2 * half :]
            return unused

        lax.fori_loop(0, fine_rows // lanes, fine_step, 0)
        width = ready.shape[3]
        left = jnp.concatenate(
            [
                jnp.concatenate(
                    [
                        shifted[pl.ds(part * half + block, fine_rows, stride=2 * half), :]
                        for block in range(half)
                    ],
                    axis=1,
                )
                for part in range(2)
            ],
            axis=0,
        )
        first, second = split(left)
        result = jnp.dot(
            jnp.concatenate([first, first, second], axis=1), weights[...], preferred_element_type=jnp.float32
        )
        for part in range(2):
            for dest in range(dest_count):
                start = part * fine_rows + dest * dest_rows
                ready[plane, dest, part * dest_rows : (part + 1) * dest_rows, :] = result[
                    start : start + dest_rows, :width
                ]
        spill = result[:fine_rows, width:] + pltpu.roll(result[fine_rows:, width:], half, 1)
        spill = spill.T[: 2 * half]
        for dest in range(dest_count):
            ready[plane, dest, 2 * dest_rows :, :] = jnp.concatenate(
                [
                    spill[:, dest * dest_rows : (dest + 1) * dest_rows],
                    jnp.zeros((2 * half, width - dest_rows), jnp.float32),
                ],
                axis=1,
            )
        pltpu.make_async_copy(ready.at[plane], out.at[plane], sems.at[plane]).start()
        return unused

    lax.fori_loop(0, planes, plane_step, 0)
    for plane in range(planes):
        pltpu.make_async_copy(ready.at[plane], out.at[plane], sems.at[plane]).wait()


def join_kernel(source_count, parts, rims, out, whole):
    dest_rows = out.shape[0]
    dirs = parts.shape[0] // source_count
    over = jnp.concatenate(
        [parts[index, 2 * dest_rows :, :lanes] for index in range(parts.shape[0])], axis=0
    ).T[:dest_rows]
    low = lax.broadcasted_iota(jnp.int32, (dest_rows, lanes), 1) < rim
    at_rim = jnp.broadcast_to(rims[...], (dest_rows, lanes)) < 0.5
    for source in range(source_count):
        for part in range(2):
            turned = []
            for index in range(dirs):
                first = (source * dirs + index) * 2 * half + part * half
                turned.append(pltpu.roll(over, (lanes - rim - first) % lanes, 1))
            for index in range(dirs):
                fix = jnp.where(at_rim, jnp.where(low, turned[index - 1], turned[(index + 1) % dirs]), 0.0)
                whole[
                    index, pl.ds(part * source_count + source, dest_rows, stride=2 * source_count), :
                ] = parts[source * dirs + index, part * dest_rows : (part + 1) * dest_rows, :] + fix

    def row_step(row, unused):
        start = pl.multiple_of(row * 2 * source_count, 2 * source_count)
        both = jnp.concatenate(
            [whole[index, pl.ds(start, 2 * source_count), :] for index in range(dirs)], axis=1
        )
        out[row, 0] = both[:source_count]
        out[row, 1] = both[source_count:]
        return unused

    lax.fori_loop(0, dest_rows, row_step, 0, unroll=8)


def per_device(
    coarse_field,
    trans_table,
    partner_ids,
    partner_types,
    partner_count,
    child_count,
    child_octant,
    dir_angles,
    stencil_ids,
    stencil_weights,
):
    rows, _, source_count, kc_dev = coarse_field.shape
    slots = partner_ids.shape[1]
    type_count = trans_table.shape[0]
    fine_rows = child_octant.shape[0]
    ring_count = lax.axis_size("ring")
    dir_count = lax.axis_size("dir")
    zed = lax.axis_index("zed")
    ring = lax.axis_index("ring")
    dir_index = lax.axis_index("dir")
    fine_count = stencil_ids.shape[0] // 4
    kf_dev = fine_count // dir_count
    kc_pad = up(kc_dev, half * lanes)
    kf_pad = up(kf_dev, lanes)
    pad_dirs = kc_pad - kc_dev
    assert source_count == planes and kc_pad == half * lanes
    dest_rows = fine_rows // dir_count

    field = jnp.pad(coarse_field, ((0, 0), (0, 0), (0, 0), (0, pad_dirs)))
    here = zed.reshape(1), ring.reshape(1)
    edge_rows = rows >> len(edge_bits(rows)[1]) if ring_count == 2 else 0
    packed = pack(here, field, [], edge_rows)
    if edge_rows:
        edges = lax.ppermute(packed[planes], "ring", [(0, 1), (1, 0)])

    def to_planes(note, step):
        if step == 0:
            return note
        return lax.ppermute(note, "zed", [(plane, plane ^ step) for plane in range(planes)])

    arrived = [to_planes(packed[step], step) for step in (3, 2, 1, 0)]

    plane_of = partner_ids // (ring_count * rows)
    ring_of = partner_ids // rows % ring_count
    local = partner_ids % rows
    live = jnp.arange(slots, dtype=jnp.int32)[None, :] < partner_count[:, None]
    if ring_count == 2:
        size = rows
        place = jnp.where(
            ring_of == ring,
            plane_of * rows + local,
            planes * rows + plane_of * edge_rows + edge_rank(local, rows),
        )
    else:
        size = ring_count * rows
        place = partner_ids
    field_rows = planes * (size + edge_rows)
    place = jnp.where(live, place, field_rows)
    together = 4
    fixed = slots // 2
    group = 3 if (slots - fixed) % 3 == 0 else 1
    index = jnp.arange(rows, dtype=jnp.int32)
    before = (partner_count[None, :] > partner_count[:, None]) | (
        (partner_count[None, :] == partner_count[:, None]) & (index[None, :] < index[:, None])
    )
    rank = jnp.sum(before.astype(jnp.int32), axis=1)
    at_rank = rank[None, :] == index[:, None]
    order = jnp.sum(jnp.where(at_rank, index[None, :], 0), axis=1)
    first = rank[None, :] == index[: rows // together, None] * together
    longest = jnp.sum(jnp.where(first, partner_count[None, :], 0), axis=1)
    turns = jnp.maximum((longest - fixed + group - 1) // group, 0)
    more = jnp.arange((slots - fixed) // group + 1, dtype=jnp.int32)
    ends = jnp.sum((turns[None, :] >= more[:, None]).astype(jnp.int32), axis=1)
    bounds = jnp.sum(jnp.where(index[None, :] <= index[:, None], child_count[None, :], 0), axis=1)
    parent = jnp.sum(
        (bounds[None, :] <= jnp.arange(fine_rows, dtype=jnp.int32)[:, None]).astype(jnp.int32), axis=1
    )
    def across(one, width=lanes):
        return jnp.pad(one, ((0, 0), (0, width - one.shape[1])))

    width = lanes // half
    turns_at = lanes // 2
    assert slots <= width and rows <= turns_at and fine_rows % lanes == 0
    assert (field_rows + 1) * 4 * half < 2 ** (31 - word_bits) and type_count * 2 * half < 2**word_bits

    in_order = jnp.dot(
        at_rank.astype(jnp.float32),
        jnp.concatenate([across(place * 4 * half, width), across(partner_types * 2 * half, width)], axis=1).astype(
            jnp.float32
        ),
        precision=lax.Precision.HIGHEST,
        preferred_element_type=jnp.float32,
    )

    def listed(side):
        return in_order[:, side * width : (side + 1) * width].reshape(rows * width // lanes, lanes)

    list_rows = rows * width // lanes
    fine_lists = fine_rows // lanes
    last = across(jnp.concatenate([across(order[None], turns_at), ends[None]], axis=1))
    stride = up(list_rows + fine_lists + 1, 8)

    def stacked(*parts):
        meta = jnp.concatenate([part.astype(jnp.float32) for part in parts])
        return jnp.pad(meta, ((0, stride - meta.shape[0]), (0, 0)))

    meta = jnp.concatenate(
        [
            stacked(listed(0), (parent * 4 * half).reshape(-1, lanes)),
            stacked(listed(1), (child_octant * 4 * half).reshape(-1, lanes), last),
        ]
    )
    plan = Plan(
        rows, slots, fine_rows, stride, width, list_rows, list_rows + fine_lists, turns_at, together, fixed, group
    )

    notes = pack(here, edges, [meta], 0) if edge_rows else [meta] * planes
    received = [to_planes(notes[step], step) for step in range(planes)]
    near, trans_table, dir_angles, stencil_ids, stencil_weights = lax.optimization_barrier(
        (received[1], trans_table, dir_angles, stencil_ids, stencil_weights)
    )
    received[1] = near
    edge_part = edge_rows * 2 * half
    numbers = jnp.stack([note[edge_part:] for note in received]).astype(jnp.int32)
    meta = numbers[:, :stride] * 2**word_bits + numbers[:, stride:]
    if ring_count != 2:
        arrived = [lax.all_gather(one, "ring", axis=0, tiled=True) for one in arrived]
        received = []

    def blocks(table):
        return jnp.pad(table, ((0, 0), (0, pad_dirs))).reshape(-1, half, lanes)

    def doubled(table, sign):
        return jnp.concatenate([blocks(table), sign * blocks(table)], axis=1)

    table = jnp.pad(trans_table, ((0, 0), (0, 0), (0, pad_dirs))).reshape(-1, lanes)
    angles = lax.dynamic_slice_in_dim(dir_angles, dir_index * kc_dev, kc_dev, axis=1)
    octants = jnp.arange(8, dtype=jnp.int32)
    sign_x = 1.0 - 2.0 * (octants % 2).astype(jnp.float32)
    sign_y = 1.0 - 2.0 * (octants // 2 % 2).astype(jnp.float32)
    sign_z = 1.0 - 2.0 * (octants // 4).astype(jnp.float32)
    unit_x = jnp.sin(angles[0]) * jnp.cos(angles[1])
    unit_y = jnp.sin(angles[0]) * jnp.sin(angles[1])
    unit_z = jnp.cos(angles[0])
    phase = wave_scale * (
        sign_x[:, None] * unit_x[None, :] + sign_y[:, None] * unit_y[None, :] + sign_z[:, None] * unit_z[None, :]
    )
    phases = jnp.concatenate(
        [doubled(jnp.cos(phase), 1.0), doubled(jnp.sin(phase), -1.0)], axis=1
    ).reshape(-1, lanes)

    ids = lax.dynamic_slice_in_dim(stencil_ids, dir_index * kc_dev, kc_dev, axis=0).T
    weights = lax.dynamic_slice_in_dim(stencil_weights, dir_index * kc_dev, kc_dev, axis=0).T

    def interp(targets):
        matrix = jnp.zeros((targets.shape[0], kc_dev), jnp.float32)
        for point in range(ids.shape[0]):
            matrix = matrix + jnp.where(
                ids[point][None, :] == targets[:, None], weights[point][None, :], 0.0
            )
        return jnp.pad(matrix, ((0, 0), (0, pad_dirs)))

    first_fine = dir_index * kf_dev
    own = jnp.arange(kf_dev, dtype=jnp.int32)
    outside = jnp.concatenate(
        [jnp.arange(-rim, 0, dtype=jnp.int32), jnp.arange(kf_dev, kf_dev + rim, dtype=jnp.int32)]
    )
    matrix = jnp.pad(interp(first_fine + own), ((0, kf_pad - kf_dev), (0, 0)))
    spill = interp((first_fine + outside) % fine_count)
    matrices = jnp.concatenate([matrix, jnp.pad(spill, ((0, lanes - half), (0, 0)))], axis=0).T
    rounded = lax.reduce_precision(matrices, 8, 7)
    high = rounded.astype(jnp.bfloat16)
    low = (matrices - rounded).astype(jnp.bfloat16)
    passes = jnp.concatenate([high, low, high], axis=0)

    whole = pl.BlockSpec(memory_space=pltpu.VMEM)
    message = (2 * dest_rows + 2 * half, kf_pad)
    local_fine, rims = pl.pallas_call(
        functools.partial(fine_kernel, plan, size, edge_rows),
        out_shape=[
            pltpu.HBM((planes, dir_count) + message, jnp.float32),
            jax.ShapeDtypeStruct((2 * half, lanes), jnp.float32),
        ],
        in_specs=[pl.BlockSpec(memory_space=pltpu.SMEM)]
        + [whole] * planes
        + [pl.BlockSpec(memory_space=pl.ANY)] * (len(received) + 1)
        + [whole] * 3,
        out_specs=[pl.BlockSpec(memory_space=pltpu.HBM), whole],
        scratch_shapes=[
            pltpu.SMEM((2, plan.stride, lanes), jnp.int32),
            pltpu.VMEM(((field_rows + 1) * 4 * half, lanes), jnp.float32),
            pltpu.VMEM((rows * 4 * half, lanes), jnp.float32),
            pltpu.VMEM((fine_rows * 2 * half, lanes), jnp.float32),
            pltpu.VMEM((planes, dir_count) + message, jnp.float32),
            pltpu.VMEM((planes, max(edge_rows, 1) * 2 * half, lanes), jnp.float32),
            pltpu.SemaphoreType.DMA((2 * planes + 2,)),
        ],
        compiler_params=pltpu.CompilerParams(vmem_limit_bytes=24 * 2**20),
        name="translate_and_interpolate",
    )(here[0], *arrived, *received, meta, table, phases, passes)

    parts = lax.all_to_all(
        local_fine.reshape((planes * dir_count,) + message),
        ("zed", "dir"),
        split_axis=0,
        concat_axis=0,
        tiled=True,
    )
    result = (dest_rows, 2, source_count, fine_count)
    if kf_dev == lanes and planes * dir_count * 2 * half == lanes and dest_rows <= lanes:
        return pl.pallas_call(
            functools.partial(join_kernel, source_count),
            out_shape=jax.ShapeDtypeStruct(result, jnp.float32),
            in_specs=[whole] * 2,
            out_specs=whole,
            scratch_shapes=[pltpu.VMEM((dir_count, dest_rows * 2 * source_count, lanes), jnp.float32)],
            compiler_params=pltpu.CompilerParams(vmem_limit_bytes=24 * 2**20),
            name="join_parts",
        )(parts, 1.0 - rims[:1])
    parts = parts.reshape((planes, dir_count) + message)
    main = parts[:, :, : 2 * dest_rows, :kf_dev].reshape(planes, dir_count, 2, dest_rows, kf_dev)
    over = parts[:, :, 2 * dest_rows :, :dest_rows].reshape(planes, dir_count, 2, 2 * rim, dest_rows)
    low = jnp.roll(over[:, :, :, :rim], -1, axis=1)
    high = jnp.roll(over[:, :, :, rim:], 1, axis=1)
    middle = jnp.zeros((planes, dir_count, 2, kf_dev - 2 * rim, dest_rows), jnp.float32)
    fix = jnp.concatenate([high, middle, low], axis=3)
    total = main.transpose(3, 2, 0, 1, 4) + fix.transpose(4, 2, 0, 1, 3)
    return total.reshape(result)


def solution(mesh):
    boxes, dirs = mesh.shape["box"], mesh.shape["dir"]
    fine_mesh = Mesh(mesh.devices.reshape(planes, boxes // planes, dirs), ("zed", "ring", "dir"))
    box = ("zed", "ring")
    placed = (
        P(box, None, None, "dir"),
        P(None, None, "dir"),
        P(box, None),
        P(box, None),
        P(box),
        P(box),
        P(box),
        P(),
        P(),
        P(),
    )
    return jax.shard_map(
        per_device,
        mesh=fine_mesh,
        in_specs=placed,
        out_specs=P(("zed", "ring", "dir"), None, None, None),
        check_vma=False,
    )
```

```python
import collections
import functools

import jax
import jax.numpy as jnp
from jax import lax
from jax.experimental import pallas as pl
from jax.experimental.pallas import tpu as pltpu
from jax.sharding import Mesh
from jax.sharding import PartitionSpec as P

wave_scale = 3.0
planes = 4
lanes = 128
half = 4
rim = 2
word_bits = 13


plan_fields = ["rows", "slots", "fine_rows", "stride", "width", "parent", "order", "turns"]
Plan = collections.namedtuple("Plan", plan_fields + ["together", "fixed", "group"])


def up(size, step):
    return -(-size // step) * step


def edge_bits(rows):
    bits = rows.bit_length() - 1
    return bits, [place for place in range(2, bits) if place % 2 == bits % 2]


def edge_rank(local, rows):
    bits, fixed = edge_bits(rows)
    rank = jnp.zeros_like(local)
    taken = 0
    for place in range(bits):
        if place not in fixed:
            rank = rank + (local // 2**place % 2) * 2**taken
            taken += 1
    return rank


def split(value):
    high = value.astype(jnp.bfloat16)
    low = (value - high.astype(jnp.float32)).astype(jnp.bfloat16)
    return high, low


def pack_kernel(source_count, note_count, zed, ring, field, *refs):
    notes, outs, whole = refs[:note_count], refs[note_count:-1], refs[-1]
    rows = field.shape[0]
    stride = 2 * source_count
    if len(outs) > planes:
        bits, fixed = edge_bits(rows)
        free = [place for place in range(bits) if place not in fixed]
        side = (1 - ring[0]) * sum(2**place for place in fixed)
        for index in range(outs[planes].shape[0]):
            base = sum((index // 2**order % 2) * 2**place for order, place in enumerate(free))
            outs[planes][index] = field[base + side]

    def row_step(row, unused):
        both = jnp.concatenate([field[row, 0], field[row, 1]], axis=0)
        for block in range(half):
            whole[block, pl.ds(pl.multiple_of(row * stride, stride), stride), :] = both[
                :, block * lanes : (block + 1) * lanes
            ]
        return unused

    lax.fori_loop(0, rows, row_step, 0, unroll=8)
    for step, out in enumerate(outs[:planes]):
        source = zed[0] ^ step
        for part in range(2):
            for block in range(half):
                out[pl.ds(part * half + block, rows, stride=2 * half), :] = whole[
                    block, pl.ds(part * source_count + source, rows, stride=stride), :
                ]
        for note in notes:
            out[rows * 2 * half :, :] = note[...]


def pack(here, field, notes, edge_rows):
    rows, _, source_count, width = field.shape
    length = rows * 2 * half + sum(note.shape[0] for note in notes)
    whole = pl.BlockSpec(memory_space=pltpu.VMEM)
    edges = [jax.ShapeDtypeStruct((edge_rows,) + field.shape[1:], jnp.float32)] if edge_rows else []
    return pl.pallas_call(
        functools.partial(pack_kernel, source_count, len(notes)),
        out_shape=[jax.ShapeDtypeStruct((length, lanes), jnp.float32)] * planes + edges,
        in_specs=[pl.BlockSpec(memory_space=pltpu.SMEM)] * 2 + [whole] * (1 + len(notes)),
        out_specs=[whole] * (planes + len(edges)),
        scratch_shapes=[pltpu.VMEM((half, rows * 2 * source_count, lanes), jnp.float32)],
        compiler_params=pltpu.CompilerParams(vmem_limit_bytes=24 * 2**20),
        name="pack_sources",
    )(*here, field, *notes)


def parts_of(word):
    return lax.shift_right_logical(word, word_bits), word & (2**word_bits - 1)


def tile(start):
    return pl.ds(pl.multiple_of(start, 2 * half), 2 * half)


def fine_kernel(plan, size, edge_size, zed, *refs):
    mains, refs = refs[:planes], refs[planes:]
    edges = refs[: planes if edge_size else 0]
    lists, refs = refs[len(edges)], refs[len(edges) + 1 :]
    table, phases, weights, out, rims, meta, field, moved, shifted, ready, landed, sems = refs
    rows, fine_rows = plan.rows, plan.fine_rows
    own = zed[0]

    def bring(step):
        return pltpu.make_async_copy(lists.at[step], meta.at[step % 2], sems.at[planes + step % 2])

    bring(0).start()
    incoming = []
    for index, edge in enumerate(edges):
        chosen = edge.at[pl.ds(0, edge_size * 2 * half)]
        incoming.append(pltpu.make_async_copy(chosen, landed.at[index], sems.at[planes + 2 + index]))
        incoming[-1].start()
    lane = lax.broadcasted_iota(jnp.int32, rims.shape, 1)
    rims[...] = ((lane < rim) | (lane >= lanes - rim)).astype(jnp.float32)

    def both(start):
        return pl.ds(pl.multiple_of(start, 4 * half), 4 * half)

    def with_turned(value):
        return jnp.concatenate([value, pltpu.roll(value, half, 0)], axis=0)

    for index, main in enumerate(mains):
        first = (own ^ (planes - 1 - index)) * size

        def main_step(row, unused, first=first, main=main):
            field[both((first + row) * 4 * half), :] = with_turned(main[tile(row * 2 * half), :])
            return unused

        lax.fori_loop(0, size, main_step, 0, unroll=8)
    for index in range(len(edges)):
        first = planes * size + (own ^ index) * edge_size
        incoming[index].wait()

        def edge_step(row, unused, first=first, index=index):
            field[both((first + row) * 4 * half), :] = with_turned(landed[index, tile(row * 2 * half), :])
            return unused

        lax.fori_loop(0, edge_size, edge_step, 0, unroll=8)
    field[both(planes * (size + edge_size) * 4 * half), :] = jnp.zeros((4 * half, lanes), jnp.float32)

    blank = jnp.zeros((2 * half, lanes), jnp.float32)
    sub = lax.broadcasted_iota(jnp.int32, (2 * half, lanes), 0)
    dest_count = out.shape[1]
    dest_rows = fine_rows // dest_count

    def plane_step(turn, unused):
        plane = own ^ turn
        slot = turn % 2
        bring(turn).wait()

        @pl.when(turn + 1 < planes)
        def _():
            bring(turn + 1).start()

        across = lanes // plan.width

        def boxes_step(slot_count, step, unused):
            ranks = [step * plan.together + each for each in range(plan.together)]
            boxes = [meta[slot, plan.order, rank] for rank in ranks]
            sums = [[blank, blank] for box in boxes]
            for pair in range(slot_count):
                for each in range(plan.together):
                    row = step * (plan.together // across) + each // across
                    place, kind = parts_of(meta[slot, row, each % across * plan.width + pair])
                    value = field[both(place), :]
                    factor = table[tile(kind), :]
                    sums[each][0] += factor * value[: 2 * half]
                    sums[each][1] += factor * value[2 * half :]
            for each in range(plan.together):
                straight, crossed = sums[each]
                total = jnp.where(
                    sub < half,
                    straight + pltpu.roll(straight, half, 0),
                    pltpu.roll(crossed, half, 0) - crossed,
                )
                moved[both(boxes[each] * 4 * half), :] = with_turned(total)
            return unused

        start = 0
        for more in reversed(range((plan.slots - plan.fixed) // plan.group + 1)):
            end = meta[slot, plan.order, plan.turns + more]
            lax.fori_loop(start, end, functools.partial(boxes_step, plan.fixed + more * plan.group), 0)
            start = end

        def fine_step(block, unused):
            for each in range(lanes):
                parent, octant = parts_of(meta[slot, plan.parent + block, each])
                value = moved[both(parent), :] * phases[both(octant), :]
                shifted[tile((block * lanes + each) * 2 * half), :] = value[: 2 * half] + value[2 * half :]
            return unused

        lax.fori_loop(0, fine_rows // lanes, fine_step, 0)
        width = ready.shape[3]
        left = jnp.concatenate(
            [
                jnp.concatenate(
                    [
                        shifted[pl.ds(part * half + block, fine_rows, stride=2 * half), :]
                        for block in range(half)
                    ],
                    axis=1,
                )
                for part in range(2)
            ],
            axis=0,
        )
        first, second = split(left)
        result = jnp.dot(
            jnp.concatenate([first, first, second], axis=1), weights[...], preferred_element_type=jnp.float32
        )
        for part in range(2):
            for dest in range(dest_count):
                start = part * fine_rows + dest * dest_rows
                ready[plane, dest, part * dest_rows : (part + 1) * dest_rows, :] = result[
                    start : start + dest_rows, :width
                ]
        spill = result[:fine_rows, width:] + pltpu.roll(result[fine_rows:, width:], half, 1)
        spill = spill.T[: 2 * half]
        for dest in range(dest_count):
            ready[plane, dest, 2 * dest_rows :, :] = jnp.concatenate(
                [
                    spill[:, dest * dest_rows : (dest + 1) * dest_rows],
                    jnp.zeros((2 * half, width - dest_rows), jnp.float32),
                ],
                axis=1,
            )
        pltpu.make_async_copy(ready.at[plane], out.at[plane], sems.at[plane]).start()
        return unused

    lax.fori_loop(0, planes, plane_step, 0)
    for plane in range(planes):
        pltpu.make_async_copy(ready.at[plane], out.at[plane], sems.at[plane]).wait()


def join_kernel(source_count, parts, rims, out, whole):
    dest_rows = out.shape[0]
    dirs = parts.shape[0] // source_count
    over = jnp.concatenate(
        [parts[index, 2 * dest_rows :, :lanes] for index in range(parts.shape[0])], axis=0
    ).T[:dest_rows]
    low = lax.broadcasted_iota(jnp.int32, (dest_rows, lanes), 1) < rim
    at_rim = jnp.broadcast_to(rims[...], (dest_rows, lanes)) < 0.5
    for source in range(source_count):
        for part in range(2):
            turned = []
            for index in range(dirs):
                first = (source * dirs + index) * 2 * half + part * half
                turned.append(pltpu.roll(over, (lanes - rim - first) % lanes, 1))
            for index in range(dirs):
                fix = jnp.where(at_rim, jnp.where(low, turned[index - 1], turned[(index + 1) % dirs]), 0.0)
                whole[
                    index, pl.ds(part * source_count + source, dest_rows, stride=2 * source_count), :
                ] = parts[source * dirs + index, part * dest_rows : (part + 1) * dest_rows, :] + fix

    def row_step(row, unused):
        start = pl.multiple_of(row * 2 * source_count, 2 * source_count)
        both = jnp.concatenate(
            [whole[index, pl.ds(start, 2 * source_count), :] for index in range(dirs)], axis=1
        )
        out[row, 0] = both[:source_count]
        out[row, 1] = both[source_count:]
        return unused

    lax.fori_loop(0, dest_rows, row_step, 0, unroll=8)


def per_device(
    coarse_field,
    trans_table,
    partner_ids,
    partner_types,
    partner_count,
    child_count,
    child_octant,
    dir_angles,
    stencil_ids,
    stencil_weights,
):
    rows, _, source_count, kc_dev = coarse_field.shape
    slots = partner_ids.shape[1]
    type_count = trans_table.shape[0]
    fine_rows = child_octant.shape[0]
    ring_count = lax.axis_size("ring")
    dir_count = lax.axis_size("dir")
    zed = lax.axis_index("zed")
    ring = lax.axis_index("ring")
    dir_index = lax.axis_index("dir")
    fine_count = stencil_ids.shape[0] // 4
    kf_dev = fine_count // dir_count
    kc_pad = up(kc_dev, half * lanes)
    kf_pad = up(kf_dev, lanes)
    pad_dirs = kc_pad - kc_dev
    assert source_count == planes and kc_pad == half * lanes
    dest_rows = fine_rows // dir_count

    field = jnp.pad(coarse_field, ((0, 0), (0, 0), (0, 0), (0, pad_dirs)))
    here = zed.reshape(1), ring.reshape(1)
    edge_rows = rows >> len(edge_bits(rows)[1]) if ring_count == 2 else 0
    packed = pack(here, field, [], edge_rows)
    if edge_rows:
        edges = lax.ppermute(packed[planes], "ring", [(0, 1), (1, 0)])

    def to_planes(note, step):
        if step == 0:
            return note
        return lax.ppermute(note, "zed", [(plane, plane ^ step) for plane in range(planes)])

    arrived = [to_planes(packed[step], step) for step in (3, 2)]

    plane_of = partner_ids // (ring_count * rows)
    ring_of = partner_ids // rows % ring_count
    local = partner_ids % rows
    live = jnp.arange(slots, dtype=jnp.int32)[None, :] < partner_count[:, None]
    if ring_count == 2:
        size = rows
        place = jnp.where(
            ring_of == ring,
            plane_of * rows + local,
            planes * rows + plane_of * edge_rows + edge_rank(local, rows),
        )
    else:
        size = ring_count * rows
        place = partner_ids
    field_rows = planes * (size + edge_rows)
    place = jnp.where(live, place, field_rows)
    together = 4
    fixed = slots // 2
    group = 3 if (slots - fixed) % 3 == 0 else 1
    index = jnp.arange(rows, dtype=jnp.int32)
    before = (partner_count[None, :] > partner_count[:, None]) | (
        (partner_count[None, :] == partner_count[:, None]) & (index[None, :] < index[:, None])
    )
    rank = jnp.sum(before.astype(jnp.int32), axis=1)
    at_rank = rank[None, :] == index[:, None]
    order = jnp.sum(jnp.where(at_rank, index[None, :], 0), axis=1)
    first = rank[None, :] == index[: rows // together, None] * together
    longest = jnp.sum(jnp.where(first, partner_count[None, :], 0), axis=1)
    turns = jnp.maximum((longest - fixed + group - 1) // group, 0)
    more = jnp.arange((slots - fixed) // group + 1, dtype=jnp.int32)
    ends = jnp.sum((turns[None, :] >= more[:, None]).astype(jnp.int32), axis=1)
    bounds = jnp.sum(jnp.where(index[None, :] <= index[:, None], child_count[None, :], 0), axis=1)
    parent = jnp.sum(
        (bounds[None, :] <= jnp.arange(fine_rows, dtype=jnp.int32)[:, None]).astype(jnp.int32), axis=1
    )
    def across(one, width=lanes):
        return jnp.pad(one, ((0, 0), (0, width - one.shape[1])))

    width = lanes // half
    turns_at = lanes // 2
    assert slots <= width and rows <= turns_at and fine_rows % lanes == 0
    assert (field_rows + 1) * 4 * half < 2 ** (31 - word_bits) and type_count * 2 * half < 2**word_bits

    in_order = jnp.dot(
        at_rank.astype(jnp.float32),
        jnp.concatenate([across(place * 4 * half, width), across(partner_types * 2 * half, width)], axis=1).astype(
            jnp.float32
        ),
        precision=lax.Precision.HIGHEST,
        preferred_element_type=jnp.float32,
    )

    def listed(side):
        return in_order[:, side * width : (side + 1) * width].reshape(rows * width // lanes, lanes)

    list_rows = rows * width // lanes
    fine_lists = fine_rows // lanes
    last = across(jnp.concatenate([across(order[None], turns_at), ends[None]], axis=1))
    stride = up(list_rows + fine_lists + 1, 8)

    def stacked(*parts):
        meta = jnp.concatenate([part.astype(jnp.float32) for part in parts])
        return jnp.pad(meta, ((0, stride - meta.shape[0]), (0, 0)))

    meta = jnp.concatenate(
        [
            stacked(listed(0), (parent * 4 * half).reshape(-1, lanes)),
            stacked(listed(1), (child_octant * 4 * half).reshape(-1, lanes), last),
        ]
    )
    plan = Plan(
        rows, slots, fine_rows, stride, width, list_rows, list_rows + fine_lists, turns_at, together, fixed, group
    )

    notes = pack(here, edges, [meta], 0) if edge_rows else [meta] * planes
    after_notes = lax.optimization_barrier(
        (notes, packed[1], trans_table, dir_angles, stencil_ids, stencil_weights)
    )
    notes, near, trans_table, dir_angles, stencil_ids, stencil_weights = after_notes
    received = [to_planes(notes[step], step) for step in range(planes)]
    arrived += [to_planes(near, 1), packed[0]]
    edge_part = edge_rows * 2 * half
    numbers = jnp.stack([note[edge_part:] for note in received]).astype(jnp.int32)
    meta = numbers[:, :stride] * 2**word_bits + numbers[:, stride:]
    if ring_count != 2:
        arrived = [lax.all_gather(one, "ring", axis=0, tiled=True) for one in arrived]
        received = []

    def blocks(table):
        return jnp.pad(table, ((0, 0), (0, pad_dirs))).reshape(-1, half, lanes)

    def doubled(table, sign):
        return jnp.concatenate([blocks(table), sign * blocks(table)], axis=1)

    table = jnp.pad(trans_table, ((0, 0), (0, 0), (0, pad_dirs))).reshape(-1, lanes)
    angles = lax.dynamic_slice_in_dim(dir_angles, dir_index * kc_dev, kc_dev, axis=1)
    octants = jnp.arange(8, dtype=jnp.int32)
    sign_x = 1.0 - 2.0 * (octants % 2).astype(jnp.float32)
    sign_y = 1.0 - 2.0 * (octants // 2 % 2).astype(jnp.float32)
    sign_z = 1.0 - 2.0 * (octants // 4).astype(jnp.float32)
    unit_x = jnp.sin(angles[0]) * jnp.cos(angles[1])
    unit_y = jnp.sin(angles[0]) * jnp.sin(angles[1])
    unit_z = jnp.cos(angles[0])
    phase = wave_scale * (
        sign_x[:, None] * unit_x[None, :] + sign_y[:, None] * unit_y[None, :] + sign_z[:, None] * unit_z[None, :]
    )
    phases = jnp.concatenate(
        [doubled(jnp.cos(phase), 1.0), doubled(jnp.sin(phase), -1.0)], axis=1
    ).reshape(-1, lanes)

    ids = lax.dynamic_slice_in_dim(stencil_ids, dir_index * kc_dev, kc_dev, axis=0).T
    weights = lax.dynamic_slice_in_dim(stencil_weights, dir_index * kc_dev, kc_dev, axis=0).T

    def interp(targets):
        matrix = jnp.zeros((targets.shape[0], kc_dev), jnp.float32)
        for point in range(ids.shape[0]):
            matrix = matrix + jnp.where(
                ids[point][None, :] == targets[:, None], weights[point][None, :], 0.0
            )
        return jnp.pad(matrix, ((0, 0), (0, pad_dirs)))

    first_fine = dir_index * kf_dev
    own = jnp.arange(kf_dev, dtype=jnp.int32)
    outside = jnp.concatenate(
        [jnp.arange(-rim, 0, dtype=jnp.int32), jnp.arange(kf_dev, kf_dev + rim, dtype=jnp.int32)]
    )
    matrix = jnp.pad(interp(first_fine + own), ((0, kf_pad - kf_dev), (0, 0)))
    spill = interp((first_fine + outside) % fine_count)
    matrices = jnp.concatenate([matrix, jnp.pad(spill, ((0, lanes - half), (0, 0)))], axis=0).T
    rounded = lax.reduce_precision(matrices, 8, 7)
    high = rounded.astype(jnp.bfloat16)
    low = (matrices - rounded).astype(jnp.bfloat16)
    passes = jnp.concatenate([high, low, high], axis=0)

    whole = pl.BlockSpec(memory_space=pltpu.VMEM)
    message = (2 * dest_rows + 2 * half, kf_pad)
    local_fine, rims = pl.pallas_call(
        functools.partial(fine_kernel, plan, size, edge_rows),
        out_shape=[
            pltpu.HBM((planes, dir_count) + message, jnp.float32),
            jax.ShapeDtypeStruct((2 * half, lanes), jnp.float32),
        ],
        in_specs=[pl.BlockSpec(memory_space=pltpu.SMEM)]
        + [whole] * planes
        + [pl.BlockSpec(memory_space=pl.ANY)] * (len(received) + 1)
        + [whole] * 3,
        out_specs=[pl.BlockSpec(memory_space=pltpu.HBM), whole],
        scratch_shapes=[
            pltpu.SMEM((2, plan.stride, lanes), jnp.int32),
            pltpu.VMEM(((field_rows + 1) * 4 * half, lanes), jnp.float32),
            pltpu.VMEM((rows * 4 * half, lanes), jnp.float32),
            pltpu.VMEM((fine_rows * 2 * half, lanes), jnp.float32),
            pltpu.VMEM((planes, dir_count) + message, jnp.float32),
            pltpu.VMEM((planes, max(edge_rows, 1) * 2 * half, lanes), jnp.float32),
            pltpu.SemaphoreType.DMA((2 * planes + 2,)),
        ],
        compiler_params=pltpu.CompilerParams(vmem_limit_bytes=24 * 2**20),
        name="translate_and_interpolate",
    )(here[0], *arrived, *received, meta, table, phases, passes)

    parts = lax.all_to_all(
        local_fine.reshape((planes * dir_count,) + message),
        ("zed", "dir"),
        split_axis=0,
        concat_axis=0,
        tiled=True,
    )
    result = (dest_rows, 2, source_count, fine_count)
    if kf_dev == lanes and planes * dir_count * 2 * half == lanes and dest_rows <= lanes:
        return pl.pallas_call(
            functools.partial(join_kernel, source_count),
            out_shape=jax.ShapeDtypeStruct(result, jnp.float32),
            in_specs=[whole] * 2,
            out_specs=whole,
            scratch_shapes=[pltpu.VMEM((dir_count, dest_rows * 2 * source_count, lanes), jnp.float32)],
            compiler_params=pltpu.CompilerParams(vmem_limit_bytes=24 * 2**20),
            name="join_parts",
        )(parts, 1.0 - rims[:1])
    parts = parts.reshape((planes, dir_count) + message)
    main = parts[:, :, : 2 * dest_rows, :kf_dev].reshape(planes, dir_count, 2, dest_rows, kf_dev)
    over = parts[:, :, 2 * dest_rows :, :dest_rows].reshape(planes, dir_count, 2, 2 * rim, dest_rows)
    low = jnp.roll(over[:, :, :, :rim], -1, axis=1)
    high = jnp.roll(over[:, :, :, rim:], 1, axis=1)
    middle = jnp.zeros((planes, dir_count, 2, kf_dev - 2 * rim, dest_rows), jnp.float32)
    fix = jnp.concatenate([high, middle, low], axis=3)
    total = main.transpose(3, 2, 0, 1, 4) + fix.transpose(4, 2, 0, 1, 3)
    return total.reshape(result)


def solution(mesh):
    boxes, dirs = mesh.shape["box"], mesh.shape["dir"]
    fine_mesh = Mesh(mesh.devices.reshape(planes, boxes // planes, dirs), ("zed", "ring", "dir"))
    box = ("zed", "ring")
    placed = (
        P(box, None, None, "dir"),
        P(None, None, "dir"),
        P(box, None),
        P(box, None),
        P(box),
        P(box),
        P(box),
        P(),
        P(),
        P(),
    )
    return jax.shard_map(
        per_device,
        mesh=fine_mesh,
        in_specs=placed,
        out_specs=P(("zed", "ring", "dir"), None, None, None),
        check_vma=False,
    )
```

```python
import collections
import functools

import jax
import jax.numpy as jnp
from jax import lax
from jax.experimental import pallas as pl
from jax.experimental.pallas import tpu as pltpu
from jax.sharding import Mesh
from jax.sharding import PartitionSpec as P

wave_scale = 3.0
planes = 4
lanes = 128
half = 4
rim = 2
word_bits = 13


plan_fields = ["rows", "slots", "fine_rows", "stride", "width", "parent", "order", "turns"]
Plan = collections.namedtuple("Plan", plan_fields + ["together", "fixed", "group"])


def up(size, step):
    return -(-size // step) * step


def edge_bits(rows):
    bits = rows.bit_length() - 1
    return bits, [place for place in range(2, bits) if place % 2 == bits % 2]


def edge_rank(local, rows):
    bits, fixed = edge_bits(rows)
    rank = jnp.zeros_like(local)
    taken = 0
    for place in range(bits):
        if place not in fixed:
            rank = rank + (local // 2**place % 2) * 2**taken
            taken += 1
    return rank


def split(value):
    high = value.astype(jnp.bfloat16)
    low = (value - high.astype(jnp.float32)).astype(jnp.bfloat16)
    return high, low


def pack_kernel(source_count, note_count, zed, ring, field, *refs):
    notes, outs, whole = refs[:note_count], refs[note_count:-1], refs[-1]
    rows = field.shape[0]
    stride = 2 * source_count
    if len(outs) > planes:
        bits, fixed = edge_bits(rows)
        free = [place for place in range(bits) if place not in fixed]
        side = (1 - ring[0]) * sum(2**place for place in fixed)
        for index in range(outs[planes].shape[0]):
            base = sum((index // 2**order % 2) * 2**place for order, place in enumerate(free))
            outs[planes][index] = field[base + side]

    def row_step(row, unused):
        both = jnp.concatenate([field[row, 0], field[row, 1]], axis=0)
        for block in range(half):
            whole[block, pl.ds(pl.multiple_of(row * stride, stride), stride), :] = both[
                :, block * lanes : (block + 1) * lanes
            ]
        return unused

    lax.fori_loop(0, rows, row_step, 0, unroll=8)
    for step, out in enumerate(outs[:planes]):
        source = zed[0] ^ step
        for part in range(2):
            for block in range(half):
                out[pl.ds(part * half + block, rows, stride=2 * half), :] = whole[
                    block, pl.ds(part * source_count + source, rows, stride=stride), :
                ]
        for note in notes:
            out[rows * 2 * half :, :] = note[...]


def pack(here, field, notes, edge_rows):
    rows, _, source_count, width = field.shape
    length = rows * 2 * half + sum(note.shape[0] for note in notes)
    whole = pl.BlockSpec(memory_space=pltpu.VMEM)
    edges = [jax.ShapeDtypeStruct((edge_rows,) + field.shape[1:], jnp.float32)] if edge_rows else []
    return pl.pallas_call(
        functools.partial(pack_kernel, source_count, len(notes)),
        out_shape=[jax.ShapeDtypeStruct((length, lanes), jnp.float32)] * planes + edges,
        in_specs=[pl.BlockSpec(memory_space=pltpu.SMEM)] * 2 + [whole] * (1 + len(notes)),
        out_specs=[whole] * (planes + len(edges)),
        scratch_shapes=[pltpu.VMEM((half, (rows + 1) * 2 * source_count, lanes), jnp.float32)],
        compiler_params=pltpu.CompilerParams(vmem_limit_bytes=24 * 2**20),
        name="pack_sources",
    )(*here, field, *notes)


def parts_of(word):
    return lax.shift_right_logical(word, word_bits), word & (2**word_bits - 1)


def tile(start):
    return pl.ds(pl.multiple_of(start, 2 * half), 2 * half)


def fine_kernel(plan, size, edge_size, zed, *refs):
    mains, refs = refs[:planes], refs[planes:]
    edges = refs[: planes if edge_size else 0]
    lists, refs = refs[len(edges)], refs[len(edges) + 1 :]
    table, phases, weights, out, rims, meta, field, moved, shifted, ready, landed, sems = refs
    rows, fine_rows = plan.rows, plan.fine_rows
    own = zed[0]

    def bring(step):
        return pltpu.make_async_copy(lists.at[step], meta.at[step % 2], sems.at[planes + step % 2])

    bring(0).start()
    incoming = []
    for index, edge in enumerate(edges):
        chosen = edge.at[pl.ds(0, edge_size * 2 * half)]
        incoming.append(pltpu.make_async_copy(chosen, landed.at[index], sems.at[planes + 2 + index]))
        incoming[-1].start()
    lane = lax.broadcasted_iota(jnp.int32, rims.shape, 1)
    rims[...] = ((lane < rim) | (lane >= lanes - rim)).astype(jnp.float32)

    def both(start):
        return pl.ds(pl.multiple_of(start, 4 * half), 4 * half)

    def with_turned(value):
        return jnp.concatenate([value, pltpu.roll(value, half, 0)], axis=0)

    for index, main in enumerate(mains):
        first = (own ^ (planes - 1 - index)) * size

        def main_step(row, unused, first=first, main=main):
            field[both((first + row) * 4 * half), :] = with_turned(main[tile(row * 2 * half), :])
            return unused

        lax.fori_loop(0, size, main_step, 0, unroll=8)
    for index in range(len(edges)):
        first = planes * size + (own ^ index) * edge_size
        incoming[index].wait()

        def edge_step(row, unused, first=first, index=index):
            field[both((first + row) * 4 * half), :] = with_turned(landed[index, tile(row * 2 * half), :])
            return unused

        lax.fori_loop(0, edge_size, edge_step, 0, unroll=8)
    field[both(planes * (size + edge_size) * 4 * half), :] = jnp.zeros((4 * half, lanes), jnp.float32)

    blank = jnp.zeros((2 * half, lanes), jnp.float32)
    sub = lax.broadcasted_iota(jnp.int32, (2 * half, lanes), 0)
    dest_count = out.shape[1]
    dest_rows = fine_rows // dest_count

    def plane_step(turn, unused):
        plane = own ^ turn
        slot = turn % 2
        bring(turn).wait()

        @pl.when(turn + 1 < planes)
        def _():
            bring(turn + 1).start()

        across = lanes // plan.width

        def boxes_step(slot_count, step, unused):
            ranks = [step * plan.together + each for each in range(plan.together)]
            boxes = [meta[slot, plan.order, rank] for rank in ranks]
            sums = [[blank, blank] for box in boxes]
            for pair in range(slot_count):
                for each in range(plan.together):
                    row = step * (plan.together // across) + each // across
                    place, kind = parts_of(meta[slot, row, each % across * plan.width + pair])
                    value = field[both(place), :]
                    factor = table[tile(kind), :]
                    sums[each][0] += factor * value[: 2 * half]
                    sums[each][1] += factor * value[2 * half :]
            for each in range(plan.together):
                straight, crossed = sums[each]
                total = jnp.where(
                    sub < half,
                    straight + pltpu.roll(straight, half, 0),
                    pltpu.roll(crossed, half, 0) - crossed,
                )
                moved[both(boxes[each] * 4 * half), :] = with_turned(total)
            return unused

        start = 0
        for more in reversed(range((plan.slots - plan.fixed) // plan.group + 1)):
            end = meta[slot, plan.order, plan.turns + more]
            lax.fori_loop(start, end, functools.partial(boxes_step, plan.fixed + more * plan.group), 0)
            start = end

        def fine_step(block, unused):
            for each in range(lanes):
                parent, octant = parts_of(meta[slot, plan.parent + block, each])
                value = moved[both(parent), :] * phases[both(octant), :]
                shifted[tile((block * lanes + each) * 2 * half), :] = value[: 2 * half] + value[2 * half :]
            return unused

        lax.fori_loop(0, fine_rows // lanes, fine_step, 0)
        width = ready.shape[3]
        left = jnp.concatenate(
            [
                jnp.concatenate(
                    [
                        shifted[pl.ds(part * half + block, fine_rows, stride=2 * half), :]
                        for block in range(half)
                    ],
                    axis=1,
                )
                for part in range(2)
            ],
            axis=0,
        )
        first, second = split(left)
        result = jnp.dot(
            jnp.concatenate([first, first, second], axis=1), weights[...], preferred_element_type=jnp.float32
        )
        for part in range(2):
            for dest in range(dest_count):
                start = part * fine_rows + dest * dest_rows
                ready[plane, dest, part * dest_rows : (part + 1) * dest_rows, :] = result[
                    start : start + dest_rows, :width
                ]
        spill = result[:fine_rows, width:] + pltpu.roll(result[fine_rows:, width:], half, 1)
        spill = spill.T[: 2 * half]
        for dest in range(dest_count):
            ready[plane, dest, 2 * dest_rows :, :] = jnp.concatenate(
                [
                    spill[:, dest * dest_rows : (dest + 1) * dest_rows],
                    jnp.zeros((2 * half, width - dest_rows), jnp.float32),
                ],
                axis=1,
            )
        pltpu.make_async_copy(ready.at[plane], out.at[plane], sems.at[plane]).start()
        return unused

    lax.fori_loop(0, planes, plane_step, 0)
    for plane in range(planes):
        pltpu.make_async_copy(ready.at[plane], out.at[plane], sems.at[plane]).wait()


def join_kernel(source_count, parts, rims, out, whole):
    dest_rows = out.shape[0]
    dirs = parts.shape[0] // source_count
    over = jnp.concatenate(
        [parts[index, 2 * dest_rows :, :lanes] for index in range(parts.shape[0])], axis=0
    ).T[:dest_rows]
    low = lax.broadcasted_iota(jnp.int32, (dest_rows, lanes), 1) < rim
    at_rim = jnp.broadcast_to(rims[...], (dest_rows, lanes)) < 0.5
    for source in range(source_count):
        for part in range(2):
            turned = []
            for index in range(dirs):
                first = (source * dirs + index) * 2 * half + part * half
                turned.append(pltpu.roll(over, (lanes - rim - first) % lanes, 1))
            for index in range(dirs):
                fix = jnp.where(at_rim, jnp.where(low, turned[index - 1], turned[(index + 1) % dirs]), 0.0)
                whole[
                    index, pl.ds(part * source_count + source, dest_rows, stride=2 * source_count), :
                ] = parts[source * dirs + index, part * dest_rows : (part + 1) * dest_rows, :] + fix

    def row_step(row, unused):
        start = pl.multiple_of(row * 2 * source_count, 2 * source_count)
        both = jnp.concatenate(
            [whole[index, pl.ds(start, 2 * source_count), :] for index in range(dirs)], axis=1
        )
        out[row, 0] = both[:source_count]
        out[row, 1] = both[source_count:]
        return unused

    lax.fori_loop(0, dest_rows, row_step, 0, unroll=8)


def per_device(
    coarse_field,
    trans_table,
    partner_ids,
    partner_types,
    partner_count,
    child_count,
    child_octant,
    dir_angles,
    stencil_ids,
    stencil_weights,
):
    rows, _, source_count, kc_dev = coarse_field.shape
    slots = partner_ids.shape[1]
    type_count = trans_table.shape[0]
    fine_rows = child_octant.shape[0]
    ring_count = lax.axis_size("ring")
    dir_count = lax.axis_size("dir")
    zed = lax.axis_index("zed")
    ring = lax.axis_index("ring")
    dir_index = lax.axis_index("dir")
    fine_count = stencil_ids.shape[0] // 4
    kf_dev = fine_count // dir_count
    kc_pad = up(kc_dev, half * lanes)
    kf_pad = up(kf_dev, lanes)
    pad_dirs = kc_pad - kc_dev
    assert source_count == planes and kc_pad == half * lanes
    dest_rows = fine_rows // dir_count

    field = jnp.pad(coarse_field, ((0, 0), (0, 0), (0, 0), (0, pad_dirs)))
    here = zed.reshape(1), ring.reshape(1)
    edge_rows = rows >> len(edge_bits(rows)[1]) if ring_count == 2 else 0
    packed = pack(here, field, [], edge_rows)
    if edge_rows:
        edges = lax.ppermute(packed[planes], "ring", [(0, 1), (1, 0)])

    def to_planes(note, step):
        if step == 0:
            return note
        return lax.ppermute(note, "zed", [(plane, plane ^ step) for plane in range(planes)])

    arrived = [to_planes(packed[step], step) for step in (3, 2, 1, 0)]

    plane_of = partner_ids // (ring_count * rows)
    ring_of = partner_ids // rows % ring_count
    local = partner_ids % rows
    live = jnp.arange(slots, dtype=jnp.int32)[None, :] < partner_count[:, None]
    if ring_count == 2:
        size = rows
        place = jnp.where(
            ring_of == ring,
            plane_of * rows + local,
            planes * rows + plane_of * edge_rows + edge_rank(local, rows),
        )
    else:
        size = ring_count * rows
        place = partner_ids
    field_rows = planes * (size + edge_rows)
    place = jnp.where(live, place, field_rows)
    together = 4
    fixed = slots // 2
    group = 3 if (slots - fixed) % 3 == 0 else 1
    index = jnp.arange(rows, dtype=jnp.int32)
    before = (partner_count[None, :] > partner_count[:, None]) | (
        (partner_count[None, :] == partner_count[:, None]) & (index[None, :] < index[:, None])
    )
    rank = jnp.sum(before.astype(jnp.int32), axis=1)
    at_rank = rank[None, :] == index[:, None]
    order = jnp.sum(jnp.where(at_rank, index[None, :], 0), axis=1)
    first = rank[None, :] == index[: rows // together, None] * together
    longest = jnp.sum(jnp.where(first, partner_count[None, :], 0), axis=1)
    turns = jnp.maximum((longest - fixed + group - 1) // group, 0)
    more = jnp.arange((slots - fixed) // group + 1, dtype=jnp.int32)
    ends = jnp.sum((turns[None, :] >= more[:, None]).astype(jnp.int32), axis=1)
    bounds = jnp.sum(jnp.where(index[None, :] <= index[:, None], child_count[None, :], 0), axis=1)
    parent = jnp.sum(
        (bounds[None, :] <= jnp.arange(fine_rows, dtype=jnp.int32)[:, None]).astype(jnp.int32), axis=1
    )
    def across(one, width=lanes):
        return jnp.pad(one, ((0, 0), (0, width - one.shape[1])))

    width = lanes // half
    turns_at = lanes // 2
    assert slots <= width and rows <= turns_at and fine_rows % lanes == 0
    assert (field_rows + 1) * 4 * half < 2 ** (31 - word_bits) and type_count * 2 * half < 2**word_bits

    in_order = jnp.dot(
        at_rank.astype(jnp.float32),
        jnp.concatenate([across(place * 4 * half, width), across(partner_types * 2 * half, width)], axis=1).astype(
            jnp.float32
        ),
        precision=lax.Precision.HIGHEST,
        preferred_element_type=jnp.float32,
    )

    def listed(side):
        return in_order[:, side * width : (side + 1) * width].reshape(rows * width // lanes, lanes)

    list_rows = rows * width // lanes
    fine_lists = fine_rows // lanes
    last = across(jnp.concatenate([across(order[None], turns_at), ends[None]], axis=1))
    stride = up(list_rows + fine_lists + 1, 8)

    def stacked(*parts):
        meta = jnp.concatenate([part.astype(jnp.float32) for part in parts])
        return jnp.pad(meta, ((0, stride - meta.shape[0]), (0, 0)))

    meta = jnp.concatenate(
        [
            stacked(listed(0), (parent * 4 * half).reshape(-1, lanes)),
            stacked(listed(1), (child_octant * 4 * half).reshape(-1, lanes), last),
        ]
    )
    plan = Plan(
        rows, slots, fine_rows, stride, width, list_rows, list_rows + fine_lists, turns_at, together, fixed, group
    )

    notes = pack(here, edges, [meta], 0) if edge_rows else [meta] * planes
    after_notes = lax.optimization_barrier((notes, trans_table, dir_angles, stencil_ids, stencil_weights))
    notes, trans_table, dir_angles, stencil_ids, stencil_weights = after_notes
    received = [to_planes(notes[step], step) for step in range(planes)]
    edge_part = edge_rows * 2 * half
    numbers = jnp.stack([note[edge_part:] for note in received]).astype(jnp.int32)
    meta = numbers[:, :stride] * 2**word_bits + numbers[:, stride:]
    if ring_count != 2:
        arrived = [lax.all_gather(one, "ring", axis=0, tiled=True) for one in arrived]
        received = []

    def blocks(table):
        return jnp.pad(table, ((0, 0), (0, pad_dirs))).reshape(-1, half, lanes)

    def doubled(table, sign):
        return jnp.concatenate([blocks(table), sign * blocks(table)], axis=1)

    table = jnp.pad(trans_table, ((0, 0), (0, 0), (0, pad_dirs))).reshape(-1, lanes)
    angles = lax.dynamic_slice_in_dim(dir_angles, dir_index * kc_dev, kc_dev, axis=1)
    octants = jnp.arange(8, dtype=jnp.int32)
    sign_x = 1.0 - 2.0 * (octants % 2).astype(jnp.float32)
    sign_y = 1.0 - 2.0 * (octants // 2 % 2).astype(jnp.float32)
    sign_z = 1.0 - 2.0 * (octants // 4).astype(jnp.float32)
    unit_x = jnp.sin(angles[0]) * jnp.cos(angles[1])
    unit_y = jnp.sin(angles[0]) * jnp.sin(angles[1])
    unit_z = jnp.cos(angles[0])
    phase = wave_scale * (
        sign_x[:, None] * unit_x[None, :] + sign_y[:, None] * unit_y[None, :] + sign_z[:, None] * unit_z[None, :]
    )
    phases = jnp.concatenate(
        [doubled(jnp.cos(phase), 1.0), doubled(jnp.sin(phase), -1.0)], axis=1
    ).reshape(-1, lanes)

    ids = lax.dynamic_slice_in_dim(stencil_ids, dir_index * kc_dev, kc_dev, axis=0).T
    weights = lax.dynamic_slice_in_dim(stencil_weights, dir_index * kc_dev, kc_dev, axis=0).T

    def interp(targets):
        matrix = jnp.zeros((targets.shape[0], kc_dev), jnp.float32)
        for point in range(ids.shape[0]):
            matrix = matrix + jnp.where(
                ids[point][None, :] == targets[:, None], weights[point][None, :], 0.0
            )
        return jnp.pad(matrix, ((0, 0), (0, pad_dirs)))

    first_fine = dir_index * kf_dev
    own = jnp.arange(kf_dev, dtype=jnp.int32)
    outside = jnp.concatenate(
        [jnp.arange(-rim, 0, dtype=jnp.int32), jnp.arange(kf_dev, kf_dev + rim, dtype=jnp.int32)]
    )
    matrix = jnp.pad(interp(first_fine + own), ((0, kf_pad - kf_dev), (0, 0)))
    spill = interp((first_fine + outside) % fine_count)
    matrices = jnp.concatenate([matrix, jnp.pad(spill, ((0, lanes - half), (0, 0)))], axis=0).T
    rounded = lax.reduce_precision(matrices, 8, 7)
    high = rounded.astype(jnp.bfloat16)
    low = (matrices - rounded).astype(jnp.bfloat16)
    passes = jnp.concatenate([high, low, high], axis=0)

    whole = pl.BlockSpec(memory_space=pltpu.VMEM)
    message = (2 * dest_rows + 2 * half, kf_pad)
    local_fine, rims = pl.pallas_call(
        functools.partial(fine_kernel, plan, size, edge_rows),
        out_shape=[
            pltpu.HBM((planes, dir_count) + message, jnp.float32),
            jax.ShapeDtypeStruct((2 * half, lanes), jnp.float32),
        ],
        in_specs=[pl.BlockSpec(memory_space=pltpu.SMEM)]
        + [whole] * planes
        + [pl.BlockSpec(memory_space=pl.ANY)] * (len(received) + 1)
        + [whole] * 3,
        out_specs=[pl.BlockSpec(memory_space=pltpu.HBM), whole],
        scratch_shapes=[
            pltpu.SMEM((2, plan.stride, lanes), jnp.int32),
            pltpu.VMEM(((field_rows + 1) * 4 * half, lanes), jnp.float32),
            pltpu.VMEM((rows * 4 * half, lanes), jnp.float32),
            pltpu.VMEM(((fine_rows + 1) * 2 * half, lanes), jnp.float32),
            pltpu.VMEM((planes, dir_count) + message, jnp.float32),
            pltpu.VMEM((planes, max(edge_rows, 1) * 2 * half, lanes), jnp.float32),
            pltpu.SemaphoreType.DMA((2 * planes + 2,)),
        ],
        compiler_params=pltpu.CompilerParams(vmem_limit_bytes=24 * 2**20),
        name="translate_and_interpolate",
    )(here[0], *arrived, *received, meta, table, phases, passes)

    parts = lax.all_to_all(
        local_fine.reshape((planes * dir_count,) + message),
        ("zed", "dir"),
        split_axis=0,
        concat_axis=0,
        tiled=True,
    )
    result = (dest_rows, 2, source_count, fine_count)
    if kf_dev == lanes and planes * dir_count * 2 * half == lanes and dest_rows <= lanes:
        return pl.pallas_call(
            functools.partial(join_kernel, source_count),
            out_shape=jax.ShapeDtypeStruct(result, jnp.float32),
            in_specs=[whole] * 2,
            out_specs=whole,
            scratch_shapes=[pltpu.VMEM((dir_count, (dest_rows + 1) * 2 * source_count, lanes), jnp.float32)],
            compiler_params=pltpu.CompilerParams(vmem_limit_bytes=24 * 2**20),
            name="join_parts",
        )(parts, 1.0 - rims[:1])
    parts = parts.reshape((planes, dir_count) + message)
    main = parts[:, :, : 2 * dest_rows, :kf_dev].reshape(planes, dir_count, 2, dest_rows, kf_dev)
    over = parts[:, :, 2 * dest_rows :, :dest_rows].reshape(planes, dir_count, 2, 2 * rim, dest_rows)
    low = jnp.roll(over[:, :, :, :rim], -1, axis=1)
    high = jnp.roll(over[:, :, :, rim:], 1, axis=1)
    middle = jnp.zeros((planes, dir_count, 2, kf_dev - 2 * rim, dest_rows), jnp.float32)
    fix = jnp.concatenate([high, middle, low], axis=3)
    total = main.transpose(3, 2, 0, 1, 4) + fix.transpose(4, 2, 0, 1, 3)
    return total.reshape(result)


def solution(mesh):
    boxes, dirs = mesh.shape["box"], mesh.shape["dir"]
    fine_mesh = Mesh(mesh.devices.reshape(planes, boxes // planes, dirs), ("zed", "ring", "dir"))
    box = ("zed", "ring")
    placed = (
        P(box, None, None, "dir"),
        P(None, None, "dir"),
        P(box, None),
        P(box, None),
        P(box),
        P(box),
        P(box),
        P(),
        P(),
        P(),
    )
    return jax.shard_map(
        per_device,
        mesh=fine_mesh,
        in_specs=placed,
        out_specs=P(("zed", "ring", "dir"), None, None, None),
        check_vma=False,
    )
```

```python
import collections
import functools

import jax
import jax.numpy as jnp
from jax import lax
from jax.experimental import pallas as pl
from jax.experimental.pallas import tpu as pltpu
from jax.sharding import Mesh
from jax.sharding import PartitionSpec as P

wave_scale = 3.0
planes = 4
lanes = 128
half = 4
rim = 2
word_bits = 13


plan_fields = ["rows", "slots", "fine_rows", "stride", "width", "parent", "order", "turns"]
Plan = collections.namedtuple("Plan", plan_fields + ["together", "fixed", "group"])


def up(size, step):
    return -(-size // step) * step


def edge_bits(rows):
    bits = rows.bit_length() - 1
    return bits, [place for place in range(2, bits) if place % 2 == bits % 2]


def edge_rank(local, rows):
    bits, fixed = edge_bits(rows)
    rank = jnp.zeros_like(local)
    taken = 0
    for place in range(bits):
        if place not in fixed:
            rank = rank + (local // 2**place % 2) * 2**taken
            taken += 1
    return rank


def split(value):
    high = value.astype(jnp.bfloat16)
    low = (value - high.astype(jnp.float32)).astype(jnp.bfloat16)
    return high, low


def pack_kernel(source_count, note_count, zed, ring, field, *refs):
    notes, outs, whole = refs[:note_count], refs[note_count:-1], refs[-1]
    rows = field.shape[0]
    stride = 2 * source_count
    if len(outs) > planes:
        bits, fixed = edge_bits(rows)
        free = [place for place in range(bits) if place not in fixed]
        side = (1 - ring[0]) * sum(2**place for place in fixed)
        for index in range(outs[planes].shape[0]):
            base = sum((index // 2**order % 2) * 2**place for order, place in enumerate(free))
            outs[planes][index] = field[base + side]

    def row_step(row, unused):
        both = jnp.concatenate([field[row, 0], field[row, 1]], axis=0)
        for block in range(half):
            whole[block, pl.ds(pl.multiple_of(row * stride, stride), stride), :] = both[
                :, block * lanes : (block + 1) * lanes
            ]
        return unused

    lax.fori_loop(0, rows, row_step, 0, unroll=8)
    for step, out in enumerate(outs[:planes]):
        source = zed[0] ^ step
        for part in range(2):
            for block in range(half):
                out[pl.ds(part * half + block, rows, stride=2 * half), :] = whole[
                    block, pl.ds(part * source_count + source, rows, stride=stride), :
                ]
        for note in notes:
            out[rows * 2 * half :, :] = note[...]


def pack(here, field, notes, edge_rows):
    rows, _, source_count, width = field.shape
    length = rows * 2 * half + sum(note.shape[0] for note in notes)
    whole = pl.BlockSpec(memory_space=pltpu.VMEM)
    edges = [jax.ShapeDtypeStruct((edge_rows,) + field.shape[1:], jnp.float32)] if edge_rows else []
    return pl.pallas_call(
        functools.partial(pack_kernel, source_count, len(notes)),
        out_shape=[jax.ShapeDtypeStruct((length, lanes), jnp.float32)] * planes + edges,
        in_specs=[pl.BlockSpec(memory_space=pltpu.SMEM)] * 2 + [whole] * (1 + len(notes)),
        out_specs=[whole] * (planes + len(edges)),
        scratch_shapes=[pltpu.VMEM((half, (rows + 1) * 2 * source_count, lanes), jnp.float32)],
        compiler_params=pltpu.CompilerParams(vmem_limit_bytes=24 * 2**20),
        name="pack_sources",
    )(*here, field, *notes)


def parts_of(word):
    return lax.shift_right_logical(word, word_bits), word & (2**word_bits - 1)


def tile(start):
    return pl.ds(pl.multiple_of(start, 2 * half), 2 * half)


def fine_kernel(plan, size, edge_size, zed, *refs):
    mains, refs = refs[:planes], refs[planes:]
    edges = refs[: planes if edge_size else 0]
    lists, refs = refs[len(edges)], refs[len(edges) + 1 :]
    table, phases, weights, out, rims, meta, field, moved, shifted, ready, landed, sems = refs
    rows, fine_rows = plan.rows, plan.fine_rows
    own = zed[0]

    def bring(step):
        return pltpu.make_async_copy(lists.at[step], meta.at[step % 2], sems.at[planes + step % 2])

    bring(0).start()
    incoming = []
    for index, edge in enumerate(edges):
        chosen = edge.at[pl.ds(0, edge_size * 2 * half)]
        incoming.append(pltpu.make_async_copy(chosen, landed.at[index], sems.at[planes + 2 + index]))
        incoming[-1].start()
    lane = lax.broadcasted_iota(jnp.int32, rims.shape, 1)
    rims[...] = ((lane < rim) | (lane >= lanes - rim)).astype(jnp.float32)

    def both(start):
        return pl.ds(pl.multiple_of(start, 4 * half), 4 * half)

    def with_turned(value):
        return jnp.concatenate([value, pltpu.roll(value, half, 0)], axis=0)

    for index, main in enumerate(mains):
        first = (own ^ (planes - 1 - index)) * size

        def main_step(row, unused, first=first, main=main):
            field[both((first + row) * 4 * half), :] = with_turned(main[tile(row * 2 * half), :])
            return unused

        lax.fori_loop(0, size, main_step, 0, unroll=8)
    for index in range(len(edges)):
        first = planes * size + (own ^ index) * edge_size
        incoming[index].wait()

        def edge_step(row, unused, first=first, index=index):
            field[both((first + row) * 4 * half), :] = with_turned(landed[index, tile(row * 2 * half), :])
            return unused

        lax.fori_loop(0, edge_size, edge_step, 0, unroll=8)
    field[both(planes * (size + edge_size) * 4 * half), :] = jnp.zeros((4 * half, lanes), jnp.float32)

    blank = jnp.zeros((2 * half, lanes), jnp.float32)
    sub = lax.broadcasted_iota(jnp.int32, (2 * half, lanes), 0)
    dest_count = out.shape[1]
    dest_rows = fine_rows // dest_count

    def plane_step(turn, unused):
        plane = own ^ turn
        slot = turn % 2
        bring(turn).wait()

        @pl.when(turn + 1 < planes)
        def _():
            bring(turn + 1).start()

        across = lanes // plan.width

        def boxes_step(slot_count, step, unused):
            ranks = [step * plan.together + each for each in range(plan.together)]
            boxes = [meta[slot, plan.order, rank] for rank in ranks]
            sums = [[blank, blank] for box in boxes]
            for pair in range(slot_count):
                for each in range(plan.together):
                    row = step * (plan.together // across) + each // across
                    place, kind = parts_of(meta[slot, row, each % across * plan.width + pair])
                    value = field[both(place), :]
                    factor = table[tile(kind), :]
                    sums[each][0] += factor * value[: 2 * half]
                    sums[each][1] += factor * value[2 * half :]
            for each in range(plan.together):
                straight, crossed = sums[each]
                total = jnp.where(
                    sub < half,
                    straight + pltpu.roll(straight, half, 0),
                    pltpu.roll(crossed, half, 0) - crossed,
                )
                moved[both(boxes[each] * 4 * half), :] = with_turned(total)
            return unused

        start = 0
        for more in reversed(range((plan.slots - plan.fixed) // plan.group + 1)):
            end = meta[slot, plan.order, plan.turns + more]
            lax.fori_loop(start, end, functools.partial(boxes_step, plan.fixed + more * plan.group), 0)
            start = end

        def fine_step(block, unused):
            for each in range(lanes):
                parent, octant = parts_of(meta[slot, plan.parent + block, each])
                value = moved[both(parent), :] * phases[both(octant), :]
                shifted[tile((block * lanes + each) * 2 * half), :] = value[: 2 * half] + value[2 * half :]
            return unused

        lax.fori_loop(0, fine_rows // lanes, fine_step, 0)
        width = ready.shape[3]
        spill = jnp.zeros((fine_rows, lanes), jnp.float32)
        for part in range(2):
            left = jnp.concatenate(
                [
                    shifted[pl.ds(part * half + block, fine_rows, stride=2 * half), :]
                    for block in range(half)
                ],
                axis=1,
            )
            first, second = split(left)
            result = jnp.dot(
                jnp.concatenate([first, first, second], axis=1), weights[...], preferred_element_type=jnp.float32
            )
            for dest in range(dest_count):
                ready[plane, dest, part * dest_rows : (part + 1) * dest_rows, :] = result[
                    dest * dest_rows : (dest + 1) * dest_rows, :width
                ]
            over = result[:, width:]
            spill = spill + (pltpu.roll(over, half, 1) if part else over)
        spill = spill.T[: 2 * half]
        for dest in range(dest_count):
            ready[plane, dest, 2 * dest_rows :, :] = jnp.concatenate(
                [
                    spill[:, dest * dest_rows : (dest + 1) * dest_rows],
                    jnp.zeros((2 * half, width - dest_rows), jnp.float32),
                ],
                axis=1,
            )
        pltpu.make_async_copy(ready.at[plane], out.at[plane], sems.at[plane]).start()
        return unused

    lax.fori_loop(0, planes, plane_step, 0)
    for plane in range(planes):
        pltpu.make_async_copy(ready.at[plane], out.at[plane], sems.at[plane]).wait()


def join_kernel(source_count, parts, rims, out, whole):
    dest_rows = out.shape[0]
    dirs = parts.shape[0] // source_count
    over = jnp.concatenate(
        [parts[index, 2 * dest_rows :, :lanes] for index in range(parts.shape[0])], axis=0
    ).T[:dest_rows]
    low = lax.broadcasted_iota(jnp.int32, (dest_rows, lanes), 1) < rim
    at_rim = jnp.broadcast_to(rims[...], (dest_rows, lanes)) < 0.5
    for source in range(source_count):
        for part in range(2):
            turned = []
            for index in range(dirs):
                first = (source * dirs + index) * 2 * half + part * half
                turned.append(pltpu.roll(over, (lanes - rim - first) % lanes, 1))
            for index in range(dirs):
                fix = jnp.where(at_rim, jnp.where(low, turned[index - 1], turned[(index + 1) % dirs]), 0.0)
                whole[
                    index, pl.ds(part * source_count + source, dest_rows, stride=2 * source_count), :
                ] = parts[source * dirs + index, part * dest_rows : (part + 1) * dest_rows, :] + fix

    def row_step(row, unused):
        start = pl.multiple_of(row * 2 * source_count, 2 * source_count)
        both = jnp.concatenate(
            [whole[index, pl.ds(start, 2 * source_count), :] for index in range(dirs)], axis=1
        )
        out[row, 0] = both[:source_count]
        out[row, 1] = both[source_count:]
        return unused

    lax.fori_loop(0, dest_rows, row_step, 0, unroll=8)


def per_device(
    coarse_field,
    trans_table,
    partner_ids,
    partner_types,
    partner_count,
    child_count,
    child_octant,
    dir_angles,
    stencil_ids,
    stencil_weights,
):
    rows, _, source_count, kc_dev = coarse_field.shape
    slots = partner_ids.shape[1]
    type_count = trans_table.shape[0]
    fine_rows = child_octant.shape[0]
    ring_count = lax.axis_size("ring")
    dir_count = lax.axis_size("dir")
    zed = lax.axis_index("zed")
    ring = lax.axis_index("ring")
    dir_index = lax.axis_index("dir")
    fine_count = stencil_ids.shape[0] // 4
    kf_dev = fine_count // dir_count
    kc_pad = up(kc_dev, half * lanes)
    kf_pad = up(kf_dev, lanes)
    pad_dirs = kc_pad - kc_dev
    assert source_count == planes and kc_pad == half * lanes
    dest_rows = fine_rows // dir_count

    field = jnp.pad(coarse_field, ((0, 0), (0, 0), (0, 0), (0, pad_dirs)))
    here = zed.reshape(1), ring.reshape(1)
    edge_rows = rows >> len(edge_bits(rows)[1]) if ring_count == 2 else 0
    packed = pack(here, field, [], edge_rows)
    if edge_rows:
        edges = lax.ppermute(packed[planes], "ring", [(0, 1), (1, 0)])

    def to_planes(note, step):
        if step == 0:
            return note
        return lax.ppermute(note, "zed", [(plane, plane ^ step) for plane in range(planes)])

    arrived = [to_planes(packed[step], step) for step in (3, 2, 1, 0)]

    plane_of = partner_ids // (ring_count * rows)
    ring_of = partner_ids // rows % ring_count
    local = partner_ids % rows
    live = jnp.arange(slots, dtype=jnp.int32)[None, :] < partner_count[:, None]
    if ring_count == 2:
        size = rows
        place = jnp.where(
            ring_of == ring,
            plane_of * rows + local,
            planes * rows + plane_of * edge_rows + edge_rank(local, rows),
        )
    else:
        size = ring_count * rows
        place = partner_ids
    field_rows = planes * (size + edge_rows)
    place = jnp.where(live, place, field_rows)
    together = 4
    fixed = slots // 2
    group = 3 if (slots - fixed) % 3 == 0 else 1
    index = jnp.arange(rows, dtype=jnp.int32)
    before = (partner_count[None, :] > partner_count[:, None]) | (
        (partner_count[None, :] == partner_count[:, None]) & (index[None, :] < index[:, None])
    )
    rank = jnp.sum(before.astype(jnp.int32), axis=1)
    at_rank = rank[None, :] == index[:, None]
    order = jnp.sum(jnp.where(at_rank, index[None, :], 0), axis=1)
    first = rank[None, :] == index[: rows // together, None] * together
    longest = jnp.sum(jnp.where(first, partner_count[None, :], 0), axis=1)
    turns = jnp.maximum((longest - fixed + group - 1) // group, 0)
    more = jnp.arange((slots - fixed) // group + 1, dtype=jnp.int32)
    ends = jnp.sum((turns[None, :] >= more[:, None]).astype(jnp.int32), axis=1)
    bounds = jnp.sum(jnp.where(index[None, :] <= index[:, None], child_count[None, :], 0), axis=1)
    parent = jnp.sum(
        (bounds[None, :] <= jnp.arange(fine_rows, dtype=jnp.int32)[:, None]).astype(jnp.int32), axis=1
    )
    def across(one, width=lanes):
        return jnp.pad(one, ((0, 0), (0, width - one.shape[1])))

    width = lanes // half
    turns_at = lanes // 2
    assert slots <= width and rows <= turns_at and fine_rows % lanes == 0
    assert (field_rows + 1) * 4 * half < 2 ** (31 - word_bits) and type_count * 2 * half < 2**word_bits

    in_order = jnp.dot(
        at_rank.astype(jnp.float32),
        jnp.concatenate([across(place * 4 * half, width), across(partner_types * 2 * half, width)], axis=1).astype(
            jnp.float32
        ),
        precision=lax.Precision.HIGHEST,
        preferred_element_type=jnp.float32,
    )

    def listed(side):
        return in_order[:, side * width : (side + 1) * width].reshape(rows * width // lanes, lanes)

    list_rows = rows * width // lanes
    fine_lists = fine_rows // lanes
    last = across(jnp.concatenate([across(order[None], turns_at), ends[None]], axis=1))
    stride = up(list_rows + fine_lists + 1, 8)

    def stacked(*parts):
        meta = jnp.concatenate([part.astype(jnp.float32) for part in parts])
        return jnp.pad(meta, ((0, stride - meta.shape[0]), (0, 0)))

    meta = jnp.concatenate(
        [
            stacked(listed(0), (parent * 4 * half).reshape(-1, lanes)),
            stacked(listed(1), (child_octant * 4 * half).reshape(-1, lanes), last),
        ]
    )
    plan = Plan(
        rows, slots, fine_rows, stride, width, list_rows, list_rows + fine_lists, turns_at, together, fixed, group
    )

    notes = pack(here, edges, [meta], 0) if edge_rows else [meta] * planes
    after_notes = lax.optimization_barrier((notes, trans_table, dir_angles, stencil_ids, stencil_weights))
    notes, trans_table, dir_angles, stencil_ids, stencil_weights = after_notes
    received = [to_planes(notes[step], step) for step in range(planes)]
    edge_part = edge_rows * 2 * half
    numbers = jnp.stack([note[edge_part:] for note in received]).astype(jnp.int32)
    meta = numbers[:, :stride] * 2**word_bits + numbers[:, stride:]
    if ring_count != 2:
        arrived = [lax.all_gather(one, "ring", axis=0, tiled=True) for one in arrived]
        received = []

    def blocks(table):
        return jnp.pad(table, ((0, 0), (0, pad_dirs))).reshape(-1, half, lanes)

    def doubled(table, sign):
        return jnp.concatenate([blocks(table), sign * blocks(table)], axis=1)

    table = jnp.pad(trans_table, ((0, 0), (0, 0), (0, pad_dirs))).reshape(-1, lanes)
    angles = lax.dynamic_slice_in_dim(dir_angles, dir_index * kc_dev, kc_dev, axis=1)
    octants = jnp.arange(8, dtype=jnp.int32)
    sign_x = 1.0 - 2.0 * (octants % 2).astype(jnp.float32)
    sign_y = 1.0 - 2.0 * (octants // 2 % 2).astype(jnp.float32)
    sign_z = 1.0 - 2.0 * (octants // 4).astype(jnp.float32)
    unit_x = jnp.sin(angles[0]) * jnp.cos(angles[1])
    unit_y = jnp.sin(angles[0]) * jnp.sin(angles[1])
    unit_z = jnp.cos(angles[0])
    phase = wave_scale * (
        sign_x[:, None] * unit_x[None, :] + sign_y[:, None] * unit_y[None, :] + sign_z[:, None] * unit_z[None, :]
    )
    phases = jnp.concatenate(
        [doubled(jnp.cos(phase), 1.0), doubled(jnp.sin(phase), -1.0)], axis=1
    ).reshape(-1, lanes)

    ids = lax.dynamic_slice_in_dim(stencil_ids, dir_index * kc_dev, kc_dev, axis=0).T
    weights = lax.dynamic_slice_in_dim(stencil_weights, dir_index * kc_dev, kc_dev, axis=0).T

    def interp(targets):
        matrix = jnp.zeros((targets.shape[0], kc_dev), jnp.float32)
        for point in range(ids.shape[0]):
            matrix = matrix + jnp.where(
                ids[point][None, :] == targets[:, None], weights[point][None, :], 0.0
            )
        return jnp.pad(matrix, ((0, 0), (0, pad_dirs)))

    first_fine = dir_index * kf_dev
    own = jnp.arange(kf_dev, dtype=jnp.int32)
    outside = jnp.concatenate(
        [jnp.arange(-rim, 0, dtype=jnp.int32), jnp.arange(kf_dev, kf_dev + rim, dtype=jnp.int32)]
    )
    matrix = jnp.pad(interp(first_fine + own), ((0, kf_pad - kf_dev), (0, 0)))
    spill = interp((first_fine + outside) % fine_count)
    matrices = jnp.concatenate([matrix, jnp.pad(spill, ((0, lanes - half), (0, 0)))], axis=0).T
    rounded = lax.reduce_precision(matrices, 8, 7)
    high = rounded.astype(jnp.bfloat16)
    low = (matrices - rounded).astype(jnp.bfloat16)
    passes = jnp.concatenate([high, low, high], axis=0)

    whole = pl.BlockSpec(memory_space=pltpu.VMEM)
    message = (2 * dest_rows + 2 * half, kf_pad)
    local_fine, rims = pl.pallas_call(
        functools.partial(fine_kernel, plan, size, edge_rows),
        out_shape=[
            pltpu.HBM((planes, dir_count) + message, jnp.float32),
            jax.ShapeDtypeStruct((2 * half, lanes), jnp.float32),
        ],
        in_specs=[pl.BlockSpec(memory_space=pltpu.SMEM)]
        + [whole] * planes
        + [pl.BlockSpec(memory_space=pl.ANY)] * (len(received) + 1)
        + [whole] * 3,
        out_specs=[pl.BlockSpec(memory_space=pltpu.HBM), whole],
        scratch_shapes=[
            pltpu.SMEM((2, plan.stride, lanes), jnp.int32),
            pltpu.VMEM(((field_rows + 1) * 4 * half, lanes), jnp.float32),
            pltpu.VMEM((rows * 4 * half, lanes), jnp.float32),
            pltpu.VMEM(((fine_rows + 1) * 2 * half, lanes), jnp.float32),
            pltpu.VMEM((planes, dir_count) + message, jnp.float32),
            pltpu.VMEM((planes, max(edge_rows, 1) * 2 * half, lanes), jnp.float32),
            pltpu.SemaphoreType.DMA((2 * planes + 2,)),
        ],
        compiler_params=pltpu.CompilerParams(vmem_limit_bytes=24 * 2**20),
        name="translate_and_interpolate",
    )(here[0], *arrived, *received, meta, table, phases, passes)

    parts = lax.all_to_all(
        local_fine.reshape((planes * dir_count,) + message),
        ("zed", "dir"),
        split_axis=0,
        concat_axis=0,
        tiled=True,
    )
    result = (dest_rows, 2, source_count, fine_count)
    if kf_dev == lanes and planes * dir_count * 2 * half == lanes and dest_rows <= lanes:
        return pl.pallas_call(
            functools.partial(join_kernel, source_count),
            out_shape=jax.ShapeDtypeStruct(result, jnp.float32),
            in_specs=[whole] * 2,
            out_specs=whole,
            scratch_shapes=[pltpu.VMEM((dir_count, (dest_rows + 1) * 2 * source_count, lanes), jnp.float32)],
            compiler_params=pltpu.CompilerParams(vmem_limit_bytes=24 * 2**20),
            name="join_parts",
        )(parts, 1.0 - rims[:1])
    parts = parts.reshape((planes, dir_count) + message)
    main = parts[:, :, : 2 * dest_rows, :kf_dev].reshape(planes, dir_count, 2, dest_rows, kf_dev)
    over = parts[:, :, 2 * dest_rows :, :dest_rows].reshape(planes, dir_count, 2, 2 * rim, dest_rows)
    low = jnp.roll(over[:, :, :, :rim], -1, axis=1)
    high = jnp.roll(over[:, :, :, rim:], 1, axis=1)
    middle = jnp.zeros((planes, dir_count, 2, kf_dev - 2 * rim, dest_rows), jnp.float32)
    fix = jnp.concatenate([high, middle, low], axis=3)
    total = main.transpose(3, 2, 0, 1, 4) + fix.transpose(4, 2, 0, 1, 3)
    return total.reshape(result)


def solution(mesh):
    boxes, dirs = mesh.shape["box"], mesh.shape["dir"]
    fine_mesh = Mesh(mesh.devices.reshape(planes, boxes // planes, dirs), ("zed", "ring", "dir"))
    box = ("zed", "ring")
    placed = (
        P(box, None, None, "dir"),
        P(None, None, "dir"),
        P(box, None),
        P(box, None),
        P(box),
        P(box),
        P(box),
        P(),
        P(),
        P(),
    )
    return jax.shard_map(
        per_device,
        mesh=fine_mesh,
        in_specs=placed,
        out_specs=P(("zed", "ring", "dir"), None, None, None),
        check_vma=False,
    )
```

```python
import collections
import functools

import jax
import jax.numpy as jnp
from jax import lax
from jax.experimental import pallas as pl
from jax.experimental.pallas import tpu as pltpu
from jax.sharding import Mesh
from jax.sharding import PartitionSpec as P

wave_scale = 3.0
planes = 4
lanes = 128
half = 4
rim = 2
word_bits = 13


plan_fields = ["rows", "slots", "fine_rows", "stride", "width", "parent", "order", "turns"]
Plan = collections.namedtuple("Plan", plan_fields + ["together", "fixed", "group"])


def up(size, step):
    return -(-size // step) * step


def edge_bits(rows):
    bits = rows.bit_length() - 1
    return bits, [place for place in range(2, bits) if place % 2 == bits % 2]


def edge_rank(local, rows):
    bits, fixed = edge_bits(rows)
    rank = jnp.zeros_like(local)
    taken = 0
    for place in range(bits):
        if place not in fixed:
            rank = rank + (local // 2**place % 2) * 2**taken
            taken += 1
    return rank


def split(value):
    high = value.astype(jnp.bfloat16)
    low = (value - high.astype(jnp.float32)).astype(jnp.bfloat16)
    return high, low


def pack_kernel(source_count, note_count, zed, ring, field, *refs):
    notes, outs, whole = refs[:note_count], refs[note_count:-1], refs[-1]
    rows = field.shape[0]
    stride = 2 * source_count
    if len(outs) > planes:
        bits, fixed = edge_bits(rows)
        free = [place for place in range(bits) if place not in fixed]
        side = (1 - ring[0]) * sum(2**place for place in fixed)
        for index in range(outs[planes].shape[0]):
            base = sum((index // 2**order % 2) * 2**place for order, place in enumerate(free))
            outs[planes][index] = field[base + side]

    def row_step(row, unused):
        both = jnp.concatenate([field[row, 0], field[row, 1]], axis=0)
        for block in range(half):
            whole[block, pl.ds(pl.multiple_of(row * stride, stride), stride), :] = both[
                :, block * lanes : (block + 1) * lanes
            ]
        return unused

    lax.fori_loop(0, rows, row_step, 0, unroll=8)
    for step, out in enumerate(outs[:planes]):
        source = zed[0] ^ step
        for part in range(2):
            for block in range(half):
                out[pl.ds(part * half + block, rows, stride=2 * half), :] = whole[
                    block, pl.ds(part * source_count + source, rows, stride=stride), :
                ]
        for note in notes:
            out[rows * 2 * half :, :] = note[...]


def pack(here, field, notes, edge_rows):
    rows, _, source_count, width = field.shape
    length = rows * 2 * half + sum(note.shape[0] for note in notes)
    whole = pl.BlockSpec(memory_space=pltpu.VMEM)
    edges = [jax.ShapeDtypeStruct((edge_rows,) + field.shape[1:], jnp.float32)] if edge_rows else []
    return pl.pallas_call(
        functools.partial(pack_kernel, source_count, len(notes)),
        out_shape=[jax.ShapeDtypeStruct((length, lanes), jnp.float32)] * planes + edges,
        in_specs=[pl.BlockSpec(memory_space=pltpu.SMEM)] * 2 + [whole] * (1 + len(notes)),
        out_specs=[whole] * (planes + len(edges)),
        scratch_shapes=[pltpu.VMEM((half, (rows + 1) * 2 * source_count, lanes), jnp.float32)],
        compiler_params=pltpu.CompilerParams(vmem_limit_bytes=24 * 2**20),
        name="pack_sources",
    )(*here, field, *notes)


def parts_of(word):
    return lax.shift_right_logical(word, word_bits), word & (2**word_bits - 1)


def tile(start):
    return pl.ds(pl.multiple_of(start, 2 * half), 2 * half)


def fine_kernel(plan, size, edge_size, zed, *refs):
    mains, refs = refs[:planes], refs[planes:]
    edges = refs[: planes if edge_size else 0]
    lists, refs = refs[len(edges)], refs[len(edges) + 1 :]
    table, phases, weights, out, rims, meta, field, moved, shifted, ready, landed, sems = refs
    rows, fine_rows = plan.rows, plan.fine_rows
    own = zed[0]

    def bring(step):
        return pltpu.make_async_copy(lists.at[step], meta.at[step % 2], sems.at[planes + step % 2])

    bring(0).start()
    incoming = []
    for index, edge in enumerate(edges):
        chosen = edge.at[pl.ds(0, edge_size * 2 * half)]
        incoming.append(pltpu.make_async_copy(chosen, landed.at[index], sems.at[planes + 2 + index]))
        incoming[-1].start()
    lane = lax.broadcasted_iota(jnp.int32, rims.shape, 1)
    rims[...] = ((lane < rim) | (lane >= lanes - rim)).astype(jnp.float32)

    def both(start):
        return pl.ds(pl.multiple_of(start, 4 * half), 4 * half)

    def with_turned(value):
        return jnp.concatenate([value, pltpu.roll(value, half, 0)], axis=0)

    for index, main in enumerate(mains):
        first = (own ^ (planes - 1 - index)) * size

        def main_step(row, unused, first=first, main=main):
            field[both((first + row) * 4 * half), :] = with_turned(main[tile(row * 2 * half), :])
            return unused

        lax.fori_loop(0, size, main_step, 0, unroll=8)
    for index in range(len(edges)):
        first = planes * size + (own ^ index) * edge_size
        incoming[index].wait()

        def edge_step(row, unused, first=first, index=index):
            field[both((first + row) * 4 * half), :] = with_turned(landed[index, tile(row * 2 * half), :])
            return unused

        lax.fori_loop(0, edge_size, edge_step, 0, unroll=8)
    field[both(planes * (size + edge_size) * 4 * half), :] = jnp.zeros((4 * half, lanes), jnp.float32)

    blank = jnp.zeros((2 * half, lanes), jnp.float32)
    sub = lax.broadcasted_iota(jnp.int32, (2 * half, lanes), 0)
    dest_count = out.shape[1]
    dest_rows = fine_rows // dest_count

    def plane_step(turn, unused):
        plane = own ^ turn
        slot = turn % 2
        bring(turn).wait()

        @pl.when(turn + 1 < planes)
        def _():
            bring(turn + 1).start()

        across = lanes // plan.width

        def boxes_step(slot_count, step, unused):
            ranks = [step * plan.together + each for each in range(plan.together)]
            boxes = [meta[slot, plan.order, rank] for rank in ranks]
            sums = [[blank, blank] for box in boxes]
            for pair in range(slot_count):
                for each in range(plan.together):
                    row = step * (plan.together // across) + each // across
                    place, kind = parts_of(meta[slot, row, each % across * plan.width + pair])
                    value = field[both(place), :]
                    factor = table[tile(kind), :]
                    sums[each][0] += factor * value[: 2 * half]
                    sums[each][1] += factor * value[2 * half :]
            for each in range(plan.together):
                straight, crossed = sums[each]
                total = jnp.where(
                    sub < half,
                    straight + pltpu.roll(straight, half, 0),
                    pltpu.roll(crossed, half, 0) - crossed,
                )
                moved[both(boxes[each] * 4 * half), :] = with_turned(total)
            return unused

        start = 0
        for more in reversed(range((plan.slots - plan.fixed) // plan.group + 1)):
            end = meta[slot, plan.order, plan.turns + more]
            lax.fori_loop(start, end, functools.partial(boxes_step, plan.fixed + more * plan.group), 0)
            start = end

        def fine_step(block, unused):
            for each in range(lanes):
                parent, octant = parts_of(meta[slot, plan.parent + block, each])
                value = moved[both(parent), :] * phases[both(octant), :]
                shifted[tile((block * lanes + each) * 2 * half), :] = value[: 2 * half] + value[2 * half :]
            return unused

        lax.fori_loop(0, fine_rows // lanes, fine_step, 0)
        width = ready.shape[3]
        chunk_rows = fine_rows // 2
        spills = [jnp.zeros((chunk_rows, lanes), jnp.float32)] * 2
        for chunk in range(2):
            for part in range(2):
                begin = chunk * chunk_rows * 2 * half + part * half
                left = jnp.concatenate(
                    [shifted[pl.ds(begin + block, chunk_rows, stride=2 * half), :] for block in range(half)],
                    axis=1,
                )
                first, second = split(left)
                result = jnp.dot(
                    jnp.concatenate([first, first, second], axis=1),
                    weights[...],
                    preferred_element_type=jnp.float32,
                )
                for dest in range(dest_count // 2):
                    ready[
                        plane, chunk * dest_count // 2 + dest, part * dest_rows : (part + 1) * dest_rows, :
                    ] = result[dest * dest_rows : (dest + 1) * dest_rows, :width]
                over = result[:, width:]
                spills[chunk] = spills[chunk] + (pltpu.roll(over, half, 1) if part else over)
        spill = jnp.concatenate(spills, axis=0)
        spill = spill.T[: 2 * half]
        for dest in range(dest_count):
            ready[plane, dest, 2 * dest_rows :, :] = jnp.concatenate(
                [
                    spill[:, dest * dest_rows : (dest + 1) * dest_rows],
                    jnp.zeros((2 * half, width - dest_rows), jnp.float32),
                ],
                axis=1,
            )
        pltpu.make_async_copy(ready.at[plane], out.at[plane], sems.at[plane]).start()
        return unused

    lax.fori_loop(0, planes, plane_step, 0)
    for plane in range(planes):
        pltpu.make_async_copy(ready.at[plane], out.at[plane], sems.at[plane]).wait()


def join_kernel(source_count, parts, rims, out, whole):
    dest_rows = out.shape[0]
    dirs = parts.shape[0] // source_count
    over = jnp.concatenate(
        [parts[index, 2 * dest_rows :, :lanes] for index in range(parts.shape[0])], axis=0
    ).T[:dest_rows]
    low = lax.broadcasted_iota(jnp.int32, (dest_rows, lanes), 1) < rim
    at_rim = jnp.broadcast_to(rims[...], (dest_rows, lanes)) < 0.5
    for source in range(source_count):
        for part in range(2):
            turned = []
            for index in range(dirs):
                first = (source * dirs + index) * 2 * half + part * half
                turned.append(pltpu.roll(over, (lanes - rim - first) % lanes, 1))
            for index in range(dirs):
                fix = jnp.where(at_rim, jnp.where(low, turned[index - 1], turned[(index + 1) % dirs]), 0.0)
                whole[
                    index, pl.ds(part * source_count + source, dest_rows, stride=2 * source_count), :
                ] = parts[source * dirs + index, part * dest_rows : (part + 1) * dest_rows, :] + fix

    def row_step(row, unused):
        start = pl.multiple_of(row * 2 * source_count, 2 * source_count)
        both = jnp.concatenate(
            [whole[index, pl.ds(start, 2 * source_count), :] for index in range(dirs)], axis=1
        )
        out[row, 0] = both[:source_count]
        out[row, 1] = both[source_count:]
        return unused

    lax.fori_loop(0, dest_rows, row_step, 0, unroll=8)


def per_device(
    coarse_field,
    trans_table,
    partner_ids,
    partner_types,
    partner_count,
    child_count,
    child_octant,
    dir_angles,
    stencil_ids,
    stencil_weights,
):
    rows, _, source_count, kc_dev = coarse_field.shape
    slots = partner_ids.shape[1]
    type_count = trans_table.shape[0]
    fine_rows = child_octant.shape[0]
    ring_count = lax.axis_size("ring")
    dir_count = lax.axis_size("dir")
    zed = lax.axis_index("zed")
    ring = lax.axis_index("ring")
    dir_index = lax.axis_index("dir")
    fine_count = stencil_ids.shape[0] // 4
    kf_dev = fine_count // dir_count
    kc_pad = up(kc_dev, half * lanes)
    kf_pad = up(kf_dev, lanes)
    pad_dirs = kc_pad - kc_dev
    assert source_count == planes and kc_pad == half * lanes
    dest_rows = fine_rows // dir_count

    field = jnp.pad(coarse_field, ((0, 0), (0, 0), (0, 0), (0, pad_dirs)))
    here = zed.reshape(1), ring.reshape(1)
    edge_rows = rows >> len(edge_bits(rows)[1]) if ring_count == 2 else 0
    packed = pack(here, field, [], edge_rows)
    if edge_rows:
        edges = lax.ppermute(packed[planes], "ring", [(0, 1), (1, 0)])

    def to_planes(note, step):
        if step == 0:
            return note
        return lax.ppermute(note, "zed", [(plane, plane ^ step) for plane in range(planes)])

    arrived = [to_planes(packed[step], step) for step in (3, 2, 1, 0)]

    plane_of = partner_ids // (ring_count * rows)
    ring_of = partner_ids // rows % ring_count
    local = partner_ids % rows
    live = jnp.arange(slots, dtype=jnp.int32)[None, :] < partner_count[:, None]
    if ring_count == 2:
        size = rows
        place = jnp.where(
            ring_of == ring,
            plane_of * rows + local,
            planes * rows + plane_of * edge_rows + edge_rank(local, rows),
        )
    else:
        size = ring_count * rows
        place = partner_ids
    field_rows = planes * (size + edge_rows)
    place = jnp.where(live, place, field_rows)
    together = 4
    fixed = slots // 2
    group = 3 if (slots - fixed) % 3 == 0 else 1
    index = jnp.arange(rows, dtype=jnp.int32)
    before = (partner_count[None, :] > partner_count[:, None]) | (
        (partner_count[None, :] == partner_count[:, None]) & (index[None, :] < index[:, None])
    )
    rank = jnp.sum(before.astype(jnp.int32), axis=1)
    at_rank = rank[None, :] == index[:, None]
    order = jnp.sum(jnp.where(at_rank, index[None, :], 0), axis=1)
    first = rank[None, :] == index[: rows // together, None] * together
    longest = jnp.sum(jnp.where(first, partner_count[None, :], 0), axis=1)
    turns = jnp.maximum((longest - fixed + group - 1) // group, 0)
    more = jnp.arange((slots - fixed) // group + 1, dtype=jnp.int32)
    ends = jnp.sum((turns[None, :] >= more[:, None]).astype(jnp.int32), axis=1)
    bounds = jnp.sum(jnp.where(index[None, :] <= index[:, None], child_count[None, :], 0), axis=1)
    parent = jnp.sum(
        (bounds[None, :] <= jnp.arange(fine_rows, dtype=jnp.int32)[:, None]).astype(jnp.int32), axis=1
    )
    def across(one, width=lanes):
        return jnp.pad(one, ((0, 0), (0, width - one.shape[1])))

    width = lanes // half
    turns_at = lanes // 2
    assert slots <= width and rows <= turns_at and fine_rows % lanes == 0
    assert (field_rows + 1) * 4 * half < 2 ** (31 - word_bits) and type_count * 2 * half < 2**word_bits

    in_order = jnp.dot(
        at_rank.astype(jnp.float32),
        jnp.concatenate([across(place * 4 * half, width), across(partner_types * 2 * half, width)], axis=1).astype(
            jnp.float32
        ),
        precision=lax.Precision.HIGHEST,
        preferred_element_type=jnp.float32,
    )

    def listed(side):
        return in_order[:, side * width : (side + 1) * width].reshape(rows * width // lanes, lanes)

    list_rows = rows * width // lanes
    fine_lists = fine_rows // lanes
    last = across(jnp.concatenate([across(order[None], turns_at), ends[None]], axis=1))
    stride = up(list_rows + fine_lists + 1, 8)

    def stacked(*parts):
        meta = jnp.concatenate([part.astype(jnp.float32) for part in parts])
        return jnp.pad(meta, ((0, stride - meta.shape[0]), (0, 0)))

    meta = jnp.concatenate(
        [
            stacked(listed(0), (parent * 4 * half).reshape(-1, lanes)),
            stacked(listed(1), (child_octant * 4 * half).reshape(-1, lanes), last),
        ]
    )
    plan = Plan(
        rows, slots, fine_rows, stride, width, list_rows, list_rows + fine_lists, turns_at, together, fixed, group
    )

    notes = pack(here, edges, [meta], 0) if edge_rows else [meta] * planes
    after_notes = lax.optimization_barrier((notes, trans_table, dir_angles, stencil_ids, stencil_weights))
    notes, trans_table, dir_angles, stencil_ids, stencil_weights = after_notes
    received = [to_planes(notes[step], step) for step in range(planes)]
    edge_part = edge_rows * 2 * half
    numbers = jnp.stack([note[edge_part:] for note in received]).astype(jnp.int32)
    meta = numbers[:, :stride] * 2**word_bits + numbers[:, stride:]
    if ring_count != 2:
        arrived = [lax.all_gather(one, "ring", axis=0, tiled=True) for one in arrived]
        received = []

    def blocks(table):
        return jnp.pad(table, ((0, 0), (0, pad_dirs))).reshape(-1, half, lanes)

    def doubled(table, sign):
        return jnp.concatenate([blocks(table), sign * blocks(table)], axis=1)

    table = jnp.pad(trans_table, ((0, 0), (0, 0), (0, pad_dirs))).reshape(-1, lanes)
    angles = lax.dynamic_slice_in_dim(dir_angles, dir_index * kc_dev, kc_dev, axis=1)
    octants = jnp.arange(8, dtype=jnp.int32)
    sign_x = 1.0 - 2.0 * (octants % 2).astype(jnp.float32)
    sign_y = 1.0 - 2.0 * (octants // 2 % 2).astype(jnp.float32)
    sign_z = 1.0 - 2.0 * (octants // 4).astype(jnp.float32)
    unit_x = jnp.sin(angles[0]) * jnp.cos(angles[1])
    unit_y = jnp.sin(angles[0]) * jnp.sin(angles[1])
    unit_z = jnp.cos(angles[0])
    phase = wave_scale * (
        sign_x[:, None] * unit_x[None, :] + sign_y[:, None] * unit_y[None, :] + sign_z[:, None] * unit_z[None, :]
    )
    phases = jnp.concatenate(
        [doubled(jnp.cos(phase), 1.0), doubled(jnp.sin(phase), -1.0)], axis=1
    ).reshape(-1, lanes)

    ids = lax.dynamic_slice_in_dim(stencil_ids, dir_index * kc_dev, kc_dev, axis=0).T
    weights = lax.dynamic_slice_in_dim(stencil_weights, dir_index * kc_dev, kc_dev, axis=0).T

    def interp(targets):
        matrix = jnp.zeros((targets.shape[0], kc_dev), jnp.float32)
        for point in range(ids.shape[0]):
            matrix = matrix + jnp.where(
                ids[point][None, :] == targets[:, None], weights[point][None, :], 0.0
            )
        return jnp.pad(matrix, ((0, 0), (0, pad_dirs)))

    first_fine = dir_index * kf_dev
    own = jnp.arange(kf_dev, dtype=jnp.int32)
    outside = jnp.concatenate(
        [jnp.arange(-rim, 0, dtype=jnp.int32), jnp.arange(kf_dev, kf_dev + rim, dtype=jnp.int32)]
    )
    matrix = jnp.pad(interp(first_fine + own), ((0, kf_pad - kf_dev), (0, 0)))
    spill = interp((first_fine + outside) % fine_count)
    matrices = jnp.concatenate([matrix, jnp.pad(spill, ((0, lanes - half), (0, 0)))], axis=0).T
    rounded = lax.reduce_precision(matrices, 8, 7)
    high = rounded.astype(jnp.bfloat16)
    low = (matrices - rounded).astype(jnp.bfloat16)
    passes = jnp.concatenate([high, low, high], axis=0)

    whole = pl.BlockSpec(memory_space=pltpu.VMEM)
    message = (2 * dest_rows + 2 * half, kf_pad)
    local_fine, rims = pl.pallas_call(
        functools.partial(fine_kernel, plan, size, edge_rows),
        out_shape=[
            pltpu.HBM((planes, dir_count) + message, jnp.float32),
            jax.ShapeDtypeStruct((2 * half, lanes), jnp.float32),
        ],
        in_specs=[pl.BlockSpec(memory_space=pltpu.SMEM)]
        + [whole] * planes
        + [pl.BlockSpec(memory_space=pl.ANY)] * (len(received) + 1)
        + [whole] * 3,
        out_specs=[pl.BlockSpec(memory_space=pltpu.HBM), whole],
        scratch_shapes=[
            pltpu.SMEM((2, plan.stride, lanes), jnp.int32),
            pltpu.VMEM(((field_rows + 1) * 4 * half, lanes), jnp.float32),
            pltpu.VMEM((rows * 4 * half, lanes), jnp.float32),
            pltpu.VMEM(((fine_rows + 1) * 2 * half, lanes), jnp.float32),
            pltpu.VMEM((planes, dir_count) + message, jnp.float32),
            pltpu.VMEM((planes, max(edge_rows, 1) * 2 * half, lanes), jnp.float32),
            pltpu.SemaphoreType.DMA((2 * planes + 2,)),
        ],
        compiler_params=pltpu.CompilerParams(vmem_limit_bytes=24 * 2**20),
        name="translate_and_interpolate",
    )(here[0], *arrived, *received, meta, table, phases, passes)

    parts = lax.all_to_all(
        local_fine.reshape((planes * dir_count,) + message),
        ("zed", "dir"),
        split_axis=0,
        concat_axis=0,
        tiled=True,
    )
    result = (dest_rows, 2, source_count, fine_count)
    if kf_dev == lanes and planes * dir_count * 2 * half == lanes and dest_rows <= lanes:
        return pl.pallas_call(
            functools.partial(join_kernel, source_count),
            out_shape=jax.ShapeDtypeStruct(result, jnp.float32),
            in_specs=[whole] * 2,
            out_specs=whole,
            scratch_shapes=[pltpu.VMEM((dir_count, (dest_rows + 1) * 2 * source_count, lanes), jnp.float32)],
            compiler_params=pltpu.CompilerParams(vmem_limit_bytes=24 * 2**20),
            name="join_parts",
        )(parts, 1.0 - rims[:1])
    parts = parts.reshape((planes, dir_count) + message)
    main = parts[:, :, : 2 * dest_rows, :kf_dev].reshape(planes, dir_count, 2, dest_rows, kf_dev)
    over = parts[:, :, 2 * dest_rows :, :dest_rows].reshape(planes, dir_count, 2, 2 * rim, dest_rows)
    low = jnp.roll(over[:, :, :, :rim], -1, axis=1)
    high = jnp.roll(over[:, :, :, rim:], 1, axis=1)
    middle = jnp.zeros((planes, dir_count, 2, kf_dev - 2 * rim, dest_rows), jnp.float32)
    fix = jnp.concatenate([high, middle, low], axis=3)
    total = main.transpose(3, 2, 0, 1, 4) + fix.transpose(4, 2, 0, 1, 3)
    return total.reshape(result)


def solution(mesh):
    boxes, dirs = mesh.shape["box"], mesh.shape["dir"]
    fine_mesh = Mesh(mesh.devices.reshape(planes, boxes // planes, dirs), ("zed", "ring", "dir"))
    box = ("zed", "ring")
    placed = (
        P(box, None, None, "dir"),
        P(None, None, "dir"),
        P(box, None),
        P(box, None),
        P(box),
        P(box),
        P(box),
        P(),
        P(),
        P(),
    )
    return jax.shard_map(
        per_device,
        mesh=fine_mesh,
        in_specs=placed,
        out_specs=P(("zed", "ring", "dir"), None, None, None),
        check_vma=False,
    )
```
